32 devices in a mesh: wide: 8 (over z, x), narrow: 4 (over y, core).
Axes of the slice: x: 2, y: 2, z: 4, core: 2. Of those that a mesh axis runs over, the one named last changes fastest.
Arguments:
- tokens: bfloat16 [2, 8, 1024, 1280], P(None, 'wide', 'narrow'), may hold values from -6 to 6
- cotangent: bfloat16 [2, 8, 1024, 1280], P(None, 'wide', 'narrow'), may hold values from -6 to 6
- cell_of: int32 [16], replicated, may hold values from 0 to 15, each once
- query_count: int32 [16], replicated, may hold values from 50 to 2000
- attn_norm_gain: bfloat16 [1280], replicated, may hold values from 0.25 to 1.75
- attn_norm_bias: bfloat16 [1280], replicated, may hold values from -1.5 to 1.5
- input_weight: bfloat16 [1280, 3, 1280], P(None, None, 'narrow'), may hold values from -0.15625 to 0.15625
- query_bias: bfloat16 [1280], P('narrow'), may hold values from -1.5 to 1.5
- value_bias: bfloat16 [1280], P('narrow'), may hold values from -0.25 to 0.25
- out_weight: bfloat16 [1280, 1280], P('narrow'), may hold values from -3.5 to 3.5
- out_bias: bfloat16 [1280], replicated, may hold values from -1 to 1
- ffn_norm_gain: bfloat16 [1280], replicated, may hold values from 0.25 to 1.75
- ffn_norm_bias: bfloat16 [1280], replicated, may hold values from -1.5 to 1.5
- up_weight: bfloat16 [1280, 5120], P(None, 'narrow'), may hold values from -0.15625 to 0.15625
- up_bias: bfloat16 [5120], P('narrow'), may hold values from -1.5 to 1.5
- down_weight: bfloat16 [5120, 1280], P('narrow'), may hold values from -0.078125 to 0.078125
- down_bias: bfloat16 [1280], replicated, may hold values from -1 to 1
Outputs:
- block_out: bfloat16 [2, 8, 1024, 1280], P(None, 'wide', 'narrow')
- tokens_grad: float32 [2, 8, 1024, 1280], P(None, 'wide', 'narrow')
- attn_norm_gain_grad: float32 [1280], replicated
- attn_norm_bias_grad: float32 [1280], replicated
- input_weight_grad: float32 [1280, 3, 1280], P(None, None, 'narrow')
- query_bias_grad: float32 [1280], P('narrow')
- value_bias_grad: float32 [1280], P('narrow')
- out_weight_grad: float32 [1280, 1280], P('narrow')
- out_bias_grad: float32 [1280], replicated
- ffn_norm_gain_grad: float32 [1280], replicated
- ffn_norm_bias_grad: float32 [1280], replicated
- up_weight_grad: float32 [1280, 5120], P(None, 'narrow')
- up_bias_grad: float32 [5120], P('narrow')
- down_weight_grad: float32 [5120, 1280], P('narrow')
- down_bias_grad: float32 [1280], replicated
The draws below stay inside these ranges and needn't reach their ends.
Inputs may be any that keep to these rules, and one draw needn't show every extreme that they name: `cell_of`: each cell id stands in exactly one slot.
All inputs are finite; a program needn't handle non-finite values.
Results may differ from the reference program's by a relative error of at most 0.019.
Values may be sent and summed in bfloat16 or wider, within the bound.
No kernel may reach another device: no remote copies, remote signals or barrier semaphores. Data moves between devices by JAX's collectives and lax.ppermute only.
A program may use at most 192 MiB of HBM per device.

```python
import jax
import jax.numpy as jnp
from jax import lax

D = 1280
HEADS = 20
HEAD = 64
FF = 5120
GENES = 1024
MICRO = 2
CELLS_MB = 8
CELLS = 16


def plant(drawn, key, smallest, largest):
    dims = drawn.shape
    place = [jax.random.randint(jax.random.fold_in(key, axis), (), 0, dims[axis]) for axis in range(len(dims))]
    drawn = drawn.at[tuple(place)].set(smallest)
    longest = dims.index(max(dims))
    place[longest] = (place[longest] + 1) % dims[longest]
    return drawn.at[tuple(place)].set(largest)


def shard_levels(stream_key, dims, split, low, top_value):
    def one(dim, shards_of):
        heights = jax.random.uniform(jax.random.fold_in(jax.random.fold_in(stream_key, 6), dim), (shards_of,), jnp.float32, low / len(split), top_value / len(split))
        return jnp.repeat(jnp.exp(heights), dims[dim] // shards_of).reshape((-1,) + (1,) * (len(dims) - dim - 1))

    gain = one(*split[0])
    for cut in split[1:]:
        gain = gain * one(*cut)
    return gain


def gaussian(own_key, dims, width, bound, shards=(), held_as=jnp.bfloat16):
    entries = jax.random.normal(own_key, dims, jnp.float32) * width
    if len(shards) > 0:
        entries = shard_levels(own_key, dims, shards, -0.22, 0.18) * entries
    return jnp.clip(entries, min=-bound, max=bound).astype(held_as)


def setup_inputs(seed: int = 0) -> dict:
    keys = jax.random.split(jax.random.key(seed), 18)
    tokens = gaussian(keys[0], (MICRO, CELLS_MB, GENES, D), 1.0, 6.0, ((1, 8), (2, 4)))
    cotangent = gaussian(keys[1], (MICRO, CELLS_MB, GENES, D), 1.0, 6.0, ((1, 8), (2, 4)))
    cell_of = jax.random.permutation(keys[2], CELLS).astype(jnp.int32)
    query_count = plant(jax.random.randint(keys[3], (CELLS,), 50, 2001), jax.random.fold_in(keys[3], 1), 50, 2000).astype(jnp.int32)
    attn_norm_gain = jnp.clip(1.0 + 0.15 * jax.random.normal(keys[4], (D,), jnp.float32), 0.25, 1.75).astype(jnp.bfloat16)
    attn_norm_bias = gaussian(keys[5], (D,), 0.3, 1.5)
    input_weight = gaussian(keys[6], (D, 3, D), D ** -0.5, 0.15625, ((2, 4),))
    query_bias = gaussian(keys[7], (D,), 0.3, 1.5, ((0, 4),))
    value_bias = gaussian(keys[8], (D,), 0.05, 0.25, ((0, 4),))
    out_weight = gaussian(keys[9], (D, D), (max(3 * D // GENES, 1)) ** -0.5, 3.5, ((0, 4),))
    out_bias = gaussian(keys[10], (D,), 0.2, 1.0)
    ffn_norm_gain = jnp.clip(1.0 + 0.15 * jax.random.normal(keys[11], (D,), jnp.float32), 0.25, 1.75).astype(jnp.bfloat16)
    ffn_norm_bias = gaussian(keys[12], (D,), 0.3, 1.5)
    up_weight = gaussian(keys[13], (D, FF), D ** -0.5, 0.15625, ((1, 4),))
    up_bias = gaussian(keys[14], (FF,), 0.3, 1.5, ((0, 4),))
    down_weight = gaussian(keys[15], (FF, D), FF ** -0.5, 0.078125, ((0, 4),))
    down_bias = gaussian(keys[16], (D,), 0.2, 1.0)
    return dict(tokens=tokens, cotangent=cotangent, cell_of=cell_of, query_count=query_count, attn_norm_gain=attn_norm_gain, attn_norm_bias=attn_norm_bias, input_weight=input_weight, query_bias=query_bias, value_bias=value_bias, out_weight=out_weight, out_bias=out_bias, ffn_norm_gain=ffn_norm_gain, ffn_norm_bias=ffn_norm_bias, up_weight=up_weight, up_bias=up_bias, down_weight=down_weight, down_bias=down_bias)


norm_eps = 1e-05
score_scale = 0.125
highest = lax.Precision.HIGHEST

@jax.custom_vjp
def low(v):
    return lax.optimization_barrier(v.astype(jnp.bfloat16)).astype(jnp.float32)

@jax.custom_vjp
def low_back(v):
    return v

def low_keep(v):
    return (low(v), None)

def low_pass(kept, grad):
    return (grad,)

def back_keep(v):
    return (v, None)

def back_low(kept, grad):
    return (low(grad),)
low.defvjp(low_keep, low_pass)
low_back.defvjp(back_keep, back_low)

def layer_norm(values, gain_vec, bias_vec):
    average = lax.optimization_barrier(jnp.mean(values, axis=-1, keepdims=True))
    centred = values - average
    variance = lax.optimization_barrier(jnp.mean(centred * centred, axis=-1, keepdims=True))
    return centred * lax.rsqrt(variance + norm_eps) * gain_vec + bias_vec

def attend_block(query_block, key_rows, value_rows):
    scores = low_back(jnp.einsum('qhe,khe->hqk', query_block, key_rows, precision=highest) * score_scale)
    top_val = lax.optimization_barrier(jnp.max(scores, axis=-1, keepdims=True))
    exp_scores = jnp.exp(scores - top_val)
    weights_f = exp_scores / lax.optimization_barrier(jnp.sum(exp_scores, axis=-1, keepdims=True))
    return jnp.einsum('hqk,khe->qhe', low(weights_f), value_rows, precision=highest)

def block_forward(rows_in, params):
    attn_norm_gain, attn_norm_bias, input_weight, query_bias, value_bias, out_weight, out_bias, ffn_norm_gain, ffn_norm_bias, up_weight, up_bias, down_weight, down_bias = params
    seq_rows = rows_in.shape[0]
    normed_one = low(layer_norm(rows_in, attn_norm_gain, attn_norm_bias))
    project = jnp.einsum('sd,dje->sje', normed_one, input_weight, precision=highest)
    head_shape = (seq_rows, HEADS, HEAD)
    queries = low_back(low(project[:, 0] + query_bias)).reshape(head_shape)
    key_rows = low_back(low(project[:, 1])).reshape(head_shape)
    value_rows = low_back(low(project[:, 2] + value_bias)).reshape(head_shape)
    block_rows = min(512, seq_rows)
    query_blocks = queries.reshape(seq_rows // block_rows, block_rows, HEADS, HEAD)

    def one_block(query_block):
        return attend_block(query_block, key_rows, value_rows)
    attended = lax.map(jax.checkpoint(one_block), query_blocks).reshape(seq_rows, D)
    attended = low_back(low(attended))
    attn_out = low_back(jnp.dot(attended, out_weight, precision=highest))
    resid = rows_in + attn_out + out_bias
    normed_two = low(layer_norm(resid, ffn_norm_gain, ffn_norm_bias))
    pre_act = low_back(jnp.dot(normed_two, up_weight, precision=highest) + up_bias)
    activ = low(jax.nn.gelu(pre_act, approximate=False))
    ffn_out = low_back(jnp.dot(activ, down_weight, precision=highest))
    return resid + ffn_out + down_bias

def tree_add(first_tree, second_tree):
    return jax.tree.map(jnp.add, first_tree, second_tree)

def reference(tokens, cotangent, cell_of, query_count, attn_norm_gain, attn_norm_bias, input_weight, query_bias, value_bias, out_weight, out_bias, ffn_norm_gain, ffn_norm_bias, up_weight, up_bias, down_weight, down_bias):
    params = tuple((weight_arr.astype(jnp.float32) for weight_arr in (attn_norm_gain, attn_norm_bias, input_weight, query_bias, value_bias, out_weight, out_bias, ffn_norm_gain, ffn_norm_bias, up_weight, up_bias, down_weight, down_bias)))
    cell_total = tokens.shape[0] * tokens.shape[1]
    cell_rows = tokens.reshape(cell_total, GENES, D)
    cell_cot = cotangent.reshape(cell_total, GENES, D)
    cell_scale = jnp.sqrt(query_count[cell_of].astype(jnp.float32) / 500.0)

    def one_cell(running, inputs):
        rows_in, cot_rows, scale_val = inputs
        result, pullback = jax.vjp(block_forward, rows_in.astype(jnp.float32), params)
        rows_grad, params_grad = pullback(cot_rows.astype(jnp.float32) * scale_val)
        return (tree_add(running, params_grad), (result.astype(jnp.bfloat16), rows_grad))
    start_sums = jax.tree.map(jnp.zeros_like, params)
    grad_sums, (results, row_grads) = lax.scan(one_cell, start_sums, (cell_rows, cell_cot, cell_scale))
    block_out = results.reshape(tokens.shape)
    tokens_grad = row_grads.reshape(tokens.shape)
    return (block_out, tokens_grad, grad_sums[0], grad_sums[1], grad_sums[2], grad_sums[3], grad_sums[4], grad_sums[5], grad_sums[6], grad_sums[7], grad_sums[8], grad_sums[9], grad_sums[10], grad_sums[11], grad_sums[12])
```

```python
import jax
import jax.numpy as jnp
from jax import lax
from jax.sharding import PartitionSpec as P

HEAD = 64


norm_eps = 1e-05
score_scale = 0.125


def layer_norm(values, gain_vec, bias_vec):
    average = jnp.mean(values, axis=-1, keepdims=True)
    centred = values - average
    variance = jnp.mean(centred * centred, axis=-1, keepdims=True)
    return centred * lax.rsqrt(variance + norm_eps) * gain_vec + bias_vec


def tree_add(first_tree, second_tree):
    return jax.tree.map(jnp.add, first_tree, second_tree)


def gelu_slope(values):
    cumul = 0.5 * (1.0 + lax.erf(values * 0.7071067811865476))
    density = jnp.exp(-0.5 * values * values) * 0.3989422804014327
    return cumul + values * density


def attend_forward(queries, key_rows, value_rows, block_rows):
    whole_rows, heads_here, head_dim = queries.shape
    blocks = whole_rows // block_rows
    query_blocks = queries.reshape(blocks, block_rows, heads_here, head_dim)

    def one_block(query_block):
        scores = (
            jnp.einsum("qhe,khe->hqk", query_block, key_rows, preferred_element_type=jnp.float32)
            * score_scale
        )
        top_val = jnp.max(scores, axis=-1, keepdims=True)
        exp_scores = jnp.exp(scores - top_val)
        totals = jnp.sum(exp_scores, axis=-1, keepdims=True)
        weights_bf = (exp_scores / totals).astype(jnp.bfloat16)
        mixed_rows = jnp.einsum(
            "hqk,khe->qhe", weights_bf, value_rows, preferred_element_type=jnp.float32
        )
        return (mixed_rows, top_val, totals)

    mixed_rows, top_vals, totals = lax.map(one_block, query_blocks)
    return (mixed_rows.reshape(whole_rows, heads_here * head_dim), top_vals, totals)


def attend_backward(queries, key_rows, value_rows, grad_out, top_vals, totals, block_rows):
    whole_rows, heads_here, head_dim = queries.shape
    blocks = whole_rows // block_rows
    query_blocks = queries.reshape(blocks, block_rows, heads_here, head_dim)
    grad_blocks = grad_out.reshape(blocks, block_rows, heads_here, head_dim)

    def one_block(carried, inputs):
        key_grad, value_grad = carried
        query_block, grad_block, top_block, total_block = inputs
        scores = (
            jnp.einsum("qhe,khe->hqk", query_block, key_rows, preferred_element_type=jnp.float32)
            * score_scale
        )
        weights_f = jnp.exp(scores - top_block) / total_block
        grad_weights = jnp.einsum(
            "qhe,khe->hqk", grad_block, value_rows, preferred_element_type=jnp.float32
        )
        inner_sum = jnp.sum(weights_f * grad_weights, axis=-1, keepdims=True)
        grad_scores = (weights_f * (grad_weights - inner_sum)).astype(jnp.bfloat16)
        query_grad = (
            jnp.einsum("hqk,khe->qhe", grad_scores, key_rows, preferred_element_type=jnp.float32)
            * score_scale
        )
        key_grad = (
            key_grad
            + jnp.einsum(
                "hqk,qhe->khe", grad_scores, query_block, preferred_element_type=jnp.float32
            )
            * score_scale
        )
        value_grad = value_grad + jnp.einsum(
            "hqk,qhe->khe",
            weights_f.astype(jnp.bfloat16),
            grad_block,
            preferred_element_type=jnp.float32,
        )
        return ((key_grad, value_grad), query_grad)

    zero_rows = jnp.zeros((whole_rows, heads_here, head_dim), jnp.float32)
    (key_grad, value_grad), query_grad = lax.scan(
        one_block, (zero_rows, zero_rows), (query_blocks, grad_blocks, top_vals, totals)
    )
    return (
        query_grad.reshape(whole_rows, heads_here * head_dim),
        key_grad.reshape(whole_rows, heads_here * head_dim),
        value_grad.reshape(whole_rows, heads_here * head_dim),
    )


def narrow_swap(values, bit):
    return lax.ppermute(values, "narrow", [(i, i ^ bit) for i in range(lax.axis_size("narrow"))])


def gather_rows(own):
    sibling = narrow_swap(own, 1)
    partner = narrow_swap(own, 2)
    across = narrow_swap(partner, 1)
    return jnp.concatenate([own, sibling, partner, across], axis=0)


def rounded_sum(first, second):
    return (first.astype(jnp.float32) + second.astype(jnp.float32)).astype(jnp.bfloat16)


def scatter_rows(far, near, rows):
    for_partner = rounded_sum(far[:rows], narrow_swap(far[rows:], 1))
    arrived = narrow_swap(for_partner, 2)
    own = near[:rows].astype(jnp.float32) + narrow_swap(near[rows:], 1).astype(jnp.float32)
    return own + arrived.astype(jnp.float32)


def ring_order(count):
    evens = list(range(0, count, 2))
    odds = list(range(1, count, 2))
    return evens + odds[::-1]


def ring_chunks(place, count, direction):
    return [jnp.mod(place - direction * (step + 1), count) for step in range(count)]


def ring_sum(chunk_of, count, direction, place):
    order = ring_order(count)
    perm = [(order[i], order[(i + direction) % count]) for i in range(count)]
    places = ring_chunks(place, count, direction)
    carried = chunk_of(places[0])
    for step in range(1, count):
        arrived = lax.ppermute(carried, "wide", perm)
        carried = rounded_sum(arrived, chunk_of(places[step]))
    pieces = [carried]
    for step in range(1, count):
        carried = lax.ppermute(carried, "wide", perm)
        pieces.append(carried)
    indices = [jnp.mod(place - direction * step, count) for step in range(count)]
    return pieces, indices


def reduce_wide(grad, splits):
    count = lax.axis_size("wide")
    rows, cols = grad.shape
    if count > 8:
        return lax.psum(grad.astype(jnp.bfloat16), "wide").astype(jnp.float32)
    order = ring_order(count)
    inverse = [order.index(i) for i in range(count)]
    place = jnp.take(jnp.array(inverse, jnp.int32), lax.axis_index("wide"))
    parts = grad.reshape(count, splits, rows // (count * splits), cols).astype(jnp.bfloat16)
    total = jnp.zeros(parts.shape, jnp.float32)
    for part in range(splits):
        direction = 1 if part % 2 == 0 else -1

        def chunk_of(index, part=part):
            return lax.dynamic_index_in_dim(parts[:, part], index, 0, keepdims=False)

        pieces, indices = ring_sum(chunk_of, count, direction, place)
        for piece, index in zip(pieces, indices):
            total = lax.dynamic_update_slice(
                total, piece.astype(jnp.float32)[None, None], (index, part, 0, 0)
            )
    return total.reshape(rows, cols)


def butterfly(values, axis):
    count = lax.axis_size(axis)
    bit = 1
    while bit < count:
        values = values + lax.ppermute(values, axis, [(i, i ^ bit) for i in range(count)])
        bit *= 2
    return values


def norm_stats(values):
    average = jnp.mean(values, axis=-1, keepdims=True)
    centred = values - average
    variance = jnp.mean(centred * centred, axis=-1, keepdims=True)
    inverse = lax.rsqrt(variance + norm_eps)
    return centred * inverse, inverse


def norm_back(grad, normed, inverse, gain_vec):
    scaled = grad * gain_vec
    mean_one = jnp.mean(scaled, axis=-1, keepdims=True)
    mean_two = jnp.mean(scaled * normed, axis=-1, keepdims=True)
    return inverse * (scaled - mean_one - normed * mean_two)


def dot32(first, second, first_dim, second_dim):
    return lax.dot_general(
        first, second, (((first_dim,), (second_dim,)), ((), ())), preferred_element_type=jnp.float32
    )


def local(
    tokens,
    cotangent,
    cell_of,
    query_count,
    attn_norm_gain,
    attn_norm_bias,
    input_weight,
    query_bias,
    value_bias,
    out_weight,
    out_bias,
    ffn_norm_gain,
    ffn_norm_bias,
    up_weight,
    up_bias,
    down_weight,
    down_bias,
):
    bf16 = jnp.bfloat16
    micro_count = tokens.shape[0]
    rows = tokens.shape[2]
    model = tokens.shape[3]
    head_local = input_weight.shape[2]
    heads_here = head_local // HEAD
    group_count = lax.axis_size("wide")
    group_index = lax.axis_index("wide")
    whole_rows = rows * lax.axis_size("narrow")
    half = whole_rows // 2
    block_rows = min(512, whole_rows)
    head_shape = (whole_rows, heads_here, HEAD)
    cell_slots = jnp.arange(cell_of.shape[0], dtype=jnp.int32)
    gain_one = attn_norm_gain.astype(jnp.float32)
    bias_one = attn_norm_bias.astype(jnp.float32)
    gain_two = ffn_norm_gain.astype(jnp.float32)
    bias_two = ffn_norm_bias.astype(jnp.float32)
    query_bias_f = query_bias.astype(jnp.float32)
    value_bias_f = value_bias.astype(jnp.float32)
    out_bias_f = out_bias.astype(jnp.float32)
    up_bias_f = up_bias.astype(jnp.float32)
    down_bias_f = down_bias.astype(jnp.float32)
    weight_flat = input_weight.reshape(model, 3 * head_local)
    micros = range(micro_count)

    rows_in, hat_one, inv_one, normed_one_all = [], [], [], []
    for m in micros:
        x = tokens[m, 0].astype(jnp.float32)
        hat, inv = norm_stats(x)
        rows_in.append(x)
        hat_one.append(hat)
        inv_one.append(inv)
        normed_one_all.append(gather_rows((hat * gain_one + bias_one).astype(bf16)))

    top_grad, top_grad_all = [], []
    for m in micros:
        slot_index = m * group_count + group_index
        cell_id = jnp.sum(jnp.where(cell_slots == slot_index, cell_of, 0))
        count_val = jnp.sum(jnp.where(cell_slots == cell_id, query_count, 0))
        loss_scale = jnp.sqrt(count_val.astype(jnp.float32) / 500.0)
        grad = cotangent[m, 0].astype(jnp.float32) * loss_scale
        top_grad.append(grad)
        top_grad_all.append(gather_rows(grad.astype(bf16)))

    queries, keys, values, attended, tops, sums = [], [], [], [], [], []
    resid, hat_two, inv_two, normed_two_all = [], [], [], []
    for m in micros:
        project = dot32(normed_one_all[m], weight_flat, 1, 0)
        queries.append((project[:, :head_local] + query_bias_f).astype(bf16).reshape(head_shape))
        keys.append(project[:, head_local : 2 * head_local].astype(bf16).reshape(head_shape))
        values.append((project[:, 2 * head_local :] + value_bias_f).astype(bf16).reshape(head_shape))
        mixed, top_vals, totals = attend_forward(queries[m], keys[m], values[m], block_rows)
        mixed = mixed.astype(bf16)
        attended.append(mixed)
        tops.append(top_vals)
        sums.append(totals)
        far = dot32(mixed[half:], out_weight, 1, 0).astype(bf16)
        near = dot32(mixed[:half], out_weight, 1, 0).astype(bf16)
        res = rows_in[m] + scatter_rows(far, near, rows) + out_bias_f
        resid.append(res)
        hat, inv = norm_stats(res)
        hat_two.append(hat)
        inv_two.append(inv)
        normed_two_all.append(gather_rows((hat * gain_two + bias_two).astype(bf16)))

    activ, pre_grad = [], []
    out_rows = []
    for m in micros:
        pre_act = dot32(normed_two_all[m], up_weight, 1, 0) + up_bias_f
        cumul = 0.5 * (1.0 + lax.erf(pre_act * 0.7071067811865476))
        density = jnp.exp(-0.5 * pre_act * pre_act) * 0.3989422804014327
        activ.append((pre_act * cumul).astype(bf16))
        act_grad = dot32(top_grad_all[m], down_weight, 1, 1)
        pre_grad.append((act_grad * (cumul + pre_act * density)).astype(bf16))
    normed_two_grad = []
    for m in micros:
        far = dot32(pre_grad[m][half:], up_weight, 1, 1).astype(bf16)
        near = dot32(pre_grad[m][:half], up_weight, 1, 1).astype(bf16)
        normed_two_grad.append(scatter_rows(far, near, rows))
    down_grad = sum(dot32(activ[m], top_grad_all[m], 0, 0) for m in micros)
    down_sum = reduce_wide(down_grad, 4)
    up_grad = sum(dot32(normed_two_all[m], pre_grad[m], 0, 0) for m in micros)
    up_sum = reduce_wide(up_grad, 4)
    up_bias_grad = sum(jnp.sum(pre_grad[m].astype(jnp.float32), axis=0) for m in micros)
    for m in micros:
        far = dot32(activ[m][half:], down_weight, 1, 0).astype(bf16)
        near = dot32(activ[m][:half], down_weight, 1, 0).astype(bf16)
        out_rows.append((resid[m] + scatter_rows(far, near, rows) + down_bias_f).astype(bf16))

    resid_grad, attn_grad_all = [], []
    for m in micros:
        grad = top_grad[m] + norm_back(normed_two_grad[m], hat_two[m], inv_two[m], gain_two)
        resid_grad.append(grad)
        attn_grad_all.append(gather_rows(grad.astype(bf16)))
    stacked, normed_one_grad = [], []
    for m in micros:
        attended_grad = dot32(attn_grad_all[m], out_weight, 1, 1).astype(bf16).reshape(head_shape)
        query_grad, key_grad, value_grad = attend_backward(
            queries[m], keys[m], values[m], attended_grad, tops[m], sums[m], block_rows
        )
        stack = jnp.concatenate([query_grad, key_grad, value_grad], axis=1).astype(bf16)
        stacked.append(stack)
        far = dot32(stack[half:], weight_flat, 1, 1).astype(bf16)
        near = dot32(stack[:half], weight_flat, 1, 1).astype(bf16)
        normed_one_grad.append(scatter_rows(far, near, rows))
    out_grad = sum(dot32(attended[m], attn_grad_all[m], 0, 0) for m in micros)
    out_sum = reduce_wide(out_grad, 2)
    input_grad = sum(dot32(normed_one_all[m], stacked[m], 0, 0) for m in micros)
    input_sum = reduce_wide(input_grad, 4)
    stack_bias = sum(jnp.sum(stacked[m].astype(jnp.float32), axis=0) for m in micros)

    grad_rows = []
    vectors = None
    for m in micros:
        grad_rows.append(
            resid_grad[m] + norm_back(normed_one_grad[m], hat_one[m], inv_one[m], gain_one)
        )
        these = jnp.stack(
            [
                jnp.sum(normed_one_grad[m] * hat_one[m], axis=0),
                jnp.sum(normed_one_grad[m], axis=0),
                jnp.sum(resid_grad[m], axis=0),
                jnp.sum(normed_two_grad[m] * hat_two[m], axis=0),
                jnp.sum(normed_two_grad[m], axis=0),
                jnp.sum(top_grad[m], axis=0),
            ]
        )
        vectors = these if vectors is None else vectors + these
    vectors = butterfly(vectors, "narrow")
    packed = jnp.concatenate(
        [vectors.reshape(-1), stack_bias[:head_local], stack_bias[2 * head_local :], up_bias_grad]
    )
    packed = butterfly(packed, "wide")
    vector_sums = packed[: 6 * model].reshape(6, model)
    tail = packed[6 * model :]
    return (
        jnp.stack(out_rows)[:, None],
        jnp.stack(grad_rows)[:, None],
        vector_sums[0],
        vector_sums[1],
        input_sum.reshape(model, 3, head_local),
        tail[:head_local],
        tail[head_local : 2 * head_local],
        out_sum,
        vector_sums[2],
        vector_sums[3],
        vector_sums[4],
        up_sum,
        tail[2 * head_local :],
        down_sum,
        vector_sums[5],
    )


def solution(mesh):
    in_specs = (
        P(None, "wide", "narrow", None),
        P(None, "wide", "narrow", None),
        P(),
        P(),
        P(),
        P(),
        P(None, None, "narrow"),
        P("narrow"),
        P("narrow"),
        P("narrow", None),
        P(),
        P(),
        P(),
        P(None, "narrow"),
        P("narrow"),
        P("narrow", None),
        P(),
    )
    out_specs = (
        P(None, "wide", "narrow", None),
        P(None, "wide", "narrow", None),
        P(),
        P(),
        P(None, None, "narrow"),
        P("narrow"),
        P("narrow"),
        P("narrow", None),
        P(),
        P(),
        P(),
        P(None, "narrow"),
        P("narrow"),
        P("narrow", None),
        P(),
    )
    return jax.shard_map(local, mesh=mesh, in_specs=in_specs, out_specs=out_specs, check_vma=False)
```

```python
import functools

import jax
import jax.numpy as jnp
from jax import lax
from jax.experimental import pallas as pl
from jax.experimental.pallas import tpu as pltpu
from jax.sharding import PartitionSpec as P

HEAD = 64
LANES = 128
TILE = 256
norm_eps = 1e-05
score_scale = 0.125
bf16 = jnp.bfloat16
f32 = jnp.float32


class Chain:
    def __init__(self):
        self.last = None

    def run(self, body, outs, *ins, smem=(), scratch=(), alias=None, anywhere=(), out_anywhere=(), limit=32):
        ins = [*smem, *ins]
        count = len(ins)
        specs = []
        for i in range(count):
            if i < len(smem):
                specs.append(pl.BlockSpec(memory_space=pltpu.SMEM))
            elif i - len(smem) in anywhere:
                specs.append(pl.BlockSpec(memory_space=pl.ANY))
            else:
                specs.append(pl.BlockSpec(memory_space=pltpu.VMEM))
        tied = self.last is not None
        if tied:
            specs.append(pl.BlockSpec(memory_space=pl.ANY))
            ins = [*ins, self.last]

        def inner(*refs):
            body(*refs[:count], *refs[count + tied :])

        made = pl.pallas_call(
            inner,
            out_shape=tuple(jax.ShapeDtypeStruct(*o) for o in outs),
            in_specs=specs,
            out_specs=tuple(
                pl.BlockSpec(memory_space=pl.ANY if i in out_anywhere else pltpu.VMEM) for i in range(len(outs))
            ),
            scratch_shapes=scratch,
            input_output_aliases={} if alias is None else {len(smem) + k: v for k, v in alias.items()},
            compiler_params=pltpu.CompilerParams(vmem_limit_bytes=limit << 20),
            cost_estimate=pl.CostEstimate(flops=0, bytes_accessed=0, transcendentals=0),
            name=body.func.__name__ if isinstance(body, functools.partial) else body.__name__,
        )(*ins)
        self.last = made[0]
        return made


def dot32(first, second, first_dim, second_dim):
    return lax.dot_general(
        first, second, (((first_dim,), (second_dim,)), ((), ())), preferred_element_type=f32
    )


def statistics(values):
    average = jnp.mean(values, axis=-1, keepdims=True)
    centred = values - average
    inverse = lax.rsqrt(jnp.mean(centred * centred, axis=-1, keepdims=True) + norm_eps)
    return centred * inverse, inverse


def norm_back(grad, normed, inverse, gain):
    scaled = grad * gain
    mean_one = jnp.mean(scaled, axis=-1, keepdims=True)
    mean_two = jnp.mean(scaled * normed, axis=-1, keepdims=True)
    return inverse * (scaled - mean_one - normed * mean_two)


def of_head(values, j, axis=1):
    if values.shape[axis] <= HEAD:
        return values
    place = lax.broadcasted_iota(jnp.int32, values.shape, axis)
    return jnp.where((place >= HEAD * j) & (place < HEAD * (j + 1)), values, jnp.zeros_like(values))


def head_pairs(width):
    return [(low, min(LANES, width - low)) for low in range(0, width, LANES)]


def norm_one(tok, gain, bias, out, *, m):
    normed, _ = statistics(tok[m, 0].astype(f32))
    out[...] = (normed * gain[...].astype(f32) + bias[...].astype(f32)).astype(bf16)


def scale_cot(scale, cot, out, *, m):
    out[...] = (cot[m, 0].astype(f32) * scale[m]).astype(bf16)


def project(*refs, parts):
    blocks = refs[:parts]
    weight, bias, scale = refs[parts : parts + 3]
    out, whole = refs[parts + 3 :]
    rows = blocks[0].shape[0]
    for b in range(parts):
        values = blocks[b][...]
        at = slice(b * rows, (b + 1) * rows)
        whole[at, :] = values
        out[at, :] = ((dot32(values, weight[...], 1, 0) + bias[...]) * scale[...]).astype(bf16)


def attend(qkv, out_weight, attended, logs, *outs, step):
    whole = qkv.shape[0]
    head = 0
    for low, wide in head_pairs(out_weight.shape[0]):
        heads = wide // HEAD
        key_pair = qkv[:, 3 * low + wide : 3 * low + 2 * wide]
        value_t = qkv[:, 3 * low + 2 * wide : 3 * low + 3 * wide].T
        keys = [of_head(key_pair, j) for j in range(heads)]
        values = [of_head(value_t, j, 0) for j in range(heads)]

        def block(i, carry, low=low, wide=wide, keys=keys, values=values, head=head):
            start = pl.multiple_of(i * step, step)
            query = qkv[pl.ds(start, step), 3 * low : 3 * low + wide]
            total = None
            for j in range(len(keys)):
                scores = dot32(keys[j], query, 1, 1)
                top = jnp.max(scores, axis=0, keepdims=True)
                powers = jnp.exp(scores - top)
                length = jnp.sum(powers, axis=0, keepdims=True)
                mixed = dot32(values[j], powers.astype(bf16), 1, 0) * (1.0 / length)
                total = mixed if total is None else total + mixed
                logs[head + j : head + j + 1, pl.ds(start, step)] = top + jnp.log(length)
            attended[pl.ds(start, step), low : low + wide] = total.T.astype(bf16)
            return carry

        lax.fori_loop(0, whole // step, block, 0)
        head += heads
    rows = whole // len(outs)
    for b in range(len(outs)):
        outs[b][...] = dot32(attended[b * rows : (b + 1) * rows, :], out_weight[...], 1, 0).astype(bf16)


def pair_sum(first, second, out):
    out[...] = (first[...].astype(f32) + second[...].astype(f32)).astype(bf16)


def three(first, second, third):
    return first[...].astype(f32) + second[...].astype(f32) + third[...].astype(f32)


def norm_two(tok, first, second, third, out_bias, gain, bias, resid, normed, *, m):
    value = tok[m, 0].astype(f32) + three(first, second, third) + out_bias[...].astype(f32)
    resid[...] = value
    hat, _ = statistics(value)
    normed[...] = (hat * gain[...].astype(f32) + bias[...].astype(f32)).astype(bf16)


def feed(*refs, parts):
    normed, grads = refs[:parts], refs[parts : 2 * parts]
    up, up_bias, down = refs[2 * parts : 2 * parts + 3]
    activ, pre_grad, bias_grad, normed_all, grads_all = refs[2 * parts + 3 :]
    rows = normed[0].shape[0]
    for b in range(parts):
        normed_all[b * rows : (b + 1) * rows, :] = normed[b][...]
        grads_all[b * rows : (b + 1) * rows, :] = grads[b][...]

    def tile(i, carry):
        cols = pl.ds(pl.multiple_of(i * TILE, TILE), TILE)
        total = None
        for b in range(parts):
            at = slice(b * rows, (b + 1) * rows)
            pre = dot32(normed[b][...], up[:, cols], 1, 0) + up_bias[:, cols].astype(f32)
            cumul = 0.5 + 0.5 * lax.erf(pre * 0.7071067811865476)
            density = jnp.exp(-0.5 * pre * pre) * 0.3989422804014327
            activ[at, cols] = (pre * cumul).astype(bf16)
            back = dot32(grads[b][...], down[cols, :], 1, 1)
            grad = (back * (cumul + pre * density)).astype(bf16)
            pre_grad[at, cols] = grad
            part = jnp.sum(grad.astype(f32), axis=0, keepdims=True)
            total = part if total is None else total + part
        bias_grad[:, cols] = total
        return carry

    lax.fori_loop(0, up.shape[1] // TILE, tile, 0)


def times(value, weight, *outs):
    rows = outs[0].shape[0]

    def tile(i, carry):
        cols = pl.ds(pl.multiple_of(i * TILE, TILE), TILE)
        for b in range(len(outs)):
            outs[b][:, cols] = dot32(value[b * rows : (b + 1) * rows, :], weight[:, cols], 1, 0).astype(bf16)
        return carry

    lax.fori_loop(0, weight.shape[1] // TILE, tile, 0)


def times_back(value, weight, *outs):
    rows = outs[0].shape[0]

    def tile(i, carry):
        cols = pl.ds(pl.multiple_of(i * TILE, TILE), TILE)
        for b in range(len(outs)):
            outs[b][:, cols] = dot32(value[b * rows : (b + 1) * rows, :], weight[cols, :], 1, 1).astype(bf16)
        return carry

    lax.fori_loop(0, weight.shape[0] // TILE, tile, 0)


def weight_grad(place, *refs, count, pairs, ring):
    firsts, seconds = refs[:pairs], refs[pairs : 2 * pairs]
    out, chunk = refs[2 * pairs :]

    def tile(i, carry):
        rows = pl.ds(pl.multiple_of(i * TILE, TILE), TILE)
        total = None
        for first, second in zip(firsts, seconds):
            part = dot32(first[:, rows], second[...], 0, 0)
            total = part if total is None else total + part
        out[rows, :] = total.astype(bf16)
        return carry

    lax.fori_loop(0, out.shape[0] // TILE, tile, 0)
    chunk[...] = out[chunk_rows(place[ring], count, out), :]


def chunk_rows(index, count, ref):
    size = ref.shape[0] // count
    return pl.ds(pl.multiple_of(index * size, size), size)


def norm_two_back(scale, cot, resid, first, second, third, gain, out, rounded, sums, *, m):
    top = cot[m, 0].astype(f32) * scale[m]
    grad = three(first, second, third)
    hat, inverse = statistics(resid[...])
    back = top + norm_back(grad, hat, inverse, gain[...].astype(f32))
    out[...] = back
    rounded[...] = back.astype(bf16)
    sums[0:1, :] = jnp.sum(back, axis=0, keepdims=True)
    sums[1:2, :] = jnp.sum(grad * hat, axis=0, keepdims=True)
    sums[2:3, :] = jnp.sum(grad, axis=0, keepdims=True)
    sums[3:4, :] = jnp.sum(top, axis=0, keepdims=True)
    sums[4:8, :] = jnp.zeros_like(sums[4:8, :])


def attend_back(qkv, logs, out_weight, *refs, parts, step, low, wide):
    grads = refs[:parts]
    out, key_grad, value_grad, given = refs[parts:]
    whole = qkv.shape[0]
    rows = whole // parts
    for b in range(parts):
        given[b * rows : (b + 1) * rows, :] = dot32(
            grads[b][...], out_weight[low : low + wide, :], 1, 1
        ).astype(bf16)
    heads = wide // HEAD
    head = low // HEAD
    key_pair = qkv[:, 3 * low + wide : 3 * low + 2 * wide]
    value_pair = qkv[:, 3 * low + 2 * wide : 3 * low + 3 * wide]
    key_t = key_pair.T
    keys = [of_head(key_pair, j) for j in range(heads)]
    values = [of_head(value_pair, j) for j in range(heads)]
    keys_t = [of_head(key_t, j, 0) for j in range(heads)]
    key_grad[...] = jnp.zeros_like(key_grad)
    value_grad[...] = jnp.zeros_like(value_grad)

    def block(i, carry):
        start = pl.multiple_of(i * step, step)
        query = qkv[pl.ds(start, step), 3 * low : 3 * low + wide]
        grad = given[pl.ds(start, step), :]
        total = None
        for j in range(heads):
            scores = dot32(keys[j], query, 1, 1)
            weights = jnp.exp(scores - logs[head + j : head + j + 1, pl.ds(start, step)])
            back = dot32(values[j], grad, 1, 1)
            inner = jnp.sum(weights * back, axis=0, keepdims=True)
            score_grad = (weights * (back - inner)).astype(bf16)
            value_grad[...] += dot32(weights.astype(bf16), of_head(grad, j), 1, 0)
            key_grad[...] += dot32(score_grad, of_head(query, j), 1, 0)
            part = dot32(keys_t[j], score_grad, 1, 0)
            total = part if total is None else total + part
        out[pl.ds(start, step), :wide] = (total.T * score_scale).astype(bf16)
        return carry

    lax.fori_loop(0, whole // step, block, 0)
    out[:, wide : 2 * wide] = key_grad[...].astype(bf16)
    out[:, 2 * wide :] = value_grad[...].astype(bf16)


def project_back(*refs, pairs):
    grads, weight, sums, outs = refs[:pairs], refs[pairs], refs[pairs + 1], refs[pairs + 2 :]
    rows = outs[0].shape[0]

    def tile(i, carry):
        cols = pl.ds(pl.multiple_of(i * TILE, TILE), TILE)
        for b in range(len(outs)):
            low = 0
            total = None
            for grad in grads:
                wide = grad.shape[1]
                part = dot32(grad[b * rows : (b + 1) * rows, :], weight[cols, low : low + wide], 1, 1)
                total = part if total is None else total + part
                low += wide
            outs[b][:, cols] = total.astype(bf16)
        return carry

    lax.fori_loop(0, weight.shape[0] // TILE, tile, 0)
    low = 0
    for grad in grads:
        wide = grad.shape[1]
        sums[:, low : low + wide] = jnp.sum(grad[...].astype(f32), axis=0, keepdims=True)
        low += wide


def projection_grad(place, *refs, count, micros, pairs):
    normed, refs = refs[:micros], refs[micros:]
    grads, refs = [refs[m * pairs : (m + 1) * pairs] for m in range(micros)], refs[micros * pairs :]
    tops, refs = [refs[4 * m : 4 * m + 4] for m in range(micros)], refs[4 * micros :]
    mixed, refs = refs[:micros], refs[micros:]
    left, right, left_chunk, right_chunk = refs
    cut = left.shape[1]
    rows_b = tops[0][0].shape[0]

    def put(rows, low, values):
        wide = values.shape[1]
        values = values.astype(bf16)
        if low + wide <= cut:
            left[rows, low : low + wide] = values
        elif low >= cut:
            right[rows, low - cut : low - cut + wide] = values
        else:
            left[rows, low:] = values[:, : cut - low]
            right[rows, : low + wide - cut] = values[:, cut - low :]

    def tile(i, carry):
        rows = pl.ds(pl.multiple_of(i * TILE, TILE), TILE)
        low = 0
        for p in range(pairs):
            total = None
            for m in range(micros):
                part = dot32(normed[m][:, rows], grads[m][p][...], 0, 0)
                total = part if total is None else total + part
            put(rows, low, total)
            low += total.shape[1]
        total = None
        for m in range(micros):
            for b in range(4):
                part = dot32(tops[m][b][:, rows], mixed[m][b * rows_b : (b + 1) * rows_b, :], 0, 0)
                total = part if total is None else total + part
        put(rows, low, total)
        return carry

    lax.fori_loop(0, left.shape[0] // TILE, tile, 0)
    left_chunk[...] = left[chunk_rows(place[0], count, left), :]
    right_chunk[...] = right[chunk_rows(place[1], count, right), :]


def ring_add(place, *refs, count, step):
    arrived, whole, outs = refs[:2], refs[2:4], refs[4:]
    for i in range(2):
        local = whole[i][chunk_rows(place[2 * step + i], count, whole[i]), :]
        outs[i][...] = (arrived[i][...].astype(f32) + local.astype(f32)).astype(bf16)


def ring_store(place, *refs, count, step):
    arrived = refs[:2]
    refs = refs[2 if step == 0 else 4 :]
    ahead, outs, buffers, sems = refs[:2], refs[2:4], refs[4:6], refs[6]
    copies = []
    for i in range(2):
        ahead[i][...] = arrived[i][...]
        buffers[i][...] = arrived[i][...].astype(f32)
        rows = chunk_rows(place[2 * step + i], count, outs[i])
        copies.append(pltpu.make_async_copy(buffers[i], outs[i].at[rows, :], sems.at[i]))
        copies[i].start()
    for copy in copies:
        copy.wait()


def norm_one_back(tok, resid_grad, first, second, third, gain, out, sums, *, m):
    grad = three(first, second, third)
    hat, inverse = statistics(tok[m, 0].astype(f32))
    out[...] = resid_grad[...] + norm_back(grad, hat, inverse, gain[...].astype(f32))
    sums[0:4, :] = jnp.zeros_like(sums[0:4, :])
    sums[4:5, :] = jnp.sum(grad * hat, axis=0, keepdims=True)
    sums[5:6, :] = jnp.sum(grad, axis=0, keepdims=True)
    sums[6:8, :] = jnp.zeros_like(sums[6:8, :])


def add_rows(resid, first, second, third, bias, out):
    out[...] = (resid[...] + three(first, second, third) + bias[...].astype(f32)).astype(bf16)


def swap(values, axis, bit):
    return lax.ppermute(values, axis, [(i, i ^ bit) for i in range(lax.axis_size(axis))])


def ring_order(count):
    return list(range(0, count, 2)) + list(range(1, count, 2))[::-1]


def butterfly(values, axis):
    bit = 1
    while bit < lax.axis_size(axis):
        values = values + swap(values, axis, bit)
        bit *= 2
    return values


class Rings:
    def __init__(self, chain, wholes, chunks, sends, keeps):
        self.chain, self.wholes = chain, wholes
        self.sends, self.keeps = sends, keeps
        self.count = lax.axis_size("wide")
        order = ring_order(self.count)
        self.perms = [[(order[i], order[(i + d) % self.count]) for i in range(self.count)] for d in (1, -1)]
        self.moving = [self.pass_on(c, i) for i, c in enumerate(chunks)]
        self.step = 1
        self.outs = None

    def pass_on(self, chunk, i):
        return lax.ppermute(chunk, "wide", self.perms[i])

    def add(self):
        shapes = [(c.shape, bf16) for c in self.moving]
        made = self.chain.run(
            functools.partial(ring_add, count=self.count, step=self.step), shapes, *self.moving, *self.wholes, smem=(self.sends,)
        )
        self.step += 1
        if self.step < self.count:
            self.moving = [self.pass_on(c, i) for i, c in enumerate(made)]
        else:
            self.moving, self.step = list(made), 0
            self.storing = True

    def store(self):
        first = self.outs is None
        shapes = [(c.shape, bf16) for c in self.moving] + [(w.shape, f32) for w in self.wholes]
        kept = () if first else self.outs
        made = self.chain.run(
            functools.partial(ring_store, count=self.count, step=self.step),
            shapes,
            *self.moving,
            *kept,
            smem=(self.keeps,),
            scratch=[pltpu.VMEM(c.shape, f32) for c in self.moving] + [pltpu.SemaphoreType.DMA((2,))],
            alias=None if first else {2: 2, 3: 3},
            anywhere=() if first else (2, 3),
            out_anywhere=(2, 3),
        )
        self.outs = made[2:]
        self.step += 1
        if self.step < self.count:
            self.moving = [self.pass_on(c, i) for i, c in enumerate(made[:2])]


class Whole:
    def __init__(self, wholes):
        self.outs = tuple(lax.psum(tuple(wholes), "wide"))
        self.outs = tuple(w.astype(f32) for w in self.outs)

    def add(self):
        pass

    def store(self):
        pass


def ring_tables(count):
    order = ring_order(count)
    sends = [[0] * (2 * count) for _ in range(count)]
    keeps = [[0] * (2 * count) for _ in range(count)]
    for place, device in enumerate(order):
        for step in range(count):
            for i, d in enumerate((1, -1)):
                sends[device][2 * step + i] = (place - d * (step + 1)) % count
                keeps[device][2 * step + i] = (place - d * step) % count
    return sends, keeps


def local(
    tokens,
    cotangent,
    cell_of,
    query_count,
    attn_norm_gain,
    attn_norm_bias,
    input_weight,
    query_bias,
    value_bias,
    out_weight,
    out_bias,
    ffn_norm_gain,
    ffn_norm_bias,
    up_weight,
    up_bias,
    down_weight,
    down_bias,
):
    micros = range(tokens.shape[0])
    rows, model = tokens.shape[2], tokens.shape[3]
    parts = lax.axis_size("narrow")
    whole = rows * parts
    width = input_weight.shape[2]
    hidden = up_weight.shape[1]
    count = lax.axis_size("wide")
    short = count <= 8
    pairs = head_pairs(width)
    chain = Chain()
    run = chain.run
    index = lax.axis_index("wide")

    block = ((rows, model), bf16)
    blocks = [block] * parts
    wide_rows = ((whole, model), bf16)
    row = lambda v: v.reshape(1, -1)
    gain_one, bias_one, gain_two, bias_two = map(row, (attn_norm_gain, attn_norm_bias, ffn_norm_gain, ffn_norm_bias))
    out_bias, down_bias, up_bias = row(out_bias), row(down_bias), row(up_bias)

    slots = index + count * jnp.arange(len(micros), dtype=jnp.int32)
    counts = jnp.stack([query_count[cell_of[slots[m]]] for m in micros])
    scale = jnp.sqrt(counts.astype(f32) / 500.0)
    sends, keeps = ring_tables(count)
    sends = lax.dynamic_index_in_dim(jnp.array(sends, jnp.int32), index, 0, keepdims=False)
    keeps = lax.dynamic_index_in_dim(jnp.array(keeps, jnp.int32), index, 0, keepdims=False)

    def by_pairs(three_parts):
        return jnp.concatenate([v[..., low : low + wide] for low, wide in pairs for v in three_parts], axis=-1)

    weight = by_pairs([input_weight[:, j] for j in range(3)])
    zero = jnp.zeros((1, width), f32)
    project_bias = by_pairs([row(query_bias).astype(f32), zero, row(value_bias).astype(f32)])
    project_scale = by_pairs([zero + score_scale, zero + 1.0, zero + 1.0])

    def gather(own):
        partner = swap(own, "narrow", 2)
        return [own, swap(own, "narrow", 1), partner, swap(partner, "narrow", 1)]

    def share(shares):
        return [*shares, swap(shares[3], "narrow", 1)]

    def send(shares):
        (both,) = run(pair_sum, [block], shares[2], shares[4])
        return [shares[0], swap(shares[1], "narrow", 1), swap(both, "narrow", 2)]

    nothing = [None, None]
    normed, given, qkv, normed_all, mixed, logs = ([*nothing] for _ in range(6))
    shares, resid, normed_two_b, activ, pre_grad, up_bias_grad, two_all, given_all = ([*nothing] for _ in range(8))
    resid_grad, top, sums_two, sums_one, stack_sums, out_rows, grad_rows = ([*nothing] for _ in range(7))
    pair_grads = [[], []]

    def do_norm_one(m):
        (own,) = run(functools.partial(norm_one, m=m), [block], tokens, gain_one, bias_one)
        normed[m] = gather(own)

    def do_scale(m):
        (own,) = run(functools.partial(scale_cot, m=m), [block], cotangent, smem=(scale,))
        given[m] = gather(own)

    def do_project(m):
        qkv[m], normed_all[m] = run(
            functools.partial(project, parts=parts),
            [((whole, 3 * width), bf16), wide_rows],
            *normed[m],
            weight,
            project_bias,
            project_scale,
        )

    def do_attend(m):
        mixed[m], logs[m], *b = run(
            functools.partial(attend, step=min(512, whole)),
            [((whole, width), bf16), ((8, whole), f32), *blocks],
            qkv[m],
            out_weight,
            limit=40,
        )
        shares[m] = share(b)

    def do_send(m):
        shares[m] = send(shares[m])

    def do_norm_two(m):
        resid[m], own = run(
            functools.partial(norm_two, m=m),
            [((rows, model), f32), block],
            tokens,
            *shares[m],
            out_bias,
            gain_two,
            bias_two,
        )
        normed_two_b[m] = gather(own)

    def do_feed(m):
        activ[m], pre_grad[m], up_bias_grad[m], two_all[m], given_all[m] = run(
            functools.partial(feed, parts=parts),
            [((whole, hidden), bf16), ((whole, hidden), bf16), ((1, hidden), f32), wide_rows, wide_rows],
            *normed_two_b[m],
            *given[m],
            up_weight,
            up_bias,
            down_weight,
            limit=48,
        )

    def do_up_back(m):
        shares[m] = share(run(times_back, blocks, pre_grad[m], up_weight))

    def do_down(m):
        shares_down[m] = share(run(times, blocks, activ[m], down_weight))

    def do_norm_two_back(m):
        resid_grad[m], own, sums_two[m] = run(
            functools.partial(norm_two_back, m=m),
            [((rows, model), f32), block, ((8, model), f32)],
            cotangent,
            resid[m],
            *shares[m],
            gain_two,
            smem=(scale,),
        )
        top[m] = gather(own)

    def do_attend_back(m, p):
        low, wide = pairs[p]
        (made,) = run(
            functools.partial(attend_back, parts=parts, step=min(512, whole), low=low, wide=wide),
            [((whole, 3 * wide), bf16)],
            qkv[m],
            logs[m],
            out_weight,
            *top[m],
            scratch=[pltpu.VMEM((whole, wide), f32)] * 2 + [pltpu.VMEM((whole, wide), bf16)],
            limit=48,
        )
        pair_grads[m].append(made)

    def do_project_back(m):
        stack_sums[m], *b = run(
            functools.partial(project_back, pairs=len(pairs)),
            [((1, 3 * width), f32), *blocks],
            *pair_grads[m],
            weight,
        )
        shares[m] = share(b)

    def do_norm_one_back(m):
        grad_rows[m], sums_one[m] = run(
            functools.partial(norm_one_back, m=m),
            [((rows, model), f32), ((8, model), f32)],
            tokens,
            resid_grad[m],
            *shares[m],
            gain_one,
        )

    def do_add_rows(m):
        (out_rows[m],) = run(add_rows, [block], resid[m], *shares_down[m], down_bias)

    def ffn_grad(firsts, seconds, ring):
        shape = (firsts[0].shape[1], seconds[0].shape[1])
        return run(
            functools.partial(weight_grad, count=count if short else 1, pairs=len(micros), ring=ring),
            [(shape, bf16), ((shape[0] // (count if short else 1), shape[1]), bf16)],
            *firsts,
            *seconds,
            smem=(sends if short else jnp.zeros((2,), jnp.int32),),
            limit=40,
        )

    shares_down = [*nothing]

    do_norm_one(0)
    do_norm_one(1)
    do_scale(0)
    do_project(0)
    do_attend(0)
    do_project(1)
    do_send(0)
    do_attend(1)
    do_norm_two(0)
    do_send(1)
    do_scale(1)
    do_norm_two(1)
    do_feed(0)
    do_up_back(0)
    do_feed(1)
    do_send(0)
    down_grad, down_chunk = ffn_grad(activ, given_all, 0)
    do_up_back(1)
    up_grad, up_chunk = ffn_grad(two_all, pre_grad, 1)
    ffn = Rings(chain, (down_grad, up_grad), (down_chunk, up_chunk), sends, keeps) if short else Whole((down_grad, up_grad))
    do_send(1)
    do_norm_two_back(0)
    ffn.add()
    do_norm_two_back(1)
    do_down(0)
    ffn.add()
    do_attend_back(0, 0)
    ffn.add()
    shares_down[0] = send(shares_down[0])
    do_attend_back(0, 1)
    ffn.add()
    do_attend_back(0, 2)
    do_project_back(0)
    ffn.add()
    do_attend_back(1, 0)
    do_send(0)
    ffn.add()
    do_attend_back(1, 1)
    ffn.add()
    ffn.store()
    do_attend_back(1, 2)
    do_project_back(1)
    ffn.store()
    left, right, left_chunk, right_chunk = run(
        functools.partial(projection_grad, count=count if short else 1, micros=len(micros), pairs=len(pairs)),
        [((model, 2 * width), bf16)] * 2 + [((model // (count if short else 1), 2 * width), bf16)] * 2,
        *normed_all,
        *pair_grads[0],
        *pair_grads[1],
        *top[0],
        *top[1],
        *mixed,
        smem=(sends if short else jnp.zeros((2,), jnp.int32),),
        limit=48,
    )
    attn = Rings(chain, (left, right), (left_chunk, right_chunk), sends, keeps) if short else Whole((left, right))
    do_send(1)
    ffn.store()
    do_norm_one_back(0)
    attn.add()
    do_down(1)
    ffn.store()
    attn.add()
    do_add_rows(0)
    do_norm_one_back(1)
    shares_down[1] = send(shares_down[1])
    ffn.store()
    attn.add()
    ffn.store()
    attn.add()
    do_add_rows(1)
    ffn.store()
    attn.add()
    ffn.store()
    attn.add()
    attn.add()
    for _ in range(count if short else 0):
        attn.store()

    vectors = sums_one[0] + sums_one[1] + sums_two[0] + sums_two[1]
    vectors = butterfly(vectors, "narrow")
    stack_sum = stack_sums[0] + stack_sums[1]
    packed = jnp.concatenate([vectors[:6].reshape(-1), (up_bias_grad[0] + up_bias_grad[1])[0], stack_sum[0]])
    packed = butterfly(packed, "wide")
    vector_sums = packed[: 6 * model].reshape(6, model)
    up_bias_sum = packed[6 * model : 6 * model + hidden]
    stack_sum = packed[6 * model + hidden :]

    def from_pairs(values, j):
        return jnp.concatenate(
            [values[..., 3 * low + j * wide : 3 * low + (j + 1) * wide] for low, wide in pairs], axis=-1
        )

    both = jnp.concatenate(attn.outs, axis=1)
    input_sum = jnp.stack([from_pairs(both[:, : 3 * width], j) for j in range(3)], axis=1)
    return (
        jnp.stack(out_rows)[:, None],
        jnp.stack(grad_rows)[:, None],
        vector_sums[4],
        vector_sums[5],
        input_sum,
        from_pairs(stack_sum, 0),
        from_pairs(stack_sum, 2),
        both[:, 3 * width :].T,
        vector_sums[0],
        vector_sums[1],
        vector_sums[2],
        ffn.outs[1],
        up_bias_sum,
        ffn.outs[0],
        vector_sums[3],
    )


def solution(mesh):
    in_specs = (
        P(None, "wide", "narrow", None),
        P(None, "wide", "narrow", None),
        P(),
        P(),
        P(),
        P(),
        P(None, None, "narrow"),
        P("narrow"),
        P("narrow"),
        P("narrow", None),
        P(),
        P(),
        P(),
        P(None, "narrow"),
        P("narrow"),
        P("narrow", None),
        P(),
    )
    out_specs = (
        P(None, "wide", "narrow", None),
        P(None, "wide", "narrow", None),
        P(),
        P(),
        P(None, None, "narrow"),
        P("narrow"),
        P("narrow"),
        P("narrow", None),
        P(),
        P(),
        P(),
        P(None, "narrow"),
        P("narrow"),
        P("narrow", None),
        P(),
    )
    return jax.shard_map(local, mesh=mesh, in_specs=in_specs, out_specs=out_specs, check_vma=False)
```

```python
import functools

import jax
import jax.numpy as jnp
from jax import lax
from jax.experimental import pallas as pl
from jax.experimental.pallas import tpu as pltpu
from jax.sharding import PartitionSpec as P

HEAD = 64
LANES = 128
TILE = 256
norm_eps = 1e-05
score_scale = 0.125
bf16 = jnp.bfloat16
f32 = jnp.float32


class Chain:
    def __init__(self):
        self.last = []
        self.held = []

    def hold(self, *arrays):
        self.held += arrays

    def run(self, body, outs, *ins, smem=(), scratch=(), alias=None, anywhere=(), out_anywhere=(), limit=12, token=0, cover=False):
        unread = [*self.last, *self.held]
        count = len(smem) + len(ins)
        specs = [pl.BlockSpec(memory_space=pltpu.SMEM)] * len(smem)
        specs += [pl.BlockSpec(memory_space=pl.ANY if i in anywhere else pltpu.VMEM) for i in range(len(ins))]
        specs += [pl.BlockSpec(memory_space=pl.ANY)] * len(unread)

        def inner(*refs):
            body(*refs[:count], *refs[count + len(unread) :])

        made = pl.pallas_call(
            inner,
            out_shape=tuple(jax.ShapeDtypeStruct(*o) for o in outs),
            in_specs=specs,
            out_specs=tuple(
                pl.BlockSpec(memory_space=pl.ANY if i in out_anywhere else pltpu.VMEM) for i in range(len(outs))
            ),
            scratch_shapes=scratch,
            input_output_aliases={} if alias is None else {len(smem) + k: v for k, v in alias.items()},
            compiler_params=pltpu.CompilerParams(vmem_limit_bytes=limit << 20),
            cost_estimate=pl.CostEstimate(flops=10**12 if cover else 1, bytes_accessed=1, transcendentals=0),
            name=body.func.__name__ if isinstance(body, functools.partial) else body.__name__,
        )(*smem, *ins, *unread)
        self.last, self.held = [made[token]], []
        return made


def dot32(first, second, first_dim, second_dim):
    return lax.dot_general(
        first, second, (((first_dim,), (second_dim,)), ((), ())), preferred_element_type=f32
    )


def statistics(values):
    average = jnp.mean(values, axis=-1, keepdims=True)
    centred = values - average
    inverse = lax.rsqrt(jnp.mean(centred * centred, axis=-1, keepdims=True) + norm_eps)
    return centred * inverse, inverse


def norm_back(grad, normed, inverse, gain):
    scaled = grad * gain
    mean_one = jnp.mean(scaled, axis=-1, keepdims=True)
    mean_two = jnp.mean(scaled * normed, axis=-1, keepdims=True)
    return inverse * (scaled - mean_one - normed * mean_two)


def of_head(values, j, axis=1):
    if values.shape[axis] <= HEAD:
        return values
    place = lax.broadcasted_iota(jnp.int32, values.shape, axis)
    return jnp.where((place >= HEAD * j) & (place < HEAD * (j + 1)), values, jnp.zeros_like(values))


def head_pairs(width):
    return [(low, min(LANES, width - low)) for low in range(0, width, LANES)]


def mark(out):
    out[...] = jnp.zeros_like(out)


def by_pairs(weight_t, out):
    width = out.shape[0] // 3
    for low, wide in head_pairs(width):
        for j in range(3):
            out[3 * low + j * wide : 3 * low + (j + 1) * wide, :] = weight_t[
                j * width + low : j * width + low + wide, :
            ]


def norm_one(tok, gain, bias, out, *, m):
    normed, _ = statistics(tok[m, 0].astype(f32))
    out[...] = (normed * gain[...].astype(f32) + bias[...].astype(f32)).astype(bf16)


def scale_cot(scale, cot, out, *, m):
    out[...] = (cot[m, 0].astype(f32) * scale[m]).astype(bf16)


def project(*refs, parts):
    blocks = refs[:parts]
    weight, bias, scale = refs[parts : parts + 3]
    out, whole = refs[parts + 3 :]
    rows = blocks[0].shape[0]
    for b in range(parts):
        values = blocks[b][...]
        at = slice(b * rows, (b + 1) * rows)
        whole[at, :] = values
        out[at, :] = ((dot32(values, weight[...], 1, 1) + bias[...]) * scale[...]).astype(bf16)


def attend(qkv, out_weight, attended, logs, *outs, step):
    whole = qkv.shape[0]
    head = 0
    for low, wide in head_pairs(out_weight.shape[0]):
        heads = wide // HEAD
        key_pair = qkv[:, 3 * low + wide : 3 * low + 2 * wide]
        value_t = qkv[:, 3 * low + 2 * wide : 3 * low + 3 * wide].T
        keys = [of_head(key_pair, j) for j in range(heads)]
        values = [of_head(value_t, j, 0) for j in range(heads)]
        for start in range(0, whole, step):
            at = slice(start, start + step)
            query = qkv[at, 3 * low : 3 * low + wide]
            total = None
            for j in range(heads):
                scores = dot32(keys[j], query, 1, 1)
                top = jnp.max(scores, axis=0, keepdims=True)
                powers = jnp.exp(scores - top)
                length = jnp.sum(powers, axis=0, keepdims=True)
                mixed = dot32(values[j], powers.astype(bf16), 1, 0) * (1.0 / length)
                total = mixed if total is None else total + mixed
                logs[head + j : head + j + 1, at] = top + jnp.log(length)
            attended[at, low : low + wide] = total.T.astype(bf16)
        head += heads
    put_shares(outs, lambda at: dot32(attended[at, :], out_weight[...], 1, 0), whole)


def put_shares(outs, share_of, whole):
    own, partner, crossing = outs
    rows = own.shape[0]
    for b, (out, at) in enumerate(((own, None), (crossing, 0), (partner, None), (crossing, 1))):
        value = share_of(slice(b * rows, (b + 1) * rows)).astype(bf16)
        if at is None:
            out[...] = value
        else:
            out[at] = value


def pair_sum(first, second, out):
    out[...] = (first[...].astype(f32) + second[1].astype(f32)).astype(bf16)


def three(first, second, third):
    return first[...].astype(f32) + second[0].astype(f32) + third[...].astype(f32)


def norm_two(tok, first, second, third, out_bias, gain, bias, resid, normed, *, m):
    value = tok[m, 0].astype(f32) + three(first, second, third) + out_bias[...].astype(f32)
    resid[...] = value
    hat, _ = statistics(value)
    normed[...] = (hat * gain[...].astype(f32) + bias[...].astype(f32)).astype(bf16)


def feed(*refs, parts):
    normed, grads = refs[:parts], refs[parts : 2 * parts]
    up, up_bias, down = refs[2 * parts : 2 * parts + 3]
    activ, pre_grad, bias_grad, normed_all, grads_all = refs[2 * parts + 3 :]
    rows = normed[0].shape[0]
    for b in range(parts):
        normed_all[b * rows : (b + 1) * rows, :] = normed[b][...]
        grads_all[b * rows : (b + 1) * rows, :] = grads[b][...]
    for low in range(0, up.shape[1], TILE):
        cols = slice(low, low + TILE)
        total = None
        for b in range(parts):
            at = slice(b * rows, (b + 1) * rows)
            pre = dot32(normed[b][...], up[:, cols], 1, 0) + up_bias[:, cols].astype(f32)
            cumul = 0.5 + 0.5 * lax.erf(pre * 0.7071067811865476)
            density = jnp.exp(-0.5 * pre * pre) * 0.3989422804014327
            activ[at, cols] = (pre * cumul).astype(bf16)
            back = dot32(grads[b][...], down[cols, :], 1, 1)
            grad = (back * (cumul + pre * density)).astype(bf16)
            pre_grad[at, cols] = grad
            part = jnp.sum(grad.astype(f32), axis=0, keepdims=True)
            total = part if total is None else total + part
        bias_grad[:, cols] = total


def times(value, weight, *outs):
    put_tiles(outs, lambda at, cols: dot32(value[at, :], weight[:, cols], 1, 0), value.shape[0])


def times_back(value, weight, *outs):
    put_tiles(outs, lambda at, cols: dot32(value[at, :], weight[cols, :], 1, 1), value.shape[0])


def put_tiles(outs, share_of, whole):
    own, partner, crossing = outs
    rows, model = own.shape

    def tile(i, carry):
        cols = pl.ds(pl.multiple_of(i * TILE, TILE), TILE)
        own[:, cols] = share_of(slice(0, rows), cols).astype(bf16)
        crossing[0, :, cols] = share_of(slice(rows, 2 * rows), cols).astype(bf16)
        partner[:, cols] = share_of(slice(2 * rows, 3 * rows), cols).astype(bf16)
        crossing[1, :, cols] = share_of(slice(3 * rows, 4 * rows), cols).astype(bf16)
        return carry

    lax.fori_loop(0, model // TILE, tile, 0)


def weight_grad(place, *refs, pairs, ring):
    firsts, seconds = refs[:pairs], refs[pairs : 2 * pairs]
    chunks, whole = refs[2 * pairs : -1], refs[-1]

    def tile(i, carry):
        rows = pl.ds(pl.multiple_of(i * TILE, TILE), TILE)
        total = None
        for first, second in zip(firsts, seconds):
            part = dot32(first[:, rows], second[...], 0, 0)
            total = part if total is None else total + part
        whole[rows, :] = total.astype(bf16)
        return carry

    lax.fori_loop(0, whole.shape[0] // TILE, tile, 0)
    put_chunks(place, chunks, whole, ring)


def put_chunks(place, chunks, whole, ring):
    for s, chunk in enumerate(chunks):
        size = chunk.shape[0]
        chunk[...] = whole[pl.ds(pl.multiple_of(place[2 * s + ring] * size, size), size), :]


def norm_two_back(scale, cot, resid, first, second, third, gain, out, rounded, sums, *, m):
    top = cot[m, 0].astype(f32) * scale[m]
    grad = three(first, second, third)
    hat, inverse = statistics(resid[...])
    back = top + norm_back(grad, hat, inverse, gain[...].astype(f32))
    out[...] = back
    rounded[...] = back.astype(bf16)
    sums[0:1, :] = jnp.sum(back, axis=0, keepdims=True)
    sums[1:2, :] = jnp.sum(grad * hat, axis=0, keepdims=True)
    sums[2:3, :] = jnp.sum(grad, axis=0, keepdims=True)
    sums[3:4, :] = jnp.sum(top, axis=0, keepdims=True)
    sums[4:8, :] = jnp.zeros_like(sums[4:8, :])


def attend_back(qkv, logs, mixed, out_weight, *refs, parts, step, low, wide):
    grads = refs[:parts]
    out, key_grad, value_grad, given, inner = refs[parts:]
    whole = qkv.shape[0]
    rows = whole // parts
    heads = wide // HEAD
    head = low // HEAD
    ones = jnp.concatenate([of_head(jnp.ones((8, wide), bf16), j) for j in range(heads)], axis=0)
    for b in range(parts):
        at = slice(b * rows, (b + 1) * rows)
        value = dot32(grads[b][...], out_weight[low : low + wide, :], 1, 1).astype(bf16)
        given[at, :] = value
        both = value.astype(f32) * mixed[at, low : low + wide].astype(f32)
        high = both.astype(bf16)
        rest = (both - high.astype(f32)).astype(bf16)
        inner[:, at] = dot32(ones, high, 1, 1) + dot32(ones, rest, 1, 1)
    key_pair = qkv[:, 3 * low + wide : 3 * low + 2 * wide]
    value_pair = qkv[:, 3 * low + 2 * wide : 3 * low + 3 * wide]
    key_t = key_pair.T
    keys = [of_head(key_pair, j) for j in range(heads)]
    values = [of_head(value_pair, j) for j in range(heads)]
    keys_t = [of_head(key_t, j, 0) for j in range(heads)]
    key_grad[...] = jnp.zeros_like(key_grad)
    value_grad[...] = jnp.zeros_like(value_grad)

    def block(i, carry):
        start = pl.multiple_of(i * step, step)
        query = qkv[pl.ds(start, step), 3 * low : 3 * low + wide]
        grad = given[pl.ds(start, step), :]
        total = None
        for j in range(heads):
            scores = dot32(keys[j], query, 1, 1)
            weights = jnp.exp(scores - logs[head + j : head + j + 1, pl.ds(start, step)])
            back = dot32(values[j], grad, 1, 1)
            score_grad = (weights * (back - inner[8 * j : 8 * j + 1, pl.ds(start, step)])).astype(bf16)
            value_grad[...] += dot32(weights.astype(bf16), of_head(grad, j), 1, 0)
            key_grad[...] += dot32(score_grad, of_head(query, j), 1, 0)
            part = dot32(keys_t[j], score_grad, 1, 0)
            total = part if total is None else total + part
        out[pl.ds(start, step), :wide] = (total.T * score_scale).astype(bf16)
        return carry

    lax.fori_loop(0, whole // step, block, 0)
    out[:, wide : 2 * wide] = key_grad[...].astype(bf16)
    out[:, 2 * wide :] = value_grad[...].astype(bf16)


def project_back(*refs, pairs):
    grads, weight, own, partner, crossing, sums = refs[:pairs], refs[pairs], *refs[pairs + 1 :]

    def share_of(at, cols):
        total, low = None, 0
        for grad in grads:
            wide = grad.shape[1]
            part = dot32(grad[at, :], weight[low : low + wide, cols], 1, 0)
            total = part if total is None else total + part
            low += wide
        return total

    put_tiles((own, partner, crossing), share_of, grads[0].shape[0])
    low = 0
    for grad in grads:
        wide = grad.shape[1]
        sums[:, low : low + wide] = jnp.sum(grad[...].astype(f32), axis=0, keepdims=True)
        low += wide


def projection_grad(place, *refs, micros, pairs, parts, count):
    normed, refs = refs[:micros], refs[micros:]
    grads, refs = [refs[m * pairs : (m + 1) * pairs] for m in range(micros)], refs[micros * pairs :]
    tops, refs = [refs[m * parts : (m + 1) * parts] for m in range(micros)], refs[micros * parts :]
    mixed, refs = refs[:micros], refs[micros:]
    chunks, (left, right) = refs[:-2], refs[-2:]
    width = mixed[0].shape[1]
    rows = tops[0][0].shape[0]
    for p, (low, wide) in enumerate(head_pairs(width)):
        total = None
        for m in range(micros):
            part = dot32(grads[m][p][...], normed[m][...], 0, 0)
            total = part if total is None else total + part
        left[low : low + wide, :] = total[:wide].astype(bf16)
        left[width + low : width + low + wide, :] = total[wide : 2 * wide].astype(bf16)
        right[low : low + wide, :] = total[2 * wide :].astype(bf16)
        total = None
        for m in range(micros):
            for b in range(parts):
                part = dot32(mixed[m][b * rows : (b + 1) * rows, low : low + wide], tops[m][b][...], 0, 0)
                total = part if total is None else total + part
        right[width + low : width + low + wide, :] = total.astype(bf16)
    put_chunks(place, chunks[:count], left, 0)
    put_chunks(place, chunks[count:], right, 1)


def ring_add(*refs):
    for i in range(2):
        refs[4 + i][...] = (refs[i][...].astype(f32) + refs[2 + i][...].astype(f32)).astype(bf16)


def ring_store(place, *refs, steps, divided):
    number = len(steps)
    moved, refs = refs[: 2 * number], refs[2 * number :]
    done, first, second, buffer, sems = refs[-5:]
    done[...] = jnp.zeros_like(done)
    size = buffer.shape[1]
    copies = []
    for k, step in enumerate(steps):
        for i in range(2):
            slot = 2 * k + i
            buffer[slot] = moved[slot][...].astype(f32)
            row = pl.multiple_of(place[2 * step + i] * size, size)
            if divided and i == 1:
                row = row + divided
                copy_second = pltpu.make_async_copy(
                    buffer.at[slot], second.at[pl.ds(pl.multiple_of(jnp.maximum(row - first.shape[0], 0), 16), size), :], sems.at[slot]
                )
                copy_first = pltpu.make_async_copy(
                    buffer.at[slot], first.at[pl.ds(pl.multiple_of(jnp.minimum(row, first.shape[0] - size), 16), size), :], sems.at[slot]
                )
                pl.when(row < first.shape[0])(copy_first.start)
                pl.when(row >= first.shape[0])(copy_second.start)
                copies.append(copy_first)
            else:
                target = second if i == 1 else first
                copies.append(pltpu.make_async_copy(buffer.at[slot], target.at[pl.ds(row, size), :], sems.at[slot]))
                copies[-1].start()
    for copy in copies:
        copy.wait()


def norm_one_back(tok, resid_grad, first, second, third, gain, out, sums, *, m):
    grad = three(first, second, third)
    hat, inverse = statistics(tok[m, 0].astype(f32))
    out[...] = resid_grad[...] + norm_back(grad, hat, inverse, gain[...].astype(f32))
    sums[0:4, :] = jnp.zeros_like(sums[0:4, :])
    sums[4:5, :] = jnp.sum(grad * hat, axis=0, keepdims=True)
    sums[5:6, :] = jnp.sum(grad, axis=0, keepdims=True)
    sums[6:8, :] = jnp.zeros_like(sums[6:8, :])


def add_rows(resid, first, second, third, bias, out):
    out[...] = (resid[...] + three(first, second, third) + bias[...].astype(f32)).astype(bf16)


def swap(values, axis, bit):
    return lax.ppermute(values, axis, [(i, i ^ bit) for i in range(lax.axis_size(axis))])


def ring_order(count):
    return list(range(0, count, 2)) + list(range(1, count, 2))[::-1]


def ring_tables(count):
    order = ring_order(count)
    sends = [[0] * (2 * count) for _ in range(count)]
    keeps = [[0] * (2 * count) for _ in range(count)]
    for place, device in enumerate(order):
        for step in range(count):
            for i, d in enumerate((1, -1)):
                sends[device][2 * step + i] = (place - d * (step + 1)) % count
                keeps[device][2 * step + i] = (place - d * step) % count
    return sends, keeps


def butterfly(values, axis):
    bit = 1
    while bit < lax.axis_size(axis):
        values = values + swap(values, axis, bit)
        bit *= 2
    return values


class Rings:
    def __init__(self, chain, keeps, shapes, divided=0):
        self.chain, self.keeps, self.shapes, self.divided = chain, keeps, shapes, divided
        self.count = lax.axis_size("wide")
        order = ring_order(self.count)
        self.perms = [[(order[i], order[(i + d) % self.count]) for i in range(self.count)] for d in (1, -1)]
        self.chunks, self.moving, self.have = [None, None], [None, None], []
        self.step = 1
        self.outs = None

    def start(self, i, chunks):
        self.chunks[i] = chunks
        self.moving[i] = lax.ppermute(chunks[0], "wide", self.perms[i])

    def hold(self, i):
        self.chain.hold(self.moving[i])

    def add(self):
        made = self.chain.run(
            ring_add, [(c.shape, bf16) for c in self.moving], *self.moving, self.chunks[0][self.step], self.chunks[1][self.step]
        )
        self.step += 1
        if self.step == self.count:
            self.have.append(made)
        self.moving = [lax.ppermute(c, "wide", self.perms[i]) for i, c in enumerate(made)]

    def forward(self):
        self.have.append(self.moving)
        self.chain.hold(*self.moving)
        if len(self.have) < self.count:
            self.moving = [lax.ppermute(c, "wide", self.perms[i]) for i, c in enumerate(self.moving)]

    def store(self, steps):
        moved = [c for s in steps for c in self.have[s]]
        kept = () if self.outs is None else self.outs
        made = self.chain.run(
            functools.partial(ring_store, steps=tuple(steps), divided=self.divided),
            [((8, LANES), f32)] + [(s, f32) for s in self.shapes],
            *moved,
            *kept,
            smem=(self.keeps,),
            scratch=[
                pltpu.VMEM((len(moved), *moved[0].shape), f32),
                pltpu.SemaphoreType.DMA((len(moved),)),
            ],
            alias={len(moved): 1, len(moved) + 1: 2} if kept else None,
            anywhere=(len(moved), len(moved) + 1) if kept else (),
            out_anywhere=(1, 2),
            limit=4 + (len(moved) * moved[0].size * 4 >> 20) + 1,
        )
        self.outs = made[1:]


class Whole:
    def __init__(self, shapes, divided=0):
        self.shapes, self.divided = shapes, divided
        self.arrays = [None, None]

    def start(self, i, chunks):
        self.arrays[i] = chunks[0]

    def hold(self, i):
        pass

    def add(self):
        pass

    def forward(self):
        pass

    def store(self, steps):
        if isinstance(self.arrays, list):
            self.arrays = lax.psum(tuple(self.arrays), "wide")
            first, second = (a.astype(f32) for a in self.arrays)
            if self.divided:
                cut = self.shapes[0][0] - self.divided
                first, second = jnp.concatenate([first, second[:cut]], axis=0), second[cut:]
            self.outs = (first, second)


def local(
    tokens,
    cotangent,
    cell_of,
    query_count,
    attn_norm_gain,
    attn_norm_bias,
    input_weight,
    query_bias,
    value_bias,
    out_weight,
    out_bias,
    ffn_norm_gain,
    ffn_norm_bias,
    up_weight,
    up_bias,
    down_weight,
    down_bias,
):
    micros = range(tokens.shape[0])
    rows, model = tokens.shape[2], tokens.shape[3]
    parts = lax.axis_size("narrow")
    whole = rows * parts
    width = input_weight.shape[2]
    hidden = up_weight.shape[1]
    count = lax.axis_size("wide")
    rings = count <= 8
    chunks = count if rings else 1
    pairs = head_pairs(width)
    step = min(512, whole)
    chain = Chain()
    run = chain.run
    index = lax.axis_index("wide")

    block = ((rows, model), bf16)
    outgoing = [block, block, ((2, rows, model), bf16)]
    wide_rows = ((whole, model), bf16)
    row = lambda v: v.reshape(1, -1)
    gain_one, bias_one, gain_two, bias_two = map(row, (attn_norm_gain, attn_norm_bias, ffn_norm_gain, ffn_norm_bias))
    out_bias, down_bias, up_bias = row(out_bias), row(down_bias), row(up_bias)

    slots = index + count * jnp.arange(len(micros), dtype=jnp.int32)
    counts = jnp.stack([query_count[cell_of[slots[m]]] for m in micros])
    scale = jnp.sqrt(counts.astype(f32) / 500.0)
    if rings:
        sends, keeps = (
            lax.dynamic_index_in_dim(jnp.array(t, jnp.int32), index, 0, keepdims=False) for t in ring_tables(count)
        )
    else:
        sends = keeps = jnp.zeros((2,), jnp.int32)

    def columns(three_parts):
        return jnp.concatenate([v[:, low : low + wide] for low, wide in pairs for v in three_parts], axis=1)

    weight_t = jnp.transpose(input_weight, (1, 2, 0)).reshape(3 * width, model)
    zero = jnp.zeros((1, width), f32)
    project_bias = columns([row(query_bias).astype(f32), zero, row(value_bias).astype(f32)])
    project_scale = columns([zero + score_scale, zero + 1.0, zero + 1.0])

    def gather(own):
        partner = swap(own, "narrow", 2)
        return [own, swap(own, "narrow", 1), partner, swap(partner, "narrow", 1)]

    def share(made):
        own, partner, crossing = made
        return [own, partner, swap(crossing, "narrow", 1)]

    def send(shares):
        own, partner, crossed = shares
        (both,) = run(pair_sum, [block], partner, crossed)
        return [own, crossed, swap(both, "narrow", 2)]

    def fresh():
        return [None] * len(micros)

    normed, given, qkv, normed_all, mixed, logs, shares, shares_down, resid, normed_two_b = (fresh() for _ in range(10))
    activ, pre_grad, up_bias_grad, two_all, given_all, resid_grad, top = (fresh() for _ in range(7))
    sums_two, sums_one, stack_sums, out_rows, grad_rows = (fresh() for _ in range(5))
    pair_grads = [[] for _ in micros]

    def do_norm_one(m):
        (own,) = run(functools.partial(norm_one, m=m), [block], tokens, gain_one, bias_one)
        normed[m] = gather(own)

    def do_scale(m):
        (own,) = run(functools.partial(scale_cot, m=m), [block], cotangent, smem=(scale,), cover=m == 0)
        given[m] = gather(own)

    def do_project(m):
        qkv[m], normed_all[m] = run(
            functools.partial(project, parts=parts),
            [((whole, 3 * width), bf16), wide_rows],
            *normed[m],
            weight,
            project_bias,
            project_scale,
        )

    def do_attend(m):
        mixed[m], logs[m], *made = run(
            functools.partial(attend, step=whole),
            [((whole, width), bf16), ((8, whole), f32), *outgoing],
            qkv[m],
            out_weight,
            limit=24,
        )
        shares[m] = share(made)

    def do_send(m):
        shares[m] = send(shares[m])

    def do_norm_two(m):
        resid[m], own = run(
            functools.partial(norm_two, m=m),
            [((rows, model), f32), block],
            tokens,
            *shares[m],
            out_bias,
            gain_two,
            bias_two,
            cover=m == 0,
        )
        normed_two_b[m] = gather(own)

    def do_feed(m):
        activ[m], pre_grad[m], up_bias_grad[m], two_all[m], given_all[m] = run(
            functools.partial(feed, parts=parts),
            [((whole, hidden), bf16), ((whole, hidden), bf16), ((1, hidden), f32), wide_rows, wide_rows],
            *normed_two_b[m],
            *given[m],
            up_weight,
            up_bias,
            down_weight,
        )

    def do_up_back(m):
        shares[m] = share(run(times_back, outgoing, pre_grad[m], up_weight))

    def do_down(m):
        shares_down[m] = share(run(times, outgoing, activ[m], down_weight))

    def do_send_down(m):
        shares_down[m] = send(shares_down[m])

    def do_norm_two_back(m):
        resid_grad[m], own, sums_two[m] = run(
            functools.partial(norm_two_back, m=m),
            [((rows, model), f32), block, ((8, model), f32)],
            cotangent,
            resid[m],
            *shares[m],
            gain_two,
            smem=(scale,),
            cover=True,
        )
        top[m] = gather(own)

    def do_attend_back(m, p):
        low, wide = pairs[p]
        (made,) = run(
            functools.partial(attend_back, parts=parts, step=step, low=low, wide=wide),
            [((whole, 3 * wide), bf16)],
            qkv[m],
            logs[m],
            mixed[m],
            out_weight,
            *top[m],
            scratch=[
                pltpu.VMEM((whole, wide), f32),
                pltpu.VMEM((whole, wide), f32),
                pltpu.VMEM((whole, wide), bf16),
                pltpu.VMEM((8 * (wide // HEAD), whole), f32),
            ],
            limit=20,
        )
        pair_grads[m].append(made)

    def do_project_back(m):
        *made, stack_sums[m] = run(
            functools.partial(project_back, pairs=len(pairs)),
            [*outgoing, ((1, 3 * width), f32)],
            *pair_grads[m],
            weight,
        )
        shares[m] = share(made)

    def do_norm_one_back(m):
        grad_rows[m], sums_one[m] = run(
            functools.partial(norm_one_back, m=m),
            [((rows, model), f32), ((8, model), f32)],
            tokens,
            resid_grad[m],
            *shares[m],
            gain_one,
        )

    def wait(*arrays):
        chain.hold(*arrays)
        run(mark, [((8, LANES), f32)], cover=True)

    def do_add_rows(m):
        (out_rows[m],) = run(add_rows, [block], resid[m], *shares_down[m], down_bias)

    def ffn_grad(firsts, seconds, ring):
        shape = (firsts[0].shape[1], seconds[0].shape[1])
        made = run(
            functools.partial(weight_grad, pairs=len(micros), ring=ring),
            [((shape[0] // chunks, shape[1]), bf16)] * chunks,
            *firsts,
            *seconds,
            smem=(sends,),
            scratch=[pltpu.VMEM(shape, bf16)],
            limit=16,
        )
        ffn.start(ring, made)

    def attn_grad():
        made = run(
            functools.partial(projection_grad, micros=len(micros), pairs=len(pairs), parts=parts, count=chunks),
            [((2 * width // chunks, model), bf16)] * (2 * chunks),
            *normed_all,
            *[g for m in micros for g in pair_grads[m]],
            *[t for m in micros for t in top[m]],
            *mixed,
            smem=(sends,),
            scratch=[pltpu.VMEM((2 * width, model), bf16)] * 2,
            limit=20,
        )
        attn.start(0, made[:chunks])
        attn.start(1, made[chunks:])

    ffn_shapes = [(hidden, model), (model, hidden)]
    attn_shapes = [(3 * width, model), (width, model)]
    ffn = Rings(chain, keeps, ffn_shapes) if rings else Whole(ffn_shapes)
    attn = Rings(chain, keeps, attn_shapes, 2 * width) if rings else Whole(attn_shapes, 2 * width)

    do_norm_one(0)
    (weight,) = run(by_pairs, [((3 * width, model), bf16)], weight_t)
    chain.hold(normed[0][1], normed[0][2])
    do_norm_one(1)
    do_project(0)
    do_attend(0)
    chain.hold(normed[1][1], normed[1][2])
    do_scale(0)
    do_send(0)
    chain.hold(given[0][1])
    do_project(1)
    do_attend(1)
    do_norm_two(0)
    do_send(1)
    chain.hold(normed_two_b[0][1])
    do_scale(1)
    do_norm_two(1)
    chain.hold(given[1][1], normed_two_b[1][1])
    do_feed(0)
    do_up_back(0)
    do_down(0)
    wait(given[1][2], normed_two_b[1][2])
    do_send(0)
    do_feed(1)
    do_up_back(1)
    do_norm_two_back(0)
    do_send(1)
    chain.hold(top[0][1])
    ffn_grad(activ, given_all, 0)
    ffn_grad(two_all, pre_grad, 1)
    ffn.hold(0)
    do_norm_two_back(1)
    chain.hold(top[1][1])
    ffn.add()
    do_attend_back(0, 0)
    ffn.add()
    do_attend_back(0, 1)
    ffn.add()
    do_attend_back(0, 2)
    ffn.add()
    do_attend_back(1, 0)
    do_send_down(0)
    ffn.add()
    do_attend_back(1, 1)
    ffn.add()
    do_attend_back(1, 2)
    ffn.add()
    attn_grad()
    ffn.forward()
    do_project_back(0)
    attn.add()
    do_send(0)
    ffn.forward()
    do_project_back(1)
    attn.add()
    do_send(1)
    ffn.forward()
    do_down(1)
    attn.add()
    do_send_down(1)
    ffn.forward()
    do_norm_one_back(0)
    attn.add()
    ffn.forward()
    do_norm_one_back(1)
    attn.add()
    ffn.forward()
    do_add_rows(0)
    attn.add()
    ffn.forward()
    do_add_rows(1)
    attn.add()
    ffn.store(range(0, 4))
    attn.forward()
    ffn.store(range(4, 8))
    attn.forward()
    attn.forward()
    attn.forward()
    attn.store(range(0, 4))
    attn.forward()
    attn.forward()
    attn.store(range(4, 7))
    attn.forward()
    attn.store(range(7, 8))

    vectors = sums_one[0] + sums_one[1] + sums_two[0] + sums_two[1]
    vectors = butterfly(vectors, "narrow")
    stack_sum = stack_sums[0] + stack_sums[1]
    packed = jnp.concatenate([vectors[:6].reshape(-1), (up_bias_grad[0] + up_bias_grad[1])[0], stack_sum[0]])
    packed = butterfly(packed, "wide")
    vector_sums = packed[: 6 * model].reshape(6, model)
    up_bias_sum = packed[6 * model : 6 * model + hidden]
    stack_sum = packed[6 * model + hidden :]

    def plain(j):
        return jnp.concatenate([stack_sum[3 * low + j * wide : 3 * low + (j + 1) * wide] for low, wide in pairs])

    return (
        jnp.stack(out_rows)[:, None],
        jnp.stack(grad_rows)[:, None],
        vector_sums[4],
        vector_sums[5],
        jnp.transpose(attn.outs[0].reshape(3, width, model), (2, 0, 1)),
        plain(0),
        plain(2),
        attn.outs[1],
        vector_sums[0],
        vector_sums[1],
        vector_sums[2],
        ffn.outs[1],
        up_bias_sum,
        ffn.outs[0],
        vector_sums[3],
    )


def solution(mesh):
    in_specs = (
        P(None, "wide", "narrow", None),
        P(None, "wide", "narrow", None),
        P(),
        P(),
        P(),
        P(),
        P(None, None, "narrow"),
        P("narrow"),
        P("narrow"),
        P("narrow", None),
        P(),
        P(),
        P(),
        P(None, "narrow"),
        P("narrow"),
        P("narrow", None),
        P(),
    )
    out_specs = (
        P(None, "wide", "narrow", None),
        P(None, "wide", "narrow", None),
        P(),
        P(),
        P(None, None, "narrow"),
        P("narrow"),
        P("narrow"),
        P("narrow", None),
        P(),
        P(),
        P(),
        P(None, "narrow"),
        P("narrow"),
        P("narrow", None),
        P(),
    )
    return jax.shard_map(local, mesh=mesh, in_specs=in_specs, out_specs=out_specs, check_vma=False)
```

```python
import functools

import jax
import jax.numpy as jnp
from jax import lax
from jax.experimental import pallas as pl
from jax.experimental.pallas import tpu as pltpu
from jax.sharding import PartitionSpec as P

HEAD = 64
LANES = 128
TILE = 256
norm_eps = 1e-05
score_scale = 0.125
bf16 = jnp.bfloat16
f32 = jnp.float32


class Chain:
    def __init__(self):
        self.last = []
        self.held = []

    def hold(self, *arrays):
        self.held += arrays

    def run(self, body, outs, *ins, smem=(), scratch=(), alias=None, anywhere=(), out_anywhere=(), limit=12, token=0, cover=False):
        unread = [*self.last, *self.held]
        count = len(smem) + len(ins)
        specs = [pl.BlockSpec(memory_space=pltpu.SMEM)] * len(smem)
        specs += [pl.BlockSpec(memory_space=pl.ANY if i in anywhere else pltpu.VMEM) for i in range(len(ins))]
        specs += [pl.BlockSpec(memory_space=pl.ANY)] * len(unread)

        def inner(*refs):
            body(*refs[:count], *refs[count + len(unread) :])

        made = pl.pallas_call(
            inner,
            out_shape=tuple(jax.ShapeDtypeStruct(*o) for o in outs),
            in_specs=specs,
            out_specs=tuple(
                pl.BlockSpec(memory_space=pl.ANY if i in out_anywhere else pltpu.VMEM) for i in range(len(outs))
            ),
            scratch_shapes=scratch,
            input_output_aliases={} if alias is None else {len(smem) + k: v for k, v in alias.items()},
            compiler_params=pltpu.CompilerParams(vmem_limit_bytes=limit << 20),
            cost_estimate=pl.CostEstimate(flops=10**12 if cover else 1, bytes_accessed=1, transcendentals=0),
            name=body.func.__name__ if isinstance(body, functools.partial) else body.__name__,
        )(*smem, *ins, *unread)
        self.last, self.held = [made[token]], []
        return made


def dot32(first, second, first_dim, second_dim):
    return lax.dot_general(
        first, second, (((first_dim,), (second_dim,)), ((), ())), preferred_element_type=f32
    )


def statistics(values):
    average = jnp.mean(values, axis=-1, keepdims=True)
    centred = values - average
    inverse = lax.rsqrt(jnp.mean(centred * centred, axis=-1, keepdims=True) + norm_eps)
    return centred * inverse, inverse


def norm_back(grad, normed, inverse, gain):
    scaled = grad * gain
    mean_one = jnp.mean(scaled, axis=-1, keepdims=True)
    mean_two = jnp.mean(scaled * normed, axis=-1, keepdims=True)
    return inverse * (scaled - mean_one - normed * mean_two)


def of_head(values, j, axis=1):
    if values.shape[axis] <= HEAD:
        return values
    place = lax.broadcasted_iota(jnp.int32, values.shape, axis)
    return jnp.where((place >= HEAD * j) & (place < HEAD * (j + 1)), values, jnp.zeros_like(values))


def head_pairs(width):
    return [(low, min(LANES, width - low)) for low in range(0, width, LANES)]


def mark(out):
    out[...] = jnp.zeros_like(out)


def by_pairs(weight_t, out):
    width = out.shape[0] // 3
    for low, wide in head_pairs(width):
        for j in range(3):
            out[3 * low + j * wide : 3 * low + (j + 1) * wide, :] = weight_t[
                j * width + low : j * width + low + wide, :
            ]


def norm_one(tok, gain, bias, out, *, m):
    normed, _ = statistics(tok[m, 0].astype(f32))
    out[...] = (normed * gain[...].astype(f32) + bias[...].astype(f32)).astype(bf16)


def loss_grad(index, cells, queries, cot, m, count):
    number = queries[cells[index[0] + m * count]]
    scale = jnp.sqrt(jnp.full((1, cot.shape[3]), number, jnp.int32).astype(f32) / 500.0)
    return cot[m, 0].astype(f32) * scale


def scale_cot(index, cells, queries, cot, out, *, m, count):
    out[...] = loss_grad(index, cells, queries, cot, m, count).astype(bf16)


def project(*refs, parts):
    blocks = refs[:parts]
    weight, bias, scale = refs[parts : parts + 3]
    out, whole = refs[parts + 3 :]
    rows = blocks[0].shape[0]
    for b in range(parts):
        values = blocks[b][...]
        at = slice(b * rows, (b + 1) * rows)
        whole[at, :] = values
        out[at, :] = ((dot32(values, weight[...], 1, 1) + bias[...]) * scale[...]).astype(bf16)


def attend(qkv, out_weight, attended, logs, *outs, step):
    whole = qkv.shape[0]
    head = 0
    for low, wide in head_pairs(out_weight.shape[0]):
        heads = wide // HEAD
        key_pair = qkv[:, 3 * low + wide : 3 * low + 2 * wide]
        value_t = qkv[:, 3 * low + 2 * wide : 3 * low + 3 * wide].T
        keys = [of_head(key_pair, j) for j in range(heads)]
        values = [of_head(value_t, j, 0) for j in range(heads)]
        for start in range(0, whole, step):
            at = slice(start, start + step)
            query = qkv[at, 3 * low : 3 * low + wide]
            total = None
            for j in range(heads):
                scores = dot32(keys[j], query, 1, 1)
                top = jnp.max(scores, axis=0, keepdims=True)
                powers = jnp.exp(scores - top)
                length = jnp.sum(powers, axis=0, keepdims=True)
                mixed = dot32(values[j], powers.astype(bf16), 1, 0) * (1.0 / length)
                total = mixed if total is None else total + mixed
                logs[head + j : head + j + 1, at] = top + jnp.log(length)
            attended[at, low : low + wide] = total.T.astype(bf16)
        head += heads
    put_shares(outs, lambda at: dot32(attended[at, :], out_weight[...], 1, 0), whole)


def put_shares(outs, share_of, whole):
    own, partner, crossing = outs
    rows = own.shape[0]
    for b, (out, at) in enumerate(((own, None), (crossing, 0), (partner, None), (crossing, 1))):
        value = share_of(slice(b * rows, (b + 1) * rows)).astype(bf16)
        if at is None:
            out[...] = value
        else:
            out[at] = value


def pair_sum(first, second, out):
    out[...] = (first[...].astype(f32) + second[1].astype(f32)).astype(bf16)


def three(first, second, third):
    return first[...].astype(f32) + second[0].astype(f32) + third[...].astype(f32)


def norm_two(tok, first, second, third, out_bias, gain, bias, resid, normed, *, m):
    value = tok[m, 0].astype(f32) + three(first, second, third) + out_bias[...].astype(f32)
    resid[...] = value
    hat, _ = statistics(value)
    normed[...] = (hat * gain[...].astype(f32) + bias[...].astype(f32)).astype(bf16)


def feed(*refs, parts):
    normed, grads = refs[:parts], refs[parts : 2 * parts]
    up, up_bias, down = refs[2 * parts : 2 * parts + 3]
    activ, pre_grad, bias_grad, normed_all, grads_all = refs[2 * parts + 3 :]
    rows = normed[0].shape[0]
    for b in range(parts):
        normed_all[b * rows : (b + 1) * rows, :] = normed[b][...]
        grads_all[b * rows : (b + 1) * rows, :] = grads[b][...]
    for low in range(0, up.shape[1], TILE):
        cols = slice(low, low + TILE)
        total = None
        for b in range(parts):
            at = slice(b * rows, (b + 1) * rows)
            pre = dot32(normed[b][...], up[:, cols], 1, 0) + up_bias[:, cols].astype(f32)
            cumul = 0.5 + 0.5 * lax.erf(pre * 0.7071067811865476)
            density = jnp.exp(-0.5 * pre * pre) * 0.3989422804014327
            activ[at, cols] = (pre * cumul).astype(bf16)
            back = dot32(grads[b][...], down[cols, :], 1, 1)
            grad = (back * (cumul + pre * density)).astype(bf16)
            pre_grad[at, cols] = grad
            part = jnp.sum(grad.astype(f32), axis=0, keepdims=True)
            total = part if total is None else total + part
        bias_grad[:, cols] = total


def times(value, weight, *outs):
    put_tiles(outs, lambda at, cols: dot32(value[at, :], weight[:, cols], 1, 0), value.shape[0])


def times_back(value, weight, *outs):
    put_tiles(outs, lambda at, cols: dot32(value[at, :], weight[cols, :], 1, 1), value.shape[0])


def put_tiles(outs, share_of, whole):
    own, partner, crossing = outs
    rows, model = own.shape

    def tile(i, carry):
        cols = pl.ds(pl.multiple_of(i * TILE, TILE), TILE)
        own[:, cols] = share_of(slice(0, rows), cols).astype(bf16)
        crossing[0, :, cols] = share_of(slice(rows, 2 * rows), cols).astype(bf16)
        partner[:, cols] = share_of(slice(2 * rows, 3 * rows), cols).astype(bf16)
        crossing[1, :, cols] = share_of(slice(3 * rows, 4 * rows), cols).astype(bf16)
        return carry

    lax.fori_loop(0, model // TILE, tile, 0)


def weight_grad(index, *refs, pairs, ring):
    firsts, seconds = refs[:pairs], refs[pairs : 2 * pairs]
    chunks, whole = refs[2 * pairs : -1], refs[-1]

    def tile(i, carry):
        rows = pl.ds(pl.multiple_of(i * TILE, TILE), TILE)
        total = None
        for first, second in zip(firsts, seconds):
            part = dot32(first[:, rows], second[...], 0, 0)
            total = part if total is None else total + part
        whole[rows, :] = total.astype(bf16)
        return carry

    lax.fori_loop(0, whole.shape[0] // TILE, tile, 0)
    put_chunks(index, chunks, whole, ring)


def ring_chunk(index, count, ring, step):
    half = index // 2
    place = jnp.where(index % 2 == 0, half, count - 1 - half)
    return lax.rem(place + (count - step if ring == 0 else step), count)


def put_chunks(index, chunks, whole, ring):
    for s, chunk in enumerate(chunks):
        size = chunk.shape[0]
        which = ring_chunk(index[0], len(chunks), ring, (s + 1) % len(chunks)) if len(chunks) > 1 else 0
        chunk[...] = whole[pl.ds(pl.multiple_of(which * size, size), size), :]


def norm_two_back(index, cells, queries, cot, resid, first, second, third, gain, out, rounded, sums, *, m, count):
    top = loss_grad(index, cells, queries, cot, m, count)
    grad = three(first, second, third)
    hat, inverse = statistics(resid[...])
    back = top + norm_back(grad, hat, inverse, gain[...].astype(f32))
    out[...] = back
    rounded[...] = back.astype(bf16)
    sums[0:1, :] = jnp.sum(back, axis=0, keepdims=True)
    sums[1:2, :] = jnp.sum(grad * hat, axis=0, keepdims=True)
    sums[2:3, :] = jnp.sum(grad, axis=0, keepdims=True)
    sums[3:4, :] = jnp.sum(top, axis=0, keepdims=True)
    sums[4:8, :] = jnp.zeros_like(sums[4:8, :])


def attend_back(qkv, logs, mixed, out_weight, *refs, parts, step, low, wide):
    grads = refs[:parts]
    out, key_grad, value_grad, given, inner = refs[parts:]
    whole = qkv.shape[0]
    rows = whole // parts
    heads = wide // HEAD
    head = low // HEAD
    ones = jnp.concatenate([of_head(jnp.ones((8, wide), bf16), j) for j in range(heads)], axis=0)
    for b in range(parts):
        at = slice(b * rows, (b + 1) * rows)
        value = dot32(grads[b][...], out_weight[low : low + wide, :], 1, 1).astype(bf16)
        given[at, :] = value
        both = value.astype(f32) * mixed[at, low : low + wide].astype(f32)
        high = both.astype(bf16)
        rest = (both - high.astype(f32)).astype(bf16)
        inner[:, at] = dot32(ones, high, 1, 1) + dot32(ones, rest, 1, 1)
    key_pair = qkv[:, 3 * low + wide : 3 * low + 2 * wide]
    value_pair = qkv[:, 3 * low + 2 * wide : 3 * low + 3 * wide]
    key_t = key_pair.T
    keys = [of_head(key_pair, j) for j in range(heads)]
    values = [of_head(value_pair, j) for j in range(heads)]
    keys_t = [of_head(key_t, j, 0) for j in range(heads)]
    key_grad[...] = jnp.zeros_like(key_grad)
    value_grad[...] = jnp.zeros_like(value_grad)

    def block(i, carry):
        start = pl.multiple_of(i * step, step)
        query = qkv[pl.ds(start, step), 3 * low : 3 * low + wide]
        grad = given[pl.ds(start, step), :]
        total = None
        for j in range(heads):
            scores = dot32(keys[j], query, 1, 1)
            weights = jnp.exp(scores - logs[head + j : head + j + 1, pl.ds(start, step)])
            back = dot32(values[j], grad, 1, 1)
            score_grad = (weights * (back - inner[8 * j : 8 * j + 1, pl.ds(start, step)])).astype(bf16)
            value_grad[...] += dot32(weights.astype(bf16), of_head(grad, j), 1, 0)
            key_grad[...] += dot32(score_grad, of_head(query, j), 1, 0)
            part = dot32(keys_t[j], score_grad, 1, 0)
            total = part if total is None else total + part
        out[pl.ds(start, step), :wide] = (total.T * score_scale).astype(bf16)
        return carry

    lax.fori_loop(0, whole // step, block, 0)
    out[:, wide : 2 * wide] = key_grad[...].astype(bf16)
    out[:, 2 * wide :] = value_grad[...].astype(bf16)


def project_back(*refs, pairs):
    grads, weight, own, partner, crossing, sums = refs[:pairs], refs[pairs], *refs[pairs + 1 :]

    def share_of(at, cols):
        total, low = None, 0
        for grad in grads:
            wide = grad.shape[1]
            part = dot32(grad[at, :], weight[low : low + wide, cols], 1, 0)
            total = part if total is None else total + part
            low += wide
        return total

    put_tiles((own, partner, crossing), share_of, grads[0].shape[0])
    low = 0
    for grad in grads:
        wide = grad.shape[1]
        sums[:, low : low + wide] = jnp.sum(grad[...].astype(f32), axis=0, keepdims=True)
        low += wide


def projection_grad(index, *refs, micros, pairs, parts, count):
    normed, refs = refs[:micros], refs[micros:]
    grads, refs = [refs[m * pairs : (m + 1) * pairs] for m in range(micros)], refs[micros * pairs :]
    tops, refs = [refs[m * parts : (m + 1) * parts] for m in range(micros)], refs[micros * parts :]
    mixed, refs = refs[:micros], refs[micros:]
    chunks, (left, right) = refs[:-2], refs[-2:]
    width = mixed[0].shape[1]
    rows = tops[0][0].shape[0]
    for p, (low, wide) in enumerate(head_pairs(width)):
        total = None
        for m in range(micros):
            part = dot32(grads[m][p][...], normed[m][...], 0, 0)
            total = part if total is None else total + part
        left[low : low + wide, :] = total[:wide].astype(bf16)
        left[width + low : width + low + wide, :] = total[wide : 2 * wide].astype(bf16)
        right[low : low + wide, :] = total[2 * wide :].astype(bf16)
        total = None
        for m in range(micros):
            for b in range(parts):
                part = dot32(mixed[m][b * rows : (b + 1) * rows, low : low + wide], tops[m][b][...], 0, 0)
                total = part if total is None else total + part
        right[width + low : width + low + wide, :] = total.astype(bf16)
    put_chunks(index, chunks[:count], left, 0)
    put_chunks(index, chunks[count:], right, 1)


def ring_add(*refs):
    for i in range(2):
        refs[4 + i][...] = (refs[i][...].astype(f32) + refs[2 + i][...].astype(f32)).astype(bf16)


def ring_store(index, *refs, steps, divided, count):
    number = len(steps)
    moved, refs = refs[: 2 * number], refs[2 * number :]
    done, first, second, buffer, sems = refs[-5:]
    done[...] = jnp.zeros_like(done)
    size = buffer.shape[1]
    copies = []
    for k, step in enumerate(steps):
        for i in range(2):
            slot = 2 * k + i
            buffer[slot] = moved[slot][...].astype(f32)
            row = pl.multiple_of(ring_chunk(index[0], count, i, step) * size, size)
            if divided and i == 1:
                row = row + divided
                copy_second = pltpu.make_async_copy(
                    buffer.at[slot], second.at[pl.ds(pl.multiple_of(jnp.maximum(row - first.shape[0], 0), 16), size), :], sems.at[slot]
                )
                copy_first = pltpu.make_async_copy(
                    buffer.at[slot], first.at[pl.ds(pl.multiple_of(jnp.minimum(row, first.shape[0] - size), 16), size), :], sems.at[slot]
                )
                pl.when(row < first.shape[0])(copy_first.start)
                pl.when(row >= first.shape[0])(copy_second.start)
                copies.append(copy_first)
            else:
                target = second if i == 1 else first
                copies.append(pltpu.make_async_copy(buffer.at[slot], target.at[pl.ds(row, size), :], sems.at[slot]))
                copies[-1].start()
    for copy in copies:
        copy.wait()


def norm_one_back(tok, resid_grad, first, second, third, gain, out, sums, *, m):
    grad = three(first, second, third)
    hat, inverse = statistics(tok[m, 0].astype(f32))
    out[...] = resid_grad[...] + norm_back(grad, hat, inverse, gain[...].astype(f32))
    sums[0:4, :] = jnp.zeros_like(sums[0:4, :])
    sums[4:5, :] = jnp.sum(grad * hat, axis=0, keepdims=True)
    sums[5:6, :] = jnp.sum(grad, axis=0, keepdims=True)
    sums[6:8, :] = jnp.zeros_like(sums[6:8, :])


def vector_sum(*refs):
    total = refs[0][...]
    for ref in refs[1:-1]:
        total = total + ref[...]
    refs[-1][...] = total


def vector_join(first, second, *refs, number):
    up_bias, stack, out = refs[:number], refs[number:-1], refs[-1]
    out[...] = first[...] + second[...]
    for row, parts in ((6, up_bias), (7, stack)):
        total = parts[0][...]
        for part in parts[1:]:
            total = total + part[...]
        out[row : row + 1, : total.shape[1]] = total


def add_rows(resid, first, second, third, bias, out):
    out[...] = (resid[...] + three(first, second, third) + bias[...].astype(f32)).astype(bf16)


def swap(values, axis, bit):
    return lax.ppermute(values, axis, [(i, i ^ bit) for i in range(lax.axis_size(axis))])


def ring_order(count):
    return list(range(0, count, 2)) + list(range(1, count, 2))[::-1]


class Rings:
    def __init__(self, chain, index, shapes, divided=0):
        self.chain, self.index, self.shapes, self.divided = chain, index, shapes, divided
        self.count = lax.axis_size("wide")
        order = ring_order(self.count)
        self.perms = [[(order[i], order[(i + d) % self.count]) for i in range(self.count)] for d in (1, -1)]
        self.chunks, self.moving, self.have = [None, None], [None, None], []
        self.step = 1
        self.outs = None

    def start(self, i, chunks):
        self.chunks[i] = chunks
        self.moving[i] = lax.ppermute(chunks[0], "wide", self.perms[i])

    def hold(self, i):
        self.chain.hold(self.moving[i])

    def add(self, cover=False):
        made = self.chain.run(
            ring_add,
            [(c.shape, bf16) for c in self.moving],
            *self.moving,
            *[c[self.step] for c in self.chunks],
            cover=cover,
        )
        self.step += 1
        if self.step == self.count:
            self.have.append(made)
        self.moving = [lax.ppermute(c, "wide", self.perms[i]) for i, c in enumerate(made)]

    def forward(self):
        self.have.append(self.moving)
        self.chain.hold(*self.moving)
        if len(self.have) < self.count:
            self.moving = [lax.ppermute(c, "wide", self.perms[i]) for i, c in enumerate(self.moving)]

    def store(self, steps):
        moved = [c for s in steps for c in self.have[s]]
        kept = () if self.outs is None else self.outs
        made = self.chain.run(
            functools.partial(ring_store, steps=tuple(steps), divided=self.divided, count=self.count),
            [((8, LANES), f32)] + [(s, f32) for s in self.shapes],
            *moved,
            *kept,
            smem=(self.index,),
            scratch=[
                pltpu.VMEM((len(moved), *moved[0].shape), f32),
                pltpu.SemaphoreType.DMA((len(moved),)),
            ],
            alias={len(moved): 1, len(moved) + 1: 2} if kept else None,
            anywhere=(len(moved), len(moved) + 1) if kept else (),
            out_anywhere=(1, 2),
            limit=3 + (len(moved) * moved[0].size * 4 >> 20),
            cover=True,
        )
        self.outs = made[1:]


class Whole:
    def __init__(self, shapes, divided=0):
        self.shapes, self.divided = shapes, divided
        self.arrays = [None, None]

    def start(self, i, chunks):
        self.arrays[i] = chunks[0]

    def hold(self, i):
        pass

    def add(self, cover=False):
        pass

    def forward(self):
        pass

    def store(self, steps):
        if isinstance(self.arrays, list):
            self.arrays = lax.psum(tuple(self.arrays), "wide")
            first, second = (a.astype(f32) for a in self.arrays)
            if self.divided:
                cut = self.shapes[0][0] - self.divided
                first, second = jnp.concatenate([first, second[:cut]], axis=0), second[cut:]
            self.outs = (first, second)


def local(
    tokens,
    cotangent,
    cell_of,
    query_count,
    attn_norm_gain,
    attn_norm_bias,
    input_weight,
    query_bias,
    value_bias,
    out_weight,
    out_bias,
    ffn_norm_gain,
    ffn_norm_bias,
    up_weight,
    up_bias,
    down_weight,
    down_bias,
):
    micros = range(tokens.shape[0])
    rows, model = tokens.shape[2], tokens.shape[3]
    parts = lax.axis_size("narrow")
    whole = rows * parts
    width = input_weight.shape[2]
    hidden = up_weight.shape[1]
    count = lax.axis_size("wide")
    rings = count <= 8
    chunks = count if rings else 1
    pairs = head_pairs(width)
    step = min(512, whole)
    chain = Chain()
    run = chain.run
    index = lax.axis_index("wide").astype(jnp.int32).reshape(1)

    block = ((rows, model), bf16)
    outgoing = [block, block, ((2, rows, model), bf16)]
    wide_rows = ((whole, model), bf16)
    row = lambda v: v.reshape(1, -1)
    gain_one, bias_one, gain_two, bias_two = map(row, (attn_norm_gain, attn_norm_bias, ffn_norm_gain, ffn_norm_bias))
    out_bias, down_bias, up_bias = row(out_bias), row(down_bias), row(up_bias)

    def columns(three_parts):
        return jnp.concatenate([v[:, low : low + wide] for low, wide in pairs for v in three_parts], axis=1)

    weight_t = jnp.transpose(input_weight, (1, 2, 0)).reshape(3 * width, model)
    zero = jnp.zeros((1, width), f32)
    project_bias = columns([row(query_bias).astype(f32), zero, row(value_bias).astype(f32)])
    project_scale = columns([zero + score_scale, zero + 1.0, zero + 1.0])

    def gather(own):
        partner = swap(own, "narrow", 2)
        return [own, swap(own, "narrow", 1), partner, swap(partner, "narrow", 1)]

    def share(made):
        own, partner, crossing = made
        return [own, partner, swap(crossing, "narrow", 1)]

    def send(shares):
        own, partner, crossed = shares
        (both,) = run(pair_sum, [block], partner, crossed)
        return [own, crossed, swap(both, "narrow", 2)]

    def fresh():
        return [None] * len(micros)

    normed, given, qkv, normed_all, mixed, logs, shares, shares_down, resid, normed_two_b = (fresh() for _ in range(10))
    activ, pre_grad, up_bias_grad, two_all, given_all, resid_grad, top = (fresh() for _ in range(7))
    sums_two, sums_one, stack_sums, out_rows, grad_rows = (fresh() for _ in range(5))
    pair_grads = [[] for _ in micros]

    def do_norm_one(m):
        (own,) = run(functools.partial(norm_one, m=m), [block], tokens, gain_one, bias_one)
        normed[m] = gather(own)

    def do_scale(m):
        (own,) = run(functools.partial(scale_cot, m=m, count=count), [block], cotangent, smem=(index, cell_of, query_count), cover=True)
        given[m] = gather(own)

    def do_project(m):
        qkv[m], normed_all[m] = run(
            functools.partial(project, parts=parts),
            [((whole, 3 * width), bf16), wide_rows],
            *normed[m],
            weight,
            project_bias,
            project_scale,
        )

    def do_attend(m):
        mixed[m], logs[m], *made = run(
            functools.partial(attend, step=whole),
            [((whole, width), bf16), ((8, whole), f32), *outgoing],
            qkv[m],
            out_weight,
            limit=24,
        )
        shares[m] = share(made)

    def do_send(m):
        shares[m] = send(shares[m])

    def do_norm_two(m):
        resid[m], own = run(
            functools.partial(norm_two, m=m),
            [((rows, model), f32), block],
            tokens,
            *shares[m],
            out_bias,
            gain_two,
            bias_two,
            cover=m == 0,
        )
        normed_two_b[m] = gather(own)

    def do_feed(m):
        activ[m], pre_grad[m], up_bias_grad[m], two_all[m], given_all[m] = run(
            functools.partial(feed, parts=parts),
            [((whole, hidden), bf16), ((whole, hidden), bf16), ((1, hidden), f32), wide_rows, wide_rows],
            *normed_two_b[m],
            *given[m],
            up_weight,
            up_bias,
            down_weight,
        )

    def do_up_back(m):
        shares[m] = share(run(times_back, outgoing, pre_grad[m], up_weight))

    def do_down(m):
        shares_down[m] = share(run(times, outgoing, activ[m], down_weight))

    def do_send_down(m):
        shares_down[m] = send(shares_down[m])

    def do_norm_two_back(m):
        resid_grad[m], own, sums_two[m] = run(
            functools.partial(norm_two_back, m=m, count=count),
            [((rows, model), f32), block, ((8, model), f32)],
            cotangent,
            resid[m],
            *shares[m],
            gain_two,
            smem=(index, cell_of, query_count),
            cover=True,
        )
        top[m] = gather(own)

    def do_attend_back(m, p):
        low, wide = pairs[p]
        (made,) = run(
            functools.partial(attend_back, parts=parts, step=step, low=low, wide=wide),
            [((whole, 3 * wide), bf16)],
            qkv[m],
            logs[m],
            mixed[m],
            out_weight,
            *top[m],
            scratch=[
                pltpu.VMEM((whole, wide), f32),
                pltpu.VMEM((whole, wide), f32),
                pltpu.VMEM((whole, wide), bf16),
                pltpu.VMEM((8 * (wide // HEAD), whole), f32),
            ],
            limit=20,
        )
        pair_grads[m].append(made)

    def do_project_back(m):
        *made, stack_sums[m] = run(
            functools.partial(project_back, pairs=len(pairs)),
            [*outgoing, ((1, 3 * width), f32)],
            *pair_grads[m],
            weight,
        )
        shares[m] = share(made)

    def do_norm_one_back(m):
        grad_rows[m], sums_one[m] = run(
            functools.partial(norm_one_back, m=m),
            [((rows, model), f32), ((8, model), f32)],
            tokens,
            resid_grad[m],
            *shares[m],
            gain_one,
        )

    def wait(*arrays):
        chain.hold(*arrays)
        run(mark, [((8, LANES), f32)], cover=True)

    hops = [("narrow", 1 << k) for k in range(parts.bit_length() - 1)]
    hops += [("wide", 1 << k) for k in range(count.bit_length() - 1)]
    vectors = []

    def do_vectors():
        done = len(vectors)
        shape = [((8, model), f32)]
        if done == 0:
            (own,) = run(vector_sum, shape, *sums_one, *sums_two)
        elif hops[done - 1][0] == "narrow" and hops[done][0] == "wide":
            own, arrived = vectors[-1]
            (own,) = run(
                functools.partial(vector_join, number=len(micros)), shape, own, arrived, *up_bias_grad, *stack_sums
            )
        else:
            (own,) = run(vector_sum, shape, *vectors[-1])
        vectors.append((own, swap(own, *hops[done]) if done < len(hops) else None))

    def do_add_rows(m):
        (out_rows[m],) = run(add_rows, [block], resid[m], *shares_down[m], down_bias)

    def ffn_grad(firsts, seconds, ring):
        shape = (firsts[0].shape[1], seconds[0].shape[1])
        made = run(
            functools.partial(weight_grad, pairs=len(micros), ring=ring),
            [((shape[0] // chunks, shape[1]), bf16)] * chunks,
            *firsts,
            *seconds,
            smem=(index,),
            scratch=[pltpu.VMEM(shape, bf16)],
            limit=16,
        )
        ffn.start(ring, made)

    def attn_grad():
        made = run(
            functools.partial(projection_grad, micros=len(micros), pairs=len(pairs), parts=parts, count=chunks),
            [((2 * width // chunks, model), bf16)] * (2 * chunks),
            *normed_all,
            *[g for m in micros for g in pair_grads[m]],
            *[t for m in micros for t in top[m]],
            *mixed,
            smem=(index,),
            scratch=[pltpu.VMEM((2 * width, model), bf16)] * 2,
            limit=20,
        )
        attn.start(0, made[:chunks])
        attn.start(1, made[chunks:])

    ffn_shapes = [(hidden, model), (model, hidden)]
    attn_shapes = [(3 * width, model), (width, model)]
    ffn = Rings(chain, index, ffn_shapes) if rings else Whole(ffn_shapes)
    attn = Rings(chain, index, attn_shapes, 2 * width) if rings else Whole(attn_shapes, 2 * width)

    do_norm_one(0)
    (weight,) = run(by_pairs, [((3 * width, model), bf16)], weight_t)
    chain.hold(normed[0][1], normed[0][2])
    do_norm_one(1)
    do_project(0)
    do_attend(0)
    chain.hold(normed[1][1], normed[1][2])
    do_scale(0)
    do_send(0)
    do_scale(1)
    chain.hold(given[0][1], given[1][1])
    do_project(1)
    do_attend(1)
    chain.hold(given[0][2], given[1][2])
    do_norm_two(0)
    do_send(1)
    chain.hold(normed_two_b[0][1])
    do_norm_two(1)
    chain.hold(normed_two_b[1][1])
    do_feed(0)
    do_up_back(0)
    do_down(0)
    wait(normed_two_b[1][2])
    do_send(0)
    do_feed(1)
    do_up_back(1)
    do_norm_two_back(0)
    do_send(1)
    chain.hold(top[0][1])
    ffn_grad(activ, given_all, 0)
    ffn_grad(two_all, pre_grad, 1)
    ffn.hold(0)
    do_norm_two_back(1)
    chain.hold(top[1][1])
    ffn.add()
    do_attend_back(0, 0)
    ffn.add()
    do_attend_back(0, 1)
    ffn.add()
    do_attend_back(0, 2)
    ffn.add()
    do_attend_back(1, 0)
    do_send_down(0)
    ffn.add()
    do_attend_back(1, 1)
    ffn.add()
    do_attend_back(1, 2)
    ffn.add()
    attn_grad()
    ffn.forward()
    attn.add(cover=True)
    do_project_back(0)
    attn.add(cover=True)
    do_send(0)
    ffn.forward()
    do_project_back(1)
    attn.add(cover=True)
    do_send(1)
    attn.add(cover=True)
    ffn.forward()
    do_norm_one_back(0)
    do_down(1)
    attn.add(cover=True)
    do_send_down(1)
    attn.add(cover=True)
    ffn.forward()
    do_norm_one_back(1)
    attn.add(cover=True)
    do_vectors()
    ffn.store(range(0, 4))
    ffn.forward()
    attn.forward()
    do_vectors()
    do_add_rows(0)
    attn.forward()
    do_vectors()
    do_add_rows(1)
    ffn.forward()
    attn.forward()
    do_vectors()
    ffn.store(range(4, 6))
    attn.forward()
    do_vectors()
    attn.store(range(0, 4))
    ffn.forward()
    attn.forward()
    do_vectors()
    ffn.store(range(6, 8))
    attn.forward()
    attn.store(range(4, 7))
    attn.forward()
    attn.store(range(7, 8))

    while len(vectors) <= len(hops):
        do_vectors()
    vector_sums = vectors[-1][0]
    up_bias_sum = vector_sums[6, :hidden]
    stack_sum = vector_sums[7, : 3 * width]

    def plain(j):
        return jnp.concatenate([stack_sum[3 * low + j * wide : 3 * low + (j + 1) * wide] for low, wide in pairs])

    return (
        jnp.stack(out_rows)[:, None],
        jnp.stack(grad_rows)[:, None],
        vector_sums[4],
        vector_sums[5],
        jnp.transpose(attn.outs[0].reshape(3, width, model), (2, 0, 1)),
        plain(0),
        plain(2),
        attn.outs[1],
        vector_sums[0],
        vector_sums[1],
        vector_sums[2],
        ffn.outs[1],
        up_bias_sum,
        ffn.outs[0],
        vector_sums[3],
    )


def solution(mesh):
    in_specs = (
        P(None, "wide", "narrow", None),
        P(None, "wide", "narrow", None),
        P(),
        P(),
        P(),
        P(),
        P(None, None, "narrow"),
        P("narrow"),
        P("narrow"),
        P("narrow", None),
        P(),
        P(),
        P(),
        P(None, "narrow"),
        P("narrow"),
        P("narrow", None),
        P(),
    )
    out_specs = (
        P(None, "wide", "narrow", None),
        P(None, "wide", "narrow", None),
        P(),
        P(),
        P(None, None, "narrow"),
        P("narrow"),
        P("narrow"),
        P("narrow", None),
        P(),
        P(),
        P(),
        P(None, "narrow"),
        P("narrow"),
        P("narrow", None),
        P(),
    )
    return jax.shard_map(local, mesh=mesh, in_specs=in_specs, out_specs=out_specs, check_vma=False)
```

```python
import functools

import jax
import jax.numpy as jnp
from jax import lax
from jax.experimental import pallas as pl
from jax.experimental.pallas import tpu as pltpu
from jax.sharding import PartitionSpec as P

HEAD = 64
LANES = 128
TILE = 256
norm_eps = 1e-05
score_scale = 0.125
bf16 = jnp.bfloat16
f32 = jnp.float32


class Chain:
    def __init__(self):
        self.last = []
        self.held = []

    def hold(self, *arrays):
        self.held += arrays

    def run(self, body, outs, *ins, smem=(), scratch=(), alias=None, anywhere=(), out_anywhere=(), limit=12, token=0, cover=False):
        unread = [*self.last, *self.held]
        count = len(smem) + len(ins)
        specs = [pl.BlockSpec(memory_space=pltpu.SMEM)] * len(smem)
        specs += [pl.BlockSpec(memory_space=pl.ANY if i in anywhere else pltpu.VMEM) for i in range(len(ins))]
        specs += [pl.BlockSpec(memory_space=pl.ANY)] * len(unread)

        def inner(*refs):
            body(*refs[:count], *refs[count + len(unread) :])

        made = pl.pallas_call(
            inner,
            out_shape=tuple(jax.ShapeDtypeStruct(*o) for o in outs),
            in_specs=specs,
            out_specs=tuple(
                pl.BlockSpec(memory_space=pl.ANY if i in out_anywhere else pltpu.VMEM) for i in range(len(outs))
            ),
            scratch_shapes=scratch,
            input_output_aliases={} if alias is None else {len(smem) + k: v for k, v in alias.items()},
            compiler_params=pltpu.CompilerParams(vmem_limit_bytes=limit << 20),
            cost_estimate=pl.CostEstimate(flops=10**12 if cover else 1, bytes_accessed=1, transcendentals=0),
            name=body.func.__name__ if isinstance(body, functools.partial) else body.__name__,
        )(*smem, *ins, *unread)
        self.last, self.held = [made[token]], []
        return made


def dot32(first, second, first_dim, second_dim):
    return lax.dot_general(
        first, second, (((first_dim,), (second_dim,)), ((), ())), preferred_element_type=f32
    )


def statistics(values):
    average = jnp.mean(values, axis=-1, keepdims=True)
    centred = values - average
    inverse = lax.rsqrt(jnp.mean(centred * centred, axis=-1, keepdims=True) + norm_eps)
    return centred * inverse, inverse


def norm_back(grad, normed, inverse, gain):
    scaled = grad * gain
    mean_one = jnp.mean(scaled, axis=-1, keepdims=True)
    mean_two = jnp.mean(scaled * normed, axis=-1, keepdims=True)
    return inverse * (scaled - mean_one - normed * mean_two)


def of_head(values, j, axis=1):
    if values.shape[axis] <= HEAD:
        return values
    place = lax.broadcasted_iota(jnp.int32, values.shape, axis)
    return jnp.where((place >= HEAD * j) & (place < HEAD * (j + 1)), values, jnp.zeros_like(values))


def head_pairs(width):
    return [(low, min(LANES, width - low)) for low in range(0, width, LANES)]


def mark(out):
    out[...] = jnp.zeros_like(out)


def by_pairs(weight_t, out):
    width = out.shape[0] // 3
    for low, wide in head_pairs(width):
        for j in range(3):
            out[3 * low + j * wide : 3 * low + (j + 1) * wide, :] = weight_t[
                j * width + low : j * width + low + wide, :
            ]


def norm_one(tok, gain, bias, out, *, m):
    normed, _ = statistics(tok[m, 0].astype(f32))
    out[...] = (normed * gain[...].astype(f32) + bias[...].astype(f32)).astype(bf16)


def loss_grad(index, cells, queries, cot, m, count):
    number = queries[cells[index[0] + m * count]]
    scale = jnp.sqrt(jnp.full((1, cot.shape[3]), number, jnp.int32).astype(f32) / 500.0)
    return cot[m, 0].astype(f32) * scale


def scale_cot(index, cells, queries, cot, out, *, m, count):
    out[...] = loss_grad(index, cells, queries, cot, m, count).astype(bf16)


def project(*refs, parts):
    blocks = refs[:parts]
    weight, bias, scale = refs[parts : parts + 3]
    out, whole = refs[parts + 3 :]
    rows = blocks[0].shape[0]
    for b in range(parts):
        values = blocks[b][...]
        at = slice(b * rows, (b + 1) * rows)
        whole[at, :] = values
        out[at, :] = ((dot32(values, weight[...], 1, 1) + bias[...]) * scale[...]).astype(bf16)


def attend(qkv, out_weight, attended, logs, *outs, step):
    whole = qkv.shape[0]
    head = 0
    for low, wide in head_pairs(out_weight.shape[0]):
        heads = wide // HEAD
        key_pair = qkv[:, 3 * low + wide : 3 * low + 2 * wide]
        value_t = qkv[:, 3 * low + 2 * wide : 3 * low + 3 * wide].T
        keys = [of_head(key_pair, j) for j in range(heads)]
        values = [of_head(value_t, j, 0) for j in range(heads)]
        for start in range(0, whole, step):
            at = slice(start, start + step)
            query = qkv[at, 3 * low : 3 * low + wide]
            total = None
            for j in range(heads):
                scores = dot32(keys[j], query, 1, 1)
                top = jnp.max(scores, axis=0, keepdims=True)
                powers = jnp.exp(scores - top)
                length = jnp.sum(powers, axis=0, keepdims=True)
                mixed = dot32(values[j], powers.astype(bf16), 1, 0) * (1.0 / length)
                total = mixed if total is None else total + mixed
                logs[head + j : head + j + 1, at] = top + jnp.log(length)
            attended[at, low : low + wide] = total.T.astype(bf16)
        head += heads
    put_shares(outs, lambda at: dot32(attended[at, :], out_weight[...], 1, 0), whole)


def put_shares(outs, share_of, whole):
    own, partner, crossing = outs
    rows = own.shape[0]
    for b, (out, at) in enumerate(((own, None), (crossing, 0), (partner, None), (crossing, 1))):
        value = share_of(slice(b * rows, (b + 1) * rows)).astype(bf16)
        if at is None:
            out[...] = value
        else:
            out[at] = value


def pair_sum(first, second, out):
    out[...] = (first[...].astype(f32) + second[1].astype(f32)).astype(bf16)


def three(first, second, third):
    return first[...].astype(f32) + second[0].astype(f32) + third[...].astype(f32)


def norm_two(tok, first, second, third, out_bias, gain, bias, resid, normed, *, m):
    value = tok[m, 0].astype(f32) + three(first, second, third) + out_bias[...].astype(f32)
    resid[...] = value
    hat, _ = statistics(value)
    normed[...] = (hat * gain[...].astype(f32) + bias[...].astype(f32)).astype(bf16)


def feed(*refs, parts):
    normed, grads = refs[:parts], refs[parts : 2 * parts]
    up, up_bias, down = refs[2 * parts : 2 * parts + 3]
    activ, pre_grad, bias_grad, normed_all, grads_all = refs[2 * parts + 3 :]
    rows = normed[0].shape[0]
    for b in range(parts):
        normed_all[b * rows : (b + 1) * rows, :] = normed[b][...]
        grads_all[b * rows : (b + 1) * rows, :] = grads[b][...]
    for low in range(0, up.shape[1], TILE):
        cols = slice(low, low + TILE)
        total = None
        for b in range(parts):
            at = slice(b * rows, (b + 1) * rows)
            pre = dot32(normed[b][...], up[:, cols], 1, 0) + up_bias[:, cols].astype(f32)
            cumul = 0.5 + 0.5 * lax.erf(pre * 0.7071067811865476)
            density = jnp.exp(-0.5 * pre * pre) * 0.3989422804014327
            activ[at, cols] = (pre * cumul).astype(bf16)
            back = dot32(grads[b][...], down[cols, :], 1, 1)
            grad = (back * (cumul + pre * density)).astype(bf16)
            pre_grad[at, cols] = grad
            part = jnp.sum(grad.astype(f32), axis=0, keepdims=True)
            total = part if total is None else total + part
        bias_grad[:, cols] = total


def times(value, weight, *outs):
    put_tiles(outs, lambda at, cols: dot32(value[at, :], weight[:, cols], 1, 0), value.shape[0])


def times_back(value, weight, *outs):
    put_tiles(outs, lambda at, cols: dot32(value[at, :], weight[cols, :], 1, 1), value.shape[0])


def put_tiles(outs, share_of, whole):
    own, partner, crossing = outs
    rows, model = own.shape

    def tile(i, carry):
        cols = pl.ds(pl.multiple_of(i * TILE, TILE), TILE)
        own[:, cols] = share_of(slice(0, rows), cols).astype(bf16)
        crossing[0, :, cols] = share_of(slice(rows, 2 * rows), cols).astype(bf16)
        partner[:, cols] = share_of(slice(2 * rows, 3 * rows), cols).astype(bf16)
        crossing[1, :, cols] = share_of(slice(3 * rows, 4 * rows), cols).astype(bf16)
        return carry

    lax.fori_loop(0, model // TILE, tile, 0)


def weight_grad(index, *refs, pairs, ring):
    firsts, seconds = refs[:pairs], refs[pairs : 2 * pairs]
    chunks, whole = refs[2 * pairs : -1], refs[-1]

    def tile(i, carry):
        rows = pl.ds(pl.multiple_of(i * TILE, TILE), TILE)
        total = None
        for first, second in zip(firsts, seconds):
            part = dot32(first[:, rows], second[...], 0, 0)
            total = part if total is None else total + part
        whole[rows, :] = total.astype(bf16)
        return carry

    lax.fori_loop(0, whole.shape[0] // TILE, tile, 0)
    put_chunks(index, chunks, whole, ring)


def ring_chunk(index, count, ring, step):
    half = index // 2
    place = jnp.where(index % 2 == 0, half, count - 1 - half)
    return lax.rem(place + (count - step if ring == 0 else step), count)


def put_chunks(index, chunks, whole, ring):
    for s, chunk in enumerate(chunks):
        size = chunk.shape[0]
        which = ring_chunk(index[0], len(chunks), ring, (s + 1) % len(chunks)) if len(chunks) > 1 else 0
        chunk[...] = whole[pl.ds(pl.multiple_of(which * size, size), size), :]


def norm_two_back(index, cells, queries, cot, resid, first, second, third, gain, out, rounded, sums, *, m, count):
    top = loss_grad(index, cells, queries, cot, m, count)
    grad = three(first, second, third)
    hat, inverse = statistics(resid[...])
    back = top + norm_back(grad, hat, inverse, gain[...].astype(f32))
    out[...] = back
    rounded[...] = back.astype(bf16)
    sums[0:1, :] = jnp.sum(back, axis=0, keepdims=True)
    sums[1:2, :] = jnp.sum(grad * hat, axis=0, keepdims=True)
    sums[2:3, :] = jnp.sum(grad, axis=0, keepdims=True)
    sums[3:4, :] = jnp.sum(top, axis=0, keepdims=True)
    sums[4:8, :] = jnp.zeros_like(sums[4:8, :])


def attend_back(qkv, logs, mixed, out_weight, *refs, parts, step, low, wide):
    grads = refs[:parts]
    out, key_grad, value_grad, given, inner = refs[parts:]
    whole = qkv.shape[0]
    rows = whole // parts
    heads = wide // HEAD
    head = low // HEAD
    ones = jnp.concatenate([of_head(jnp.ones((8, wide), bf16), j) for j in range(heads)], axis=0)
    for b in range(parts):
        at = slice(b * rows, (b + 1) * rows)
        value = dot32(grads[b][...], out_weight[low : low + wide, :], 1, 1).astype(bf16)
        given[at, :] = value
        both = value.astype(f32) * mixed[at, low : low + wide].astype(f32)
        high = both.astype(bf16)
        rest = (both - high.astype(f32)).astype(bf16)
        inner[:, at] = dot32(ones, high, 1, 1) + dot32(ones, rest, 1, 1)
    key_pair = qkv[:, 3 * low + wide : 3 * low + 2 * wide]
    value_pair = qkv[:, 3 * low + 2 * wide : 3 * low + 3 * wide]
    key_t = key_pair.T
    keys = [of_head(key_pair, j) for j in range(heads)]
    values = [of_head(value_pair, j) for j in range(heads)]
    keys_t = [of_head(key_t, j, 0) for j in range(heads)]
    key_grad[...] = jnp.zeros_like(key_grad)
    value_grad[...] = jnp.zeros_like(value_grad)

    def block(i, carry):
        start = pl.multiple_of(i * step, step)
        query = qkv[pl.ds(start, step), 3 * low : 3 * low + wide]
        grad = given[pl.ds(start, step), :]
        total = None
        for j in range(heads):
            scores = dot32(keys[j], query, 1, 1)
            weights = jnp.exp(scores - logs[head + j : head + j + 1, pl.ds(start, step)])
            back = dot32(values[j], grad, 1, 1)
            score_grad = (weights * (back - inner[8 * j : 8 * j + 1, pl.ds(start, step)])).astype(bf16)
            value_grad[...] += dot32(weights.astype(bf16), of_head(grad, j), 1, 0)
            key_grad[...] += dot32(score_grad, of_head(query, j), 1, 0)
            part = dot32(keys_t[j], score_grad, 1, 0)
            total = part if total is None else total + part
        out[pl.ds(start, step), :wide] = (total.T * score_scale).astype(bf16)
        return carry

    lax.fori_loop(0, whole // step, block, 0)
    out[:, wide : 2 * wide] = key_grad[...].astype(bf16)
    out[:, 2 * wide :] = value_grad[...].astype(bf16)


def project_back(*refs, pairs):
    grads, weight, own, partner, crossing, sums = refs[:pairs], refs[pairs], *refs[pairs + 1 :]

    def share_of(at, cols):
        total, low = None, 0
        for grad in grads:
            wide = grad.shape[1]
            part = dot32(grad[at, :], weight[low : low + wide, cols], 1, 0)
            total = part if total is None else total + part
            low += wide
        return total

    put_tiles((own, partner, crossing), share_of, grads[0].shape[0])
    low = 0
    for grad in grads:
        wide = grad.shape[1]
        sums[:, low : low + wide] = jnp.sum(grad[...].astype(f32), axis=0, keepdims=True)
        low += wide


def projection_grad(index, *refs, micros, pairs, parts, count):
    normed, refs = refs[:micros], refs[micros:]
    grads, refs = [refs[m * pairs : (m + 1) * pairs] for m in range(micros)], refs[micros * pairs :]
    tops, refs = [refs[m * parts : (m + 1) * parts] for m in range(micros)], refs[micros * parts :]
    mixed, refs = refs[:micros], refs[micros:]
    chunks, (left, right) = refs[:-2], refs[-2:]
    width = mixed[0].shape[1]
    rows = tops[0][0].shape[0]
    for p, (low, wide) in enumerate(head_pairs(width)):
        total = None
        for m in range(micros):
            part = dot32(grads[m][p][...], normed[m][...], 0, 0)
            total = part if total is None else total + part
        left[low : low + wide, :] = total[:wide].astype(bf16)
        left[width + low : width + low + wide, :] = total[wide : 2 * wide].astype(bf16)
        right[low : low + wide, :] = total[2 * wide :].astype(bf16)
        total = None
        for m in range(micros):
            for b in range(parts):
                part = dot32(mixed[m][b * rows : (b + 1) * rows, low : low + wide], tops[m][b][...], 0, 0)
                total = part if total is None else total + part
        right[width + low : width + low + wide, :] = total.astype(bf16)
    put_chunks(index, chunks[:count], left, 0)
    put_chunks(index, chunks[count:], right, 1)


def ring_add(*refs):
    for i in range(2):
        refs[4 + i][...] = (refs[i][...].astype(f32) + refs[2 + i][...].astype(f32)).astype(bf16)


def ring_store(index, *refs, steps, divided, count):
    number = len(steps)
    moved, refs = refs[: 2 * number], refs[2 * number :]
    done, first, second, buffer, sems = refs[-5:]
    done[...] = jnp.zeros_like(done)
    size = buffer.shape[1]
    copies = []
    for k, step in enumerate(steps):
        for i in range(2):
            slot = 2 * k + i
            buffer[slot] = moved[slot][...].astype(f32)
            row = pl.multiple_of(ring_chunk(index[0], count, i, step) * size, size)
            if divided and i == 1:
                row = row + divided
                copy_second = pltpu.make_async_copy(
                    buffer.at[slot], second.at[pl.ds(pl.multiple_of(jnp.maximum(row - first.shape[0], 0), 16), size), :], sems.at[slot]
                )
                copy_first = pltpu.make_async_copy(
                    buffer.at[slot], first.at[pl.ds(pl.multiple_of(jnp.minimum(row, first.shape[0] - size), 16), size), :], sems.at[slot]
                )
                pl.when(row < first.shape[0])(copy_first.start)
                pl.when(row >= first.shape[0])(copy_second.start)
                copies.append(copy_first)
            else:
                target = second if i == 1 else first
                copies.append(pltpu.make_async_copy(buffer.at[slot], target.at[pl.ds(row, size), :], sems.at[slot]))
                copies[-1].start()
    for copy in copies:
        copy.wait()


def norm_one_back(tok, resid_grad, first, second, third, gain, out, sums, *, m):
    grad = three(first, second, third)
    hat, inverse = statistics(tok[m, 0].astype(f32))
    out[...] = resid_grad[...] + norm_back(grad, hat, inverse, gain[...].astype(f32))
    sums[0:4, :] = jnp.zeros_like(sums[0:4, :])
    sums[4:5, :] = jnp.sum(grad * hat, axis=0, keepdims=True)
    sums[5:6, :] = jnp.sum(grad, axis=0, keepdims=True)
    sums[6:8, :] = jnp.zeros_like(sums[6:8, :])


def vector_sum(*refs):
    total = refs[0][...]
    for ref in refs[1:-1]:
        total = total + ref[...]
    refs[-1][...] = total


def vector_join(first, second, *refs, number):
    up_bias, stack, out = refs[:number], refs[number:-1], refs[-1]
    out[...] = first[...] + second[...]
    for row, parts in ((6, up_bias), (7, stack)):
        total = parts[0][...]
        for part in parts[1:]:
            total = total + part[...]
        out[row : row + 1, : total.shape[1]] = total


def add_rows(resid, first, second, third, bias, out):
    out[...] = (resid[...] + three(first, second, third) + bias[...].astype(f32)).astype(bf16)


def swap(values, axis, bit):
    return lax.ppermute(values, axis, [(i, i ^ bit) for i in range(lax.axis_size(axis))])


def ring_order(count):
    return list(range(0, count, 2)) + list(range(1, count, 2))[::-1]


class Rings:
    def __init__(self, chain, index, shapes, divided=0):
        self.chain, self.index, self.shapes, self.divided = chain, index, shapes, divided
        self.count = lax.axis_size("wide")
        order = ring_order(self.count)
        self.perms = [[(order[i], order[(i + d) % self.count]) for i in range(self.count)] for d in (1, -1)]
        self.chunks, self.moving, self.have = [None, None], [None, None], []
        self.step = 1
        self.outs = None

    def start(self, i, chunks):
        self.chunks[i] = chunks
        self.moving[i] = lax.ppermute(chunks[0], "wide", self.perms[i])

    def hold(self, i):
        self.chain.hold(self.moving[i])

    def add(self, cover=False):
        made = self.chain.run(
            ring_add,
            [(c.shape, bf16) for c in self.moving],
            *self.moving,
            *[c[self.step] for c in self.chunks],
            cover=cover,
        )
        self.step += 1
        if self.step == self.count:
            self.have.append(made)
        self.moving = [lax.ppermute(c, "wide", self.perms[i]) for i, c in enumerate(made)]

    def forward(self):
        self.have.append(self.moving)
        self.chain.hold(*self.moving)
        if len(self.have) < self.count:
            self.moving = [lax.ppermute(c, "wide", self.perms[i]) for i, c in enumerate(self.moving)]

    def store(self, steps):
        moved = [c for s in steps for c in self.have[s]]
        kept = () if self.outs is None else self.outs
        made = self.chain.run(
            functools.partial(ring_store, steps=tuple(steps), divided=self.divided, count=self.count),
            [((8, LANES), f32)] + [(s, f32) for s in self.shapes],
            *moved,
            *kept,
            smem=(self.index,),
            scratch=[
                pltpu.VMEM((len(moved), *moved[0].shape), f32),
                pltpu.SemaphoreType.DMA((len(moved),)),
            ],
            alias={len(moved): 1, len(moved) + 1: 2} if kept else None,
            anywhere=(len(moved), len(moved) + 1) if kept else (),
            out_anywhere=(1, 2),
            limit=3 + (len(moved) * moved[0].size * 4 >> 20),
            cover=True,
        )
        self.outs = made[1:]


class Whole:
    def __init__(self, shapes, divided=0):
        self.shapes, self.divided = shapes, divided
        self.arrays = [None, None]

    def start(self, i, chunks):
        self.arrays[i] = chunks[0]

    def hold(self, i):
        pass

    def add(self, cover=False):
        pass

    def forward(self):
        pass

    def store(self, steps):
        if isinstance(self.arrays, list):
            self.arrays = lax.psum(tuple(self.arrays), "wide")
            first, second = (a.astype(f32) for a in self.arrays)
            if self.divided:
                cut = self.shapes[0][0] - self.divided
                first, second = jnp.concatenate([first, second[:cut]], axis=0), second[cut:]
            self.outs = (first, second)


def local(
    tokens,
    cotangent,
    cell_of,
    query_count,
    attn_norm_gain,
    attn_norm_bias,
    input_weight,
    query_bias,
    value_bias,
    out_weight,
    out_bias,
    ffn_norm_gain,
    ffn_norm_bias,
    up_weight,
    up_bias,
    down_weight,
    down_bias,
):
    micros = range(tokens.shape[0])
    rows, model = tokens.shape[2], tokens.shape[3]
    parts = lax.axis_size("narrow")
    whole = rows * parts
    width = input_weight.shape[2]
    hidden = up_weight.shape[1]
    count = lax.axis_size("wide")
    rings = count <= 8
    chunks = count if rings else 1
    pairs = head_pairs(width)
    step = min(512, whole)
    chain = Chain()
    run = chain.run
    index = lax.axis_index("wide").astype(jnp.int32).reshape(1)

    block = ((rows, model), bf16)
    outgoing = [block, block, ((2, rows, model), bf16)]
    wide_rows = ((whole, model), bf16)
    row = lambda v: v.reshape(1, -1)
    gain_one, bias_one, gain_two, bias_two = map(row, (attn_norm_gain, attn_norm_bias, ffn_norm_gain, ffn_norm_bias))
    out_bias, down_bias, up_bias = row(out_bias), row(down_bias), row(up_bias)

    def columns(three_parts):
        return jnp.concatenate([v[:, low : low + wide] for low, wide in pairs for v in three_parts], axis=1)

    weight_t = jnp.transpose(input_weight, (1, 2, 0)).reshape(3 * width, model)
    zero = jnp.zeros((1, width), f32)
    project_bias = columns([row(query_bias).astype(f32), zero, row(value_bias).astype(f32)])
    project_scale = columns([zero + score_scale, zero + 1.0, zero + 1.0])

    def gather(own):
        partner = swap(own, "narrow", 2)
        return [own, swap(own, "narrow", 1), partner, swap(partner, "narrow", 1)]

    def share(made):
        own, partner, crossing = made
        return [own, partner, swap(crossing, "narrow", 1)]

    def send(shares):
        own, partner, crossed = shares
        (both,) = run(pair_sum, [block], partner, crossed)
        return [own, crossed, swap(both, "narrow", 2)]

    def fresh():
        return [None] * len(micros)

    normed, given, qkv, normed_all, mixed, logs, shares, shares_down, resid, normed_two_b = (fresh() for _ in range(10))
    activ, pre_grad, up_bias_grad, two_all, given_all, resid_grad, top = (fresh() for _ in range(7))
    sums_two, sums_one, stack_sums, out_rows, grad_rows = (fresh() for _ in range(5))
    pair_grads = [[] for _ in micros]

    def do_norm_one(m):
        (own,) = run(functools.partial(norm_one, m=m), [block], tokens, gain_one, bias_one)
        normed[m] = gather(own)

    def do_scale(m):
        (own,) = run(functools.partial(scale_cot, m=m, count=count), [block], cotangent, smem=(index, cell_of, query_count), cover=True)
        given[m] = gather(own)

    def do_project(m):
        qkv[m], normed_all[m] = run(
            functools.partial(project, parts=parts),
            [((whole, 3 * width), bf16), wide_rows],
            *normed[m],
            weight,
            project_bias,
            project_scale,
        )

    def do_attend(m):
        mixed[m], logs[m], *made = run(
            functools.partial(attend, step=whole),
            [((whole, width), bf16), ((8, whole), f32), *outgoing],
            qkv[m],
            out_weight,
            limit=24,
        )
        shares[m] = share(made)

    def do_send(m):
        shares[m] = send(shares[m])

    def do_norm_two(m):
        resid[m], own = run(
            functools.partial(norm_two, m=m),
            [((rows, model), f32), block],
            tokens,
            *shares[m],
            out_bias,
            gain_two,
            bias_two,
            cover=m == 0,
        )
        normed_two_b[m] = gather(own)

    def do_feed(m):
        activ[m], pre_grad[m], up_bias_grad[m], two_all[m], given_all[m] = run(
            functools.partial(feed, parts=parts),
            [((whole, hidden), bf16), ((whole, hidden), bf16), ((1, hidden), f32), wide_rows, wide_rows],
            *normed_two_b[m],
            *given[m],
            up_weight,
            up_bias,
            down_weight,
        )

    def do_up_back(m):
        shares[m] = share(run(times_back, outgoing, pre_grad[m], up_weight))

    def do_down(m):
        shares_down[m] = share(run(times, outgoing, activ[m], down_weight))

    def do_send_down(m):
        shares_down[m] = send(shares_down[m])

    def do_norm_two_back(m):
        resid_grad[m], own, sums_two[m] = run(
            functools.partial(norm_two_back, m=m, count=count),
            [((rows, model), f32), block, ((8, model), f32)],
            cotangent,
            resid[m],
            *shares[m],
            gain_two,
            smem=(index, cell_of, query_count),
            cover=True,
        )
        top[m] = gather(own)

    def do_attend_back(m, p):
        low, wide = pairs[p]
        (made,) = run(
            functools.partial(attend_back, parts=parts, step=step, low=low, wide=wide),
            [((whole, 3 * wide), bf16)],
            qkv[m],
            logs[m],
            mixed[m],
            out_weight,
            *top[m],
            scratch=[
                pltpu.VMEM((whole, wide), f32),
                pltpu.VMEM((whole, wide), f32),
                pltpu.VMEM((whole, wide), bf16),
                pltpu.VMEM((8 * (wide // HEAD), whole), f32),
            ],
            limit=20,
        )
        pair_grads[m].append(made)

    def do_project_back(m):
        *made, stack_sums[m] = run(
            functools.partial(project_back, pairs=len(pairs)),
            [*outgoing, ((1, 3 * width), f32)],
            *pair_grads[m],
            weight,
        )
        shares[m] = share(made)

    def do_norm_one_back(m):
        grad_rows[m], sums_one[m] = run(
            functools.partial(norm_one_back, m=m),
            [((rows, model), f32), ((8, model), f32)],
            tokens,
            resid_grad[m],
            *shares[m],
            gain_one,
        )

    def wait(*arrays):
        chain.hold(*arrays)
        run(mark, [((8, LANES), f32)], cover=True)

    hops = [("narrow", 1 << k) for k in range(parts.bit_length() - 1)]
    hops += [("wide", 1 << k) for k in range(count.bit_length() - 1)]
    vectors = []

    def do_vectors():
        done = len(vectors)
        shape = [((8, model), f32)]
        if done == 0:
            (own,) = run(vector_sum, shape, *sums_one, *sums_two)
        elif hops[done - 1][0] == "narrow" and hops[done][0] == "wide":
            own, arrived = vectors[-1]
            (own,) = run(
                functools.partial(vector_join, number=len(micros)), shape, own, arrived, *up_bias_grad, *stack_sums
            )
        else:
            (own,) = run(vector_sum, shape, *vectors[-1])
        vectors.append((own, swap(own, *hops[done]) if done < len(hops) else None))

    def do_add_rows(m):
        (out_rows[m],) = run(add_rows, [block], resid[m], *shares_down[m], down_bias)

    def ffn_grad(firsts, seconds, ring):
        shape = (firsts[0].shape[1], seconds[0].shape[1])
        made = run(
            functools.partial(weight_grad, pairs=len(micros), ring=ring),
            [((shape[0] // chunks, shape[1]), bf16)] * chunks,
            *firsts,
            *seconds,
            smem=(index,),
            scratch=[pltpu.VMEM(shape, bf16)],
            limit=16,
        )
        ffn.start(ring, made)

    def attn_grad():
        made = run(
            functools.partial(projection_grad, micros=len(micros), pairs=len(pairs), parts=parts, count=chunks),
            [((2 * width // chunks, model), bf16)] * (2 * chunks),
            *normed_all,
            *[g for m in micros for g in pair_grads[m]],
            *[t for m in micros for t in top[m]],
            *mixed,
            smem=(index,),
            scratch=[pltpu.VMEM((2 * width, model), bf16)] * 2,
            limit=20,
            cover=True,
        )
        attn.start(0, made[:chunks])
        attn.start(1, made[chunks:])

    ffn_shapes = [(hidden, model), (model, hidden)]
    attn_shapes = [(3 * width, model), (width, model)]
    ffn = Rings(chain, index, ffn_shapes) if rings else Whole(ffn_shapes)
    attn = Rings(chain, index, attn_shapes, 2 * width) if rings else Whole(attn_shapes, 2 * width)

    do_norm_one(0)
    (weight,) = run(by_pairs, [((3 * width, model), bf16)], weight_t)
    chain.hold(normed[0][1], normed[0][2])
    do_norm_one(1)
    do_scale(0)
    do_project(0)
    do_attend(0)
    chain.hold(normed[1][1], normed[1][2], given[0][1], given[0][2])
    do_scale(1)
    do_send(0)
    chain.hold(given[1][1])
    do_project(1)
    do_attend(1)
    chain.hold(given[1][2])
    do_norm_two(0)
    do_send(1)
    chain.hold(normed_two_b[0][1])
    do_norm_two(1)
    chain.hold(normed_two_b[1][1])
    do_feed(0)
    do_up_back(0)
    do_down(0)
    wait(normed_two_b[1][2])
    do_send(0)
    do_feed(1)
    do_up_back(1)
    do_norm_two_back(0)
    chain.hold(top[0][1])
    ffn_grad(activ, given_all, 0)
    ffn_grad(two_all, pre_grad, 1)
    ffn.hold(0)
    wait(top[0][2])
    do_send(1)
    ffn.add()
    do_attend_back(0, 0)
    ffn.add()
    do_attend_back(0, 1)
    do_norm_two_back(1)
    ffn.add()
    do_attend_back(0, 2)
    ffn.add()
    do_project_back(0)
    ffn.hold(0)
    ffn.hold(1)
    wait(top[1][1], top[1][2])
    do_send(0)
    ffn.add()
    do_attend_back(1, 0)
    do_send_down(0)
    ffn.add()
    do_attend_back(1, 1)
    ffn.add()
    do_attend_back(1, 2)
    attn_grad()
    ffn.forward()
    do_norm_one_back(0)
    attn.add()
    do_project_back(1)
    ffn.forward()
    attn.add()
    ffn.forward()
    ffn.store(range(0, 2))
    do_send(1)
    attn.add()
    do_down(1)
    ffn.forward()
    attn.add()
    ffn.store(range(2, 4))
    do_send_down(1)
    ffn.forward()
    attn.add()
    do_norm_one_back(1)
    ffn.forward()
    attn.add()
    do_vectors()
    ffn.store(range(4, 6))
    ffn.forward()
    attn.add()
    do_vectors()
    ffn.store(range(6, 8))
    attn.forward()
    do_vectors()
    do_add_rows(0)
    attn.forward()
    do_vectors()
    attn.store(range(0, 2))
    attn.forward()
    do_vectors()
    do_add_rows(1)
    attn.forward()
    do_vectors()
    attn.store(range(2, 4))
    attn.forward()
    attn.forward()
    attn.store(range(4, 6))
    attn.forward()
    attn.store(range(6, 8))

    while len(vectors) <= len(hops):
        do_vectors()
    vector_sums = vectors[-1][0]
    up_bias_sum = vector_sums[6, :hidden]
    stack_sum = vector_sums[7, : 3 * width]

    def plain(j):
        return jnp.concatenate([stack_sum[3 * low + j * wide : 3 * low + (j + 1) * wide] for low, wide in pairs])

    return (
        jnp.stack(out_rows)[:, None],
        jnp.stack(grad_rows)[:, None],
        vector_sums[4],
        vector_sums[5],
        jnp.transpose(attn.outs[0].reshape(3, width, model), (2, 0, 1)),
        plain(0),
        plain(2),
        attn.outs[1],
        vector_sums[0],
        vector_sums[1],
        vector_sums[2],
        ffn.outs[1],
        up_bias_sum,
        ffn.outs[0],
        vector_sums[3],
    )


def solution(mesh):
    in_specs = (
        P(None, "wide", "narrow", None),
        P(None, "wide", "narrow", None),
        P(),
        P(),
        P(),
        P(),
        P(None, None, "narrow"),
        P("narrow"),
        P("narrow"),
        P("narrow", None),
        P(),
        P(),
        P(),
        P(None, "narrow"),
        P("narrow"),
        P("narrow", None),
        P(),
    )
    out_specs = (
        P(None, "wide", "narrow", None),
        P(None, "wide", "narrow", None),
        P(),
        P(),
        P(None, None, "narrow"),
        P("narrow"),
        P("narrow"),
        P("narrow", None),
        P(),
        P(),
        P(),
        P(None, "narrow"),
        P("narrow"),
        P("narrow", None),
        P(),
    )
    return jax.shard_map(local, mesh=mesh, in_specs=in_specs, out_specs=out_specs, check_vma=False)
```

```python
import functools

import jax
import jax.numpy as jnp
from jax import lax
from jax.experimental import pallas as pl
from jax.experimental.pallas import tpu as pltpu
from jax.sharding import PartitionSpec as P

HEAD = 64
LANES = 128
TILE = 256
norm_eps = 1e-05
score_scale = 0.125
bf16 = jnp.bfloat16
f32 = jnp.float32


class Chain:
    def __init__(self):
        self.last = []
        self.held = []

    def hold(self, *arrays):
        self.held += arrays

    def run(self, body, outs, *ins, smem=(), scratch=(), alias=None, anywhere=(), out_anywhere=(), limit=12, token=0, cover=False):
        unread = [*self.last, *self.held]
        count = len(smem) + len(ins)
        specs = [pl.BlockSpec(memory_space=pltpu.SMEM)] * len(smem)
        specs += [pl.BlockSpec(memory_space=pl.ANY if i in anywhere else pltpu.VMEM) for i in range(len(ins))]
        specs += [pl.BlockSpec(memory_space=pl.ANY)] * len(unread)

        def inner(*refs):
            body(*refs[:count], *refs[count + len(unread) :])

        made = pl.pallas_call(
            inner,
            out_shape=tuple(jax.ShapeDtypeStruct(*o) for o in outs),
            in_specs=specs,
            out_specs=tuple(
                pl.BlockSpec(memory_space=pl.ANY if i in out_anywhere else pltpu.VMEM) for i in range(len(outs))
            ),
            scratch_shapes=scratch,
            input_output_aliases={} if alias is None else {len(smem) + k: v for k, v in alias.items()},
            compiler_params=pltpu.CompilerParams(vmem_limit_bytes=limit << 20),
            cost_estimate=pl.CostEstimate(flops=10**12 if cover else 1, bytes_accessed=1, transcendentals=0),
            name=body.func.__name__ if isinstance(body, functools.partial) else body.__name__,
        )(*smem, *ins, *unread)
        self.last, self.held = [made[token]], []
        return made


def dot32(first, second, first_dim, second_dim):
    return lax.dot_general(
        first, second, (((first_dim,), (second_dim,)), ((), ())), preferred_element_type=f32
    )


def statistics(values):
    average = jnp.mean(values, axis=-1, keepdims=True)
    centred = values - average
    inverse = lax.rsqrt(jnp.mean(centred * centred, axis=-1, keepdims=True) + norm_eps)
    return centred * inverse, inverse


def norm_back(grad, normed, inverse, gain):
    scaled = grad * gain
    mean_one = jnp.mean(scaled, axis=-1, keepdims=True)
    mean_two = jnp.mean(scaled * normed, axis=-1, keepdims=True)
    return inverse * (scaled - mean_one - normed * mean_two)


def of_head(values, j, axis=1):
    if values.shape[axis] <= HEAD:
        return values
    place = lax.broadcasted_iota(jnp.int32, values.shape, axis)
    return jnp.where((place >= HEAD * j) & (place < HEAD * (j + 1)), values, jnp.zeros_like(values))


def head_pairs(width):
    return [(low, min(LANES, width - low)) for low in range(0, width, LANES)]


def mark(out):
    out[...] = jnp.zeros_like(out)


def by_pairs(weight_t, out):
    width = out.shape[0] // 3
    for low, wide in head_pairs(width):
        for j in range(3):
            out[3 * low + j * wide : 3 * low + (j + 1) * wide, :] = weight_t[
                j * width + low : j * width + low + wide, :
            ]


def norm_one(tok, gain, bias, out, *, m):
    normed, _ = statistics(tok[m, 0].astype(f32))
    out[...] = (normed * gain[...].astype(f32) + bias[...].astype(f32)).astype(bf16)


def loss_grad(index, cells, queries, cot, m, count):
    number = queries[cells[index[0] + m * count]]
    scale = jnp.sqrt(jnp.full((1, cot.shape[3]), number, jnp.int32).astype(f32) / 500.0)
    return cot[m, 0].astype(f32) * scale


def scale_cot(index, cells, queries, cot, out, *, m, count):
    out[...] = loss_grad(index, cells, queries, cot, m, count).astype(bf16)


def project(*refs, parts):
    blocks = refs[:parts]
    weight, bias, scale = refs[parts : parts + 3]
    out, whole = refs[parts + 3 :]
    rows = blocks[0].shape[0]
    for b in range(parts):
        values = blocks[b][...]
        at = slice(b * rows, (b + 1) * rows)
        whole[at, :] = values
        out[at, :] = ((dot32(values, weight[...], 1, 1) + bias[...]) * scale[...]).astype(bf16)


def attend(qkv, out_weight, attended, logs, *outs, step):
    whole = qkv.shape[0]
    head = 0
    for low, wide in head_pairs(out_weight.shape[0]):
        heads = wide // HEAD
        key_pair = qkv[:, 3 * low + wide : 3 * low + 2 * wide]
        value_t = qkv[:, 3 * low + 2 * wide : 3 * low + 3 * wide].T
        keys = [of_head(key_pair, j) for j in range(heads)]
        values = [of_head(value_t, j, 0) for j in range(heads)]
        for start in range(0, whole, step):
            at = slice(start, start + step)
            query = qkv[at, 3 * low : 3 * low + wide]
            total = None
            for j in range(heads):
                scores = dot32(keys[j], query, 1, 1)
                top = jnp.max(scores, axis=0, keepdims=True)
                powers = jnp.exp(scores - top)
                length = jnp.sum(powers, axis=0, keepdims=True)
                mixed = dot32(values[j], powers.astype(bf16), 1, 0) * (1.0 / length)
                total = mixed if total is None else total + mixed
                logs[head + j : head + j + 1, at] = top + jnp.log(length)
            attended[at, low : low + wide] = total.T.astype(bf16)
        head += heads
    put_shares(outs, lambda at: dot32(attended[at, :], out_weight[...], 1, 0), whole)


def put_shares(outs, share_of, whole):
    own, partner, crossing = outs
    rows = own.shape[0]
    for b, (out, at) in enumerate(((own, None), (crossing, 0), (partner, None), (crossing, 1))):
        value = share_of(slice(b * rows, (b + 1) * rows)).astype(bf16)
        if at is None:
            out[...] = value
        else:
            out[at] = value


def pair_sum(first, second, out):
    out[...] = (first[...].astype(f32) + second[1].astype(f32)).astype(bf16)


def three(first, second, third):
    return first[...].astype(f32) + second[0].astype(f32) + third[...].astype(f32)


def norm_two(tok, first, second, third, out_bias, gain, bias, resid, normed, *, m):
    value = tok[m, 0].astype(f32) + three(first, second, third) + out_bias[...].astype(f32)
    resid[...] = value
    hat, _ = statistics(value)
    normed[...] = (hat * gain[...].astype(f32) + bias[...].astype(f32)).astype(bf16)


def feed(*refs, parts):
    normed, grads = refs[:parts], refs[parts : 2 * parts]
    up, up_bias, down = refs[2 * parts : 2 * parts + 3]
    activ, pre_grad, bias_grad, normed_all, grads_all = refs[2 * parts + 3 :]
    rows = normed[0].shape[0]
    for b in range(parts):
        normed_all[b * rows : (b + 1) * rows, :] = normed[b][...]
        grads_all[b * rows : (b + 1) * rows, :] = grads[b][...]
    for low in range(0, up.shape[1], TILE):
        cols = slice(low, low + TILE)
        total = None
        for b in range(parts):
            at = slice(b * rows, (b + 1) * rows)
            pre = dot32(normed[b][...], up[:, cols], 1, 0) + up_bias[:, cols].astype(f32)
            cumul = 0.5 + 0.5 * lax.erf(pre * 0.7071067811865476)
            density = jnp.exp(-0.5 * pre * pre) * 0.3989422804014327
            activ[at, cols] = (pre * cumul).astype(bf16)
            back = dot32(grads[b][...], down[cols, :], 1, 1)
            grad = (back * (cumul + pre * density)).astype(bf16)
            pre_grad[at, cols] = grad
            part = jnp.sum(grad.astype(f32), axis=0, keepdims=True)
            total = part if total is None else total + part
        bias_grad[:, cols] = total


def times(value, weight, *outs):
    put_tiles(outs, lambda at, cols: dot32(value[at, :], weight[:, cols], 1, 0), value.shape[0])


def times_back(value, weight, *outs):
    put_tiles(outs, lambda at, cols: dot32(value[at, :], weight[cols, :], 1, 1), value.shape[0])


def put_tiles(outs, share_of, whole):
    own, partner, crossing = outs
    rows, model = own.shape

    def tile(i, carry):
        cols = pl.ds(pl.multiple_of(i * TILE, TILE), TILE)
        own[:, cols] = share_of(slice(0, rows), cols).astype(bf16)
        crossing[0, :, cols] = share_of(slice(rows, 2 * rows), cols).astype(bf16)
        partner[:, cols] = share_of(slice(2 * rows, 3 * rows), cols).astype(bf16)
        crossing[1, :, cols] = share_of(slice(3 * rows, 4 * rows), cols).astype(bf16)
        return carry

    lax.fori_loop(0, model // TILE, tile, 0)


def weight_grad(index, *refs, pairs, ring):
    firsts, seconds = refs[:pairs], refs[pairs : 2 * pairs]
    chunks, whole = refs[2 * pairs : -1], refs[-1]

    def tile(i, carry):
        rows = pl.ds(pl.multiple_of(i * TILE, TILE), TILE)
        total = None
        for first, second in zip(firsts, seconds):
            part = dot32(first[:, rows], second[...], 0, 0)
            total = part if total is None else total + part
        whole[rows, :] = total.astype(bf16)
        return carry

    lax.fori_loop(0, whole.shape[0] // TILE, tile, 0)
    put_chunks(index, chunks, whole, ring)


def ring_chunk(index, count, ring, step):
    half = index // 2
    place = jnp.where(index % 2 == 0, half, count - 1 - half)
    return lax.rem(place + (count - step if ring == 0 else step), count)


def put_chunks(index, chunks, whole, ring):
    for s, chunk in enumerate(chunks):
        size = chunk.shape[0]
        which = ring_chunk(index[0], len(chunks), ring, (s + 1) % len(chunks)) if len(chunks) > 1 else 0
        chunk[...] = whole[pl.ds(pl.multiple_of(which * size, size), size), :]


def norm_two_back(index, cells, queries, cot, resid, first, second, third, gain, out, rounded, sums, *, m, count):
    top = loss_grad(index, cells, queries, cot, m, count)
    grad = three(first, second, third)
    hat, inverse = statistics(resid[...])
    back = top + norm_back(grad, hat, inverse, gain[...].astype(f32))
    out[...] = back
    rounded[...] = back.astype(bf16)
    sums[0:1, :] = jnp.sum(back, axis=0, keepdims=True)
    sums[1:2, :] = jnp.sum(grad * hat, axis=0, keepdims=True)
    sums[2:3, :] = jnp.sum(grad, axis=0, keepdims=True)
    sums[3:4, :] = jnp.sum(top, axis=0, keepdims=True)
    sums[4:8, :] = jnp.zeros_like(sums[4:8, :])


def attend_back(qkv, logs, mixed, out_weight, *refs, parts, step, low, wide):
    grads = refs[:parts]
    out, key_grad, value_grad, given, inner = refs[parts:]
    whole = qkv.shape[0]
    rows = whole // parts
    heads = wide // HEAD
    head = low // HEAD
    ones = jnp.concatenate([of_head(jnp.ones((8, wide), bf16), j) for j in range(heads)], axis=0)
    for b in range(parts):
        at = slice(b * rows, (b + 1) * rows)
        value = dot32(grads[b][...], out_weight[low : low + wide, :], 1, 1).astype(bf16)
        given[at, :] = value
        both = value.astype(f32) * mixed[at, low : low + wide].astype(f32)
        high = both.astype(bf16)
        rest = (both - high.astype(f32)).astype(bf16)
        inner[:, at] = dot32(ones, high, 1, 1) + dot32(ones, rest, 1, 1)
    key_pair = qkv[:, 3 * low + wide : 3 * low + 2 * wide]
    value_pair = qkv[:, 3 * low + 2 * wide : 3 * low + 3 * wide]
    key_t = key_pair.T
    keys = [of_head(key_pair, j) for j in range(heads)]
    values = [of_head(value_pair, j) for j in range(heads)]
    keys_t = [of_head(key_t, j, 0) for j in range(heads)]
    key_grad[...] = jnp.zeros_like(key_grad)
    value_grad[...] = jnp.zeros_like(value_grad)

    def block(i, carry):
        start = pl.multiple_of(i * step, step)
        query = qkv[pl.ds(start, step), 3 * low : 3 * low + wide]
        grad = given[pl.ds(start, step), :]
        total = None
        for j in range(heads):
            scores = dot32(keys[j], query, 1, 1)
            weights = jnp.exp(scores - logs[head + j : head + j + 1, pl.ds(start, step)])
            back = dot32(values[j], grad, 1, 1)
            score_grad = (weights * (back - inner[8 * j : 8 * j + 1, pl.ds(start, step)])).astype(bf16)
            value_grad[...] += dot32(weights.astype(bf16), of_head(grad, j), 1, 0)
            key_grad[...] += dot32(score_grad, of_head(query, j), 1, 0)
            part = dot32(keys_t[j], score_grad, 1, 0)
            total = part if total is None else total + part
        out[pl.ds(start, step), :wide] = (total.T * score_scale).astype(bf16)
        return carry

    lax.fori_loop(0, whole // step, block, 0)
    out[:, wide : 2 * wide] = key_grad[...].astype(bf16)
    out[:, 2 * wide :] = value_grad[...].astype(bf16)


def project_back(*refs, pairs):
    grads, weight, own, partner, crossing, sums = refs[:pairs], refs[pairs], *refs[pairs + 1 :]

    def share_of(at, cols):
        total, low = None, 0
        for grad in grads:
            wide = grad.shape[1]
            part = dot32(grad[at, :], weight[low : low + wide, cols], 1, 0)
            total = part if total is None else total + part
            low += wide
        return total

    put_tiles((own, partner, crossing), share_of, grads[0].shape[0])
    low = 0
    for grad in grads:
        wide = grad.shape[1]
        sums[:, low : low + wide] = jnp.sum(grad[...].astype(f32), axis=0, keepdims=True)
        low += wide


def projection_grad(index, *refs, micros, pairs, parts, count):
    normed, refs = refs[:micros], refs[micros:]
    grads, refs = [refs[m * pairs : (m + 1) * pairs] for m in range(micros)], refs[micros * pairs :]
    tops, refs = [refs[m * parts : (m + 1) * parts] for m in range(micros)], refs[micros * parts :]
    mixed, refs = refs[:micros], refs[micros:]
    chunks, (left, right) = refs[:-2], refs[-2:]
    width = mixed[0].shape[1]
    rows = tops[0][0].shape[0]
    for p, (low, wide) in enumerate(head_pairs(width)):
        total = None
        for m in range(micros):
            part = dot32(grads[m][p][...], normed[m][...], 0, 0)
            total = part if total is None else total + part
        left[low : low + wide, :] = total[:wide].astype(bf16)
        left[width + low : width + low + wide, :] = total[wide : 2 * wide].astype(bf16)
        right[low : low + wide, :] = total[2 * wide :].astype(bf16)
        total = None
        for m in range(micros):
            for b in range(parts):
                part = dot32(mixed[m][b * rows : (b + 1) * rows, low : low + wide], tops[m][b][...], 0, 0)
                total = part if total is None else total + part
        right[width + low : width + low + wide, :] = total.astype(bf16)
    put_chunks(index, chunks[:count], left, 0)
    put_chunks(index, chunks[count:], right, 1)


def ring_add(*refs):
    for i in range(2):
        refs[4 + i][...] = (refs[i][...].astype(f32) + refs[2 + i][...].astype(f32)).astype(bf16)


def ring_store(index, *refs, steps, divided, count):
    number = len(steps)
    moved, refs = refs[: 2 * number], refs[2 * number :]
    done, first, second, buffer, sems = refs[-5:]
    done[...] = jnp.zeros_like(done)
    size = buffer.shape[1]
    copies = []
    for k, step in enumerate(steps):
        for i in range(2):
            slot = 2 * k + i
            buffer[slot] = moved[slot][...].astype(f32)
            row = pl.multiple_of(ring_chunk(index[0], count, i, step) * size, size)
            if divided and i == 1:
                row = row + divided
                copy_second = pltpu.make_async_copy(
                    buffer.at[slot], second.at[pl.ds(pl.multiple_of(jnp.maximum(row - first.shape[0], 0), 16), size), :], sems.at[slot]
                )
                copy_first = pltpu.make_async_copy(
                    buffer.at[slot], first.at[pl.ds(pl.multiple_of(jnp.minimum(row, first.shape[0] - size), 16), size), :], sems.at[slot]
                )
                pl.when(row < first.shape[0])(copy_first.start)
                pl.when(row >= first.shape[0])(copy_second.start)
                copies.append(copy_first)
            else:
                target = second if i == 1 else first
                copies.append(pltpu.make_async_copy(buffer.at[slot], target.at[pl.ds(row, size), :], sems.at[slot]))
                copies[-1].start()
    for copy in copies:
        copy.wait()


def norm_one_back(tok, resid_grad, first, second, third, gain, out, sums, *, m):
    grad = three(first, second, third)
    hat, inverse = statistics(tok[m, 0].astype(f32))
    out[...] = resid_grad[...] + norm_back(grad, hat, inverse, gain[...].astype(f32))
    sums[0:4, :] = jnp.zeros_like(sums[0:4, :])
    sums[4:5, :] = jnp.sum(grad * hat, axis=0, keepdims=True)
    sums[5:6, :] = jnp.sum(grad, axis=0, keepdims=True)
    sums[6:8, :] = jnp.zeros_like(sums[6:8, :])


def vector_sum(*refs):
    total = refs[0][...]
    for ref in refs[1:-1]:
        total = total + ref[...]
    refs[-1][...] = total


def vector_join(first, second, *refs, number):
    up_bias, stack, out = refs[:number], refs[number:-1], refs[-1]
    out[...] = first[...] + second[...]
    for row, parts in ((6, up_bias), (7, stack)):
        total = parts[0][...]
        for part in parts[1:]:
            total = total + part[...]
        out[row : row + 1, : total.shape[1]] = total


def add_rows(resid, first, second, third, bias, out):
    out[...] = (resid[...] + three(first, second, third) + bias[...].astype(f32)).astype(bf16)


def swap(values, axis, bit):
    return lax.ppermute(values, axis, [(i, i ^ bit) for i in range(lax.axis_size(axis))])


def ring_order(count):
    return list(range(0, count, 2)) + list(range(1, count, 2))[::-1]


class Rings:
    def __init__(self, chain, index, shapes, divided=0):
        self.chain, self.index, self.shapes, self.divided = chain, index, shapes, divided
        self.count = lax.axis_size("wide")
        order = ring_order(self.count)
        self.perms = [[(order[i], order[(i + d) % self.count]) for i in range(self.count)] for d in (1, -1)]
        self.chunks, self.moving, self.have = [None, None], [None, None], []
        self.step = 1
        self.outs = None

    def start(self, i, chunks):
        self.chunks[i] = chunks
        self.moving[i] = lax.ppermute(chunks[0], "wide", self.perms[i])

    def hold(self, i):
        self.chain.hold(self.moving[i])

    def add(self, cover=False):
        made = self.chain.run(
            ring_add,
            [(c.shape, bf16) for c in self.moving],
            *self.moving,
            *[c[self.step] for c in self.chunks],
            cover=cover,
        )
        self.step += 1
        if self.step == self.count:
            self.have.append(made)
        self.moving = [lax.ppermute(c, "wide", self.perms[i]) for i, c in enumerate(made)]

    def forward(self):
        self.have.append(self.moving)
        self.chain.hold(*self.moving)
        if len(self.have) < self.count:
            self.moving = [lax.ppermute(c, "wide", self.perms[i]) for i, c in enumerate(self.moving)]

    def store(self, steps):
        moved = [c for s in steps for c in self.have[s]]
        kept = () if self.outs is None else self.outs
        made = self.chain.run(
            functools.partial(ring_store, steps=tuple(steps), divided=self.divided, count=self.count),
            [((8, LANES), f32)] + [(s, f32) for s in self.shapes],
            *moved,
            *kept,
            smem=(self.index,),
            scratch=[
                pltpu.VMEM((len(moved), *moved[0].shape), f32),
                pltpu.SemaphoreType.DMA((len(moved),)),
            ],
            alias={len(moved): 1, len(moved) + 1: 2} if kept else None,
            anywhere=(len(moved), len(moved) + 1) if kept else (),
            out_anywhere=(1, 2),
            limit=3 + (len(moved) * moved[0].size * 4 >> 20),
            cover=True,
        )
        self.outs = made[1:]


class Whole:
    def __init__(self, shapes, divided=0):
        self.shapes, self.divided = shapes, divided
        self.arrays = [None, None]

    def start(self, i, chunks):
        self.arrays[i] = chunks[0]

    def hold(self, i):
        pass

    def add(self, cover=False):
        pass

    def forward(self):
        pass

    def store(self, steps):
        if isinstance(self.arrays, list):
            self.arrays = lax.psum(tuple(self.arrays), "wide")
            first, second = (a.astype(f32) for a in self.arrays)
            if self.divided:
                cut = self.shapes[0][0] - self.divided
                first, second = jnp.concatenate([first, second[:cut]], axis=0), second[cut:]
            self.outs = (first, second)


def local(
    tokens,
    cotangent,
    cell_of,
    query_count,
    attn_norm_gain,
    attn_norm_bias,
    input_weight,
    query_bias,
    value_bias,
    out_weight,
    out_bias,
    ffn_norm_gain,
    ffn_norm_bias,
    up_weight,
    up_bias,
    down_weight,
    down_bias,
):
    micros = range(tokens.shape[0])
    rows, model = tokens.shape[2], tokens.shape[3]
    parts = lax.axis_size("narrow")
    whole = rows * parts
    width = input_weight.shape[2]
    hidden = up_weight.shape[1]
    count = lax.axis_size("wide")
    rings = count <= 8
    chunks = count if rings else 1
    pairs = head_pairs(width)
    step = min(512, whole)
    chain = Chain()
    run = chain.run
    index = lax.axis_index("wide").astype(jnp.int32).reshape(1)

    block = ((rows, model), bf16)
    outgoing = [block, block, ((2, rows, model), bf16)]
    wide_rows = ((whole, model), bf16)
    row = lambda v: v.reshape(1, -1)
    gain_one, bias_one, gain_two, bias_two = map(row, (attn_norm_gain, attn_norm_bias, ffn_norm_gain, ffn_norm_bias))
    out_bias, down_bias, up_bias = row(out_bias), row(down_bias), row(up_bias)

    def columns(three_parts):
        return jnp.concatenate([v[:, low : low + wide] for low, wide in pairs for v in three_parts], axis=1)

    weight_t = jnp.transpose(input_weight, (1, 2, 0)).reshape(3 * width, model)
    zero = jnp.zeros((1, width), f32)
    project_bias = columns([row(query_bias).astype(f32), zero, row(value_bias).astype(f32)])
    project_scale = columns([zero + score_scale, zero + 1.0, zero + 1.0])

    def gather(own):
        partner = swap(own, "narrow", 2)
        return [own, swap(own, "narrow", 1), partner, swap(partner, "narrow", 1)]

    def share(made):
        own, partner, crossing = made
        return [own, partner, swap(crossing, "narrow", 1)]

    def send(shares):
        own, partner, crossed = shares
        (both,) = run(pair_sum, [block], partner, crossed)
        return [own, crossed, swap(both, "narrow", 2)]

    def fresh():
        return [None] * len(micros)

    normed, given, qkv, normed_all, mixed, logs, shares, shares_down, resid, normed_two_b = (fresh() for _ in range(10))
    activ, pre_grad, up_bias_grad, two_all, given_all, resid_grad, top = (fresh() for _ in range(7))
    sums_two, sums_one, stack_sums, out_rows, grad_rows = (fresh() for _ in range(5))
    pair_grads = [[] for _ in micros]

    def do_norm_one(m):
        (own,) = run(functools.partial(norm_one, m=m), [block], tokens, gain_one, bias_one)
        normed[m] = gather(own)

    def do_scale(m):
        (own,) = run(functools.partial(scale_cot, m=m, count=count), [block], cotangent, smem=(index, cell_of, query_count), cover=True)
        given[m] = gather(own)

    def do_project(m):
        qkv[m], normed_all[m] = run(
            functools.partial(project, parts=parts),
            [((whole, 3 * width), bf16), wide_rows],
            *normed[m],
            weight,
            project_bias,
            project_scale,
        )

    def do_attend(m):
        mixed[m], logs[m], *made = run(
            functools.partial(attend, step=whole),
            [((whole, width), bf16), ((8, whole), f32), *outgoing],
            qkv[m],
            out_weight,
            limit=24,
        )
        shares[m] = share(made)

    def do_send(m):
        shares[m] = send(shares[m])

    def do_norm_two(m):
        resid[m], own = run(
            functools.partial(norm_two, m=m),
            [((rows, model), f32), block],
            tokens,
            *shares[m],
            out_bias,
            gain_two,
            bias_two,
            cover=m == 0,
        )
        normed_two_b[m] = gather(own)

    def do_feed(m):
        activ[m], pre_grad[m], up_bias_grad[m], two_all[m], given_all[m] = run(
            functools.partial(feed, parts=parts),
            [((whole, hidden), bf16), ((whole, hidden), bf16), ((1, hidden), f32), wide_rows, wide_rows],
            *normed_two_b[m],
            *given[m],
            up_weight,
            up_bias,
            down_weight,
        )

    def do_up_back(m):
        shares[m] = share(run(times_back, outgoing, pre_grad[m], up_weight))

    def do_down(m):
        shares_down[m] = share(run(times, outgoing, activ[m], down_weight))

    def do_send_down(m):
        shares_down[m] = send(shares_down[m])

    def do_norm_two_back(m):
        resid_grad[m], own, sums_two[m] = run(
            functools.partial(norm_two_back, m=m, count=count),
            [((rows, model), f32), block, ((8, model), f32)],
            cotangent,
            resid[m],
            *shares[m],
            gain_two,
            smem=(index, cell_of, query_count),
            cover=True,
        )
        top[m] = gather(own)

    def do_attend_back(m, p):
        low, wide = pairs[p]
        (made,) = run(
            functools.partial(attend_back, parts=parts, step=step, low=low, wide=wide),
            [((whole, 3 * wide), bf16)],
            qkv[m],
            logs[m],
            mixed[m],
            out_weight,
            *top[m],
            scratch=[
                pltpu.VMEM((whole, wide), f32),
                pltpu.VMEM((whole, wide), f32),
                pltpu.VMEM((whole, wide), bf16),
                pltpu.VMEM((8 * (wide // HEAD), whole), f32),
            ],
            limit=20,
        )
        pair_grads[m].append(made)

    def do_project_back(m):
        *made, stack_sums[m] = run(
            functools.partial(project_back, pairs=len(pairs)),
            [*outgoing, ((1, 3 * width), f32)],
            *pair_grads[m],
            weight,
        )
        shares[m] = share(made)

    def do_norm_one_back(m):
        grad_rows[m], sums_one[m] = run(
            functools.partial(norm_one_back, m=m),
            [((rows, model), f32), ((8, model), f32)],
            tokens,
            resid_grad[m],
            *shares[m],
            gain_one,
        )

    def wait(*arrays):
        chain.hold(*arrays)
        run(mark, [((8, LANES), f32)], cover=True)

    hops = [("narrow", 1 << k) for k in range(parts.bit_length() - 1)]
    hops += [("wide", 1 << k) for k in range(count.bit_length() - 1)]
    vectors = []

    def do_vectors():
        done = len(vectors)
        shape = [((8, model), f32)]
        if done == 0:
            (own,) = run(vector_sum, shape, *sums_one, *sums_two)
        elif hops[done - 1][0] == "narrow" and hops[done][0] == "wide":
            own, arrived = vectors[-1]
            (own,) = run(
                functools.partial(vector_join, number=len(micros)), shape, own, arrived, *up_bias_grad, *stack_sums
            )
        else:
            (own,) = run(vector_sum, shape, *vectors[-1])
        vectors.append((own, swap(own, *hops[done]) if done < len(hops) else None))

    def do_add_rows(m):
        (out_rows[m],) = run(add_rows, [block], resid[m], *shares_down[m], down_bias)

    def ffn_grad(firsts, seconds, ring):
        shape = (firsts[0].shape[1], seconds[0].shape[1])
        made = run(
            functools.partial(weight_grad, pairs=len(micros), ring=ring),
            [((shape[0] // chunks, shape[1]), bf16)] * chunks,
            *firsts,
            *seconds,
            smem=(index,),
            scratch=[pltpu.VMEM(shape, bf16)],
            limit=16,
        )
        ffn.start(ring, made)

    def attn_grad():
        made = run(
            functools.partial(projection_grad, micros=len(micros), pairs=len(pairs), parts=parts, count=chunks),
            [((2 * width // chunks, model), bf16)] * (2 * chunks),
            *normed_all,
            *[g for m in micros for g in pair_grads[m]],
            *[t for m in micros for t in top[m]],
            *mixed,
            smem=(index,),
            scratch=[pltpu.VMEM((2 * width, model), bf16)] * 2,
            limit=20,
        )
        attn.start(0, made[:chunks])
        attn.start(1, made[chunks:])

    ffn_shapes = [(hidden, model), (model, hidden)]
    attn_shapes = [(3 * width, model), (width, model)]
    ffn = Rings(chain, index, ffn_shapes) if rings else Whole(ffn_shapes)
    attn = Rings(chain, index, attn_shapes, 2 * width) if rings else Whole(attn_shapes, 2 * width)

    do_norm_one(0)
    (weight,) = run(by_pairs, [((3 * width, model), bf16)], weight_t)
    chain.hold(normed[0][1], normed[0][2])
    do_norm_one(1)
    do_scale(0)
    do_project(0)
    do_attend(0)
    chain.hold(normed[1][1], normed[1][2], given[0][1], given[0][2])
    do_scale(1)
    do_send(0)
    chain.hold(given[1][1])
    do_project(1)
    do_attend(1)
    chain.hold(given[1][2])
    do_norm_two(0)
    do_send(1)
    chain.hold(normed_two_b[0][1])
    do_norm_two(1)
    chain.hold(normed_two_b[1][1])
    do_feed(0)
    do_up_back(0)
    do_down(0)
    wait(normed_two_b[1][2])
    do_send(0)
    do_feed(1)
    do_up_back(1)
    do_norm_two_back(0)
    chain.hold(top[0][1])
    ffn_grad(activ, given_all, 0)
    ffn_grad(two_all, pre_grad, 1)
    ffn.hold(0)
    wait(top[0][2])
    do_send(1)
    do_attend_back(0, 0)
    ffn.add()
    do_attend_back(0, 1)
    do_norm_two_back(1)
    ffn.add()
    do_attend_back(0, 2)
    ffn.add()
    chain.hold(top[1][1])
    wait(top[1][2])
    do_attend_back(1, 0)
    do_send_down(0)
    ffn.add()
    do_attend_back(1, 1)
    chain.hold(shares_down[0][2])
    ffn.add()
    do_attend_back(1, 2)
    do_add_rows(0)
    ffn.add()
    attn_grad()
    ffn.add()
    attn.add(cover=True)
    do_project_back(0)
    attn.add(cover=True)
    do_send(0)
    ffn.forward()
    do_project_back(1)
    attn.add(cover=True)
    do_send(1)
    attn.add(cover=True)
    ffn.forward()
    do_norm_one_back(0)
    do_down(1)
    attn.add(cover=True)
    do_send_down(1)
    attn.add(cover=True)
    ffn.forward()
    do_norm_one_back(1)
    attn.add(cover=True)
    do_vectors()
    ffn.store(range(0, 2))
    chain.hold(shares_down[1][2])
    ffn.forward()
    attn.forward()
    do_vectors()
    attn.forward()
    ffn.store(range(2, 3))
    do_vectors()
    ffn.forward()
    attn.forward()
    do_add_rows(1)
    do_vectors()
    attn.store(range(0, 2))
    attn.forward()
    do_vectors()
    ffn.store(range(3, 5))
    ffn.forward()
    attn.forward()
    do_vectors()
    attn.store(range(2, 4))
    attn.forward()
    ffn.store(range(5, 6))
    ffn.forward()
    attn.forward()
    attn.store(range(4, 7))
    ffn.store(range(6, 8))
    attn.store(range(7, 8))

    while len(vectors) <= len(hops):
        do_vectors()
    vector_sums = vectors[-1][0]
    up_bias_sum = vector_sums[6, :hidden]
    stack_sum = vector_sums[7, : 3 * width]

    def plain(j):
        return jnp.concatenate([stack_sum[3 * low + j * wide : 3 * low + (j + 1) * wide] for low, wide in pairs])

    return (
        jnp.stack(out_rows)[:, None],
        jnp.stack(grad_rows)[:, None],
        vector_sums[4],
        vector_sums[5],
        jnp.transpose(attn.outs[0].reshape(3, width, model), (2, 0, 1)),
        plain(0),
        plain(2),
        attn.outs[1],
        vector_sums[0],
        vector_sums[1],
        vector_sums[2],
        ffn.outs[1],
        up_bias_sum,
        ffn.outs[0],
        vector_sums[3],
    )


def solution(mesh):
    in_specs = (
        P(None, "wide", "narrow", None),
        P(None, "wide", "narrow", None),
        P(),
        P(),
        P(),
        P(),
        P(None, None, "narrow"),
        P("narrow"),
        P("narrow"),
        P("narrow", None),
        P(),
        P(),
        P(),
        P(None, "narrow"),
        P("narrow"),
        P("narrow", None),
        P(),
    )
    out_specs = (
        P(None, "wide", "narrow", None),
        P(None, "wide", "narrow", None),
        P(),
        P(),
        P(None, None, "narrow"),
        P("narrow"),
        P("narrow"),
        P("narrow", None),
        P(),
        P(),
        P(),
        P(None, "narrow"),
        P("narrow"),
        P("narrow", None),
        P(),
    )
    return jax.shard_map(local, mesh=mesh, in_specs=in_specs, out_specs=out_specs, check_vma=False)
```

```python
import functools

import jax
import jax.numpy as jnp
from jax import lax
from jax.experimental import pallas as pl
from jax.experimental.pallas import tpu as pltpu
from jax.sharding import PartitionSpec as P

HEAD = 64
LANES = 128
TILE = 256
norm_eps = 1e-05
score_scale = 0.125
bf16 = jnp.bfloat16
f32 = jnp.float32


class Chain:
    def __init__(self):
        self.last = []
        self.held = []

    def hold(self, *arrays):
        self.held += arrays

    def run(self, body, outs, *ins, smem=(), scratch=(), alias=None, anywhere=(), out_anywhere=(), limit=12, token=0, cover=False):
        unread = [*self.last, *self.held]
        count = len(smem) + len(ins)
        specs = [pl.BlockSpec(memory_space=pltpu.SMEM)] * len(smem)
        specs += [pl.BlockSpec(memory_space=pl.ANY if i in anywhere else pltpu.VMEM) for i in range(len(ins))]
        specs += [pl.BlockSpec(memory_space=pl.ANY)] * len(unread)

        def inner(*refs):
            body(*refs[:count], *refs[count + len(unread) :])

        made = pl.pallas_call(
            inner,
            out_shape=tuple(jax.ShapeDtypeStruct(*o) for o in outs),
            in_specs=specs,
            out_specs=tuple(
                pl.BlockSpec(memory_space=pl.ANY if i in out_anywhere else pltpu.VMEM) for i in range(len(outs))
            ),
            scratch_shapes=scratch,
            input_output_aliases={} if alias is None else {len(smem) + k: v for k, v in alias.items()},
            compiler_params=pltpu.CompilerParams(vmem_limit_bytes=limit << 20),
            cost_estimate=pl.CostEstimate(flops=10**12 if cover else 1, bytes_accessed=1, transcendentals=0),
            name=body.func.__name__ if isinstance(body, functools.partial) else body.__name__,
        )(*smem, *ins, *unread)
        self.last, self.held = [made[token]], []
        return made


def dot32(first, second, first_dim, second_dim):
    return lax.dot_general(
        first, second, (((first_dim,), (second_dim,)), ((), ())), preferred_element_type=f32
    )


def statistics(values):
    average = jnp.mean(values, axis=-1, keepdims=True)
    centred = values - average
    inverse = lax.rsqrt(jnp.mean(centred * centred, axis=-1, keepdims=True) + norm_eps)
    return centred * inverse, inverse


def norm_back(grad, normed, inverse, gain):
    scaled = grad * gain
    mean_one = jnp.mean(scaled, axis=-1, keepdims=True)
    mean_two = jnp.mean(scaled * normed, axis=-1, keepdims=True)
    return inverse * (scaled - mean_one - normed * mean_two)


def of_head(values, j, axis=1):
    if values.shape[axis] <= HEAD:
        return values
    place = lax.broadcasted_iota(jnp.int32, values.shape, axis)
    return jnp.where((place >= HEAD * j) & (place < HEAD * (j + 1)), values, jnp.zeros_like(values))


def head_pairs(width):
    return [(low, min(LANES, width - low)) for low in range(0, width, LANES)]


def mark(out):
    out[...] = jnp.zeros_like(out)


def by_pairs(weight_t, out):
    width = out.shape[0] // 3
    for low, wide in head_pairs(width):
        for j in range(3):
            out[3 * low + j * wide : 3 * low + (j + 1) * wide, :] = weight_t[
                j * width + low : j * width + low + wide, :
            ]


def norm_one(tok, gain, bias, out, *, m):
    normed, _ = statistics(tok[m, 0].astype(f32))
    out[...] = (normed * gain[...].astype(f32) + bias[...].astype(f32)).astype(bf16)


def loss_grad(where, cells, queries, cot, m, count):
    number = queries[cells[where[0] + m * count]]
    scale = jnp.sqrt(jnp.full((1, cot.shape[3]), number, jnp.int32).astype(f32) / 500.0)
    return cot[m, 0].astype(f32) * scale


def scale_cot(where, cells, queries, cot, out, *, m, count):
    out[...] = loss_grad(where, cells, queries, cot, m, count).astype(bf16)


def project(*refs, parts):
    blocks = refs[:parts]
    weight, bias, scale = refs[parts : parts + 3]
    out, whole = refs[parts + 3 :]
    rows = blocks[0].shape[0]
    for b in range(parts):
        values = blocks[b][...]
        at = slice(b * rows, (b + 1) * rows)
        whole[at, :] = values
        out[at, :] = ((dot32(values, weight[...], 1, 1) + bias[...]) * scale[...]).astype(bf16)


def attend(qkv, out_weight, attended, logs, *outs, step):
    whole = qkv.shape[0]
    head = 0
    for low, wide in head_pairs(out_weight.shape[0]):
        heads = wide // HEAD
        key_pair = qkv[:, 3 * low + wide : 3 * low + 2 * wide]
        value_t = qkv[:, 3 * low + 2 * wide : 3 * low + 3 * wide].T
        keys = [of_head(key_pair, j) for j in range(heads)]
        values = [of_head(value_t, j, 0) for j in range(heads)]
        for start in range(0, whole, step):
            at = slice(start, start + step)
            query = qkv[at, 3 * low : 3 * low + wide]
            total = None
            for j in range(heads):
                scores = dot32(keys[j], query, 1, 1)
                top = jnp.max(scores, axis=0, keepdims=True)
                powers = jnp.exp(scores - top)
                length = jnp.sum(powers, axis=0, keepdims=True)
                mixed = dot32(values[j], powers.astype(bf16), 1, 0) * (1.0 / length)
                total = mixed if total is None else total + mixed
                logs[head + j : head + j + 1, at] = top + jnp.log(length)
            attended[at, low : low + wide] = total.T.astype(bf16)
        head += heads
    put_shares(outs, lambda at: dot32(attended[at, :], out_weight[...], 1, 0), whole)


def put_shares(outs, share_of, whole):
    own, partner, crossing = outs
    rows = own.shape[0]
    for b, (out, at) in enumerate(((own, None), (crossing, 0), (partner, None), (crossing, 1))):
        value = share_of(slice(b * rows, (b + 1) * rows)).astype(bf16)
        if at is None:
            out[...] = value
        else:
            out[at] = value


def pair_sum(first, second, out):
    out[...] = (first[...].astype(f32) + second[1].astype(f32)).astype(bf16)


def three(first, second, third):
    return first[...].astype(f32) + second[0].astype(f32) + third[...].astype(f32)


def norm_two(tok, first, second, third, out_bias, gain, bias, resid, normed, *, m):
    value = tok[m, 0].astype(f32) + three(first, second, third) + out_bias[...].astype(f32)
    resid[...] = value
    hat, _ = statistics(value)
    normed[...] = (hat * gain[...].astype(f32) + bias[...].astype(f32)).astype(bf16)


def feed(*refs, parts):
    normed, grads = refs[:parts], refs[parts : 2 * parts]
    up, up_bias, down = refs[2 * parts : 2 * parts + 3]
    activ, pre_grad, bias_grad, normed_all, grads_all = refs[2 * parts + 3 :]
    rows = normed[0].shape[0]
    for b in range(parts):
        normed_all[b * rows : (b + 1) * rows, :] = normed[b][...]
        grads_all[b * rows : (b + 1) * rows, :] = grads[b][...]
    for low in range(0, up.shape[1], TILE):
        cols = slice(low, low + TILE)
        total = None
        for b in range(parts):
            at = slice(b * rows, (b + 1) * rows)
            pre = dot32(normed[b][...], up[:, cols], 1, 0) + up_bias[:, cols].astype(f32)
            cumul = 0.5 + 0.5 * lax.erf(pre * 0.7071067811865476)
            density = jnp.exp(-0.5 * pre * pre) * 0.3989422804014327
            activ[at, cols] = (pre * cumul).astype(bf16)
            back = dot32(grads[b][...], down[cols, :], 1, 1)
            grad = (back * (cumul + pre * density)).astype(bf16)
            pre_grad[at, cols] = grad
            part = jnp.sum(grad.astype(f32), axis=0, keepdims=True)
            total = part if total is None else total + part
        bias_grad[:, cols] = total


def times(value, weight, *outs):
    put_tiles(outs, lambda at, cols: dot32(value[at, :], weight[:, cols], 1, 0), value.shape[0])


def times_back(value, weight, *outs):
    put_tiles(outs, lambda at, cols: dot32(value[at, :], weight[cols, :], 1, 1), value.shape[0])


def put_tiles(outs, share_of, whole):
    own, partner, crossing = outs
    rows, model = own.shape

    def tile(i, carry):
        cols = pl.ds(pl.multiple_of(i * TILE, TILE), TILE)
        own[:, cols] = share_of(slice(0, rows), cols).astype(bf16)
        crossing[0, :, cols] = share_of(slice(rows, 2 * rows), cols).astype(bf16)
        partner[:, cols] = share_of(slice(2 * rows, 3 * rows), cols).astype(bf16)
        crossing[1, :, cols] = share_of(slice(3 * rows, 4 * rows), cols).astype(bf16)
        return carry

    lax.fori_loop(0, model // TILE, tile, 0)


def weight_grad(where, *refs, pairs, before):
    firsts, seconds, refs = refs[:pairs], refs[pairs : 2 * pairs], refs[2 * pairs :]
    chunks, whole = refs[before:-1], refs[-1]

    def tile(i, carry):
        rows = pl.ds(pl.multiple_of(i * TILE, TILE), TILE)
        total = None
        for first, second in zip(firsts, seconds):
            part = dot32(first[:, rows], second[...], 0, 0)
            total = part if total is None else total + part
        whole[rows, :] = total.astype(bf16)
        return carry

    lax.fori_loop(0, whole.shape[0] // TILE, tile, 0)
    if before:
        chunks, both = chunks[:-1], chunks[-1]
        size = chunks[0].shape[0]
        both[:size, :] = refs[0][...]
        put_chunks(where, chunks, whole)
        both[size:, :] = chunks[0][...]
    else:
        put_chunks(where, chunks, whole)


def ring_chunk(where, count, step):
    half = where[0] // 2
    place = jnp.where(where[0] % 2 == 0, half, count - 1 - half)
    return lax.rem(place + jnp.where(where[1] % 2 == 0, count - step, step), count)


def put_chunks(where, chunks, whole):
    for s, chunk in enumerate(chunks):
        size = chunk.shape[0]
        which = ring_chunk(where, len(chunks), (s + 1) % len(chunks)) if len(chunks) > 1 else 0
        chunk[...] = whole[pl.ds(pl.multiple_of(which * size, size), size), :]


def norm_two_back(where, cells, queries, cot, resid, first, second, third, gain, out, rounded, sums, *, m, count):
    top = loss_grad(where, cells, queries, cot, m, count)
    grad = three(first, second, third)
    hat, inverse = statistics(resid[...])
    back = top + norm_back(grad, hat, inverse, gain[...].astype(f32))
    out[...] = back
    rounded[...] = back.astype(bf16)
    sums[0:1, :] = jnp.sum(back, axis=0, keepdims=True)
    sums[1:2, :] = jnp.sum(grad * hat, axis=0, keepdims=True)
    sums[2:3, :] = jnp.sum(grad, axis=0, keepdims=True)
    sums[3:4, :] = jnp.sum(top, axis=0, keepdims=True)
    sums[4:8, :] = jnp.zeros_like(sums[4:8, :])


def attend_back(qkv, logs, mixed, out_weight, *refs, parts, step, low, wide):
    grads = refs[:parts]
    out, key_grad, value_grad, given, inner = refs[parts:]
    whole = qkv.shape[0]
    rows = whole // parts
    heads = wide // HEAD
    head = low // HEAD
    ones = jnp.concatenate([of_head(jnp.ones((8, wide), bf16), j) for j in range(heads)], axis=0)
    for b in range(parts):
        at = slice(b * rows, (b + 1) * rows)
        value = dot32(grads[b][...], out_weight[low : low + wide, :], 1, 1).astype(bf16)
        given[at, :] = value
        both = value.astype(f32) * mixed[at, low : low + wide].astype(f32)
        high = both.astype(bf16)
        rest = (both - high.astype(f32)).astype(bf16)
        inner[:, at] = dot32(ones, high, 1, 1) + dot32(ones, rest, 1, 1)
    key_pair = qkv[:, 3 * low + wide : 3 * low + 2 * wide]
    value_pair = qkv[:, 3 * low + 2 * wide : 3 * low + 3 * wide]
    key_t = key_pair.T
    keys = [of_head(key_pair, j) for j in range(heads)]
    values = [of_head(value_pair, j) for j in range(heads)]
    keys_t = [of_head(key_t, j, 0) for j in range(heads)]
    key_grad[...] = jnp.zeros_like(key_grad)
    value_grad[...] = jnp.zeros_like(value_grad)

    def block(i, carry):
        start = pl.multiple_of(i * step, step)
        query = qkv[pl.ds(start, step), 3 * low : 3 * low + wide]
        grad = given[pl.ds(start, step), :]
        total = None
        for j in range(heads):
            scores = dot32(keys[j], query, 1, 1)
            weights = jnp.exp(scores - logs[head + j : head + j + 1, pl.ds(start, step)])
            back = dot32(values[j], grad, 1, 1)
            score_grad = (weights * (back - inner[8 * j : 8 * j + 1, pl.ds(start, step)])).astype(bf16)
            value_grad[...] += dot32(weights.astype(bf16), of_head(grad, j), 1, 0)
            key_grad[...] += dot32(score_grad, of_head(query, j), 1, 0)
            part = dot32(keys_t[j], score_grad, 1, 0)
            total = part if total is None else total + part
        out[pl.ds(start, step), :wide] = (total.T * score_scale).astype(bf16)
        return carry

    lax.fori_loop(0, whole // step, block, 0)
    out[:, wide : 2 * wide] = key_grad[...].astype(bf16)
    out[:, 2 * wide :] = value_grad[...].astype(bf16)


def project_back(*refs, pairs):
    grads, weight, own, partner, crossing, sums = refs[:pairs], refs[pairs], *refs[pairs + 1 :]

    def share_of(at, cols):
        total, low = None, 0
        for grad in grads:
            wide = grad.shape[1]
            part = dot32(grad[at, :], weight[low : low + wide, cols], 1, 0)
            total = part if total is None else total + part
            low += wide
        return total

    put_tiles((own, partner, crossing), share_of, grads[0].shape[0])
    low = 0
    for grad in grads:
        wide = grad.shape[1]
        sums[:, low : low + wide] = jnp.sum(grad[...].astype(f32), axis=0, keepdims=True)
        low += wide


def projection_grad(where, *refs, micros, pairs, parts):
    normed, refs = refs[:micros], refs[micros:]
    grads, refs = [refs[m * pairs : (m + 1) * pairs] for m in range(micros)], refs[micros * pairs :]
    tops, refs = [refs[m * parts : (m + 1) * parts] for m in range(micros)], refs[micros * parts :]
    mixed, refs = refs[:micros], refs[micros:]
    chunks, out = refs[:-1], refs[-1]
    width = mixed[0].shape[1]
    rows = tops[0][0].shape[0]
    for p, (low, wide) in enumerate(head_pairs(width)):
        total = None
        for m in range(micros):
            part = dot32(grads[m][p][...], normed[m][...], 0, 0)
            total = part if total is None else total + part
        for j in range(3):
            out[j * width + low : j * width + low + wide, :] = total[j * wide : (j + 1) * wide].astype(bf16)
        total = None
        for m in range(micros):
            for b in range(parts):
                part = dot32(mixed[m][b * rows : (b + 1) * rows, low : low + wide], tops[m][b][...], 0, 0)
                total = part if total is None else total + part
        out[3 * width + low : 3 * width + low + wide, :] = total.astype(bf16)
    put_chunks(where, chunks, out)


def ring_add(arrived, *refs):
    low = 0
    for part in refs[:-1]:
        at = slice(low, low + part.shape[0])
        refs[-1][at, :] = (arrived[at, :].astype(f32) + part[...].astype(f32)).astype(bf16)
        low += part.shape[0]


def ring_store(where, *refs, steps, count, stacked):
    moved, refs = refs[: len(steps)], refs[len(steps) :]
    done, first, second, buffer, sems = refs[-5:]
    done[...] = jnp.zeros_like(done)
    size = buffer.shape[1] // 2 if stacked else buffer.shape[1]
    copies = []
    for k, step in enumerate(steps):
        buffer[k] = moved[k][...].astype(f32)
        row = pl.multiple_of(ring_chunk(where, count, step) * size, size)
        if stacked:
            for i, target in enumerate((first, second)):
                source = buffer.at[k, pl.ds(i * size, size), :]
                copies.append(pltpu.make_async_copy(source, target.at[pl.ds(row, size), :], sems.at[2 * k + i]))
                copies[-1].start()
        else:
            last = first.shape[0] - size
            to_first = pl.multiple_of(jnp.minimum(row, last), 16)
            to_second = pl.multiple_of(jnp.maximum(row - first.shape[0], 0), 16)
            copy_first = pltpu.make_async_copy(buffer.at[k], first.at[pl.ds(to_first, size), :], sems.at[2 * k])
            copy_second = pltpu.make_async_copy(buffer.at[k], second.at[pl.ds(to_second, size), :], sems.at[2 * k])
            pl.when(row <= last)(copy_first.start)
            pl.when(row > last)(copy_second.start)
            copies.append(copy_first)
    for copy in copies:
        copy.wait()


def norm_one_back(tok, resid_grad, first, second, third, gain, out, sums, *, m):
    grad = three(first, second, third)
    hat, inverse = statistics(tok[m, 0].astype(f32))
    out[...] = resid_grad[...] + norm_back(grad, hat, inverse, gain[...].astype(f32))
    sums[0:4, :] = jnp.zeros_like(sums[0:4, :])
    sums[4:5, :] = jnp.sum(grad * hat, axis=0, keepdims=True)
    sums[5:6, :] = jnp.sum(grad, axis=0, keepdims=True)
    sums[6:8, :] = jnp.zeros_like(sums[6:8, :])


def vector_sum(*refs):
    total = refs[0][...]
    for ref in refs[1:-1]:
        total = total + ref[...]
    refs[-1][...] = total


def vector_join(first, second, *refs, number):
    up_bias, stack, out = refs[:number], refs[number:-1], refs[-1]
    out[...] = first[...] + second[...]
    for row, parts in ((6, up_bias), (7, stack)):
        total = parts[0][...]
        for part in parts[1:]:
            total = total + part[...]
        out[row : row + 1, : total.shape[1]] = total


def add_rows(resid, first, second, third, bias, out):
    out[...] = (resid[...] + three(first, second, third) + bias[...].astype(f32)).astype(bf16)


def swap(values, axis, bit):
    return lax.ppermute(values, axis, [(i, i ^ bit) for i in range(lax.axis_size(axis))])


def ring_order(count):
    return list(range(0, count, 2)) + list(range(1, count, 2))[::-1]


class Ring:
    def __init__(self, chain, where, shapes, stacked):
        self.chain, self.where, self.shapes, self.stacked = chain, where, shapes, stacked
        self.count = lax.axis_size("wide")
        cores = lax.axis_size("narrow")
        order = ring_order(self.count)
        self.perm = [
            (order[i] * cores + n, order[(i + (1 if n % 2 == 0 else -1)) % self.count] * cores + n)
            for i in range(self.count)
            for n in range(cores)
        ]
        self.have, self.step, self.outs = [], 1, None

    def pass_on(self, chunk):
        self.moving = lax.ppermute(chunk, ("wide", "narrow"), self.perm)

    def start(self, chunk, parts):
        self.parts = parts
        self.pass_on(chunk)

    def hold(self):
        self.chain.hold(self.moving)

    def add(self, cover=False):
        (made,) = self.chain.run(
            ring_add,
            [(self.moving.shape, bf16)],
            self.moving,
            *[p[self.step] for p in self.parts],
            cover=cover,
        )
        self.step += 1
        if self.step == self.count:
            self.have.append(made)
        self.pass_on(made)

    def forward(self):
        self.have.append(self.moving)
        self.hold()
        if len(self.have) < self.count:
            self.pass_on(self.moving)

    def store(self, steps):
        moved = [self.have[s] for s in steps]
        kept = () if self.outs is None else self.outs
        number = len(moved)
        made = self.chain.run(
            functools.partial(ring_store, steps=tuple(steps), count=self.count, stacked=self.stacked),
            [((8, LANES), f32)] + [(s, f32) for s in self.shapes],
            *moved,
            *kept,
            smem=(self.where,),
            scratch=[pltpu.VMEM((number, *moved[0].shape), f32), pltpu.SemaphoreType.DMA((2 * number,))],
            alias={number: 1, number + 1: 2} if kept else None,
            anywhere=(number, number + 1) if kept else (),
            out_anywhere=(1, 2),
            limit=6 + (number * moved[0].size * 4 >> 20),
            cover=True,
        )
        self.outs = made[1:]


class Whole:
    def __init__(self, shapes):
        self.shapes = shapes

    def start(self, chunk, parts):
        total = lax.psum(chunk, "wide").astype(f32)
        self.outs = (total[: self.shapes[0][0]], total[self.shapes[0][0] :])

    def hold(self):
        pass

    def add(self, cover=False):
        pass

    def forward(self):
        pass

    def store(self, steps):
        pass


def local(
    tokens,
    cotangent,
    cell_of,
    query_count,
    attn_norm_gain,
    attn_norm_bias,
    input_weight,
    query_bias,
    value_bias,
    out_weight,
    out_bias,
    ffn_norm_gain,
    ffn_norm_bias,
    up_weight,
    up_bias,
    down_weight,
    down_bias,
):
    micros = range(tokens.shape[0])
    rows, model = tokens.shape[2], tokens.shape[3]
    parts = lax.axis_size("narrow")
    whole = rows * parts
    width = input_weight.shape[2]
    hidden = up_weight.shape[1]
    count = lax.axis_size("wide")
    rings = count <= 8
    chunks = count if rings else 1
    pairs = head_pairs(width)
    step = min(512, whole)
    chain = Chain()
    run = chain.run
    where = jnp.stack([lax.axis_index("wide"), lax.axis_index("narrow")]).astype(jnp.int32)

    block = ((rows, model), bf16)
    outgoing = [block, block, ((2, rows, model), bf16)]
    wide_rows = ((whole, model), bf16)
    row = lambda v: v.reshape(1, -1)
    gain_one, bias_one, gain_two, bias_two = map(row, (attn_norm_gain, attn_norm_bias, ffn_norm_gain, ffn_norm_bias))
    out_bias, down_bias, up_bias = row(out_bias), row(down_bias), row(up_bias)

    def columns(three_parts):
        return jnp.concatenate([v[:, low : low + wide] for low, wide in pairs for v in three_parts], axis=1)

    weight_t = jnp.transpose(input_weight, (1, 2, 0)).reshape(3 * width, model)
    zero = jnp.zeros((1, width), f32)
    project_bias = columns([row(query_bias).astype(f32), zero, row(value_bias).astype(f32)])
    project_scale = columns([zero + score_scale, zero + 1.0, zero + 1.0])

    def gather(own):
        partner = swap(own, "narrow", 2)
        return [own, swap(own, "narrow", 1), partner, swap(partner, "narrow", 1)]

    def share(made):
        own, partner, crossing = made
        return [own, partner, swap(crossing, "narrow", 1)]

    def send(shares):
        own, partner, crossed = shares
        (both,) = run(pair_sum, [block], partner, crossed)
        return [own, crossed, swap(both, "narrow", 2)]

    def fresh():
        return [None] * len(micros)

    normed, given, qkv, normed_all, mixed, logs, shares, shares_down, resid, normed_two_b = (fresh() for _ in range(10))
    activ, pre_grad, up_bias_grad, two_all, given_all, resid_grad, top = (fresh() for _ in range(7))
    sums_two, sums_one, stack_sums, out_rows, grad_rows = (fresh() for _ in range(5))
    pair_grads = [[] for _ in micros]

    def do_norm_one(m):
        (own,) = run(functools.partial(norm_one, m=m), [block], tokens, gain_one, bias_one)
        normed[m] = gather(own)

    def do_scale(m):
        (own,) = run(functools.partial(scale_cot, m=m, count=count), [block], cotangent, smem=(where, cell_of, query_count), cover=True)
        given[m] = gather(own)

    def do_project(m):
        qkv[m], normed_all[m] = run(
            functools.partial(project, parts=parts),
            [((whole, 3 * width), bf16), wide_rows],
            *normed[m],
            weight,
            project_bias,
            project_scale,
        )

    def do_attend(m):
        mixed[m], logs[m], *made = run(
            functools.partial(attend, step=whole),
            [((whole, width), bf16), ((8, whole), f32), *outgoing],
            qkv[m],
            out_weight,
            limit=24,
        )
        shares[m] = share(made)

    def do_send(m):
        shares[m] = send(shares[m])

    def do_norm_two(m):
        resid[m], own = run(
            functools.partial(norm_two, m=m),
            [((rows, model), f32), block],
            tokens,
            *shares[m],
            out_bias,
            gain_two,
            bias_two,
            cover=m == 0,
        )
        normed_two_b[m] = gather(own)

    def do_feed(m):
        activ[m], pre_grad[m], up_bias_grad[m], two_all[m], given_all[m] = run(
            functools.partial(feed, parts=parts),
            [((whole, hidden), bf16), ((whole, hidden), bf16), ((1, hidden), f32), wide_rows, wide_rows],
            *normed_two_b[m],
            *given[m],
            up_weight,
            up_bias,
            down_weight,
        )

    def do_up_back(m):
        shares[m] = share(run(times_back, outgoing, pre_grad[m], up_weight))

    def do_down(m):
        shares_down[m] = share(run(times, outgoing, activ[m], down_weight))

    def do_send_down(m):
        shares_down[m] = send(shares_down[m])

    def do_norm_two_back(m):
        resid_grad[m], own, sums_two[m] = run(
            functools.partial(norm_two_back, m=m, count=count),
            [((rows, model), f32), block, ((8, model), f32)],
            cotangent,
            resid[m],
            *shares[m],
            gain_two,
            smem=(where, cell_of, query_count),
            cover=True,
        )
        top[m] = gather(own)

    def do_attend_back(m, p):
        low, wide = pairs[p]
        (made,) = run(
            functools.partial(attend_back, parts=parts, step=step, low=low, wide=wide),
            [((whole, 3 * wide), bf16)],
            qkv[m],
            logs[m],
            mixed[m],
            out_weight,
            *top[m],
            scratch=[
                pltpu.VMEM((whole, wide), f32),
                pltpu.VMEM((whole, wide), f32),
                pltpu.VMEM((whole, wide), bf16),
                pltpu.VMEM((8 * (wide // HEAD), whole), f32),
            ],
            limit=20,
        )
        pair_grads[m].append(made)

    def do_project_back(m):
        *made, stack_sums[m] = run(
            functools.partial(project_back, pairs=len(pairs)),
            [*outgoing, ((1, 3 * width), f32)],
            *pair_grads[m],
            weight,
        )
        shares[m] = share(made)

    def do_norm_one_back(m):
        grad_rows[m], sums_one[m] = run(
            functools.partial(norm_one_back, m=m),
            [((rows, model), f32), ((8, model), f32)],
            tokens,
            resid_grad[m],
            *shares[m],
            gain_one,
        )

    def wait(*arrays):
        chain.hold(*arrays)
        run(mark, [((8, LANES), f32)], cover=True)

    hops = [("narrow", 1 << k) for k in range(parts.bit_length() - 1)]
    hops += [("wide", 1 << k) for k in range(count.bit_length() - 1)]
    vectors = []

    def do_vectors():
        done = len(vectors)
        shape = [((8, model), f32)]
        if done == 0:
            (own,) = run(vector_sum, shape, *sums_one, *sums_two)
        elif hops[done - 1][0] == "narrow" and hops[done][0] == "wide":
            own, arrived = vectors[-1]
            (own,) = run(
                functools.partial(vector_join, number=len(micros)), shape, own, arrived, *up_bias_grad, *stack_sums
            )
        else:
            (own,) = run(vector_sum, shape, *vectors[-1])
        vectors.append((own, swap(own, *hops[done]) if done < len(hops) else None))

    def do_add_rows(m):
        (out_rows[m],) = run(add_rows, [block], resid[m], *shares_down[m], down_bias)

    def ffn_grad(firsts, seconds, before=()):
        rows, cols = firsts[0].shape[1], seconds[0].shape[1]
        shapes = [((rows // chunks, cols), bf16)] * chunks
        if before:
            shapes.append(((2 * rows // chunks, cols), bf16))
        return run(
            functools.partial(weight_grad, pairs=len(micros), before=len(before[:1])),
            shapes,
            *firsts,
            *seconds,
            *before[:1],
            smem=(where,),
            scratch=[pltpu.VMEM((rows, cols), bf16)],
            limit=16,
        )

    def do_down_grad():
        return ffn_grad(activ, given_all)

    def do_up_grad(down_chunks):
        *made, both = ffn_grad(two_all, pre_grad, down_chunks)
        ffn.start(both, (down_chunks, made))

    def attn_grad():
        made = run(
            functools.partial(projection_grad, micros=len(micros), pairs=len(pairs), parts=parts),
            [((4 * width // chunks, model), bf16)] * chunks,
            *normed_all,
            *[g for m in micros for g in pair_grads[m]],
            *[t for m in micros for t in top[m]],
            *mixed,
            smem=(where,),
            scratch=[pltpu.VMEM((4 * width, model), bf16)],
            limit=20,
        )
        attn.start(made[0], (made,))

    ffn_shapes = [(hidden, model), (model, hidden)]
    attn_shapes = [(3 * width, model), (width, model)]
    ffn = Ring(chain, where, ffn_shapes, True) if rings else Whole(ffn_shapes)
    attn = Ring(chain, where, attn_shapes, False) if rings else Whole(attn_shapes)

    do_norm_one(0)
    (weight,) = run(by_pairs, [((3 * width, model), bf16)], weight_t)
    chain.hold(normed[0][1], normed[0][2])
    do_norm_one(1)
    do_scale(0)
    do_project(0)
    do_attend(0)
    chain.hold(normed[1][1], normed[1][2], given[0][1], given[0][2])
    do_scale(1)
    do_send(0)
    chain.hold(given[1][1])
    do_project(1)
    do_attend(1)
    chain.hold(given[1][2])
    do_norm_two(0)
    do_send(1)
    chain.hold(normed_two_b[0][1])
    do_norm_two(1)
    chain.hold(normed_two_b[1][1])
    do_feed(0)
    do_up_back(0)
    do_down(0)
    wait(normed_two_b[1][2])
    do_send(0)
    do_feed(1)
    do_up_back(1)
    do_norm_two_back(0)
    chain.hold(top[0][1])
    down_chunks = do_down_grad()
    do_up_grad(down_chunks)
    wait(top[0][2])
    do_send(1)
    do_attend_back(0, 0)
    ffn.add()
    do_attend_back(0, 1)
    do_norm_two_back(1)
    ffn.add()
    do_attend_back(0, 2)
    ffn.add()
    chain.hold(top[1][1])
    wait(top[1][2])
    do_attend_back(1, 0)
    do_send_down(0)
    ffn.add()
    do_attend_back(1, 1)
    chain.hold(shares_down[0][2])
    ffn.add()
    do_attend_back(1, 2)
    do_add_rows(0)
    ffn.add()
    attn_grad()
    ffn.add()
    attn.add(cover=True)
    do_project_back(0)
    attn.add(cover=True)
    do_send(0)
    ffn.forward()
    do_project_back(1)
    attn.add(cover=True)
    do_send(1)
    attn.add(cover=True)
    ffn.forward()
    do_norm_one_back(0)
    do_down(1)
    attn.add(cover=True)
    do_send_down(1)
    attn.add(cover=True)
    ffn.forward()
    do_norm_one_back(1)
    attn.add(cover=True)
    do_vectors()
    chain.hold(shares_down[1][2])
    ffn.forward()
    ffn.store(range(0, 3))
    attn.forward()
    do_vectors()
    do_add_rows(1)
    attn.forward()
    do_vectors()
    ffn.forward()
    attn.store(range(0, 2))
    attn.forward()
    do_vectors()
    ffn.store(range(3, 5))
    attn.forward()
    do_vectors()
    ffn.forward()
    attn.store(range(2, 4))
    attn.forward()
    do_vectors()
    ffn.store(range(5, 7))
    ffn.forward()
    attn.forward()
    attn.store(range(4, 7))
    ffn.store(range(7, 8))
    attn.forward()
    attn.store(range(7, 8))

    while len(vectors) <= len(hops):
        do_vectors()
    vector_sums = vectors[-1][0]
    up_bias_sum = vector_sums[6, :hidden]
    stack_sum = vector_sums[7, : 3 * width]

    def plain(j):
        return jnp.concatenate([stack_sum[3 * low + j * wide : 3 * low + (j + 1) * wide] for low, wide in pairs])

    return (
        jnp.stack(out_rows)[:, None],
        jnp.stack(grad_rows)[:, None],
        vector_sums[4],
        vector_sums[5],
        jnp.transpose(attn.outs[0].reshape(3, width, model), (2, 0, 1)),
        plain(0),
        plain(2),
        attn.outs[1],
        vector_sums[0],
        vector_sums[1],
        vector_sums[2],
        ffn.outs[1],
        up_bias_sum,
        ffn.outs[0],
        vector_sums[3],
    )


def solution(mesh):
    in_specs = (
        P(None, "wide", "narrow", None),
        P(None, "wide", "narrow", None),
        P(),
        P(),
        P(),
        P(),
        P(None, None, "narrow"),
        P("narrow"),
        P("narrow"),
        P("narrow", None),
        P(),
        P(),
        P(),
        P(None, "narrow"),
        P("narrow"),
        P("narrow", None),
        P(),
    )
    out_specs = (
        P(None, "wide", "narrow", None),
        P(None, "wide", "narrow", None),
        P(),
        P(),
        P(None, None, "narrow"),
        P("narrow"),
        P("narrow"),
        P("narrow", None),
        P(),
        P(),
        P(),
        P(None, "narrow"),
        P("narrow"),
        P("narrow", None),
        P(),
    )
    return jax.shard_map(local, mesh=mesh, in_specs=in_specs, out_specs=out_specs, check_vma=False)
```

```python
import functools

import jax
import jax.numpy as jnp
from jax import lax
from jax.experimental import pallas as pl
from jax.experimental.pallas import tpu as pltpu
from jax.sharding import PartitionSpec as P

HEAD = 64
LANES = 128
TILE = 256
norm_eps = 1e-05
score_scale = 0.125
bf16 = jnp.bfloat16
f32 = jnp.float32


class Chain:
    def __init__(self):
        self.last = []
        self.held = []

    def hold(self, *arrays):
        self.held += arrays

    def run(self, body, outs, *ins, smem=(), scratch=(), alias=None, anywhere=(), out_anywhere=(), limit=12, token=0, cover=False):
        unread = [*self.last, *self.held]
        count = len(smem) + len(ins)
        specs = [pl.BlockSpec(memory_space=pltpu.SMEM)] * len(smem)
        specs += [pl.BlockSpec(memory_space=pl.ANY if i in anywhere else pltpu.VMEM) for i in range(len(ins))]
        specs += [pl.BlockSpec(memory_space=pl.ANY)] * len(unread)

        def inner(*refs):
            body(*refs[:count], *refs[count + len(unread) :])

        made = pl.pallas_call(
            inner,
            out_shape=tuple(jax.ShapeDtypeStruct(*o) for o in outs),
            in_specs=specs,
            out_specs=tuple(
                pl.BlockSpec(memory_space=pl.ANY if i in out_anywhere else pltpu.VMEM) for i in range(len(outs))
            ),
            scratch_shapes=scratch,
            input_output_aliases={} if alias is None else {len(smem) + k: v for k, v in alias.items()},
            compiler_params=pltpu.CompilerParams(vmem_limit_bytes=limit << 20),
            cost_estimate=pl.CostEstimate(flops=10**12 if cover else 1, bytes_accessed=1, transcendentals=0),
            name=body.func.__name__ if isinstance(body, functools.partial) else body.__name__,
        )(*smem, *ins, *unread)
        self.last, self.held = [made[token]], []
        return made


def dot32(first, second, first_dim, second_dim):
    return lax.dot_general(
        first, second, (((first_dim,), (second_dim,)), ((), ())), preferred_element_type=f32
    )


def statistics(values):
    average = jnp.mean(values, axis=-1, keepdims=True)
    centred = values - average
    inverse = lax.rsqrt(jnp.mean(centred * centred, axis=-1, keepdims=True) + norm_eps)
    return centred * inverse, inverse


def norm_back(grad, normed, inverse, gain):
    scaled = grad * gain
    mean_one = jnp.mean(scaled, axis=-1, keepdims=True)
    mean_two = jnp.mean(scaled * normed, axis=-1, keepdims=True)
    return inverse * (scaled - mean_one - normed * mean_two)


def of_head(values, j, axis=1):
    if values.shape[axis] <= HEAD:
        return values
    place = lax.broadcasted_iota(jnp.int32, values.shape, axis)
    return jnp.where((place >= HEAD * j) & (place < HEAD * (j + 1)), values, jnp.zeros_like(values))


def head_pairs(width):
    return [(low, min(LANES, width - low)) for low in range(0, width, LANES)]


def relay(*refs):
    number = len(refs) // 2
    for arrived, out in zip(refs[:number], refs[number:]):
        out[...] = arrived[...]


def by_pairs(weight_t, out):
    width = out.shape[0] // 3
    for low, wide in head_pairs(width):
        for j in range(3):
            out[3 * low + j * wide : 3 * low + (j + 1) * wide, :] = weight_t[
                j * width + low : j * width + low + wide, :
            ]


def norm_one(tok, gain, bias, out, *, m):
    normed, _ = statistics(tok[m, 0].astype(f32))
    out[...] = (normed * gain[...].astype(f32) + bias[...].astype(f32)).astype(bf16)


def loss_grad(where, cells, queries, cot, m, count):
    number = queries[cells[where[0] + m * count]]
    scale = jnp.sqrt(jnp.full((1, cot.shape[3]), number, jnp.int32).astype(f32) / 500.0)
    return cot[m, 0].astype(f32) * scale


def scale_cot(where, cells, queries, cot, out, *, m, count):
    out[...] = loss_grad(where, cells, queries, cot, m, count).astype(bf16)


def project(*refs, parts):
    blocks = refs[:parts]
    weight, bias, scale = refs[parts : parts + 3]
    out, whole = refs[parts + 3 :]
    rows = blocks[0].shape[0]
    for b in range(parts):
        values = blocks[b][...]
        at = slice(b * rows, (b + 1) * rows)
        whole[at, :] = values
        out[at, :] = ((dot32(values, weight[...], 1, 1) + bias[...]) * scale[...]).astype(bf16)


def attend(qkv, out_weight, attended, logs, *outs, step):
    whole = qkv.shape[0]
    head = 0
    for low, wide in head_pairs(out_weight.shape[0]):
        heads = wide // HEAD
        key_pair = qkv[:, 3 * low + wide : 3 * low + 2 * wide]
        value_t = qkv[:, 3 * low + 2 * wide : 3 * low + 3 * wide].T
        keys = [of_head(key_pair, j) for j in range(heads)]
        values = [of_head(value_t, j, 0) for j in range(heads)]
        for start in range(0, whole, step):
            at = slice(start, start + step)
            query = qkv[at, 3 * low : 3 * low + wide]
            total = None
            for j in range(heads):
                scores = dot32(keys[j], query, 1, 1)
                top = jnp.max(scores, axis=0, keepdims=True)
                powers = jnp.exp(scores - top)
                length = jnp.sum(powers, axis=0, keepdims=True)
                mixed = dot32(values[j], powers.astype(bf16), 1, 0) * (1.0 / length)
                total = mixed if total is None else total + mixed
                logs[head + j : head + j + 1, at] = top + jnp.log(length)
            attended[at, low : low + wide] = total.T.astype(bf16)
        head += heads
    rows = whole // len(outs)
    for b, out in enumerate(outs):
        out[...] = dot32(attended[b * rows : (b + 1) * rows, :], out_weight[...], 1, 0).astype(bf16)


def pair_sum(first, second, out):
    out[...] = (first[...].astype(f32) + second[...].astype(f32)).astype(bf16)


def three(first, second, third):
    return first[...].astype(f32) + second[...].astype(f32) + third[...].astype(f32)


def norm_two(tok, first, second, third, out_bias, gain, bias, resid, normed, *, m):
    value = tok[m, 0].astype(f32) + three(first, second, third) + out_bias[...].astype(f32)
    resid[...] = value
    hat, _ = statistics(value)
    normed[...] = (hat * gain[...].astype(f32) + bias[...].astype(f32)).astype(bf16)


def feed(*refs, parts):
    normed, grads = refs[:parts], refs[parts : 2 * parts]
    up, up_bias, down = refs[2 * parts : 2 * parts + 3]
    activ, pre_grad, bias_grad, normed_all, grads_all = refs[2 * parts + 3 :]
    rows = normed[0].shape[0]
    for b in range(parts):
        normed_all[b * rows : (b + 1) * rows, :] = normed[b][...]
        grads_all[b * rows : (b + 1) * rows, :] = grads[b][...]
    for low in range(0, up.shape[1], TILE):
        cols = slice(low, low + TILE)
        total = None
        for b in range(parts):
            at = slice(b * rows, (b + 1) * rows)
            pre = dot32(normed[b][...], up[:, cols], 1, 0) + up_bias[:, cols].astype(f32)
            cumul = 0.5 + 0.5 * lax.erf(pre * 0.7071067811865476)
            density = jnp.exp(-0.5 * pre * pre) * 0.3989422804014327
            activ[at, cols] = (pre * cumul).astype(bf16)
            back = dot32(grads[b][...], down[cols, :], 1, 1)
            grad = (back * (cumul + pre * density)).astype(bf16)
            pre_grad[at, cols] = grad
            part = jnp.sum(grad.astype(f32), axis=0, keepdims=True)
            total = part if total is None else total + part
        bias_grad[:, cols] = total


def times(value, weight, *outs):
    put_tiles(outs, lambda at, cols: dot32(value[at, :], weight[:, cols], 1, 0), value.shape[0])


def times_back(value, weight, *outs):
    put_tiles(outs, lambda at, cols: dot32(value[at, :], weight[cols, :], 1, 1), value.shape[0])


def put_tiles(outs, share_of, whole):
    rows, model = outs[0].shape

    def tile(i, carry):
        cols = pl.ds(pl.multiple_of(i * TILE, TILE), TILE)
        for b, out in enumerate(outs):
            out[:, cols] = share_of(slice(b * rows, (b + 1) * rows), cols).astype(bf16)
        return carry

    lax.fori_loop(0, model // TILE, tile, 0)


def weight_grad(where, *refs, pairs, before):
    firsts, seconds, refs = refs[:pairs], refs[pairs : 2 * pairs], refs[2 * pairs :]
    chunks, whole = refs[before:-1], refs[-1]

    def tile(i, carry):
        rows = pl.ds(pl.multiple_of(i * TILE, TILE), TILE)
        total = None
        for first, second in zip(firsts, seconds):
            part = dot32(first[:, rows], second[...], 0, 0)
            total = part if total is None else total + part
        whole[rows, :] = total.astype(bf16)
        return carry

    lax.fori_loop(0, whole.shape[0] // TILE, tile, 0)
    if before:
        chunks, both = chunks[:-1], chunks[-1]
        size = chunks[0].shape[0]
        both[:size, :] = refs[0][...]
        put_chunks(where, chunks, whole)
        both[size:, :] = chunks[0][...]
    else:
        put_chunks(where, chunks, whole)


def ring_chunk(where, count, step):
    half = where[0] // 2
    place = jnp.where(where[0] % 2 == 0, half, count - 1 - half)
    return lax.rem(place + jnp.where(where[1] % 2 == 0, count - step, step), count)


def put_chunks(where, chunks, whole):
    for s, chunk in enumerate(chunks):
        size = chunk.shape[0]
        which = ring_chunk(where, len(chunks), (s + 1) % len(chunks)) if len(chunks) > 1 else 0
        chunk[...] = whole[pl.ds(pl.multiple_of(which * size, size), size), :]


def norm_two_back(where, cells, queries, cot, resid, first, second, third, gain, out, rounded, sums, *, m, count):
    top = loss_grad(where, cells, queries, cot, m, count)
    grad = three(first, second, third)
    hat, inverse = statistics(resid[...])
    back = top + norm_back(grad, hat, inverse, gain[...].astype(f32))
    out[...] = back
    rounded[...] = back.astype(bf16)
    sums[0:1, :] = jnp.sum(back, axis=0, keepdims=True)
    sums[1:2, :] = jnp.sum(grad * hat, axis=0, keepdims=True)
    sums[2:3, :] = jnp.sum(grad, axis=0, keepdims=True)
    sums[3:4, :] = jnp.sum(top, axis=0, keepdims=True)
    sums[4:8, :] = jnp.zeros_like(sums[4:8, :])


def attend_back(qkv, logs, mixed, out_weight, *refs, parts, step, low, wide):
    grads = refs[:parts]
    out, key_grad, value_grad, given, inner = refs[parts:]
    whole = qkv.shape[0]
    rows = whole // parts
    heads = wide // HEAD
    head = low // HEAD
    ones = jnp.concatenate([of_head(jnp.ones((8, wide), bf16), j) for j in range(heads)], axis=0)
    for b in range(parts):
        at = slice(b * rows, (b + 1) * rows)
        value = dot32(grads[b][...], out_weight[low : low + wide, :], 1, 1).astype(bf16)
        given[at, :] = value
        both = value.astype(f32) * mixed[at, low : low + wide].astype(f32)
        high = both.astype(bf16)
        rest = (both - high.astype(f32)).astype(bf16)
        inner[:, at] = dot32(ones, high, 1, 1) + dot32(ones, rest, 1, 1)
    key_pair = qkv[:, 3 * low + wide : 3 * low + 2 * wide]
    value_pair = qkv[:, 3 * low + 2 * wide : 3 * low + 3 * wide]
    key_t = key_pair.T
    keys = [of_head(key_pair, j) for j in range(heads)]
    values = [of_head(value_pair, j) for j in range(heads)]
    keys_t = [of_head(key_t, j, 0) for j in range(heads)]
    key_grad[...] = jnp.zeros_like(key_grad)
    value_grad[...] = jnp.zeros_like(value_grad)

    def block(i, carry):
        start = pl.multiple_of(i * step, step)
        query = qkv[pl.ds(start, step), 3 * low : 3 * low + wide]
        grad = given[pl.ds(start, step), :]
        total = None
        for j in range(heads):
            scores = dot32(keys[j], query, 1, 1)
            weights = jnp.exp(scores - logs[head + j : head + j + 1, pl.ds(start, step)])
            back = dot32(values[j], grad, 1, 1)
            score_grad = (weights * (back - inner[8 * j : 8 * j + 1, pl.ds(start, step)])).astype(bf16)
            value_grad[...] += dot32(weights.astype(bf16), of_head(grad, j), 1, 0)
            key_grad[...] += dot32(score_grad, of_head(query, j), 1, 0)
            part = dot32(keys_t[j], score_grad, 1, 0)
            total = part if total is None else total + part
        out[pl.ds(start, step), :wide] = (total.T * score_scale).astype(bf16)
        return carry

    lax.fori_loop(0, whole // step, block, 0)
    out[:, wide : 2 * wide] = key_grad[...].astype(bf16)
    out[:, 2 * wide :] = value_grad[...].astype(bf16)


def project_back(*refs, pairs):
    grads, weight, outs, sums = refs[:pairs], refs[pairs], refs[pairs + 1 : -1], refs[-1]

    def share_of(at, cols):
        total, low = None, 0
        for grad in grads:
            wide = grad.shape[1]
            part = dot32(grad[at, :], weight[low : low + wide, cols], 1, 0)
            total = part if total is None else total + part
            low += wide
        return total

    put_tiles(outs, share_of, grads[0].shape[0])
    low = 0
    for grad in grads:
        wide = grad.shape[1]
        sums[:, low : low + wide] = jnp.sum(grad[...].astype(f32), axis=0, keepdims=True)
        low += wide


def projection_grad(where, *refs, micros, pairs, parts):
    normed, refs = refs[:micros], refs[micros:]
    grads, refs = [refs[m * pairs : (m + 1) * pairs] for m in range(micros)], refs[micros * pairs :]
    tops, refs = [refs[m * parts : (m + 1) * parts] for m in range(micros)], refs[micros * parts :]
    mixed, refs = refs[:micros], refs[micros:]
    chunks, out = refs[:-1], refs[-1]
    width = mixed[0].shape[1]
    rows = tops[0][0].shape[0]
    for p, (low, wide) in enumerate(head_pairs(width)):
        total = None
        for m in range(micros):
            part = dot32(grads[m][p][...], normed[m][...], 0, 0)
            total = part if total is None else total + part
        for j in range(3):
            out[j * width + low : j * width + low + wide, :] = total[j * wide : (j + 1) * wide].astype(bf16)
        total = None
        for m in range(micros):
            for b in range(parts):
                part = dot32(mixed[m][b * rows : (b + 1) * rows, low : low + wide], tops[m][b][...], 0, 0)
                total = part if total is None else total + part
        out[3 * width + low : 3 * width + low + wide, :] = total.astype(bf16)
    put_chunks(where, chunks, out)


def ring_add(arrived, *refs):
    low = 0
    for part in refs[:-1]:
        at = slice(low, low + part.shape[0])
        refs[-1][at, :] = (arrived[at, :].astype(f32) + part[...].astype(f32)).astype(bf16)
        low += part.shape[0]


def ring_store(where, *refs, steps, count, stacked):
    moved, refs = refs[: len(steps)], refs[len(steps) :]
    done, first, second, buffer, sems = refs[-5:]
    done[...] = jnp.zeros_like(done)
    size = buffer.shape[1] // 2 if stacked else buffer.shape[1]
    copies = []
    for k, step in enumerate(steps):
        buffer[k] = moved[k][...].astype(f32)
        row = pl.multiple_of(ring_chunk(where, count, step) * size, size)
        if stacked:
            for i, target in enumerate((first, second)):
                source = buffer.at[k, pl.ds(i * size, size), :]
                copies.append(pltpu.make_async_copy(source, target.at[pl.ds(row, size), :], sems.at[2 * k + i]))
                copies[-1].start()
        else:
            last = first.shape[0] - size
            to_first = pl.multiple_of(jnp.minimum(row, last), 16)
            to_second = pl.multiple_of(jnp.maximum(row - first.shape[0], 0), 16)
            copy_first = pltpu.make_async_copy(buffer.at[k], first.at[pl.ds(to_first, size), :], sems.at[2 * k])
            copy_second = pltpu.make_async_copy(buffer.at[k], second.at[pl.ds(to_second, size), :], sems.at[2 * k])
            pl.when(row <= last)(copy_first.start)
            pl.when(row > last)(copy_second.start)
            copies.append(copy_first)
    for copy in copies:
        copy.wait()


def norm_one_back(tok, resid_grad, first, second, third, gain, out, sums, *, m):
    grad = three(first, second, third)
    hat, inverse = statistics(tok[m, 0].astype(f32))
    out[...] = resid_grad[...] + norm_back(grad, hat, inverse, gain[...].astype(f32))
    sums[0:4, :] = jnp.zeros_like(sums[0:4, :])
    sums[4:5, :] = jnp.sum(grad * hat, axis=0, keepdims=True)
    sums[5:6, :] = jnp.sum(grad, axis=0, keepdims=True)
    sums[6:8, :] = jnp.zeros_like(sums[6:8, :])


def vector_sum(*refs):
    total = refs[0][...]
    for ref in refs[1:-1]:
        total = total + ref[...]
    refs[-1][...] = total


def vector_join(first, second, *refs, number):
    up_bias, stack, out = refs[:number], refs[number:-1], refs[-1]
    out[...] = first[...] + second[...]
    for row, parts in ((6, up_bias), (7, stack)):
        total = parts[0][...]
        for part in parts[1:]:
            total = total + part[...]
        out[row : row + 1, : total.shape[1]] = total


def add_rows(resid, first, second, third, bias, out):
    out[...] = (resid[...] + three(first, second, third) + bias[...].astype(f32)).astype(bf16)


def swap(values, axis, bit):
    return lax.ppermute(values, axis, [(i, i ^ bit) for i in range(lax.axis_size(axis))])


def ring_order(count):
    return list(range(0, count, 2)) + list(range(1, count, 2))[::-1]


class Ring:
    def __init__(self, chain, where, shapes, stacked):
        self.chain, self.where, self.shapes, self.stacked = chain, where, shapes, stacked
        self.count = lax.axis_size("wide")
        cores = lax.axis_size("narrow")
        order = ring_order(self.count)
        self.perm = [
            (order[i] * cores + n, order[(i + (1 if n % 2 == 0 else -1)) % self.count] * cores + n)
            for i in range(self.count)
            for n in range(cores)
        ]
        self.have, self.step, self.outs = [], 1, None

    def pass_on(self, chunk):
        self.moving = lax.ppermute(chunk, ("wide", "narrow"), self.perm)

    def start(self, chunk, parts):
        self.parts = parts
        self.pass_on(chunk)

    def hold(self):
        self.chain.hold(self.moving)

    def add(self, cover=False):
        (made,) = self.chain.run(
            ring_add,
            [(self.moving.shape, bf16)],
            self.moving,
            *[p[self.step] for p in self.parts],
            cover=cover,
        )
        self.step += 1
        if self.step == self.count:
            self.have.append(made)
        self.pass_on(made)

    def forward(self):
        self.have.append(self.moving)
        self.hold()
        if len(self.have) < self.count:
            self.pass_on(self.moving)

    def store(self, steps):
        moved = [self.have[s] for s in steps]
        kept = () if self.outs is None else self.outs
        number = len(moved)
        made = self.chain.run(
            functools.partial(ring_store, steps=tuple(steps), count=self.count, stacked=self.stacked),
            [((8, LANES), f32)] + [(s, f32) for s in self.shapes],
            *moved,
            *kept,
            smem=(self.where,),
            scratch=[pltpu.VMEM((number, *moved[0].shape), f32), pltpu.SemaphoreType.DMA((2 * number,))],
            alias={number: 1, number + 1: 2} if kept else None,
            anywhere=(number, number + 1) if kept else (),
            out_anywhere=(1, 2),
            limit=6 + (number * moved[0].size * 4 >> 20),
        )
        self.outs = made[1:]


class Whole:
    def __init__(self, shapes):
        self.shapes = shapes

    def start(self, chunk, parts):
        total = lax.psum(chunk, "wide").astype(f32)
        self.outs = (total[: self.shapes[0][0]], total[self.shapes[0][0] :])

    def hold(self):
        pass

    def add(self, cover=False):
        pass

    def forward(self):
        pass

    def store(self, steps):
        pass


def local(
    tokens,
    cotangent,
    cell_of,
    query_count,
    attn_norm_gain,
    attn_norm_bias,
    input_weight,
    query_bias,
    value_bias,
    out_weight,
    out_bias,
    ffn_norm_gain,
    ffn_norm_bias,
    up_weight,
    up_bias,
    down_weight,
    down_bias,
):
    micros = range(tokens.shape[0])
    rows, model = tokens.shape[2], tokens.shape[3]
    parts = lax.axis_size("narrow")
    whole = rows * parts
    width = input_weight.shape[2]
    hidden = up_weight.shape[1]
    count = lax.axis_size("wide")
    rings = count <= 8
    chunks = count if rings else 1
    pairs = head_pairs(width)
    step = min(512, whole)
    chain = Chain()
    run = chain.run
    where = jnp.stack([lax.axis_index("wide"), lax.axis_index("narrow")]).astype(jnp.int32)

    block = ((rows, model), bf16)
    outgoing = [block] * parts
    wide_rows = ((whole, model), bf16)
    row = lambda v: v.reshape(1, -1)
    gain_one, bias_one, gain_two, bias_two = map(row, (attn_norm_gain, attn_norm_bias, ffn_norm_gain, ffn_norm_bias))
    out_bias, down_bias, up_bias = row(out_bias), row(down_bias), row(up_bias)

    def columns(three_parts):
        return jnp.concatenate([v[:, low : low + wide] for low, wide in pairs for v in three_parts], axis=1)

    weight_t = jnp.transpose(input_weight, (1, 2, 0)).reshape(3 * width, model)
    zero = jnp.zeros((1, width), f32)
    project_bias = columns([row(query_bias).astype(f32), zero, row(value_bias).astype(f32)])
    project_scale = columns([zero + score_scale, zero + 1.0, zero + 1.0])

    def gather(own):
        return [own, swap(own, "narrow", 1), swap(own, "narrow", 2)]

    def finish(*rows, cover=False):
        made = run(relay, [block] * len(rows), *[r[2] for r in rows], cover=cover)
        for r, copy in zip(rows, made):
            r[2] = copy
            r.append(swap(copy, "narrow", 1))

    def share(made):
        own, near, partner, far = made
        return [own, partner, swap(far, "narrow", 1), swap(near, "narrow", 1)]

    def send(shares):
        own, partner, far, near = shares
        (both,) = run(pair_sum, [block], partner, far)
        return [own, near, swap(both, "narrow", 2)]

    def fresh():
        return [None] * len(micros)

    normed, given, qkv, normed_all, mixed, logs, shares, shares_down, resid, normed_two_b = (fresh() for _ in range(10))
    activ, pre_grad, up_bias_grad, two_all, given_all, resid_grad, top = (fresh() for _ in range(7))
    sums_two, sums_one, stack_sums, out_rows, grad_rows = (fresh() for _ in range(5))
    pair_grads = [[] for _ in micros]

    def do_norm_one(m):
        (own,) = run(functools.partial(norm_one, m=m), [block], tokens, gain_one, bias_one)
        normed[m] = gather(own)

    def do_scale(m):
        (own,) = run(functools.partial(scale_cot, m=m, count=count), [block], cotangent, smem=(where, cell_of, query_count), cover=True)
        given[m] = gather(own)

    def do_project(m):
        qkv[m], normed_all[m] = run(
            functools.partial(project, parts=parts),
            [((whole, 3 * width), bf16), wide_rows],
            *normed[m],
            weight,
            project_bias,
            project_scale,
        )

    def do_attend(m):
        mixed[m], logs[m], *made = run(
            functools.partial(attend, step=whole),
            [((whole, width), bf16), ((8, whole), f32), *outgoing],
            qkv[m],
            out_weight,
            limit=24,
        )
        shares[m] = share(made)

    def do_send(m):
        shares[m] = send(shares[m])

    def do_norm_two(m):
        resid[m], own = run(
            functools.partial(norm_two, m=m),
            [((rows, model), f32), block],
            tokens,
            *shares[m],
            out_bias,
            gain_two,
            bias_two,
            cover=m == 0,
        )
        normed_two_b[m] = gather(own)

    def do_feed(m):
        activ[m], pre_grad[m], up_bias_grad[m], two_all[m], given_all[m] = run(
            functools.partial(feed, parts=parts),
            [((whole, hidden), bf16), ((whole, hidden), bf16), ((1, hidden), f32), wide_rows, wide_rows],
            *normed_two_b[m],
            *given[m],
            up_weight,
            up_bias,
            down_weight,
        )

    def do_up_back(m):
        shares[m] = share(run(times_back, outgoing, pre_grad[m], up_weight))

    def do_down(m):
        shares_down[m] = share(run(times, outgoing, activ[m], down_weight))

    def do_send_down(m):
        shares_down[m] = send(shares_down[m])

    def do_norm_two_back(m):
        resid_grad[m], own, sums_two[m] = run(
            functools.partial(norm_two_back, m=m, count=count),
            [((rows, model), f32), block, ((8, model), f32)],
            cotangent,
            resid[m],
            *shares[m],
            gain_two,
            smem=(where, cell_of, query_count),
            cover=True,
        )
        top[m] = gather(own)

    def do_attend_back(m, p):
        low, wide = pairs[p]
        (made,) = run(
            functools.partial(attend_back, parts=parts, step=step, low=low, wide=wide),
            [((whole, 3 * wide), bf16)],
            qkv[m],
            logs[m],
            mixed[m],
            out_weight,
            *top[m],
            scratch=[
                pltpu.VMEM((whole, wide), f32),
                pltpu.VMEM((whole, wide), f32),
                pltpu.VMEM((whole, wide), bf16),
                pltpu.VMEM((8 * (wide // HEAD), whole), f32),
            ],
            limit=20,
        )
        pair_grads[m].append(made)

    def do_project_back(m):
        *made, stack_sums[m] = run(
            functools.partial(project_back, pairs=len(pairs)),
            [*outgoing, ((1, 3 * width), f32)],
            *pair_grads[m],
            weight,
        )
        shares[m] = share(made)

    def do_norm_one_back(m):
        grad_rows[m], sums_one[m] = run(
            functools.partial(norm_one_back, m=m),
            [((rows, model), f32), ((8, model), f32)],
            tokens,
            resid_grad[m],
            *shares[m],
            gain_one,
        )

    hops = [("narrow", 1 << k) for k in range(parts.bit_length() - 1)]
    hops += [("wide", 1 << k) for k in range(count.bit_length() - 1)]
    vectors = []

    def do_vectors():
        done = len(vectors)
        shape = [((8, model), f32)]
        if done == 0:
            (own,) = run(vector_sum, shape, *sums_one, *sums_two)
        elif hops[done - 1][0] == "narrow" and hops[done][0] == "wide":
            own, arrived = vectors[-1]
            (own,) = run(
                functools.partial(vector_join, number=len(micros)), shape, own, arrived, *up_bias_grad, *stack_sums
            )
        else:
            (own,) = run(vector_sum, shape, *vectors[-1])
        vectors.append((own, swap(own, *hops[done]) if done < len(hops) else None))

    def do_add_rows(m):
        (out_rows[m],) = run(add_rows, [block], resid[m], *shares_down[m], down_bias)

    def ffn_grad(firsts, seconds, before=()):
        rows, cols = firsts[0].shape[1], seconds[0].shape[1]
        shapes = [((rows // chunks, cols), bf16)] * chunks
        if before:
            shapes.append(((2 * rows // chunks, cols), bf16))
        return run(
            functools.partial(weight_grad, pairs=len(micros), before=len(before[:1])),
            shapes,
            *firsts,
            *seconds,
            *before[:1],
            smem=(where,),
            scratch=[pltpu.VMEM((rows, cols), bf16)],
            limit=16,
        )

    def do_down_grad():
        return ffn_grad(activ, given_all)

    def do_up_grad(down_chunks):
        *made, both = ffn_grad(two_all, pre_grad, down_chunks)
        ffn.start(both, (down_chunks, made))

    def attn_grad():
        made = run(
            functools.partial(projection_grad, micros=len(micros), pairs=len(pairs), parts=parts),
            [((4 * width // chunks, model), bf16)] * chunks,
            *normed_all,
            *[g for m in micros for g in pair_grads[m]],
            *[t for m in micros for t in top[m]],
            *mixed,
            smem=(where,),
            scratch=[pltpu.VMEM((4 * width, model), bf16)],
            limit=20,
        )
        attn.start(made[0], (made,))

    ffn_shapes = [(hidden, model), (model, hidden)]
    attn_shapes = [(3 * width, model), (width, model)]
    ffn = Ring(chain, where, ffn_shapes, True) if rings else Whole(ffn_shapes)
    attn = Ring(chain, where, attn_shapes, False) if rings else Whole(attn_shapes)

    do_norm_one(0)
    (weight,) = run(by_pairs, [((3 * width, model), bf16)], weight_t)
    chain.hold(normed[0][1])
    finish(normed[0])
    do_norm_one(1)
    do_scale(0)
    do_project(0)
    do_attend(0)
    chain.hold(normed[1][1], given[0][1])
    finish(normed[1], given[0], cover=True)
    do_scale(1)
    do_send(0)
    chain.hold(given[1][1])
    do_project(1)
    do_attend(1)
    chain.hold(given[1][2])
    do_norm_two(0)
    do_send(1)
    finish(given[1])
    chain.hold(normed_two_b[0][1])
    finish(normed_two_b[0])
    do_norm_two(1)
    chain.hold(normed_two_b[1][1])
    do_feed(0)
    do_up_back(0)
    do_down(0)
    finish(normed_two_b[1], cover=True)
    do_send(0)
    do_feed(1)
    do_up_back(1)
    do_norm_two_back(0)
    chain.hold(top[0][1])
    down_chunks = do_down_grad()
    do_up_grad(down_chunks)
    finish(top[0], cover=True)
    do_send(1)
    do_attend_back(0, 0)
    ffn.add()
    do_attend_back(0, 1)
    do_norm_two_back(1)
    ffn.add()
    do_attend_back(0, 2)
    ffn.add()
    chain.hold(top[1][1])
    finish(top[1], cover=True)
    do_attend_back(1, 0)
    do_send_down(0)
    ffn.add()
    do_attend_back(1, 1)
    ffn.add()
    do_attend_back(1, 2)
    ffn.add()
    attn_grad()
    ffn.add()
    attn.add()
    do_project_back(0)
    attn.add()
    do_project_back(1)
    ffn.forward()
    attn.add()
    do_send(0)
    attn.add()
    do_send(1)
    ffn.forward()
    attn.add()
    do_norm_one_back(0)
    attn.add()
    do_norm_one_back(1)
    do_vectors()
    ffn.forward()
    attn.add()
    do_down(1)
    do_vectors()
    attn.forward()
    ffn.store(range(0, 2))
    do_vectors()
    ffn.forward()
    attn.forward()
    do_send_down(1)
    do_vectors()
    attn.forward()
    ffn.store(range(2, 4))
    do_vectors()
    ffn.forward()
    attn.forward()
    attn.store(range(0, 3))
    do_vectors()
    attn.forward()
    do_add_rows(0)
    ffn.forward()
    attn.forward()
    do_add_rows(1)
    ffn.store(range(4, 6))
    ffn.forward()
    attn.store(range(3, 7))
    attn.forward()
    ffn.store(range(6, 8))
    attn.store(range(7, 8))

    while len(vectors) <= len(hops):
        do_vectors()
    vector_sums = vectors[-1][0]
    up_bias_sum = vector_sums[6, :hidden]
    stack_sum = vector_sums[7, : 3 * width]

    def plain(j):
        return jnp.concatenate([stack_sum[3 * low + j * wide : 3 * low + (j + 1) * wide] for low, wide in pairs])

    return (
        jnp.stack(out_rows)[:, None],
        jnp.stack(grad_rows)[:, None],
        vector_sums[4],
        vector_sums[5],
        jnp.transpose(attn.outs[0].reshape(3, width, model), (2, 0, 1)),
        plain(0),
        plain(2),
        attn.outs[1],
        vector_sums[0],
        vector_sums[1],
        vector_sums[2],
        ffn.outs[1],
        up_bias_sum,
        ffn.outs[0],
        vector_sums[3],
    )


def solution(mesh):
    in_specs = (
        P(None, "wide", "narrow", None),
        P(None, "wide", "narrow", None),
        P(),
        P(),
        P(),
        P(),
        P(None, None, "narrow"),
        P("narrow"),
        P("narrow"),
        P("narrow", None),
        P(),
        P(),
        P(),
        P(None, "narrow"),
        P("narrow"),
        P("narrow", None),
        P(),
    )
    out_specs = (
        P(None, "wide", "narrow", None),
        P(None, "wide", "narrow", None),
        P(),
        P(),
        P(None, None, "narrow"),
        P("narrow"),
        P("narrow"),
        P("narrow", None),
        P(),
        P(),
        P(),
        P(None, "narrow"),
        P("narrow"),
        P("narrow", None),
        P(),
    )
    return jax.shard_map(local, mesh=mesh, in_specs=in_specs, out_specs=out_specs, check_vma=False)
```

```python
import functools

import jax
import jax.numpy as jnp
from jax import lax
from jax.experimental import pallas as pl
from jax.experimental.pallas import tpu as pltpu
from jax.sharding import PartitionSpec as P

HEAD = 64
LANES = 128
TILE = 256
norm_eps = 1e-05
score_scale = 0.125
bf16 = jnp.bfloat16
f32 = jnp.float32


class Chain:
    def __init__(self):
        self.last = []
        self.held = []

    def hold(self, *arrays):
        self.held += arrays

    def run(self, body, outs, *ins, smem=(), scratch=(), alias=None, anywhere=(), out_anywhere=(), limit=12, token=0, cover=False):
        unread = [*self.last, *self.held]
        count = len(smem) + len(ins)
        specs = [pl.BlockSpec(memory_space=pltpu.SMEM)] * len(smem)
        specs += [pl.BlockSpec(memory_space=pl.ANY if i in anywhere else pltpu.VMEM) for i in range(len(ins))]
        specs += [pl.BlockSpec(memory_space=pl.ANY)] * len(unread)

        def inner(*refs):
            body(*refs[:count], *refs[count + len(unread) :])

        made = pl.pallas_call(
            inner,
            out_shape=tuple(jax.ShapeDtypeStruct(*o) for o in outs),
            in_specs=specs,
            out_specs=tuple(
                pl.BlockSpec(memory_space=pl.ANY if i in out_anywhere else pltpu.VMEM) for i in range(len(outs))
            ),
            scratch_shapes=scratch,
            input_output_aliases={} if alias is None else {len(smem) + k: v for k, v in alias.items()},
            compiler_params=pltpu.CompilerParams(vmem_limit_bytes=limit << 20),
            cost_estimate=pl.CostEstimate(flops=10**12 if cover else 1, bytes_accessed=1, transcendentals=0),
            name=body.func.__name__ if isinstance(body, functools.partial) else body.__name__,
        )(*smem, *ins, *unread)
        self.last, self.held = [made[token]], []
        return made


def dot32(first, second, first_dim, second_dim):
    return lax.dot_general(
        first, second, (((first_dim,), (second_dim,)), ((), ())), preferred_element_type=f32
    )


def statistics(values):
    average = jnp.mean(values, axis=-1, keepdims=True)
    centred = values - average
    inverse = lax.rsqrt(jnp.mean(centred * centred, axis=-1, keepdims=True) + norm_eps)
    return centred * inverse, inverse


def norm_back(grad, normed, inverse, gain):
    scaled = grad * gain
    mean_one = jnp.mean(scaled, axis=-1, keepdims=True)
    mean_two = jnp.mean(scaled * normed, axis=-1, keepdims=True)
    return inverse * (scaled - mean_one - normed * mean_two)


def of_head(values, j, axis=1):
    if values.shape[axis] <= HEAD:
        return values
    place = lax.broadcasted_iota(jnp.int32, values.shape, axis)
    return jnp.where((place >= HEAD * j) & (place < HEAD * (j + 1)), values, jnp.zeros_like(values))


def head_pairs(width):
    return [(low, min(LANES, width - low)) for low in range(0, width, LANES)]


def relay(*refs, number):
    arrived, outs = refs[:number], refs[number:]
    each = len(outs) // number
    for i, rows in enumerate(arrived):
        size = rows.shape[0] // each
        for k in range(each):
            outs[i * each + k][...] = rows[k * size : (k + 1) * size, :]


def by_pairs(weight_t, out):
    width = out.shape[0] // 3
    for low, wide in head_pairs(width):
        for j in range(3):
            out[3 * low + j * wide : 3 * low + (j + 1) * wide, :] = weight_t[
                j * width + low : j * width + low + wide, :
            ]


def norm_one(tok, gain, bias, out, *, m):
    normed, _ = statistics(tok[m, 0].astype(f32))
    out[...] = (normed * gain[...].astype(f32) + bias[...].astype(f32)).astype(bf16)


def loss_grad(where, cells, queries, cot, m, count):
    number = queries[cells[where[0] + m * count]]
    scale = jnp.sqrt(jnp.full((1, cot.shape[3]), number, jnp.int32).astype(f32) / 500.0)
    return cot[m, 0].astype(f32) * scale


def scale_cot(where, cells, queries, cot, out, *, m, count):
    out[...] = loss_grad(where, cells, queries, cot, m, count).astype(bf16)


def project(*refs, parts):
    blocks = refs[:parts]
    weight, bias, scale = refs[parts : parts + 3]
    out, whole = refs[parts + 3 :]
    rows = blocks[0].shape[0]
    for b in range(parts):
        values = blocks[b][...]
        at = slice(b * rows, (b + 1) * rows)
        whole[at, :] = values
        out[at, :] = ((dot32(values, weight[...], 1, 1) + bias[...]) * scale[...]).astype(bf16)


def attend(qkv, out_weight, attended, logs, *outs, step):
    whole = qkv.shape[0]
    head = 0
    for low, wide in head_pairs(out_weight.shape[0]):
        heads = wide // HEAD
        key_pair = qkv[:, 3 * low + wide : 3 * low + 2 * wide]
        value_t = qkv[:, 3 * low + 2 * wide : 3 * low + 3 * wide].T
        keys = [of_head(key_pair, j) for j in range(heads)]
        values = [of_head(value_t, j, 0) for j in range(heads)]
        for start in range(0, whole, step):
            at = slice(start, start + step)
            query = qkv[at, 3 * low : 3 * low + wide]
            total = None
            for j in range(heads):
                scores = dot32(keys[j], query, 1, 1)
                top = jnp.max(scores, axis=0, keepdims=True)
                powers = jnp.exp(scores - top)
                length = jnp.sum(powers, axis=0, keepdims=True)
                mixed = dot32(values[j], powers.astype(bf16), 1, 0) * (1.0 / length)
                total = mixed if total is None else total + mixed
                logs[head + j : head + j + 1, at] = top + jnp.log(length)
            attended[at, low : low + wide] = total.T.astype(bf16)
        head += heads
    rows = whole // len(outs)
    for b, out in enumerate(outs):
        out[...] = dot32(attended[b * rows : (b + 1) * rows, :], out_weight[...], 1, 0).astype(bf16)


def pair_sum(first, second, out):
    out[...] = (first[...].astype(f32) + second[...].astype(f32)).astype(bf16)


def three(first, second, third):
    return first[...].astype(f32) + second[...].astype(f32) + third[...].astype(f32)


def norm_two(tok, first, second, third, out_bias, gain, bias, resid, normed, *, m):
    value = tok[m, 0].astype(f32) + three(first, second, third) + out_bias[...].astype(f32)
    resid[...] = value
    hat, _ = statistics(value)
    normed[...] = (hat * gain[...].astype(f32) + bias[...].astype(f32)).astype(bf16)


def feed(*refs, parts, blocks):
    normed, grads, refs = refs[:blocks], refs[blocks : blocks + parts], refs[blocks + parts :]
    up, up_bias, down, activ, pre_grad, bias_grad, normed_all, grads_all = refs
    for whole, pieces in ((normed_all, normed), (grads_all, grads)):
        low = 0
        for piece in pieces:
            whole[low : low + piece.shape[0], :] = piece[...]
            low += piece.shape[0]
    rows = grads[0].shape[0]
    for low in range(0, up.shape[1], TILE):
        cols = slice(low, low + TILE)
        total = None
        for b in range(parts):
            at = slice(b * rows, (b + 1) * rows)
            pre = dot32(normed_all[at, :], up[:, cols], 1, 0) + up_bias[:, cols].astype(f32)
            cumul = 0.5 + 0.5 * lax.erf(pre * 0.7071067811865476)
            density = jnp.exp(-0.5 * pre * pre) * 0.3989422804014327
            activ[at, cols] = (pre * cumul).astype(bf16)
            back = dot32(grads_all[at, :], down[cols, :], 1, 1)
            grad = (back * (cumul + pre * density)).astype(bf16)
            pre_grad[at, cols] = grad
            part = jnp.sum(grad.astype(f32), axis=0, keepdims=True)
            total = part if total is None else total + part
        bias_grad[:, cols] = total


def times(value, weight, *outs):
    put_tiles(outs, lambda at, cols: dot32(value[at, :], weight[:, cols], 1, 0), value.shape[0])


def times_back(value, weight, *outs):
    put_tiles(outs, lambda at, cols: dot32(value[at, :], weight[cols, :], 1, 1), value.shape[0])


def put_tiles(outs, share_of, whole):
    rows, model = outs[0].shape

    def tile(i, carry):
        cols = pl.ds(pl.multiple_of(i * TILE, TILE), TILE)
        for b, out in enumerate(outs):
            out[:, cols] = share_of(slice(b * rows, (b + 1) * rows), cols).astype(bf16)
        return carry

    lax.fori_loop(0, model // TILE, tile, 0)


def product(first, second, out):
    def tile(i, carry):
        rows = pl.ds(pl.multiple_of(i * TILE, TILE), TILE)
        out[rows, :] = dot32(first[:, rows], second[...], 0, 0).astype(bf16)
        return carry

    lax.fori_loop(0, out.shape[0] // TILE, tile, 0)


def weight_grad(where, first, second, other, *refs, before):
    chunks, whole = refs[before:-1], refs[-1]

    def tile(i, carry):
        rows = pl.ds(pl.multiple_of(i * TILE, TILE), TILE)
        total = dot32(first[:, rows], second[...], 0, 0) + other[rows, :].astype(f32)
        whole[rows, :] = total.astype(bf16)
        return carry

    lax.fori_loop(0, whole.shape[0] // TILE, tile, 0)
    if before:
        chunks, both = chunks[:-1], chunks[-1]
        size = chunks[0].shape[0]
        both[:size, :] = refs[0][...]
        put_chunks(where, chunks, whole)
        both[size:, :] = chunks[0][...]
    else:
        put_chunks(where, chunks, whole)


def ring_chunk(where, count, step):
    half = where[0] // 2
    place = jnp.where(where[0] % 2 == 0, half, count - 1 - half)
    return lax.rem(place + jnp.where(where[1] % 2 == 0, count - step, step), count)


def put_chunks(where, chunks, whole):
    for s, chunk in enumerate(chunks):
        size = chunk.shape[0]
        which = ring_chunk(where, len(chunks), (s + 1) % len(chunks)) if len(chunks) > 1 else 0
        chunk[...] = whole[pl.ds(pl.multiple_of(which * size, size), size), :]


def norm_two_back(where, cells, queries, cot, resid, first, second, third, gain, out, rounded, sums, *, m, count):
    top = loss_grad(where, cells, queries, cot, m, count)
    grad = three(first, second, third)
    hat, inverse = statistics(resid[...])
    back = top + norm_back(grad, hat, inverse, gain[...].astype(f32))
    out[...] = back
    rounded[...] = back.astype(bf16)
    sums[0:1, :] = jnp.sum(back, axis=0, keepdims=True)
    sums[1:2, :] = jnp.sum(grad * hat, axis=0, keepdims=True)
    sums[2:3, :] = jnp.sum(grad, axis=0, keepdims=True)
    sums[3:4, :] = jnp.sum(top, axis=0, keepdims=True)
    sums[4:8, :] = jnp.zeros_like(sums[4:8, :])


def attend_back(qkv, logs, mixed, out_weight, *refs, parts, step, low, wide):
    grads = refs[:parts]
    out, key_grad, value_grad, given, inner = refs[parts:]
    whole = qkv.shape[0]
    rows = whole // parts
    heads = wide // HEAD
    head = low // HEAD
    ones = jnp.concatenate([of_head(jnp.ones((8, wide), bf16), j) for j in range(heads)], axis=0)
    for b in range(parts):
        at = slice(b * rows, (b + 1) * rows)
        value = dot32(grads[b][...], out_weight[low : low + wide, :], 1, 1).astype(bf16)
        given[at, :] = value
        both = value.astype(f32) * mixed[at, low : low + wide].astype(f32)
        high = both.astype(bf16)
        rest = (both - high.astype(f32)).astype(bf16)
        inner[:, at] = dot32(ones, high, 1, 1) + dot32(ones, rest, 1, 1)
    key_pair = qkv[:, 3 * low + wide : 3 * low + 2 * wide]
    value_pair = qkv[:, 3 * low + 2 * wide : 3 * low + 3 * wide]
    key_t = key_pair.T
    keys = [of_head(key_pair, j) for j in range(heads)]
    values = [of_head(value_pair, j) for j in range(heads)]
    keys_t = [of_head(key_t, j, 0) for j in range(heads)]
    key_grad[...] = jnp.zeros_like(key_grad)
    value_grad[...] = jnp.zeros_like(value_grad)

    def block(i, carry):
        start = pl.multiple_of(i * step, step)
        query = qkv[pl.ds(start, step), 3 * low : 3 * low + wide]
        grad = given[pl.ds(start, step), :]
        total = None
        for j in range(heads):
            scores = dot32(keys[j], query, 1, 1)
            weights = jnp.exp(scores - logs[head + j : head + j + 1, pl.ds(start, step)])
            back = dot32(values[j], grad, 1, 1)
            score_grad = (weights * (back - inner[8 * j : 8 * j + 1, pl.ds(start, step)])).astype(bf16)
            value_grad[...] += dot32(weights.astype(bf16), of_head(grad, j), 1, 0)
            key_grad[...] += dot32(score_grad, of_head(query, j), 1, 0)
            part = dot32(keys_t[j], score_grad, 1, 0)
            total = part if total is None else total + part
        out[pl.ds(start, step), :wide] = (total.T * score_scale).astype(bf16)
        return carry

    lax.fori_loop(0, whole // step, block, 0)
    out[:, wide : 2 * wide] = key_grad[...].astype(bf16)
    out[:, 2 * wide :] = value_grad[...].astype(bf16)


def project_back(*refs, pairs):
    grads, weight, outs, sums = refs[:pairs], refs[pairs], refs[pairs + 1 : -1], refs[-1]

    def share_of(at, cols):
        total, low = None, 0
        for grad in grads:
            wide = grad.shape[1]
            part = dot32(grad[at, :], weight[low : low + wide, cols], 1, 0)
            total = part if total is None else total + part
            low += wide
        return total

    put_tiles(outs, share_of, grads[0].shape[0])
    low = 0
    for grad in grads:
        wide = grad.shape[1]
        sums[:, low : low + wide] = jnp.sum(grad[...].astype(f32), axis=0, keepdims=True)
        low += wide


def projection_grad(where, *refs, micros, pairs, parts):
    normed, refs = refs[:micros], refs[micros:]
    grads, refs = [refs[m * pairs : (m + 1) * pairs] for m in range(micros)], refs[micros * pairs :]
    tops, refs = [refs[m * parts : (m + 1) * parts] for m in range(micros)], refs[micros * parts :]
    mixed, refs = refs[:micros], refs[micros:]
    chunks, out = refs[:-1], refs[-1]
    width = mixed[0].shape[1]
    rows = tops[0][0].shape[0]
    for p, (low, wide) in enumerate(head_pairs(width)):
        total = None
        for m in range(micros):
            part = dot32(grads[m][p][...], normed[m][...], 0, 0)
            total = part if total is None else total + part
        for j in range(3):
            out[j * width + low : j * width + low + wide, :] = total[j * wide : (j + 1) * wide].astype(bf16)
        total = None
        for m in range(micros):
            for b in range(parts):
                part = dot32(mixed[m][b * rows : (b + 1) * rows, low : low + wide], tops[m][b][...], 0, 0)
                total = part if total is None else total + part
        out[3 * width + low : 3 * width + low + wide, :] = total.astype(bf16)
    put_chunks(where, chunks, out)


def ring_add(arrived, *refs):
    low = 0
    for part in refs[:-1]:
        at = slice(low, low + part.shape[0])
        refs[-1][at, :] = (arrived[at, :].astype(f32) + part[...].astype(f32)).astype(bf16)
        low += part.shape[0]


def ring_store(where, *refs, steps, count, stacked):
    moved, refs = refs[: len(steps)], refs[len(steps) :]
    done, first, second, buffer, sems = refs[-5:]
    done[...] = jnp.zeros_like(done)
    size = buffer.shape[1] // 2 if stacked else buffer.shape[1]
    copies = []
    for k, step in enumerate(steps):
        buffer[k] = moved[k][...].astype(f32)
        row = pl.multiple_of(ring_chunk(where, count, step) * size, size)
        if stacked:
            for i, target in enumerate((first, second)):
                source = buffer.at[k, pl.ds(i * size, size), :]
                copies.append(pltpu.make_async_copy(source, target.at[pl.ds(row, size), :], sems.at[2 * k + i]))
                copies[-1].start()
        else:
            last = first.shape[0] - size
            to_first = pl.multiple_of(jnp.minimum(row, last), 16)
            to_second = pl.multiple_of(jnp.maximum(row - first.shape[0], 0), 16)
            copy_first = pltpu.make_async_copy(buffer.at[k], first.at[pl.ds(to_first, size), :], sems.at[2 * k])
            copy_second = pltpu.make_async_copy(buffer.at[k], second.at[pl.ds(to_second, size), :], sems.at[2 * k])
            pl.when(row <= last)(copy_first.start)
            pl.when(row > last)(copy_second.start)
            copies.append(copy_first)
    for copy in copies:
        copy.wait()


def norm_one_back(tok, resid_grad, first, second, third, gain, out, sums, *, m):
    grad = three(first, second, third)
    hat, inverse = statistics(tok[m, 0].astype(f32))
    out[...] = resid_grad[...] + norm_back(grad, hat, inverse, gain[...].astype(f32))
    sums[0:4, :] = jnp.zeros_like(sums[0:4, :])
    sums[4:5, :] = jnp.sum(grad * hat, axis=0, keepdims=True)
    sums[5:6, :] = jnp.sum(grad, axis=0, keepdims=True)
    sums[6:8, :] = jnp.zeros_like(sums[6:8, :])


def vector_sum(*refs):
    total = refs[0][...]
    for ref in refs[1:-1]:
        total = total + ref[...]
    refs[-1][...] = total


def vector_join(first, second, *refs, number):
    up_bias, stack, out = refs[:number], refs[number:-1], refs[-1]
    out[...] = first[...] + second[...]
    for row, parts in ((6, up_bias), (7, stack)):
        total = parts[0][...]
        for part in parts[1:]:
            total = total + part[...]
        out[row : row + 1, : total.shape[1]] = total


def add_rows(resid, first, second, third, bias, out):
    out[...] = (resid[...] + three(first, second, third) + bias[...].astype(f32)).astype(bf16)


def swap(values, axis, bit):
    return lax.ppermute(values, axis, [(i, i ^ bit) for i in range(lax.axis_size(axis))])


def ring_order(count):
    return list(range(0, count, 2)) + list(range(1, count, 2))[::-1]


class Ring:
    def __init__(self, chain, where, shapes, stacked):
        self.chain, self.where, self.shapes, self.stacked = chain, where, shapes, stacked
        self.count = lax.axis_size("wide")
        cores = lax.axis_size("narrow")
        order = ring_order(self.count)
        self.perm = [
            (order[i] * cores + n, order[(i + (1 if n % 2 == 0 else -1)) % self.count] * cores + n)
            for i in range(self.count)
            for n in range(cores)
        ]
        self.have, self.step, self.outs = [], 1, None

    def pass_on(self, chunk):
        self.moving = lax.ppermute(chunk, ("wide", "narrow"), self.perm)

    def start(self, chunk, parts):
        self.parts = parts
        self.pass_on(chunk)

    def hold(self):
        self.chain.hold(self.moving)

    def add(self, cover=False):
        (made,) = self.chain.run(
            ring_add,
            [(self.moving.shape, bf16)],
            self.moving,
            *[p[self.step] for p in self.parts],
            cover=cover,
        )
        self.step += 1
        if self.step == self.count:
            self.have.append(made)
        self.pass_on(made)

    def forward(self):
        self.have.append(self.moving)
        self.hold()
        if len(self.have) < self.count:
            self.pass_on(self.moving)

    def store(self, steps):
        moved = [self.have[s] for s in steps]
        kept = () if self.outs is None else self.outs
        number = len(moved)
        made = self.chain.run(
            functools.partial(ring_store, steps=tuple(steps), count=self.count, stacked=self.stacked),
            [((8, LANES), f32)] + [(s, f32) for s in self.shapes],
            *moved,
            *kept,
            smem=(self.where,),
            scratch=[pltpu.VMEM((number, *moved[0].shape), f32), pltpu.SemaphoreType.DMA((2 * number,))],
            alias={number: 1, number + 1: 2} if kept else None,
            anywhere=(number, number + 1) if kept else (),
            out_anywhere=(1, 2),
            limit=6 + (number * moved[0].size * 4 >> 20),
        )
        self.outs = made[1:]


class Whole:
    def __init__(self, shapes):
        self.shapes = shapes

    def start(self, chunk, parts):
        total = lax.psum(chunk, "wide").astype(f32)
        self.outs = (total[: self.shapes[0][0]], total[self.shapes[0][0] :])

    def hold(self):
        pass

    def add(self, cover=False):
        pass

    def forward(self):
        pass

    def store(self, steps):
        pass


def local(
    tokens,
    cotangent,
    cell_of,
    query_count,
    attn_norm_gain,
    attn_norm_bias,
    input_weight,
    query_bias,
    value_bias,
    out_weight,
    out_bias,
    ffn_norm_gain,
    ffn_norm_bias,
    up_weight,
    up_bias,
    down_weight,
    down_bias,
):
    micros = range(tokens.shape[0])
    rows, model = tokens.shape[2], tokens.shape[3]
    parts = lax.axis_size("narrow")
    whole = rows * parts
    width = input_weight.shape[2]
    hidden = up_weight.shape[1]
    count = lax.axis_size("wide")
    rings = count <= 8
    chunks = count if rings else 1
    pairs = head_pairs(width)
    step = min(512, whole)
    chain = Chain()
    run = chain.run
    where = jnp.stack([lax.axis_index("wide"), lax.axis_index("narrow")]).astype(jnp.int32)

    block = ((rows, model), bf16)
    outgoing = [block] * parts
    wide_rows = ((whole, model), bf16)
    row = lambda v: v.reshape(1, -1)
    gain_one, bias_one, gain_two, bias_two = map(row, (attn_norm_gain, attn_norm_bias, ffn_norm_gain, ffn_norm_bias))
    out_bias, down_bias, up_bias = row(out_bias), row(down_bias), row(up_bias)

    def columns(three_parts):
        return jnp.concatenate([v[:, low : low + wide] for low, wide in pairs for v in three_parts], axis=1)

    weight_t = jnp.transpose(input_weight, (1, 2, 0)).reshape(3 * width, model)
    zero = jnp.zeros((1, width), f32)
    project_bias = columns([row(query_bias).astype(f32), zero, row(value_bias).astype(f32)])
    project_scale = columns([zero + score_scale, zero + 1.0, zero + 1.0])

    def gather(own):
        return [own, swap(own, "narrow", 1), swap(own, "narrow", 2)]

    def finish(*arrived, pieces=1, cover=False):
        made = run(
            functools.partial(relay, number=len(arrived)),
            [((rows // pieces, model), bf16)] * (len(arrived) * pieces),
            *[a[2] for a in arrived],
            cover=cover,
        )
        for i, a in enumerate(arrived):
            own = made[i * pieces : (i + 1) * pieces]
            a[2:] = [*own, *[swap(piece, "narrow", 1) for piece in own]]

    def share(made):
        own, near, partner, far = made
        return [own, partner, swap(far, "narrow", 1), swap(near, "narrow", 1)]

    def send(shares):
        own, partner, far, near = shares
        (both,) = run(pair_sum, [block], partner, far)
        return [own, near, swap(both, "narrow", 2)]

    def fresh():
        return [None] * len(micros)

    normed, given, qkv, normed_all, mixed, logs, shares, shares_down, resid, normed_two_b = (fresh() for _ in range(10))
    activ, pre_grad, up_bias_grad, two_all, given_all, resid_grad, top = (fresh() for _ in range(7))
    sums_two, sums_one, stack_sums, out_rows, grad_rows = (fresh() for _ in range(5))
    pair_grads = [[] for _ in micros]

    def do_norm_one(m):
        (own,) = run(functools.partial(norm_one, m=m), [block], tokens, gain_one, bias_one)
        normed[m] = gather(own)

    def do_scale(m):
        (own,) = run(functools.partial(scale_cot, m=m, count=count), [block], cotangent, smem=(where, cell_of, query_count), cover=True)
        given[m] = gather(own)

    def do_project(m):
        qkv[m], normed_all[m] = run(
            functools.partial(project, parts=parts),
            [((whole, 3 * width), bf16), wide_rows],
            *normed[m],
            weight,
            project_bias,
            project_scale,
        )

    def do_attend(m):
        mixed[m], logs[m], *made = run(
            functools.partial(attend, step=whole),
            [((whole, width), bf16), ((8, whole), f32), *outgoing],
            qkv[m],
            out_weight,
            limit=24,
        )
        shares[m] = share(made)

    def do_send(m):
        shares[m] = send(shares[m])

    def do_norm_two(m):
        resid[m], own = run(
            functools.partial(norm_two, m=m),
            [((rows, model), f32), block],
            tokens,
            *shares[m],
            out_bias,
            gain_two,
            bias_two,
            cover=m == 0,
        )
        normed_two_b[m] = gather(own)

    def do_feed(m):
        activ[m], pre_grad[m], up_bias_grad[m], two_all[m], given_all[m] = run(
            functools.partial(feed, parts=parts, blocks=len(normed_two_b[m])),
            [((whole, hidden), bf16), ((whole, hidden), bf16), ((1, hidden), f32), wide_rows, wide_rows],
            *normed_two_b[m],
            *given[m],
            up_weight,
            up_bias,
            down_weight,
        )

    def do_up_back(m):
        shares[m] = share(run(times_back, outgoing, pre_grad[m], up_weight))

    def do_down(m):
        shares_down[m] = share(run(times, outgoing, activ[m], down_weight))

    def do_send_down(m):
        shares_down[m] = send(shares_down[m])

    def do_norm_two_back(m):
        resid_grad[m], own, sums_two[m] = run(
            functools.partial(norm_two_back, m=m, count=count),
            [((rows, model), f32), block, ((8, model), f32)],
            cotangent,
            resid[m],
            *shares[m],
            gain_two,
            smem=(where, cell_of, query_count),
            cover=True,
        )
        top[m] = gather(own)

    def do_attend_back(m, p):
        low, wide = pairs[p]
        (made,) = run(
            functools.partial(attend_back, parts=parts, step=step, low=low, wide=wide),
            [((whole, 3 * wide), bf16)],
            qkv[m],
            logs[m],
            mixed[m],
            out_weight,
            *top[m],
            scratch=[
                pltpu.VMEM((whole, wide), f32),
                pltpu.VMEM((whole, wide), f32),
                pltpu.VMEM((whole, wide), bf16),
                pltpu.VMEM((8 * (wide // HEAD), whole), f32),
            ],
            limit=20,
        )
        pair_grads[m].append(made)

    def do_project_back(m):
        *made, stack_sums[m] = run(
            functools.partial(project_back, pairs=len(pairs)),
            [*outgoing, ((1, 3 * width), f32)],
            *pair_grads[m],
            weight,
        )
        shares[m] = share(made)

    def do_norm_one_back(m):
        grad_rows[m], sums_one[m] = run(
            functools.partial(norm_one_back, m=m),
            [((rows, model), f32), ((8, model), f32)],
            tokens,
            resid_grad[m],
            *shares[m],
            gain_one,
        )

    hops = [("narrow", 1 << k) for k in range(parts.bit_length() - 1)]
    hops += [("wide", 1 << k) for k in range(count.bit_length() - 1)]
    vectors = []

    def do_vectors():
        done = len(vectors)
        shape = [((8, model), f32)]
        if done == 0:
            (own,) = run(vector_sum, shape, *sums_one, *sums_two)
        elif hops[done - 1][0] == "narrow" and hops[done][0] == "wide":
            own, arrived = vectors[-1]
            (own,) = run(
                functools.partial(vector_join, number=len(micros)), shape, own, arrived, *up_bias_grad, *stack_sums
            )
        else:
            (own,) = run(vector_sum, shape, *vectors[-1])
        vectors.append((own, swap(own, *hops[done]) if done < len(hops) else None))

    def do_add_rows(m):
        (out_rows[m],) = run(add_rows, [block], resid[m], *shares_down[m], down_bias)

    def first_product(first, second):
        return run(product, [((first.shape[1], second.shape[1]), bf16)], first, second)[0]

    def ffn_grad(first, second, other, before=()):
        rows, cols = other.shape
        shapes = [((rows // chunks, cols), bf16)] * chunks
        if before:
            shapes.append(((2 * rows // chunks, cols), bf16))
        return run(
            functools.partial(weight_grad, before=len(before[:1])),
            shapes,
            first,
            second,
            other,
            *before[:1],
            smem=(where,),
            scratch=[pltpu.VMEM((rows, cols), bf16)],
            limit=16,
        )

    def attn_grad():
        made = run(
            functools.partial(projection_grad, micros=len(micros), pairs=len(pairs), parts=parts),
            [((4 * width // chunks, model), bf16)] * chunks,
            *normed_all,
            *[g for m in micros for g in pair_grads[m]],
            *[t for m in micros for t in top[m]],
            *mixed,
            smem=(where,),
            scratch=[pltpu.VMEM((4 * width, model), bf16)],
            limit=20,
        )
        attn.start(made[0], (made,))

    ffn_shapes = [(hidden, model), (model, hidden)]
    attn_shapes = [(3 * width, model), (width, model)]
    ffn = Ring(chain, where, ffn_shapes, True) if rings else Whole(ffn_shapes)
    attn = Ring(chain, where, attn_shapes, False) if rings else Whole(attn_shapes)

    do_norm_one(0)
    (weight,) = run(by_pairs, [((3 * width, model), bf16)], weight_t)
    chain.hold(normed[0][1])
    finish(normed[0])
    do_norm_one(1)
    do_scale(0)
    do_project(0)
    do_attend(0)
    chain.hold(normed[1][1], given[0][1])
    finish(normed[1], given[0], cover=True)
    do_scale(1)
    do_send(0)
    chain.hold(given[1][1])
    do_project(1)
    do_attend(1)
    chain.hold(given[1][2])
    do_norm_two(0)
    do_send(1)
    finish(given[1])
    chain.hold(normed_two_b[0][1])
    finish(normed_two_b[0], pieces=4)
    do_feed(0)
    do_norm_two(1)
    chain.hold(normed_two_b[1][1])
    do_up_back(0)
    down_first = first_product(activ[0], given_all[0])
    up_first = first_product(two_all[0], pre_grad[0])
    do_down(0)
    finish(normed_two_b[1], cover=True)
    do_send(0)
    do_feed(1)
    do_up_back(1)
    do_norm_two_back(0)
    chain.hold(top[0][1])
    down_chunks = ffn_grad(activ[1], given_all[1], down_first)
    *up_chunks, both = ffn_grad(two_all[1], pre_grad[1], up_first, down_chunks)
    ffn.start(both, (down_chunks, up_chunks))
    finish(top[0], cover=True)
    do_send(1)
    do_attend_back(0, 0)
    ffn.add()
    do_attend_back(0, 1)
    do_norm_two_back(1)
    ffn.add()
    do_attend_back(0, 2)
    do_project_back(0)
    ffn.add()
    chain.hold(top[1][1])
    finish(top[1], cover=True)
    do_attend_back(1, 0)
    do_send_down(0)
    ffn.add()
    do_send(0)
    do_attend_back(1, 1)
    ffn.add()
    do_attend_back(1, 2)
    ffn.add()
    attn_grad()
    ffn.add()
    attn.add()
    do_project_back(1)
    attn.add()
    do_norm_one_back(0)
    ffn.forward()
    do_down(1)
    attn.add()
    do_send(1)
    attn.add()
    do_send_down(1)
    ffn.forward()
    attn.add()
    attn.add()
    do_norm_one_back(1)
    do_vectors()
    ffn.forward()
    ffn.store(range(0, 2))
    attn.add()
    do_vectors()
    do_add_rows(0)
    attn.forward()
    do_vectors()
    ffn.forward()
    do_add_rows(1)
    attn.forward()
    do_vectors()
    ffn.store(range(2, 4))
    attn.forward()
    do_vectors()
    ffn.forward()
    attn.store(range(0, 3))
    attn.forward()
    do_vectors()
    attn.forward()
    ffn.store(range(4, 6))
    ffn.forward()
    attn.store(range(3, 5))
    attn.forward()
    attn.store(range(5, 6))
    ffn.forward()
    ffn.store(range(6, 8))
    attn.forward()
    attn.store(range(6, 8))

    while len(vectors) <= len(hops):
        do_vectors()
    vector_sums = vectors[-1][0]
    up_bias_sum = vector_sums[6, :hidden]
    stack_sum = vector_sums[7, : 3 * width]

    def plain(j):
        return jnp.concatenate([stack_sum[3 * low + j * wide : 3 * low + (j + 1) * wide] for low, wide in pairs])

    return (
        jnp.stack(out_rows)[:, None],
        jnp.stack(grad_rows)[:, None],
        vector_sums[4],
        vector_sums[5],
        jnp.transpose(attn.outs[0].reshape(3, width, model), (2, 0, 1)),
        plain(0),
        plain(2),
        attn.outs[1],
        vector_sums[0],
        vector_sums[1],
        vector_sums[2],
        ffn.outs[1],
        up_bias_sum,
        ffn.outs[0],
        vector_sums[3],
    )


def solution(mesh):
    in_specs = (
        P(None, "wide", "narrow", None),
        P(None, "wide", "narrow", None),
        P(),
        P(),
        P(),
        P(),
        P(None, None, "narrow"),
        P("narrow"),
        P("narrow"),
        P("narrow", None),
        P(),
        P(),
        P(),
        P(None, "narrow"),
        P("narrow"),
        P("narrow", None),
        P(),
    )
    out_specs = (
        P(None, "wide", "narrow", None),
        P(None, "wide", "narrow", None),
        P(),
        P(),
        P(None, None, "narrow"),
        P("narrow"),
        P("narrow"),
        P("narrow", None),
        P(),
        P(),
        P(),
        P(None, "narrow"),
        P("narrow"),
        P("narrow", None),
        P(),
    )
    return jax.shard_map(local, mesh=mesh, in_specs=in_specs, out_specs=out_specs, check_vma=False)
```

```python
import functools

import jax
import jax.numpy as jnp
from jax import lax
from jax.experimental import pallas as pl
from jax.experimental.pallas import tpu as pltpu
from jax.sharding import PartitionSpec as P

HEAD = 64
LANES = 128
TILE = 256
norm_eps = 1e-05
score_scale = 0.125
bf16 = jnp.bfloat16
f32 = jnp.float32


class Chain:
    def __init__(self):
        self.last = []
        self.held = []

    def hold(self, *arrays):
        self.held += arrays

    def run(self, body, outs, *ins, smem=(), scratch=(), alias=None, anywhere=(), out_anywhere=(), limit=6, token=0, cover=False):
        unread = [*self.last, *self.held]
        count = len(smem) + len(ins)
        specs = [pl.BlockSpec(memory_space=pltpu.SMEM)] * len(smem)
        specs += [pl.BlockSpec(memory_space=pl.ANY if i in anywhere else pltpu.VMEM) for i in range(len(ins))]
        specs += [pl.BlockSpec(memory_space=pl.ANY)] * len(unread)

        def inner(*refs):
            body(*refs[:count], *refs[count + len(unread) :])

        made = pl.pallas_call(
            inner,
            out_shape=tuple(jax.ShapeDtypeStruct(*o) for o in outs),
            in_specs=specs,
            out_specs=tuple(
                pl.BlockSpec(memory_space=pl.ANY if i in out_anywhere else pltpu.VMEM) for i in range(len(outs))
            ),
            scratch_shapes=scratch,
            input_output_aliases={} if alias is None else {len(smem) + k: v for k, v in alias.items()},
            compiler_params=pltpu.CompilerParams(vmem_limit_bytes=limit << 20),
            cost_estimate=pl.CostEstimate(flops=10**12 if cover else 1, bytes_accessed=1, transcendentals=0),
            name=body.func.__name__ if isinstance(body, functools.partial) else body.__name__,
        )(*smem, *ins, *unread)
        self.last, self.held = [made[token]], []
        return made


def dot32(first, second, first_dim, second_dim):
    return lax.dot_general(
        first, second, (((first_dim,), (second_dim,)), ((), ())), preferred_element_type=f32
    )


def statistics(values):
    average = jnp.mean(values, axis=-1, keepdims=True)
    centred = values - average
    inverse = lax.rsqrt(jnp.mean(centred * centred, axis=-1, keepdims=True) + norm_eps)
    return centred * inverse, inverse


def norm_back(grad, normed, inverse, gain):
    scaled = grad * gain
    mean_one = jnp.mean(scaled, axis=-1, keepdims=True)
    mean_two = jnp.mean(scaled * normed, axis=-1, keepdims=True)
    return inverse * (scaled - mean_one - normed * mean_two)


def of_head(values, j, axis=1):
    if values.shape[axis] <= HEAD:
        return values
    place = lax.broadcasted_iota(jnp.int32, values.shape, axis)
    return jnp.where((place >= HEAD * j) & (place < HEAD * (j + 1)), values, jnp.zeros_like(values))


def head_pairs(width):
    return [(low, min(LANES, width - low)) for low in range(0, width, LANES)]


def relay(*refs, number):
    arrived, outs = refs[:number], refs[number:]
    each = len(outs) // number
    for i, rows in enumerate(arrived):
        size = rows.shape[0] // each
        for k in range(each):
            outs[i * each + k][...] = rows[k * size : (k + 1) * size, :]


def by_pairs(weight_t, out):
    width = out.shape[0] // 3
    for low, wide in head_pairs(width):
        for j in range(3):
            out[3 * low + j * wide : 3 * low + (j + 1) * wide, :] = weight_t[
                j * width + low : j * width + low + wide, :
            ]


def norm_one(tok, gain, bias, out, *, m):
    normed, _ = statistics(tok[m, 0].astype(f32))
    out[...] = (normed * gain[...].astype(f32) + bias[...].astype(f32)).astype(bf16)


def loss_grad(where, cells, queries, cot, m, count):
    number = queries[cells[where[0] + m * count]]
    scale = jnp.sqrt(jnp.full((1, cot.shape[3]), number, jnp.int32).astype(f32) / 500.0)
    return cot[m, 0].astype(f32) * scale


def scale_cot(where, cells, queries, cot, out, *, m, count):
    out[...] = loss_grad(where, cells, queries, cot, m, count).astype(bf16)


def project(*refs, parts):
    blocks = refs[:parts]
    weight, bias, scale = refs[parts : parts + 3]
    out, whole = refs[parts + 3 :]
    rows = blocks[0].shape[0]
    for b in range(parts):
        values = blocks[b][...]
        at = slice(b * rows, (b + 1) * rows)
        whole[at, :] = values
        out[at, :] = ((dot32(values, weight[...], 1, 1) + bias[...]) * scale[...]).astype(bf16)


def attend(qkv, out_weight, attended, logs, *outs, step):
    whole = qkv.shape[0]
    head = 0
    for low, wide in head_pairs(out_weight.shape[0]):
        heads = wide // HEAD
        key_pair = qkv[:, 3 * low + wide : 3 * low + 2 * wide]
        value_t = qkv[:, 3 * low + 2 * wide : 3 * low + 3 * wide].T
        keys = [of_head(key_pair, j) for j in range(heads)]
        values = [of_head(value_t, j, 0) for j in range(heads)]
        for start in range(0, whole, step):
            at = slice(start, start + step)
            query = qkv[at, 3 * low : 3 * low + wide]
            total = None
            for j in range(heads):
                scores = dot32(keys[j], query, 1, 1)
                top = jnp.max(scores, axis=0, keepdims=True)
                powers = jnp.exp(scores - top)
                length = jnp.sum(powers, axis=0, keepdims=True)
                mixed = dot32(values[j], powers.astype(bf16), 1, 0) * (1.0 / length)
                total = mixed if total is None else total + mixed
                logs[head + j : head + j + 1, at] = top + jnp.log(length)
            attended[at, low : low + wide] = total.T.astype(bf16)
        head += heads
    rows = whole // len(outs)
    for b, out in enumerate(outs):
        out[...] = dot32(attended[b * rows : (b + 1) * rows, :], out_weight[...], 1, 0).astype(bf16)


def pair_sum(first, second, out):
    out[...] = (first[...].astype(f32) + second[...].astype(f32)).astype(bf16)


def three(first, second, third):
    return first[...].astype(f32) + second[...].astype(f32) + third[...].astype(f32)


def norm_two(tok, first, second, third, out_bias, gain, bias, resid, normed, *, m):
    value = tok[m, 0].astype(f32) + three(first, second, third) + out_bias[...].astype(f32)
    resid[...] = value
    hat, _ = statistics(value)
    normed[...] = (hat * gain[...].astype(f32) + bias[...].astype(f32)).astype(bf16)


def feed(*refs, parts, blocks):
    normed, grads, refs = refs[:blocks], refs[blocks : blocks + parts], refs[blocks + parts :]
    up, up_bias, down, activ, pre_grad, bias_grad, normed_all, grads_all = refs
    for whole, pieces in ((normed_all, normed), (grads_all, grads)):
        low = 0
        for piece in pieces:
            whole[low : low + piece.shape[0], :] = piece[...]
            low += piece.shape[0]
    rows = grads[0].shape[0]
    for low in range(0, up.shape[1], TILE):
        cols = slice(low, low + TILE)
        total = None
        for b in range(parts):
            at = slice(b * rows, (b + 1) * rows)
            pre = dot32(normed_all[at, :], up[:, cols], 1, 0) + up_bias[:, cols].astype(f32)
            cumul = 0.5 + 0.5 * lax.erf(pre * 0.7071067811865476)
            density = jnp.exp(-0.5 * pre * pre) * 0.3989422804014327
            activ[at, cols] = (pre * cumul).astype(bf16)
            back = dot32(grads_all[at, :], down[cols, :], 1, 1)
            grad = (back * (cumul + pre * density)).astype(bf16)
            pre_grad[at, cols] = grad
            part = jnp.sum(grad.astype(f32), axis=0, keepdims=True)
            total = part if total is None else total + part
        bias_grad[:, cols] = total


def times(value, weight, *outs):
    put_tiles(outs, lambda at, cols: dot32(value[at, :], weight[:, cols], 1, 0), value.shape[0])


def times_back(value, weight, *outs):
    put_tiles(outs, lambda at, cols: dot32(value[at, :], weight[cols, :], 1, 1), value.shape[0])


def put_tiles(outs, share_of, whole):
    rows, model = outs[0].shape

    def tile(i, carry):
        cols = pl.ds(pl.multiple_of(i * TILE, TILE), TILE)
        for b, out in enumerate(outs):
            out[:, cols] = share_of(slice(b * rows, (b + 1) * rows), cols).astype(bf16)
        return carry

    lax.fori_loop(0, model // TILE, tile, 0)


def product(first, second, out):
    def tile(i, carry):
        rows = pl.ds(pl.multiple_of(i * TILE, TILE), TILE)
        out[rows, :] = dot32(first[:, rows], second[...], 0, 0).astype(bf16)
        return carry

    lax.fori_loop(0, out.shape[0] // TILE, tile, 0)


def weight_grad(where, first, second, other, *refs, before):
    chunks, whole = refs[before:-1], refs[-1]

    def tile(i, carry):
        rows = pl.ds(pl.multiple_of(i * TILE, TILE), TILE)
        total = dot32(first[:, rows], second[...], 0, 0) + other[rows, :].astype(f32)
        whole[rows, :] = total.astype(bf16)
        return carry

    lax.fori_loop(0, whole.shape[0] // TILE, tile, 0)
    if before:
        chunks, both = chunks[:-1], chunks[-1]
        size = chunks[0].shape[0]
        both[:size, :] = refs[0][...]
        put_chunks(where, chunks, whole)
        both[size:, :] = chunks[0][...]
    else:
        put_chunks(where, chunks, whole)


def ring_chunk(where, count, step):
    half = where[0] // 2
    place = jnp.where(where[0] % 2 == 0, half, count - 1 - half)
    return lax.rem(place + jnp.where(where[1] % 2 == 0, count - step, step), count)


def put_chunks(where, chunks, whole):
    for s, chunk in enumerate(chunks):
        size = chunk.shape[0]
        which = ring_chunk(where, len(chunks), (s + 1) % len(chunks)) if len(chunks) > 1 else 0
        chunk[...] = whole[pl.ds(pl.multiple_of(which * size, size), size), :]


def norm_two_back(where, cells, queries, cot, resid, first, second, third, gain, out, rounded, sums, *, m, count):
    top = loss_grad(where, cells, queries, cot, m, count)
    grad = three(first, second, third)
    hat, inverse = statistics(resid[...])
    back = top + norm_back(grad, hat, inverse, gain[...].astype(f32))
    out[...] = back
    rounded[...] = back.astype(bf16)
    sums[0:1, :] = jnp.sum(back, axis=0, keepdims=True)
    sums[1:2, :] = jnp.sum(grad * hat, axis=0, keepdims=True)
    sums[2:3, :] = jnp.sum(grad, axis=0, keepdims=True)
    sums[3:4, :] = jnp.sum(top, axis=0, keepdims=True)
    sums[4:8, :] = jnp.zeros_like(sums[4:8, :])


def attend_back(qkv, logs, mixed, out_weight, *refs, parts, step, low, wide):
    grads = refs[:parts]
    out, key_grad, value_grad, given, inner = refs[parts:]
    whole = qkv.shape[0]
    rows = whole // parts
    heads = wide // HEAD
    head = low // HEAD
    ones = jnp.concatenate([of_head(jnp.ones((8, wide), bf16), j) for j in range(heads)], axis=0)
    for b in range(parts):
        at = slice(b * rows, (b + 1) * rows)
        value = dot32(grads[b][...], out_weight[low : low + wide, :], 1, 1).astype(bf16)
        given[at, :] = value
        both = value.astype(f32) * mixed[at, low : low + wide].astype(f32)
        high = both.astype(bf16)
        rest = (both - high.astype(f32)).astype(bf16)
        inner[:, at] = dot32(ones, high, 1, 1) + dot32(ones, rest, 1, 1)
    key_pair = qkv[:, 3 * low + wide : 3 * low + 2 * wide]
    value_pair = qkv[:, 3 * low + 2 * wide : 3 * low + 3 * wide]
    key_t = key_pair.T
    keys = [of_head(key_pair, j) for j in range(heads)]
    values = [of_head(value_pair, j) for j in range(heads)]
    keys_t = [of_head(key_t, j, 0) for j in range(heads)]
    key_grad[...] = jnp.zeros_like(key_grad)
    value_grad[...] = jnp.zeros_like(value_grad)

    def block(i, carry):
        start = pl.multiple_of(i * step, step)
        query = qkv[pl.ds(start, step), 3 * low : 3 * low + wide]
        grad = given[pl.ds(start, step), :]
        total = None
        for j in range(heads):
            scores = dot32(keys[j], query, 1, 1)
            weights = jnp.exp(scores - logs[head + j : head + j + 1, pl.ds(start, step)])
            back = dot32(values[j], grad, 1, 1)
            score_grad = (weights * (back - inner[8 * j : 8 * j + 1, pl.ds(start, step)])).astype(bf16)
            value_grad[...] += dot32(weights.astype(bf16), of_head(grad, j), 1, 0)
            key_grad[...] += dot32(score_grad, of_head(query, j), 1, 0)
            part = dot32(keys_t[j], score_grad, 1, 0)
            total = part if total is None else total + part
        out[pl.ds(start, step), :wide] = (total.T * score_scale).astype(bf16)
        return carry

    lax.fori_loop(0, whole // step, block, 0)
    out[:, wide : 2 * wide] = key_grad[...].astype(bf16)
    out[:, 2 * wide :] = value_grad[...].astype(bf16)


def project_back(*refs, pairs):
    grads, weight, outs, sums = refs[:pairs], refs[pairs], refs[pairs + 1 : -1], refs[-1]

    def share_of(at, cols):
        total, low = None, 0
        for grad in grads:
            wide = grad.shape[1]
            part = dot32(grad[at, :], weight[low : low + wide, cols], 1, 0)
            total = part if total is None else total + part
            low += wide
        return total

    put_tiles(outs, share_of, grads[0].shape[0])
    low = 0
    for grad in grads:
        wide = grad.shape[1]
        sums[:, low : low + wide] = jnp.sum(grad[...].astype(f32), axis=0, keepdims=True)
        low += wide


def projection_grad(where, *refs, micros, pairs, parts):
    normed, refs = refs[:micros], refs[micros:]
    grads, refs = [refs[m * pairs : (m + 1) * pairs] for m in range(micros)], refs[micros * pairs :]
    tops, refs = [refs[m * parts : (m + 1) * parts] for m in range(micros)], refs[micros * parts :]
    mixed, refs = refs[:micros], refs[micros:]
    chunks, out = refs[:-1], refs[-1]
    width = mixed[0].shape[1]
    rows = tops[0][0].shape[0]
    for p, (low, wide) in enumerate(head_pairs(width)):
        total = None
        for m in range(micros):
            part = dot32(grads[m][p][...], normed[m][...], 0, 0)
            total = part if total is None else total + part
        for j in range(3):
            out[j * width + low : j * width + low + wide, :] = total[j * wide : (j + 1) * wide].astype(bf16)
        total = None
        for m in range(micros):
            for b in range(parts):
                part = dot32(mixed[m][b * rows : (b + 1) * rows, low : low + wide], tops[m][b][...], 0, 0)
                total = part if total is None else total + part
        out[3 * width + low : 3 * width + low + wide, :] = total.astype(bf16)
    put_chunks(where, chunks, out)


def ring_add(arrived, *refs):
    low = 0
    for part in refs[:-1]:
        at = slice(low, low + part.shape[0])
        refs[-1][at, :] = (arrived[at, :].astype(f32) + part[...].astype(f32)).astype(bf16)
        low += part.shape[0]


def ring_store(where, *refs, steps, count, stacked):
    moved, refs = refs[: len(steps)], refs[len(steps) :]
    done, first, second, buffer, sems = refs[-5:]
    done[...] = jnp.zeros_like(done)
    size = buffer.shape[1] // 2 if stacked else buffer.shape[1]
    copies = []
    for k, step in enumerate(steps):
        buffer[k] = moved[k][...].astype(f32)
        row = pl.multiple_of(ring_chunk(where, count, step) * size, size)
        if stacked:
            for i, target in enumerate((first, second)):
                source = buffer.at[k, pl.ds(i * size, size), :]
                copies.append(pltpu.make_async_copy(source, target.at[pl.ds(row, size), :], sems.at[2 * k + i]))
                copies[-1].start()
        else:
            last = first.shape[0] - size
            to_first = pl.multiple_of(jnp.minimum(row, last), 16)
            to_second = pl.multiple_of(jnp.maximum(row - first.shape[0], 0), 16)
            copy_first = pltpu.make_async_copy(buffer.at[k], first.at[pl.ds(to_first, size), :], sems.at[2 * k])
            copy_second = pltpu.make_async_copy(buffer.at[k], second.at[pl.ds(to_second, size), :], sems.at[2 * k])
            pl.when(row <= last)(copy_first.start)
            pl.when(row > last)(copy_second.start)
            copies.append(copy_first)
    for copy in copies:
        copy.wait()


def norm_one_back(tok, resid_grad, first, second, third, gain, out, sums, *, m):
    grad = three(first, second, third)
    hat, inverse = statistics(tok[m, 0].astype(f32))
    out[...] = resid_grad[...] + norm_back(grad, hat, inverse, gain[...].astype(f32))
    sums[0:4, :] = jnp.zeros_like(sums[0:4, :])
    sums[4:5, :] = jnp.sum(grad * hat, axis=0, keepdims=True)
    sums[5:6, :] = jnp.sum(grad, axis=0, keepdims=True)
    sums[6:8, :] = jnp.zeros_like(sums[6:8, :])


def vector_sum(*refs):
    total = refs[0][...]
    for ref in refs[1:-1]:
        total = total + ref[...]
    refs[-1][...] = total


def vector_join(first, second, *refs, number):
    up_bias, stack, out = refs[:number], refs[number:-1], refs[-1]
    out[...] = first[...] + second[...]
    for row, parts in ((6, up_bias), (7, stack)):
        total = parts[0][...]
        for part in parts[1:]:
            total = total + part[...]
        out[row : row + 1, : total.shape[1]] = total


def add_rows(resid, first, second, third, bias, out):
    out[...] = (resid[...] + three(first, second, third) + bias[...].astype(f32)).astype(bf16)


def swap(values, axis, bit):
    return lax.ppermute(values, axis, [(i, i ^ bit) for i in range(lax.axis_size(axis))])


def ring_order(count):
    return list(range(0, count, 2)) + list(range(1, count, 2))[::-1]


class Ring:
    def __init__(self, chain, where, shapes, stacked):
        self.chain, self.where, self.shapes, self.stacked = chain, where, shapes, stacked
        self.count = lax.axis_size("wide")
        cores = lax.axis_size("narrow")
        order = ring_order(self.count)
        self.perm = [
            (order[i] * cores + n, order[(i + (1 if n % 2 == 0 else -1)) % self.count] * cores + n)
            for i in range(self.count)
            for n in range(cores)
        ]
        self.have, self.step, self.outs = [], 1, None

    def pass_on(self, chunk):
        self.moving = lax.ppermute(chunk, ("wide", "narrow"), self.perm)

    def start(self, chunk, parts):
        self.parts = parts
        self.pass_on(chunk)

    def hold(self):
        self.chain.hold(self.moving)

    def add(self, cover=False):
        (made,) = self.chain.run(
            ring_add,
            [(self.moving.shape, bf16)],
            self.moving,
            *[p[self.step] for p in self.parts],
            cover=cover,
        )
        self.step += 1
        if self.step == self.count:
            self.have.append(made)
        self.pass_on(made)

    def forward(self):
        self.have.append(self.moving)
        self.hold()
        if len(self.have) < self.count:
            self.pass_on(self.moving)

    def store(self, steps):
        moved = [self.have[s] for s in steps]
        kept = () if self.outs is None else self.outs
        number = len(moved)
        made = self.chain.run(
            functools.partial(ring_store, steps=tuple(steps), count=self.count, stacked=self.stacked),
            [((8, LANES), f32)] + [(s, f32) for s in self.shapes],
            *moved,
            *kept,
            smem=(self.where,),
            scratch=[pltpu.VMEM((number, *moved[0].shape), f32), pltpu.SemaphoreType.DMA((2 * number,))],
            alias={number: 1, number + 1: 2} if kept else None,
            anywhere=(number, number + 1) if kept else (),
            out_anywhere=(1, 2),
            limit=6 + (number * moved[0].size * 4 >> 20),
        )
        self.outs = made[1:]


class Whole:
    def __init__(self, shapes):
        self.shapes = shapes

    def start(self, chunk, parts):
        total = lax.psum(chunk, "wide").astype(f32)
        self.outs = (total[: self.shapes[0][0]], total[self.shapes[0][0] :])

    def hold(self):
        pass

    def add(self, cover=False):
        pass

    def forward(self):
        pass

    def store(self, steps):
        pass


def local(
    tokens,
    cotangent,
    cell_of,
    query_count,
    attn_norm_gain,
    attn_norm_bias,
    input_weight,
    query_bias,
    value_bias,
    out_weight,
    out_bias,
    ffn_norm_gain,
    ffn_norm_bias,
    up_weight,
    up_bias,
    down_weight,
    down_bias,
):
    micros = range(tokens.shape[0])
    rows, model = tokens.shape[2], tokens.shape[3]
    parts = lax.axis_size("narrow")
    whole = rows * parts
    width = input_weight.shape[2]
    hidden = up_weight.shape[1]
    count = lax.axis_size("wide")
    rings = count <= 8
    chunks = count if rings else 1
    pairs = head_pairs(width)
    step = min(512, whole)
    chain = Chain()
    run = chain.run
    where = jnp.stack([lax.axis_index("wide"), lax.axis_index("narrow")]).astype(jnp.int32)

    block = ((rows, model), bf16)
    outgoing = [block] * parts
    wide_rows = ((whole, model), bf16)
    row = lambda v: v.reshape(1, -1)
    gain_one, bias_one, gain_two, bias_two = map(row, (attn_norm_gain, attn_norm_bias, ffn_norm_gain, ffn_norm_bias))
    out_bias, down_bias, up_bias = row(out_bias), row(down_bias), row(up_bias)

    def columns(three_parts):
        return jnp.concatenate([v[:, low : low + wide] for low, wide in pairs for v in three_parts], axis=1)

    weight_t = jnp.transpose(input_weight, (1, 2, 0)).reshape(3 * width, model)
    zero = jnp.zeros((1, width), f32)
    project_bias = columns([row(query_bias).astype(f32), zero, row(value_bias).astype(f32)])
    project_scale = columns([zero + score_scale, zero + 1.0, zero + 1.0])

    def gather(own):
        return [own, swap(own, "narrow", 1), swap(own, "narrow", 2)]

    def finish(*arrived, pieces=1, cover=False):
        made = run(
            functools.partial(relay, number=len(arrived)),
            [((rows // pieces, model), bf16)] * (len(arrived) * pieces),
            *[a[2] for a in arrived],
            cover=cover,
        )
        for i, a in enumerate(arrived):
            own = made[i * pieces : (i + 1) * pieces]
            a[2:] = [*own, *[swap(piece, "narrow", 1) for piece in own]]

    def share(made):
        own, near, partner, far = made
        return [own, partner, swap(far, "narrow", 1), swap(near, "narrow", 1)]

    def send(shares):
        own, partner, far, near = shares
        (both,) = run(pair_sum, [block], partner, far)
        return [own, near, swap(both, "narrow", 2)]

    def fresh():
        return [None] * len(micros)

    normed, given, qkv, normed_all, mixed, logs, shares, shares_down, resid, normed_two_b = (fresh() for _ in range(10))
    activ, pre_grad, up_bias_grad, two_all, given_all, resid_grad, top = (fresh() for _ in range(7))
    sums_two, sums_one, stack_sums, out_rows, grad_rows = (fresh() for _ in range(5))
    pair_grads = [[] for _ in micros]

    def do_norm_one(m):
        (own,) = run(functools.partial(norm_one, m=m), [block], tokens, gain_one, bias_one)
        normed[m] = gather(own)

    def do_scale(m):
        (own,) = run(functools.partial(scale_cot, m=m, count=count), [block], cotangent, smem=(where, cell_of, query_count), cover=True)
        given[m] = gather(own)

    def do_project(m):
        qkv[m], normed_all[m] = run(
            functools.partial(project, parts=parts),
            [((whole, 3 * width), bf16), wide_rows],
            *normed[m],
            weight,
            project_bias,
            project_scale,
        )

    def do_attend(m):
        mixed[m], logs[m], *made = run(
            functools.partial(attend, step=whole),
            [((whole, width), bf16), ((8, whole), f32), *outgoing],
            qkv[m],
            out_weight,
            limit=24,
        )
        shares[m] = share(made)

    def do_send(m):
        shares[m] = send(shares[m])

    def do_norm_two(m):
        resid[m], own = run(
            functools.partial(norm_two, m=m),
            [((rows, model), f32), block],
            tokens,
            *shares[m],
            out_bias,
            gain_two,
            bias_two,
            cover=m == 0,
        )
        normed_two_b[m] = gather(own)

    def do_feed(m):
        activ[m], pre_grad[m], up_bias_grad[m], two_all[m], given_all[m] = run(
            functools.partial(feed, parts=parts, blocks=len(normed_two_b[m])),
            [((whole, hidden), bf16), ((whole, hidden), bf16), ((1, hidden), f32), wide_rows, wide_rows],
            *normed_two_b[m],
            *given[m],
            up_weight,
            up_bias,
            down_weight,
        )

    def do_up_back(m):
        shares[m] = share(run(times_back, outgoing, pre_grad[m], up_weight))

    def do_down(m):
        shares_down[m] = share(run(times, outgoing, activ[m], down_weight))

    def do_send_down(m):
        shares_down[m] = send(shares_down[m])

    def do_norm_two_back(m):
        resid_grad[m], own, sums_two[m] = run(
            functools.partial(norm_two_back, m=m, count=count),
            [((rows, model), f32), block, ((8, model), f32)],
            cotangent,
            resid[m],
            *shares[m],
            gain_two,
            smem=(where, cell_of, query_count),
            cover=True,
        )
        top[m] = gather(own)

    def do_attend_back(m, p):
        low, wide = pairs[p]
        (made,) = run(
            functools.partial(attend_back, parts=parts, step=step, low=low, wide=wide),
            [((whole, 3 * wide), bf16)],
            qkv[m],
            logs[m],
            mixed[m],
            out_weight,
            *top[m],
            scratch=[
                pltpu.VMEM((whole, wide), f32),
                pltpu.VMEM((whole, wide), f32),
                pltpu.VMEM((whole, wide), bf16),
                pltpu.VMEM((8 * (wide // HEAD), whole), f32),
            ],
            limit=20,
        )
        pair_grads[m].append(made)

    def do_project_back(m):
        *made, stack_sums[m] = run(
            functools.partial(project_back, pairs=len(pairs)),
            [*outgoing, ((1, 3 * width), f32)],
            *pair_grads[m],
            weight,
        )
        shares[m] = share(made)

    def do_norm_one_back(m):
        grad_rows[m], sums_one[m] = run(
            functools.partial(norm_one_back, m=m),
            [((rows, model), f32), ((8, model), f32)],
            tokens,
            resid_grad[m],
            *shares[m],
            gain_one,
        )

    hops = [("narrow", 1 << k) for k in range(parts.bit_length() - 1)]
    hops += [("wide", 1 << k) for k in range(count.bit_length() - 1)]
    vectors = []

    def do_vectors():
        done = len(vectors)
        shape = [((8, model), f32)]
        if done == 0:
            (own,) = run(vector_sum, shape, *sums_one, *sums_two)
        elif hops[done - 1][0] == "narrow" and hops[done][0] == "wide":
            own, arrived = vectors[-1]
            (own,) = run(
                functools.partial(vector_join, number=len(micros)), shape, own, arrived, *up_bias_grad, *stack_sums
            )
        else:
            (own,) = run(vector_sum, shape, *vectors[-1])
        vectors.append((own, swap(own, *hops[done]) if done < len(hops) else None))

    def do_add_rows(m):
        (out_rows[m],) = run(add_rows, [block], resid[m], *shares_down[m], down_bias)

    def first_product(first, second):
        return run(product, [((first.shape[1], second.shape[1]), bf16)], first, second)[0]

    def ffn_grad(first, second, other, before=()):
        rows, cols = other.shape
        shapes = [((rows // chunks, cols), bf16)] * chunks
        if before:
            shapes.append(((2 * rows // chunks, cols), bf16))
        return run(
            functools.partial(weight_grad, before=len(before[:1])),
            shapes,
            first,
            second,
            other,
            *before[:1],
            smem=(where,),
            scratch=[pltpu.VMEM((rows, cols), bf16)],
            limit=16,
        )

    def attn_grad():
        made = run(
            functools.partial(projection_grad, micros=len(micros), pairs=len(pairs), parts=parts),
            [((4 * width // chunks, model), bf16)] * chunks,
            *normed_all,
            *[g for m in micros for g in pair_grads[m]],
            *[t for m in micros for t in top[m]],
            *mixed,
            smem=(where,),
            scratch=[pltpu.VMEM((4 * width, model), bf16)],
            limit=20,
        )
        attn.start(made[0], (made,))

    ffn_shapes = [(hidden, model), (model, hidden)]
    attn_shapes = [(3 * width, model), (width, model)]
    ffn = Ring(chain, where, ffn_shapes, True) if rings else Whole(ffn_shapes)
    attn = Ring(chain, where, attn_shapes, False) if rings else Whole(attn_shapes)

    do_norm_one(0)
    (weight,) = run(by_pairs, [((3 * width, model), bf16)], weight_t)
    chain.hold(normed[0][1])
    finish(normed[0])
    do_norm_one(1)
    do_scale(0)
    do_project(0)
    do_attend(0)
    chain.hold(normed[1][1], given[0][1])
    finish(normed[1], given[0], cover=True)
    do_scale(1)
    do_send(0)
    chain.hold(given[1][1])
    do_project(1)
    do_attend(1)
    chain.hold(given[1][2])
    do_norm_two(0)
    do_send(1)
    finish(given[1])
    chain.hold(normed_two_b[0][1])
    finish(normed_two_b[0], pieces=4)
    do_feed(0)
    do_norm_two(1)
    chain.hold(normed_two_b[1][1])
    do_up_back(0)
    down_first = first_product(activ[0], given_all[0])
    up_first = first_product(two_all[0], pre_grad[0])
    do_down(0)
    finish(normed_two_b[1], cover=True)
    do_send(0)
    do_feed(1)
    down_chunks = ffn_grad(activ[1], given_all[1], down_first)
    do_norm_two_back(0)
    chain.hold(top[0][1])
    *up_chunks, both = ffn_grad(two_all[1], pre_grad[1], up_first, down_chunks)
    ffn.start(both, (down_chunks, up_chunks))
    do_up_back(1)
    ffn.hold()
    finish(top[0], cover=True)
    do_send(1)
    ffn.add()
    do_attend_back(0, 0)
    ffn.add()
    do_attend_back(0, 1)
    do_norm_two_back(1)
    ffn.add()
    do_attend_back(0, 2)
    do_project_back(0)
    ffn.add()
    chain.hold(top[1][1])
    finish(top[1], cover=True)
    do_attend_back(1, 0)
    do_send_down(0)
    ffn.add()
    do_send(0)
    do_attend_back(1, 1)
    ffn.add()
    do_attend_back(1, 2)
    ffn.add()
    attn_grad()
    ffn.forward()
    attn.add()
    do_project_back(1)
    attn.add()
    do_norm_one_back(0)
    do_down(1)
    ffn.forward()
    attn.add()
    do_send(1)
    attn.add()
    do_send_down(1)
    ffn.forward()
    attn.add()
    attn.add()
    do_norm_one_back(1)
    do_vectors()
    ffn.store(range(0, 2))
    ffn.forward()
    attn.add()
    do_vectors()
    do_add_rows(0)
    attn.forward()
    do_vectors()
    do_add_rows(1)
    ffn.forward()
    attn.forward()
    do_vectors()
    ffn.store(range(2, 4))
    attn.forward()
    do_vectors()
    attn.store(range(0, 3))
    ffn.forward()
    attn.forward()
    do_vectors()
    ffn.store(range(4, 6))
    attn.forward()
    attn.store(range(3, 5))
    ffn.forward()
    attn.forward()
    ffn.store(range(6, 8))
    attn.store(range(5, 7))
    attn.forward()
    attn.store(range(7, 8))

    while len(vectors) <= len(hops):
        do_vectors()
    vector_sums = vectors[-1][0]
    up_bias_sum = vector_sums[6, :hidden]
    stack_sum = vector_sums[7, : 3 * width]

    def plain(j):
        return jnp.concatenate([stack_sum[3 * low + j * wide : 3 * low + (j + 1) * wide] for low, wide in pairs])

    return (
        jnp.stack(out_rows)[:, None],
        jnp.stack(grad_rows)[:, None],
        vector_sums[4],
        vector_sums[5],
        jnp.transpose(attn.outs[0].reshape(3, width, model), (2, 0, 1)),
        plain(0),
        plain(2),
        attn.outs[1],
        vector_sums[0],
        vector_sums[1],
        vector_sums[2],
        ffn.outs[1],
        up_bias_sum,
        ffn.outs[0],
        vector_sums[3],
    )


def solution(mesh):
    in_specs = (
        P(None, "wide", "narrow", None),
        P(None, "wide", "narrow", None),
        P(),
        P(),
        P(),
        P(),
        P(None, None, "narrow"),
        P("narrow"),
        P("narrow"),
        P("narrow", None),
        P(),
        P(),
        P(),
        P(None, "narrow"),
        P("narrow"),
        P("narrow", None),
        P(),
    )
    out_specs = (
        P(None, "wide", "narrow", None),
        P(None, "wide", "narrow", None),
        P(),
        P(),
        P(None, None, "narrow"),
        P("narrow"),
        P("narrow"),
        P("narrow", None),
        P(),
        P(),
        P(),
        P(None, "narrow"),
        P("narrow"),
        P("narrow", None),
        P(),
    )
    return jax.shard_map(local, mesh=mesh, in_specs=in_specs, out_specs=out_specs, check_vma=False)
```

```python
import functools

import jax
import jax.numpy as jnp
from jax import lax
from jax.experimental import pallas as pl
from jax.experimental.pallas import tpu as pltpu
from jax.sharding import PartitionSpec as P

HEAD = 64
LANES = 128
TILE = 256
norm_eps = 1e-05
score_scale = 0.125
bf16 = jnp.bfloat16
f32 = jnp.float32


class Chain:
    def __init__(self):
        self.last = []
        self.held = []

    def hold(self, *arrays):
        self.held += arrays

    def run(self, body, outs, *ins, smem=(), scratch=(), alias=None, anywhere=(), out_anywhere=(), limit=6, token=0, cover=False):
        unread = [*self.last, *self.held]
        count = len(smem) + len(ins)
        specs = [pl.BlockSpec(memory_space=pltpu.SMEM)] * len(smem)
        specs += [pl.BlockSpec(memory_space=pl.ANY if i in anywhere else pltpu.VMEM) for i in range(len(ins))]
        specs += [pl.BlockSpec(memory_space=pl.ANY)] * len(unread)

        def inner(*refs):
            body(*refs[:count], *refs[count + len(unread) :])

        made = pl.pallas_call(
            inner,
            out_shape=tuple(jax.ShapeDtypeStruct(*o) for o in outs),
            in_specs=specs,
            out_specs=tuple(
                pl.BlockSpec(memory_space=pl.ANY if i in out_anywhere else pltpu.VMEM) for i in range(len(outs))
            ),
            scratch_shapes=scratch,
            input_output_aliases={} if alias is None else {len(smem) + k: v for k, v in alias.items()},
            compiler_params=pltpu.CompilerParams(vmem_limit_bytes=limit << 20),
            cost_estimate=pl.CostEstimate(flops=10**12 if cover else 1, bytes_accessed=1, transcendentals=0),
            name=body.func.__name__ if isinstance(body, functools.partial) else body.__name__,
        )(*smem, *ins, *unread)
        self.last, self.held = [made[token]], []
        return made


def dot32(first, second, first_dim, second_dim):
    return lax.dot_general(
        first, second, (((first_dim,), (second_dim,)), ((), ())), preferred_element_type=f32
    )


def statistics(values):
    average = jnp.mean(values, axis=-1, keepdims=True)
    centred = values - average
    inverse = lax.rsqrt(jnp.mean(centred * centred, axis=-1, keepdims=True) + norm_eps)
    return centred * inverse, inverse


def norm_back(grad, normed, inverse, gain):
    scaled = grad * gain
    mean_one = jnp.mean(scaled, axis=-1, keepdims=True)
    mean_two = jnp.mean(scaled * normed, axis=-1, keepdims=True)
    return inverse * (scaled - mean_one - normed * mean_two)


def of_head(values, j, axis=1):
    if values.shape[axis] <= HEAD:
        return values
    place = lax.broadcasted_iota(jnp.int32, values.shape, axis)
    return jnp.where((place >= HEAD * j) & (place < HEAD * (j + 1)), values, jnp.zeros_like(values))


def head_pairs(width):
    return [(low, min(LANES, width - low)) for low in range(0, width, LANES)]


def relay(*refs, number):
    arrived, outs = refs[:number], refs[number:]
    each = len(outs) // number
    for i, rows in enumerate(arrived):
        size = rows.shape[0] // each
        for k in range(each):
            outs[i * each + k][...] = rows[k * size : (k + 1) * size, :]


def by_pairs(weight_t, out):
    width = out.shape[0] // 3
    for low, wide in head_pairs(width):
        for j in range(3):
            out[3 * low + j * wide : 3 * low + (j + 1) * wide, :] = weight_t[
                j * width + low : j * width + low + wide, :
            ]


def norm_one(tok, gain, bias, out, *, m):
    normed, _ = statistics(tok[m, 0].astype(f32))
    out[...] = (normed * gain[...].astype(f32) + bias[...].astype(f32)).astype(bf16)


def loss_grad(where, cells, queries, cot, m, count):
    number = queries[cells[where[0] + m * count]]
    scale = jnp.sqrt(jnp.full((1, cot.shape[3]), number, jnp.int32).astype(f32) / 500.0)
    return cot[m, 0].astype(f32) * scale


def scale_cot(where, cells, queries, cot, out, *, m, count):
    out[...] = loss_grad(where, cells, queries, cot, m, count).astype(bf16)


def project(*refs, parts):
    blocks = refs[:parts]
    weight, bias, scale = refs[parts : parts + 3]
    out, whole = refs[parts + 3 :]
    rows = blocks[0].shape[0]
    for b in range(parts):
        values = blocks[b][...]
        at = slice(b * rows, (b + 1) * rows)
        whole[at, :] = values
        out[at, :] = ((dot32(values, weight[...], 1, 1) + bias[...]) * scale[...]).astype(bf16)


def attend(qkv, out_weight, attended, logs, *outs, step):
    whole = qkv.shape[0]
    head = 0
    for low, wide in head_pairs(out_weight.shape[0]):
        heads = wide // HEAD
        key_pair = qkv[:, 3 * low + wide : 3 * low + 2 * wide]
        value_t = qkv[:, 3 * low + 2 * wide : 3 * low + 3 * wide].T
        keys = [of_head(key_pair, j) for j in range(heads)]
        values = [of_head(value_t, j, 0) for j in range(heads)]
        for start in range(0, whole, step):
            at = slice(start, start + step)
            query = qkv[at, 3 * low : 3 * low + wide]
            total = None
            for j in range(heads):
                scores = dot32(keys[j], query, 1, 1)
                top = jnp.max(scores, axis=0, keepdims=True)
                powers = jnp.exp(scores - top)
                length = jnp.sum(powers, axis=0, keepdims=True)
                mixed = dot32(values[j], powers.astype(bf16), 1, 0) * (1.0 / length)
                total = mixed if total is None else total + mixed
                logs[head + j : head + j + 1, at] = top + jnp.log(length)
            attended[at, low : low + wide] = total.T.astype(bf16)
        head += heads
    rows = whole // len(outs)
    for b, out in enumerate(outs):
        out[...] = dot32(attended[b * rows : (b + 1) * rows, :], out_weight[...], 1, 0).astype(bf16)


def pair_sum(first, second, out):
    out[...] = (first[...].astype(f32) + second[...].astype(f32)).astype(bf16)


def three(first, second, third):
    return first[...].astype(f32) + second[...].astype(f32) + third[...].astype(f32)


def norm_two(tok, first, second, third, out_bias, gain, bias, resid, normed, *, m):
    value = tok[m, 0].astype(f32) + three(first, second, third) + out_bias[...].astype(f32)
    resid[...] = value
    hat, _ = statistics(value)
    normed[...] = (hat * gain[...].astype(f32) + bias[...].astype(f32)).astype(bf16)


def feed(*refs, parts, blocks):
    normed, grads, refs = refs[:blocks], refs[blocks : blocks + parts], refs[blocks + parts :]
    up, up_bias, down, activ, pre_grad, bias_grad, normed_all, grads_all = refs
    for whole, pieces in ((normed_all, normed), (grads_all, grads)):
        low = 0
        for piece in pieces:
            whole[low : low + piece.shape[0], :] = piece[...]
            low += piece.shape[0]
    rows = grads[0].shape[0]
    for low in range(0, up.shape[1], TILE):
        cols = slice(low, low + TILE)
        total = None
        for b in range(parts):
            at = slice(b * rows, (b + 1) * rows)
            pre = dot32(normed_all[at, :], up[:, cols], 1, 0) + up_bias[:, cols].astype(f32)
            cumul = 0.5 + 0.5 * lax.erf(pre * 0.7071067811865476)
            density = jnp.exp(-0.5 * pre * pre) * 0.3989422804014327
            activ[at, cols] = (pre * cumul).astype(bf16)
            back = dot32(grads_all[at, :], down[cols, :], 1, 1)
            grad = (back * (cumul + pre * density)).astype(bf16)
            pre_grad[at, cols] = grad
            part = jnp.sum(grad.astype(f32), axis=0, keepdims=True)
            total = part if total is None else total + part
        bias_grad[:, cols] = total


def times(value, weight, *outs):
    put_tiles(outs, lambda at, cols: dot32(value[at, :], weight[:, cols], 1, 0), value.shape[0])


def times_back(value, weight, *outs):
    put_tiles(outs, lambda at, cols: dot32(value[at, :], weight[cols, :], 1, 1), value.shape[0])


def put_tiles(outs, share_of, whole):
    rows, model = outs[0].shape

    def tile(i, carry):
        cols = pl.ds(pl.multiple_of(i * TILE, TILE), TILE)
        for b, out in enumerate(outs):
            out[:, cols] = share_of(slice(b * rows, (b + 1) * rows), cols).astype(bf16)
        return carry

    lax.fori_loop(0, model // TILE, tile, 0)


def product(first, second, out):
    def tile(i, carry):
        rows = pl.ds(pl.multiple_of(i * TILE, TILE), TILE)
        out[rows, :] = dot32(first[:, rows], second[...], 0, 0).astype(bf16)
        return carry

    lax.fori_loop(0, out.shape[0] // TILE, tile, 0)


def weight_grad(where, first, second, other, *refs, before):
    chunks, whole = refs[before:-1], refs[-1]

    def tile(i, carry):
        rows = pl.ds(pl.multiple_of(i * TILE, TILE), TILE)
        total = dot32(first[:, rows], second[...], 0, 0) + other[rows, :].astype(f32)
        whole[rows, :] = total.astype(bf16)
        return carry

    lax.fori_loop(0, whole.shape[0] // TILE, tile, 0)
    if before:
        chunks, both = chunks[:-1], chunks[-1]
        size = chunks[0].shape[0]
        both[:size, :] = refs[0][...]
        put_chunks(where, chunks, whole)
        both[size:, :] = chunks[0][...]
    else:
        put_chunks(where, chunks, whole)


def ring_chunk(where, count, step):
    half = where[0] // 2
    place = jnp.where(where[0] % 2 == 0, half, count - 1 - half)
    return lax.rem(place + jnp.where(where[1] % 2 == 0, count - step, step), count)


def put_chunks(where, chunks, whole):
    for s, chunk in enumerate(chunks):
        size = chunk.shape[0]
        which = ring_chunk(where, len(chunks), (s + 1) % len(chunks)) if len(chunks) > 1 else 0
        chunk[...] = whole[pl.ds(pl.multiple_of(which * size, size), size), :]


def norm_two_back(where, cells, queries, cot, resid, first, second, third, gain, out, rounded, sums, *, m, count):
    top = loss_grad(where, cells, queries, cot, m, count)
    grad = three(first, second, third)
    hat, inverse = statistics(resid[...])
    back = top + norm_back(grad, hat, inverse, gain[...].astype(f32))
    out[...] = back
    rounded[...] = back.astype(bf16)
    sums[0:1, :] = jnp.sum(back, axis=0, keepdims=True)
    sums[1:2, :] = jnp.sum(grad * hat, axis=0, keepdims=True)
    sums[2:3, :] = jnp.sum(grad, axis=0, keepdims=True)
    sums[3:4, :] = jnp.sum(top, axis=0, keepdims=True)
    sums[4:8, :] = jnp.zeros_like(sums[4:8, :])


def attend_back(qkv, logs, mixed, out_weight, *refs, parts, step, low, wide):
    grads = refs[:parts]
    out, key_grad, value_grad, given, inner = refs[parts:]
    whole = qkv.shape[0]
    rows = whole // parts
    heads = wide // HEAD
    head = low // HEAD
    ones = jnp.concatenate([of_head(jnp.ones((8, wide), bf16), j) for j in range(heads)], axis=0)
    for b in range(parts):
        at = slice(b * rows, (b + 1) * rows)
        value = dot32(grads[b][...], out_weight[low : low + wide, :], 1, 1).astype(bf16)
        given[at, :] = value
        both = value.astype(f32) * mixed[at, low : low + wide].astype(f32)
        high = both.astype(bf16)
        rest = (both - high.astype(f32)).astype(bf16)
        inner[:, at] = dot32(ones, high, 1, 1) + dot32(ones, rest, 1, 1)
    key_pair = qkv[:, 3 * low + wide : 3 * low + 2 * wide]
    value_pair = qkv[:, 3 * low + 2 * wide : 3 * low + 3 * wide]
    key_t = key_pair.T
    keys = [of_head(key_pair, j) for j in range(heads)]
    values = [of_head(value_pair, j) for j in range(heads)]
    keys_t = [of_head(key_t, j, 0) for j in range(heads)]
    key_grad[...] = jnp.zeros_like(key_grad)
    value_grad[...] = jnp.zeros_like(value_grad)

    def block(i, carry):
        start = pl.multiple_of(i * step, step)
        query = qkv[pl.ds(start, step), 3 * low : 3 * low + wide]
        grad = given[pl.ds(start, step), :]
        total = None
        for j in range(heads):
            scores = dot32(keys[j], query, 1, 1)
            weights = jnp.exp(scores - logs[head + j : head + j + 1, pl.ds(start, step)])
            back = dot32(values[j], grad, 1, 1)
            score_grad = (weights * (back - inner[8 * j : 8 * j + 1, pl.ds(start, step)])).astype(bf16)
            value_grad[...] += dot32(weights.astype(bf16), of_head(grad, j), 1, 0)
            key_grad[...] += dot32(score_grad, of_head(query, j), 1, 0)
            part = dot32(keys_t[j], score_grad, 1, 0)
            total = part if total is None else total + part
        out[pl.ds(start, step), :wide] = (total.T * score_scale).astype(bf16)
        return carry

    lax.fori_loop(0, whole // step, block, 0)
    out[:, wide : 2 * wide] = key_grad[...].astype(bf16)
    out[:, 2 * wide :] = value_grad[...].astype(bf16)


def project_back(*refs, pairs):
    grads, weight, outs, sums = refs[:pairs], refs[pairs], refs[pairs + 1 : -1], refs[-1]

    def share_of(at, cols):
        total, low = None, 0
        for grad in grads:
            wide = grad.shape[1]
            part = dot32(grad[at, :], weight[low : low + wide, cols], 1, 0)
            total = part if total is None else total + part
            low += wide
        return total

    put_tiles(outs, share_of, grads[0].shape[0])
    low = 0
    for grad in grads:
        wide = grad.shape[1]
        sums[:, low : low + wide] = jnp.sum(grad[...].astype(f32), axis=0, keepdims=True)
        low += wide


def projection_grad(where, *refs, micros, pairs, parts):
    normed, refs = refs[:micros], refs[micros:]
    grads, refs = [refs[m * pairs : (m + 1) * pairs] for m in range(micros)], refs[micros * pairs :]
    tops, refs = [refs[m * parts : (m + 1) * parts] for m in range(micros)], refs[micros * parts :]
    mixed, refs = refs[:micros], refs[micros:]
    chunks, out = refs[:-1], refs[-1]
    width = mixed[0].shape[1]
    rows = tops[0][0].shape[0]
    for p, (low, wide) in enumerate(head_pairs(width)):
        total = None
        for m in range(micros):
            part = dot32(grads[m][p][...], normed[m][...], 0, 0)
            total = part if total is None else total + part
        for j in range(3):
            out[j * width + low : j * width + low + wide, :] = total[j * wide : (j + 1) * wide].astype(bf16)
        total = None
        for m in range(micros):
            for b in range(parts):
                part = dot32(mixed[m][b * rows : (b + 1) * rows, low : low + wide], tops[m][b][...], 0, 0)
                total = part if total is None else total + part
        out[3 * width + low : 3 * width + low + wide, :] = total.astype(bf16)
    put_chunks(where, chunks, out)


def ring_add(arrived, *refs):
    low = 0
    for part in refs[:-1]:
        at = slice(low, low + part.shape[0])
        refs[-1][at, :] = (arrived[at, :].astype(f32) + part[...].astype(f32)).astype(bf16)
        low += part.shape[0]


def ring_store(where, *refs, steps, count, stacked):
    moved, refs = refs[: len(steps)], refs[len(steps) :]
    done, first, second, buffer, sems = refs[-5:]
    done[...] = jnp.zeros_like(done)
    size = buffer.shape[1] // 2 if stacked else buffer.shape[1]
    copies = []
    for k, step in enumerate(steps):
        buffer[k] = moved[k][...].astype(f32)
        row = pl.multiple_of(ring_chunk(where, count, step) * size, size)
        if stacked:
            for i, target in enumerate((first, second)):
                source = buffer.at[k, pl.ds(i * size, size), :]
                copies.append(pltpu.make_async_copy(source, target.at[pl.ds(row, size), :], sems.at[2 * k + i]))
                copies[-1].start()
        else:
            last = first.shape[0] - size
            to_first = pl.multiple_of(jnp.minimum(row, last), 16)
            to_second = pl.multiple_of(jnp.maximum(row - first.shape[0], 0), 16)
            copy_first = pltpu.make_async_copy(buffer.at[k], first.at[pl.ds(to_first, size), :], sems.at[2 * k])
            copy_second = pltpu.make_async_copy(buffer.at[k], second.at[pl.ds(to_second, size), :], sems.at[2 * k])
            pl.when(row <= last)(copy_first.start)
            pl.when(row > last)(copy_second.start)
            copies.append(copy_first)
    for copy in copies:
        copy.wait()


def norm_one_back(tok, resid_grad, first, second, third, gain, out, sums, *, m):
    grad = three(first, second, third)
    hat, inverse = statistics(tok[m, 0].astype(f32))
    out[...] = resid_grad[...] + norm_back(grad, hat, inverse, gain[...].astype(f32))
    sums[0:4, :] = jnp.zeros_like(sums[0:4, :])
    sums[4:5, :] = jnp.sum(grad * hat, axis=0, keepdims=True)
    sums[5:6, :] = jnp.sum(grad, axis=0, keepdims=True)
    sums[6:8, :] = jnp.zeros_like(sums[6:8, :])


def vector_sum(*refs):
    total = refs[0][...]
    for ref in refs[1:-1]:
        total = total + ref[...]
    refs[-1][...] = total


def vector_join(first, second, *refs, number):
    up_bias, stack, out = refs[:number], refs[number:-1], refs[-1]
    out[...] = first[...] + second[...]
    for row, parts in ((6, up_bias), (7, stack)):
        total = parts[0][...]
        for part in parts[1:]:
            total = total + part[...]
        out[row : row + 1, : total.shape[1]] = total


def add_rows(resid, first, second, third, bias, out):
    out[...] = (resid[...] + three(first, second, third) + bias[...].astype(f32)).astype(bf16)


def swap(values, axis, bit):
    return lax.ppermute(values, axis, [(i, i ^ bit) for i in range(lax.axis_size(axis))])


def ring_order(count):
    return list(range(0, count, 2)) + list(range(1, count, 2))[::-1]


class Ring:
    def __init__(self, chain, where, shapes, stacked):
        self.chain, self.where, self.shapes, self.stacked = chain, where, shapes, stacked
        self.count = lax.axis_size("wide")
        cores = lax.axis_size("narrow")
        order = ring_order(self.count)
        self.perm = [
            (order[i] * cores + n, order[(i + (1 if n % 2 == 0 else -1)) % self.count] * cores + n)
            for i in range(self.count)
            for n in range(cores)
        ]
        self.have, self.step, self.outs = [], 1, None

    def pass_on(self, chunk):
        self.moving = lax.ppermute(chunk, ("wide", "narrow"), self.perm)

    def start(self, chunk, parts):
        self.parts = parts
        self.pass_on(chunk)

    def hold(self):
        self.chain.hold(self.moving)

    def add(self, cover=False):
        (made,) = self.chain.run(
            ring_add,
            [(self.moving.shape, bf16)],
            self.moving,
            *[p[self.step] for p in self.parts],
            cover=cover,
        )
        self.step += 1
        if self.step == self.count:
            self.have.append(made)
        self.pass_on(made)

    def forward(self):
        self.have.append(self.moving)
        self.hold()
        if len(self.have) < self.count:
            self.pass_on(self.moving)

    def store(self, steps):
        moved = [self.have[s] for s in steps]
        kept = () if self.outs is None else self.outs
        number = len(moved)
        made = self.chain.run(
            functools.partial(ring_store, steps=tuple(steps), count=self.count, stacked=self.stacked),
            [((8, LANES), f32)] + [(s, f32) for s in self.shapes],
            *moved,
            *kept,
            smem=(self.where,),
            scratch=[pltpu.VMEM((number, *moved[0].shape), f32), pltpu.SemaphoreType.DMA((2 * number,))],
            alias={number: 1, number + 1: 2} if kept else None,
            anywhere=(number, number + 1) if kept else (),
            out_anywhere=(1, 2),
            limit=6 + (number * moved[0].size * 4 >> 20),
        )
        self.outs = made[1:]


class Whole:
    def __init__(self, shapes):
        self.shapes = shapes

    def start(self, chunk, parts):
        total = lax.psum(chunk, "wide").astype(f32)
        self.outs = (total[: self.shapes[0][0]], total[self.shapes[0][0] :])

    def hold(self):
        pass

    def add(self, cover=False):
        pass

    def forward(self):
        pass

    def store(self, steps):
        pass


def local(
    tokens,
    cotangent,
    cell_of,
    query_count,
    attn_norm_gain,
    attn_norm_bias,
    input_weight,
    query_bias,
    value_bias,
    out_weight,
    out_bias,
    ffn_norm_gain,
    ffn_norm_bias,
    up_weight,
    up_bias,
    down_weight,
    down_bias,
):
    micros = range(tokens.shape[0])
    rows, model = tokens.shape[2], tokens.shape[3]
    parts = lax.axis_size("narrow")
    whole = rows * parts
    width = input_weight.shape[2]
    hidden = up_weight.shape[1]
    count = lax.axis_size("wide")
    rings = count <= 8
    chunks = count if rings else 1
    pairs = head_pairs(width)
    step = min(512, whole)
    chain = Chain()
    run = chain.run
    where = jnp.stack([lax.axis_index("wide"), lax.axis_index("narrow")]).astype(jnp.int32)

    block = ((rows, model), bf16)
    outgoing = [block] * parts
    wide_rows = ((whole, model), bf16)
    row = lambda v: v.reshape(1, -1)
    gain_one, bias_one, gain_two, bias_two = map(row, (attn_norm_gain, attn_norm_bias, ffn_norm_gain, ffn_norm_bias))
    out_bias, down_bias, up_bias = row(out_bias), row(down_bias), row(up_bias)

    def columns(three_parts):
        return jnp.concatenate([v[:, low : low + wide] for low, wide in pairs for v in three_parts], axis=1)

    weight_t = jnp.transpose(input_weight, (1, 2, 0)).reshape(3 * width, model)
    zero = jnp.zeros((1, width), f32)
    project_bias = columns([row(query_bias).astype(f32), zero, row(value_bias).astype(f32)])
    project_scale = columns([zero + score_scale, zero + 1.0, zero + 1.0])

    def gather(own):
        return [own, swap(own, "narrow", 1), swap(own, "narrow", 2)]

    def finish(*arrived, pieces=1, cover=False):
        made = run(
            functools.partial(relay, number=len(arrived)),
            [((rows // pieces, model), bf16)] * (len(arrived) * pieces),
            *[a[2] for a in arrived],
            cover=cover,
        )
        for i, a in enumerate(arrived):
            own = made[i * pieces : (i + 1) * pieces]
            a[2:] = [*own, *[swap(piece, "narrow", 1) for piece in own]]

    def share(made):
        own, near, partner, far = made
        return [own, partner, swap(far, "narrow", 1), swap(near, "narrow", 1)]

    def send(shares):
        own, partner, far, near = shares
        (both,) = run(pair_sum, [block], partner, far)
        return [own, near, swap(both, "narrow", 2)]

    def fresh():
        return [None] * len(micros)

    normed, given, qkv, normed_all, mixed, logs, shares, shares_down, resid, normed_two_b = (fresh() for _ in range(10))
    activ, pre_grad, up_bias_grad, two_all, given_all, resid_grad, top = (fresh() for _ in range(7))
    sums_two, sums_one, stack_sums, out_rows, grad_rows = (fresh() for _ in range(5))
    pair_grads = [[] for _ in micros]

    def do_norm_one(m):
        (own,) = run(functools.partial(norm_one, m=m), [block], tokens, gain_one, bias_one)
        normed[m] = gather(own)

    def do_scale(m):
        (own,) = run(functools.partial(scale_cot, m=m, count=count), [block], cotangent, smem=(where, cell_of, query_count), cover=True)
        given[m] = gather(own)

    def do_project(m):
        qkv[m], normed_all[m] = run(
            functools.partial(project, parts=parts),
            [((whole, 3 * width), bf16), wide_rows],
            *normed[m],
            weight,
            project_bias,
            project_scale,
        )

    def do_attend(m):
        mixed[m], logs[m], *made = run(
            functools.partial(attend, step=whole),
            [((whole, width), bf16), ((8, whole), f32), *outgoing],
            qkv[m],
            out_weight,
            limit=24,
        )
        shares[m] = share(made)

    def do_send(m):
        shares[m] = send(shares[m])

    def do_norm_two(m):
        resid[m], own = run(
            functools.partial(norm_two, m=m),
            [((rows, model), f32), block],
            tokens,
            *shares[m],
            out_bias,
            gain_two,
            bias_two,
            cover=m == 0,
        )
        normed_two_b[m] = gather(own)

    def do_feed(m):
        activ[m], pre_grad[m], up_bias_grad[m], two_all[m], given_all[m] = run(
            functools.partial(feed, parts=parts, blocks=len(normed_two_b[m])),
            [((whole, hidden), bf16), ((whole, hidden), bf16), ((1, hidden), f32), wide_rows, wide_rows],
            *normed_two_b[m],
            *given[m],
            up_weight,
            up_bias,
            down_weight,
        )

    def do_up_back(m):
        shares[m] = share(run(times_back, outgoing, pre_grad[m], up_weight))

    def do_down(m):
        shares_down[m] = share(run(times, outgoing, activ[m], down_weight))

    def do_send_down(m):
        shares_down[m] = send(shares_down[m])

    def do_norm_two_back(m):
        resid_grad[m], own, sums_two[m] = run(
            functools.partial(norm_two_back, m=m, count=count),
            [((rows, model), f32), block, ((8, model), f32)],
            cotangent,
            resid[m],
            *shares[m],
            gain_two,
            smem=(where, cell_of, query_count),
            cover=True,
        )
        top[m] = gather(own)

    def do_attend_back(m, p):
        low, wide = pairs[p]
        (made,) = run(
            functools.partial(attend_back, parts=parts, step=step, low=low, wide=wide),
            [((whole, 3 * wide), bf16)],
            qkv[m],
            logs[m],
            mixed[m],
            out_weight,
            *top[m],
            scratch=[
                pltpu.VMEM((whole, wide), f32),
                pltpu.VMEM((whole, wide), f32),
                pltpu.VMEM((whole, wide), bf16),
                pltpu.VMEM((8 * (wide // HEAD), whole), f32),
            ],
            limit=20,
        )
        pair_grads[m].append(made)

    def do_project_back(m):
        *made, stack_sums[m] = run(
            functools.partial(project_back, pairs=len(pairs)),
            [*outgoing, ((1, 3 * width), f32)],
            *pair_grads[m],
            weight,
        )
        shares[m] = share(made)

    def do_norm_one_back(m):
        grad_rows[m], sums_one[m] = run(
            functools.partial(norm_one_back, m=m),
            [((rows, model), f32), ((8, model), f32)],
            tokens,
            resid_grad[m],
            *shares[m],
            gain_one,
        )

    hops = [("narrow", 1 << k) for k in range(parts.bit_length() - 1)]
    hops += [("wide", 1 << k) for k in range(count.bit_length() - 1)]
    vectors = []

    def do_vectors():
        done = len(vectors)
        shape = [((8, model), f32)]
        if done == 0:
            (own,) = run(vector_sum, shape, *sums_one, *sums_two)
        elif hops[done - 1][0] == "narrow" and hops[done][0] == "wide":
            own, arrived = vectors[-1]
            (own,) = run(
                functools.partial(vector_join, number=len(micros)), shape, own, arrived, *up_bias_grad, *stack_sums
            )
        else:
            (own,) = run(vector_sum, shape, *vectors[-1])
        vectors.append((own, swap(own, *hops[done]) if done < len(hops) else None))

    def do_add_rows(m):
        (out_rows[m],) = run(add_rows, [block], resid[m], *shares_down[m], down_bias)

    def first_product(first, second):
        return run(product, [((first.shape[1], second.shape[1]), bf16)], first, second)[0]

    def ffn_grad(first, second, other, before=()):
        rows, cols = other.shape
        shapes = [((rows // chunks, cols), bf16)] * chunks
        if before:
            shapes.append(((2 * rows // chunks, cols), bf16))
        return run(
            functools.partial(weight_grad, before=len(before[:1])),
            shapes,
            first,
            second,
            other,
            *before[:1],
            smem=(where,),
            scratch=[pltpu.VMEM((rows, cols), bf16)],
            limit=16,
        )

    def attn_grad():
        made = run(
            functools.partial(projection_grad, micros=len(micros), pairs=len(pairs), parts=parts),
            [((4 * width // chunks, model), bf16)] * chunks,
            *normed_all,
            *[g for m in micros for g in pair_grads[m]],
            *[t for m in micros for t in top[m]],
            *mixed,
            smem=(where,),
            scratch=[pltpu.VMEM((4 * width, model), bf16)],
            limit=20,
        )
        attn.start(made[0], (made,))

    ffn_shapes = [(hidden, model), (model, hidden)]
    attn_shapes = [(3 * width, model), (width, model)]
    ffn = Ring(chain, where, ffn_shapes, True) if rings else Whole(ffn_shapes)
    attn = Ring(chain, where, attn_shapes, False) if rings else Whole(attn_shapes)

    do_norm_one(0)
    (weight,) = run(by_pairs, [((3 * width, model), bf16)], weight_t)
    chain.hold(normed[0][1])
    finish(normed[0])
    do_norm_one(1)
    do_scale(0)
    do_project(0)
    do_attend(0)
    chain.hold(normed[1][1], given[0][1])
    finish(normed[1], given[0], cover=True)
    do_scale(1)
    do_send(0)
    chain.hold(given[1][1])
    do_project(1)
    do_attend(1)
    chain.hold(given[1][2])
    do_norm_two(0)
    do_send(1)
    finish(given[1])
    chain.hold(normed_two_b[0][1])
    finish(normed_two_b[0], pieces=4)
    do_feed(0)
    do_norm_two(1)
    chain.hold(normed_two_b[1][1])
    do_up_back(0)
    down_first = first_product(activ[0], given_all[0])
    up_first = first_product(two_all[0], pre_grad[0])
    do_down(0)
    finish(normed_two_b[1], cover=True)
    do_send(0)
    do_feed(1)
    do_up_back(1)
    do_norm_two_back(0)
    chain.hold(top[0][1])
    down_chunks = ffn_grad(activ[1], given_all[1], down_first)
    *up_chunks, both = ffn_grad(two_all[1], pre_grad[1], up_first, down_chunks)
    ffn.start(both, (down_chunks, up_chunks))
    finish(top[0], cover=True)
    do_send(1)
    ffn.add()
    do_attend_back(0, 0)
    ffn.add()
    do_attend_back(0, 1)
    do_norm_two_back(1)
    ffn.add()
    do_attend_back(0, 2)
    do_project_back(0)
    ffn.add()
    chain.hold(top[1][1])
    finish(top[1], cover=True)
    do_attend_back(1, 0)
    do_send_down(0)
    ffn.add()
    do_send(0)
    do_attend_back(1, 1)
    ffn.add()
    do_attend_back(1, 2)
    attn_grad()
    ffn.add()
    attn.add()
    do_project_back(1)
    attn.add()
    do_send(1)
    ffn.forward()
    do_norm_one_back(0)
    attn.add()
    do_down(1)
    attn.add()
    do_norm_one_back(1)
    do_vectors()
    ffn.forward()
    attn.add()
    do_vectors()
    do_send_down(1)
    attn.add()
    do_vectors()
    ffn.forward()
    ffn.store(range(0, 2))
    attn.add()
    do_vectors()
    attn.forward()
    do_add_rows(0)
    do_vectors()
    ffn.forward()
    attn.forward()
    do_vectors()
    ffn.store(range(2, 4))
    attn.forward()
    do_add_rows(1)
    attn.store(range(0, 3))
    ffn.forward()
    attn.forward()
    ffn.store(range(4, 6))
    attn.forward()
    attn.store(range(3, 5))
    ffn.forward()
    attn.forward()
    attn.store(range(5, 7))
    ffn.forward()
    ffn.store(range(6, 8))
    attn.forward()
    attn.store(range(7, 8))

    while len(vectors) <= len(hops):
        do_vectors()
    vector_sums = vectors[-1][0]
    up_bias_sum = vector_sums[6, :hidden]
    stack_sum = vector_sums[7, : 3 * width]

    def plain(j):
        return jnp.concatenate([stack_sum[3 * low + j * wide : 3 * low + (j + 1) * wide] for low, wide in pairs])

    return (
        jnp.stack(out_rows)[:, None],
        jnp.stack(grad_rows)[:, None],
        vector_sums[4],
        vector_sums[5],
        jnp.transpose(attn.outs[0].reshape(3, width, model), (2, 0, 1)),
        plain(0),
        plain(2),
        attn.outs[1],
        vector_sums[0],
        vector_sums[1],
        vector_sums[2],
        ffn.outs[1],
        up_bias_sum,
        ffn.outs[0],
        vector_sums[3],
    )


def solution(mesh):
    in_specs = (
        P(None, "wide", "narrow", None),
        P(None, "wide", "narrow", None),
        P(),
        P(),
        P(),
        P(),
        P(None, None, "narrow"),
        P("narrow"),
        P("narrow"),
        P("narrow", None),
        P(),
        P(),
        P(),
        P(None, "narrow"),
        P("narrow"),
        P("narrow", None),
        P(),
    )
    out_specs = (
        P(None, "wide", "narrow", None),
        P(None, "wide", "narrow", None),
        P(),
        P(),
        P(None, None, "narrow"),
        P("narrow"),
        P("narrow"),
        P("narrow", None),
        P(),
        P(),
        P(),
        P(None, "narrow"),
        P("narrow"),
        P("narrow", None),
        P(),
    )
    return jax.shard_map(local, mesh=mesh, in_specs=in_specs, out_specs=out_specs, check_vma=False)
```

```python
import functools

import jax
import jax.numpy as jnp
from jax import lax
from jax.experimental import pallas as pl
from jax.experimental.pallas import tpu as pltpu
from jax.sharding import PartitionSpec as P

HEAD = 64
LANES = 128
TILE = 256
norm_eps = 1e-05
score_scale = 0.125
bf16 = jnp.bfloat16
f32 = jnp.float32


class Chain:
    def __init__(self):
        self.last = []
        self.held = []

    def hold(self, *arrays):
        self.held += arrays

    def run(self, body, outs, *ins, smem=(), scratch=(), alias=None, anywhere=(), out_anywhere=(), limit=6, token=0, cover=False):
        unread = [*self.last, *self.held]
        count = len(smem) + len(ins)
        specs = [pl.BlockSpec(memory_space=pltpu.SMEM)] * len(smem)
        specs += [pl.BlockSpec(memory_space=pl.ANY if i in anywhere else pltpu.VMEM) for i in range(len(ins))]
        specs += [pl.BlockSpec(memory_space=pl.ANY)] * len(unread)

        def inner(*refs):
            body(*refs[:count], *refs[count + len(unread) :])

        made = pl.pallas_call(
            inner,
            out_shape=tuple(jax.ShapeDtypeStruct(*o) for o in outs),
            in_specs=specs,
            out_specs=tuple(
                pl.BlockSpec(memory_space=pl.ANY if i in out_anywhere else pltpu.VMEM) for i in range(len(outs))
            ),
            scratch_shapes=scratch,
            input_output_aliases={} if alias is None else {len(smem) + k: v for k, v in alias.items()},
            compiler_params=pltpu.CompilerParams(vmem_limit_bytes=limit << 20),
            cost_estimate=pl.CostEstimate(flops=10**12 if cover else 1, bytes_accessed=1, transcendentals=0),
            name=body.func.__name__ if isinstance(body, functools.partial) else body.__name__,
        )(*smem, *ins, *unread)
        self.last, self.held = [made[token]], []
        return made


def dot32(first, second, first_dim, second_dim):
    return lax.dot_general(
        first, second, (((first_dim,), (second_dim,)), ((), ())), preferred_element_type=f32
    )


def statistics(values):
    average = jnp.mean(values, axis=-1, keepdims=True)
    centred = values - average
    inverse = lax.rsqrt(jnp.mean(centred * centred, axis=-1, keepdims=True) + norm_eps)
    return centred * inverse, inverse


def norm_back(grad, normed, inverse, gain):
    scaled = grad * gain
    mean_one = jnp.mean(scaled, axis=-1, keepdims=True)
    mean_two = jnp.mean(scaled * normed, axis=-1, keepdims=True)
    return inverse * (scaled - mean_one - normed * mean_two)


def of_head(values, j, axis=1):
    if values.shape[axis] <= HEAD:
        return values
    place = lax.broadcasted_iota(jnp.int32, values.shape, axis)
    return jnp.where((place >= HEAD * j) & (place < HEAD * (j + 1)), values, jnp.zeros_like(values))


def head_pairs(width):
    return [(low, min(LANES, width - low)) for low in range(0, width, LANES)]


def relay(*refs, number):
    arrived, outs = refs[:number], refs[number:]
    each = len(outs) // number
    for i, rows in enumerate(arrived):
        size = rows.shape[0] // each
        for k in range(each):
            outs[i * each + k][...] = rows[k * size : (k + 1) * size, :]


def by_pairs(weight_t, out):
    width = out.shape[0] // 3
    for low, wide in head_pairs(width):
        for j in range(3):
            out[3 * low + j * wide : 3 * low + (j + 1) * wide, :] = weight_t[
                j * width + low : j * width + low + wide, :
            ]


def norm_one(tok, gain, bias, out, *, m):
    normed, _ = statistics(tok[m, 0].astype(f32))
    out[...] = (normed * gain[...].astype(f32) + bias[...].astype(f32)).astype(bf16)


def loss_grad(where, cells, queries, cot, m, count):
    number = queries[cells[where[0] + m * count]]
    scale = jnp.sqrt(jnp.full((1, cot.shape[3]), number, jnp.int32).astype(f32) / 500.0)
    return cot[m, 0].astype(f32) * scale


def scale_cot(where, cells, queries, cot, out, *, m, count):
    out[...] = loss_grad(where, cells, queries, cot, m, count).astype(bf16)


def project(*refs, parts):
    blocks = refs[:parts]
    weight, bias, scale = refs[parts : parts + 3]
    out, whole = refs[parts + 3 :]
    rows = blocks[0].shape[0]
    for b in range(parts):
        values = blocks[b][...]
        at = slice(b * rows, (b + 1) * rows)
        whole[at, :] = values
        out[at, :] = ((dot32(values, weight[...], 1, 1) + bias[...]) * scale[...]).astype(bf16)


def attend(qkv, out_weight, attended, logs, *outs, step):
    whole = qkv.shape[0]
    head = 0
    for low, wide in head_pairs(out_weight.shape[0]):
        heads = wide // HEAD
        key_pair = qkv[:, 3 * low + wide : 3 * low + 2 * wide]
        value_t = qkv[:, 3 * low + 2 * wide : 3 * low + 3 * wide].T
        keys = [of_head(key_pair, j) for j in range(heads)]
        values = [of_head(value_t, j, 0) for j in range(heads)]
        for start in range(0, whole, step):
            at = slice(start, start + step)
            query = qkv[at, 3 * low : 3 * low + wide]
            total = None
            for j in range(heads):
                scores = dot32(keys[j], query, 1, 1)
                top = jnp.max(scores, axis=0, keepdims=True)
                powers = jnp.exp(scores - top)
                length = jnp.sum(powers, axis=0, keepdims=True)
                mixed = dot32(values[j], powers.astype(bf16), 1, 0) * (1.0 / length)
                total = mixed if total is None else total + mixed
                logs[head + j : head + j + 1, at] = top + jnp.log(length)
            attended[at, low : low + wide] = total.T.astype(bf16)
        head += heads
    rows = whole // len(outs)
    for b, out in enumerate(outs):
        out[...] = dot32(attended[b * rows : (b + 1) * rows, :], out_weight[...], 1, 0).astype(bf16)


def pair_sum(first, second, out):
    out[...] = (first[...].astype(f32) + second[...].astype(f32)).astype(bf16)


def three(first, second, third):
    return first[...].astype(f32) + second[...].astype(f32) + third[...].astype(f32)


def norm_two(tok, first, second, third, out_bias, gain, bias, resid, normed, *, m):
    value = tok[m, 0].astype(f32) + three(first, second, third) + out_bias[...].astype(f32)
    resid[...] = value
    hat, _ = statistics(value)
    normed[...] = (hat * gain[...].astype(f32) + bias[...].astype(f32)).astype(bf16)


def feed(*refs, parts, blocks):
    normed, grads, refs = refs[:blocks], refs[blocks : blocks + parts], refs[blocks + parts :]
    up, up_bias, down, activ, pre_grad, bias_grad, normed_all, grads_all = refs
    for whole, pieces in ((normed_all, normed), (grads_all, grads)):
        low = 0
        for piece in pieces:
            whole[low : low + piece.shape[0], :] = piece[...]
            low += piece.shape[0]
    rows = grads[0].shape[0]
    for low in range(0, up.shape[1], TILE):
        cols = slice(low, low + TILE)
        total = None
        for b in range(parts):
            at = slice(b * rows, (b + 1) * rows)
            pre = dot32(normed_all[at, :], up[:, cols], 1, 0) + up_bias[:, cols].astype(f32)
            cumul = 0.5 + 0.5 * lax.erf(pre * 0.7071067811865476)
            density = jnp.exp(-0.5 * pre * pre) * 0.3989422804014327
            activ[at, cols] = (pre * cumul).astype(bf16)
            back = dot32(grads_all[at, :], down[cols, :], 1, 1)
            grad = (back * (cumul + pre * density)).astype(bf16)
            pre_grad[at, cols] = grad
            part = jnp.sum(grad.astype(f32), axis=0, keepdims=True)
            total = part if total is None else total + part
        bias_grad[:, cols] = total


def times(value, weight, *outs):
    put_tiles(outs, lambda at, cols: dot32(value[at, :], weight[:, cols], 1, 0), value.shape[0])


def times_back(value, weight, *outs):
    put_tiles(outs, lambda at, cols: dot32(value[at, :], weight[cols, :], 1, 1), value.shape[0])


def put_tiles(outs, share_of, whole):
    rows, model = outs[0].shape

    def tile(i, carry):
        cols = pl.ds(pl.multiple_of(i * TILE, TILE), TILE)
        for b, out in enumerate(outs):
            out[:, cols] = share_of(slice(b * rows, (b + 1) * rows), cols).astype(bf16)
        return carry

    lax.fori_loop(0, model // TILE, tile, 0)


def product(first, second, out):
    def tile(i, carry):
        rows = pl.ds(pl.multiple_of(i * TILE, TILE), TILE)
        out[rows, :] = dot32(first[:, rows], second[...], 0, 0).astype(bf16)
        return carry

    lax.fori_loop(0, out.shape[0] // TILE, tile, 0)


def weight_grad(where, first, second, other, *refs, before):
    chunks, whole = refs[before:-1], refs[-1]

    def tile(i, carry):
        rows = pl.ds(pl.multiple_of(i * TILE, TILE), TILE)
        total = dot32(first[:, rows], second[...], 0, 0) + other[rows, :].astype(f32)
        whole[rows, :] = total.astype(bf16)
        return carry

    lax.fori_loop(0, whole.shape[0] // TILE, tile, 0)
    if before:
        chunks, both = chunks[:-1], chunks[-1]
        size = chunks[0].shape[0]
        both[:size, :] = refs[0][...]
        put_chunks(where, chunks, whole)
        both[size:, :] = chunks[0][...]
    else:
        put_chunks(where, chunks, whole)


def ring_chunk(where, count, step):
    half = where[0] // 2
    place = jnp.where(where[0] % 2 == 0, half, count - 1 - half)
    return lax.rem(place + jnp.where(where[1] % 2 == 0, count - step, step), count)


def put_chunks(where, chunks, whole):
    for s, chunk in enumerate(chunks):
        size = chunk.shape[0]
        which = ring_chunk(where, len(chunks), (s + 1) % len(chunks)) if len(chunks) > 1 else 0
        chunk[...] = whole[pl.ds(pl.multiple_of(which * size, size), size), :]


def norm_two_back(where, cells, queries, cot, resid, first, second, third, gain, out, rounded, sums, *, m, count):
    top = loss_grad(where, cells, queries, cot, m, count)
    grad = three(first, second, third)
    hat, inverse = statistics(resid[...])
    back = top + norm_back(grad, hat, inverse, gain[...].astype(f32))
    out[...] = back
    rounded[...] = back.astype(bf16)
    sums[0:1, :] = jnp.sum(back, axis=0, keepdims=True)
    sums[1:2, :] = jnp.sum(grad * hat, axis=0, keepdims=True)
    sums[2:3, :] = jnp.sum(grad, axis=0, keepdims=True)
    sums[3:4, :] = jnp.sum(top, axis=0, keepdims=True)
    sums[4:8, :] = jnp.zeros_like(sums[4:8, :])


def attend_back(qkv, logs, mixed, out_weight, *refs, parts, step, low, wide):
    grads = refs[:parts]
    out, key_grad, value_grad, given, inner = refs[parts:]
    whole = qkv.shape[0]
    rows = whole // parts
    heads = wide // HEAD
    head = low // HEAD
    ones = jnp.concatenate([of_head(jnp.ones((8, wide), bf16), j) for j in range(heads)], axis=0)
    for b in range(parts):
        at = slice(b * rows, (b + 1) * rows)
        value = dot32(grads[b][...], out_weight[low : low + wide, :], 1, 1).astype(bf16)
        given[at, :] = value
        both = value.astype(f32) * mixed[at, low : low + wide].astype(f32)
        high = both.astype(bf16)
        rest = (both - high.astype(f32)).astype(bf16)
        inner[:, at] = dot32(ones, high, 1, 1) + dot32(ones, rest, 1, 1)
    key_pair = qkv[:, 3 * low + wide : 3 * low + 2 * wide]
    value_pair = qkv[:, 3 * low + 2 * wide : 3 * low + 3 * wide]
    key_t = key_pair.T
    keys = [of_head(key_pair, j) for j in range(heads)]
    values = [of_head(value_pair, j) for j in range(heads)]
    keys_t = [of_head(key_t, j, 0) for j in range(heads)]
    key_grad[...] = jnp.zeros_like(key_grad)
    value_grad[...] = jnp.zeros_like(value_grad)

    def block(i, carry):
        start = pl.multiple_of(i * step, step)
        query = qkv[pl.ds(start, step), 3 * low : 3 * low + wide]
        grad = given[pl.ds(start, step), :]
        total = None
        for j in range(heads):
            scores = dot32(keys[j], query, 1, 1)
            weights = jnp.exp(scores - logs[head + j : head + j + 1, pl.ds(start, step)])
            back = dot32(values[j], grad, 1, 1)
            score_grad = (weights * (back - inner[8 * j : 8 * j + 1, pl.ds(start, step)])).astype(bf16)
            value_grad[...] += dot32(weights.astype(bf16), of_head(grad, j), 1, 0)
            key_grad[...] += dot32(score_grad, of_head(query, j), 1, 0)
            part = dot32(keys_t[j], score_grad, 1, 0)
            total = part if total is None else total + part
        out[pl.ds(start, step), :wide] = (total.T * score_scale).astype(bf16)
        return carry

    lax.fori_loop(0, whole // step, block, 0)
    out[:, wide : 2 * wide] = key_grad[...].astype(bf16)
    out[:, 2 * wide :] = value_grad[...].astype(bf16)


def project_back(*refs, pairs):
    grads, weight, outs, sums = refs[:pairs], refs[pairs], refs[pairs + 1 : -1], refs[-1]

    def share_of(at, cols):
        total, low = None, 0
        for grad in grads:
            wide = grad.shape[1]
            part = dot32(grad[at, :], weight[low : low + wide, cols], 1, 0)
            total = part if total is None else total + part
            low += wide
        return total

    put_tiles(outs, share_of, grads[0].shape[0])
    low = 0
    for grad in grads:
        wide = grad.shape[1]
        sums[:, low : low + wide] = jnp.sum(grad[...].astype(f32), axis=0, keepdims=True)
        low += wide


def projection_grad(where, *refs, micros, pairs, parts):
    normed, refs = refs[:micros], refs[micros:]
    grads, refs = [refs[m * pairs : (m + 1) * pairs] for m in range(micros)], refs[micros * pairs :]
    tops, refs = [refs[m * parts : (m + 1) * parts] for m in range(micros)], refs[micros * parts :]
    mixed, refs = refs[:micros], refs[micros:]
    chunks, out = refs[:-1], refs[-1]
    width = mixed[0].shape[1]
    rows = tops[0][0].shape[0]
    for p, (low, wide) in enumerate(head_pairs(width)):
        total = None
        for m in range(micros):
            part = dot32(grads[m][p][...], normed[m][...], 0, 0)
            total = part if total is None else total + part
        for j in range(3):
            out[j * width + low : j * width + low + wide, :] = total[j * wide : (j + 1) * wide].astype(bf16)
        total = None
        for m in range(micros):
            for b in range(parts):
                part = dot32(mixed[m][b * rows : (b + 1) * rows, low : low + wide], tops[m][b][...], 0, 0)
                total = part if total is None else total + part
        out[3 * width + low : 3 * width + low + wide, :] = total.astype(bf16)
    put_chunks(where, chunks, out)


def ring_add(arrived, *refs):
    low = 0
    for part in refs[:-1]:
        at = slice(low, low + part.shape[0])
        refs[-1][at, :] = (arrived[at, :].astype(f32) + part[...].astype(f32)).astype(bf16)
        low += part.shape[0]


def ring_store(where, *refs, steps, count, stacked):
    moved, refs = refs[: len(steps)], refs[len(steps) :]
    ahead, first, second, buffer, sems = refs[-5:]
    ahead[...] = moved[-1][...]
    size = buffer.shape[1] // 2 if stacked else buffer.shape[1]
    copies = []
    for k, step in enumerate(steps):
        buffer[k] = moved[k][...].astype(f32)
        row = pl.multiple_of(ring_chunk(where, count, step) * size, size)
        if stacked:
            for i, target in enumerate((first, second)):
                source = buffer.at[k, pl.ds(i * size, size), :]
                copies.append(pltpu.make_async_copy(source, target.at[pl.ds(row, size), :], sems.at[2 * k + i]))
                copies[-1].start()
        else:
            last = first.shape[0] - size
            to_first = pl.multiple_of(jnp.minimum(row, last), 16)
            to_second = pl.multiple_of(jnp.maximum(row - first.shape[0], 0), 16)
            copy_first = pltpu.make_async_copy(buffer.at[k], first.at[pl.ds(to_first, size), :], sems.at[2 * k])
            copy_second = pltpu.make_async_copy(buffer.at[k], second.at[pl.ds(to_second, size), :], sems.at[2 * k])
            pl.when(row <= last)(copy_first.start)
            pl.when(row > last)(copy_second.start)
            copies.append(copy_first)
    for copy in copies:
        copy.wait()


def norm_one_back(tok, resid_grad, first, second, third, gain, out, sums, *, m):
    grad = three(first, second, third)
    hat, inverse = statistics(tok[m, 0].astype(f32))
    out[...] = resid_grad[...] + norm_back(grad, hat, inverse, gain[...].astype(f32))
    sums[0:4, :] = jnp.zeros_like(sums[0:4, :])
    sums[4:5, :] = jnp.sum(grad * hat, axis=0, keepdims=True)
    sums[5:6, :] = jnp.sum(grad, axis=0, keepdims=True)
    sums[6:8, :] = jnp.zeros_like(sums[6:8, :])


def vector_sum(*refs):
    total = refs[0][...]
    for ref in refs[1:-1]:
        total = total + ref[...]
    refs[-1][...] = total


def ring_pass(moving, *refs, number, joined):
    refs[number][...] = moving[...]
    if joined:
        vector_join(*refs[:number], refs[number + 1], number=joined)
    elif number:
        vector_sum(*refs[:number], refs[number + 1])


def vector_join(first, second, *refs, number):
    up_bias, stack, out = refs[:number], refs[number:-1], refs[-1]
    out[...] = first[...] + second[...]
    for row, parts in ((6, up_bias), (7, stack)):
        total = parts[0][...]
        for part in parts[1:]:
            total = total + part[...]
        out[row : row + 1, : total.shape[1]] = total


def add_rows(resid, first, second, third, bias, out):
    out[...] = (resid[...] + three(first, second, third) + bias[...].astype(f32)).astype(bf16)


def swap(values, axis, bit):
    return lax.ppermute(values, axis, [(i, i ^ bit) for i in range(lax.axis_size(axis))])


def ring_order(count):
    return list(range(0, count, 2)) + list(range(1, count, 2))[::-1]


class Ring:
    def __init__(self, chain, where, shapes, stacked):
        self.chain, self.where, self.shapes, self.stacked = chain, where, shapes, stacked
        self.count = lax.axis_size("wide")
        cores = lax.axis_size("narrow")
        order = ring_order(self.count)
        self.perm = [
            (order[i] * cores + n, order[(i + (1 if n % 2 == 0 else -1)) % self.count] * cores + n)
            for i in range(self.count)
            for n in range(cores)
        ]
        self.have, self.step, self.stored, self.outs = [], 1, 0, None

    def pass_on(self, chunk):
        self.moving = lax.ppermute(chunk, ("wide", "narrow"), self.perm)

    def start(self, chunk, parts):
        self.parts = parts
        self.pass_on(chunk)

    def hold(self):
        self.chain.hold(self.moving)

    def add(self, cover=False):
        (made,) = self.chain.run(
            ring_add,
            [(self.moving.shape, bf16)],
            self.moving,
            *[p[self.step] for p in self.parts],
            cover=cover,
        )
        self.step += 1
        if self.step == self.count:
            self.have.append(made)
        self.pass_on(made)

    def forward(self):
        self.have.append(self.moving)
        copy = self.store()
        if len(self.have) < self.count:
            self.pass_on(copy)

    def arrive(self, made):
        self.have.append(made)
        if len(self.have) < self.count:
            self.pass_on(made)

    def store(self):
        steps = range(self.stored, len(self.have))
        self.stored = len(self.have)
        moved = [self.have[s] for s in steps]
        kept = () if self.outs is None else self.outs
        number = len(moved)
        made = self.chain.run(
            functools.partial(ring_store, steps=tuple(steps), count=self.count, stacked=self.stacked),
            [(moved[-1].shape, bf16)] + [(s, f32) for s in self.shapes],
            *moved,
            *kept,
            smem=(self.where,),
            scratch=[pltpu.VMEM((number, *moved[0].shape), f32), pltpu.SemaphoreType.DMA((2 * number,))],
            alias={number: 1, number + 1: 2} if kept else None,
            anywhere=(number, number + 1) if kept else (),
            out_anywhere=(1, 2),
            limit=6 + (number * moved[0].size * 4 >> 20),
        )
        self.outs = made[1:]
        return made[0]


class Whole:
    def __init__(self, shapes):
        self.shapes = shapes

    def start(self, chunk, parts):
        total = lax.psum(chunk, "wide").astype(f32)
        self.outs = (total[: self.shapes[0][0]], total[self.shapes[0][0] :])

    def hold(self):
        pass

    def add(self, cover=False):
        pass

    def forward(self):
        pass

    def store(self):
        pass


def local(
    tokens,
    cotangent,
    cell_of,
    query_count,
    attn_norm_gain,
    attn_norm_bias,
    input_weight,
    query_bias,
    value_bias,
    out_weight,
    out_bias,
    ffn_norm_gain,
    ffn_norm_bias,
    up_weight,
    up_bias,
    down_weight,
    down_bias,
):
    micros = range(tokens.shape[0])
    rows, model = tokens.shape[2], tokens.shape[3]
    parts = lax.axis_size("narrow")
    whole = rows * parts
    width = input_weight.shape[2]
    hidden = up_weight.shape[1]
    count = lax.axis_size("wide")
    rings = count <= 8
    chunks = count if rings else 1
    pairs = head_pairs(width)
    step = min(512, whole)
    chain = Chain()
    run = chain.run
    where = jnp.stack([lax.axis_index("wide"), lax.axis_index("narrow")]).astype(jnp.int32)

    block = ((rows, model), bf16)
    outgoing = [block] * parts
    wide_rows = ((whole, model), bf16)
    row = lambda v: v.reshape(1, -1)
    gain_one, bias_one, gain_two, bias_two = map(row, (attn_norm_gain, attn_norm_bias, ffn_norm_gain, ffn_norm_bias))
    out_bias, down_bias, up_bias = row(out_bias), row(down_bias), row(up_bias)

    def columns(three_parts):
        return jnp.concatenate([v[:, low : low + wide] for low, wide in pairs for v in three_parts], axis=1)

    weight_t = jnp.transpose(input_weight, (1, 2, 0)).reshape(3 * width, model)
    zero = jnp.zeros((1, width), f32)
    project_bias = columns([row(query_bias).astype(f32), zero, row(value_bias).astype(f32)])
    project_scale = columns([zero + score_scale, zero + 1.0, zero + 1.0])

    def gather(own):
        return [own, swap(own, "narrow", 1), swap(own, "narrow", 2)]

    def finish(*arrived, pieces=1, cover=False):
        made = run(
            functools.partial(relay, number=len(arrived)),
            [((rows // pieces, model), bf16)] * (len(arrived) * pieces),
            *[a[2] for a in arrived],
            cover=cover,
        )
        for i, a in enumerate(arrived):
            own = made[i * pieces : (i + 1) * pieces]
            a[2:] = [*own, *[swap(piece, "narrow", 1) for piece in own]]

    def share(made):
        own, near, partner, far = made
        return [own, partner, swap(far, "narrow", 1), swap(near, "narrow", 1)]

    def send(shares):
        own, partner, far, near = shares
        (both,) = run(pair_sum, [block], partner, far)
        return [own, near, swap(both, "narrow", 2)]

    def fresh():
        return [None] * len(micros)

    normed, given, qkv, normed_all, mixed, logs, shares, shares_down, resid, normed_two_b = (fresh() for _ in range(10))
    activ, pre_grad, up_bias_grad, two_all, given_all, resid_grad, top = (fresh() for _ in range(7))
    sums_two, sums_one, stack_sums, out_rows, grad_rows = (fresh() for _ in range(5))
    pair_grads = [[] for _ in micros]

    def do_norm_one(m):
        (own,) = run(functools.partial(norm_one, m=m), [block], tokens, gain_one, bias_one)
        normed[m] = gather(own)

    def do_scale(m):
        (own,) = run(functools.partial(scale_cot, m=m, count=count), [block], cotangent, smem=(where, cell_of, query_count), cover=True)
        given[m] = gather(own)

    def do_project(m):
        qkv[m], normed_all[m] = run(
            functools.partial(project, parts=parts),
            [((whole, 3 * width), bf16), wide_rows],
            *normed[m],
            weight,
            project_bias,
            project_scale,
        )

    def do_attend(m):
        mixed[m], logs[m], *made = run(
            functools.partial(attend, step=whole),
            [((whole, width), bf16), ((8, whole), f32), *outgoing],
            qkv[m],
            out_weight,
            limit=24,
        )
        shares[m] = share(made)

    def do_send(m):
        shares[m] = send(shares[m])

    def do_norm_two(m):
        resid[m], own = run(
            functools.partial(norm_two, m=m),
            [((rows, model), f32), block],
            tokens,
            *shares[m],
            out_bias,
            gain_two,
            bias_two,
            cover=m == 0,
        )
        normed_two_b[m] = gather(own)

    def do_feed(m):
        activ[m], pre_grad[m], up_bias_grad[m], two_all[m], given_all[m] = run(
            functools.partial(feed, parts=parts, blocks=len(normed_two_b[m])),
            [((whole, hidden), bf16), ((whole, hidden), bf16), ((1, hidden), f32), wide_rows, wide_rows],
            *normed_two_b[m],
            *given[m],
            up_weight,
            up_bias,
            down_weight,
        )

    def do_up_back(m):
        shares[m] = share(run(times_back, outgoing, pre_grad[m], up_weight))

    def do_down(m):
        shares_down[m] = share(run(times, outgoing, activ[m], down_weight))

    def do_send_down(m):
        shares_down[m] = send(shares_down[m])

    def do_norm_two_back(m):
        resid_grad[m], own, sums_two[m] = run(
            functools.partial(norm_two_back, m=m, count=count),
            [((rows, model), f32), block, ((8, model), f32)],
            cotangent,
            resid[m],
            *shares[m],
            gain_two,
            smem=(where, cell_of, query_count),
            cover=True,
        )
        top[m] = gather(own)

    def do_attend_back(m, p):
        low, wide = pairs[p]
        (made,) = run(
            functools.partial(attend_back, parts=parts, step=step, low=low, wide=wide),
            [((whole, 3 * wide), bf16)],
            qkv[m],
            logs[m],
            mixed[m],
            out_weight,
            *top[m],
            scratch=[
                pltpu.VMEM((whole, wide), f32),
                pltpu.VMEM((whole, wide), f32),
                pltpu.VMEM((whole, wide), bf16),
                pltpu.VMEM((8 * (wide // HEAD), whole), f32),
            ],
            limit=20,
        )
        pair_grads[m].append(made)

    def do_project_back(m):
        *made, stack_sums[m] = run(
            functools.partial(project_back, pairs=len(pairs)),
            [*outgoing, ((1, 3 * width), f32)],
            *pair_grads[m],
            weight,
        )
        shares[m] = share(made)

    def do_norm_one_back(m):
        grad_rows[m], sums_one[m] = run(
            functools.partial(norm_one_back, m=m),
            [((rows, model), f32), ((8, model), f32)],
            tokens,
            resid_grad[m],
            *shares[m],
            gain_one,
        )

    hops = [("narrow", 1 << k) for k in range(parts.bit_length() - 1)]
    hops += [("wide", 1 << k) for k in range(count.bit_length() - 1)]
    vectors = []

    def next_vectors():
        done = len(vectors)
        if done == 0:
            return [*sums_one, *sums_two], 0
        if hops[done - 1][0] == "narrow" and hops[done][0] == "wide":
            return [*vectors[-1], *up_bias_grad, *stack_sums], len(micros)
        return vectors[-1], 0

    def add_vectors(own):
        done = len(vectors)
        vectors.append((own, swap(own, *hops[done])) if done < len(hops) else (own,))

    def do_vectors():
        given_now, joined = next_vectors()
        body = functools.partial(vector_join, number=joined) if joined else vector_sum
        add_vectors(run(body, [((8, model), f32)], *given_now)[0])

    def do_pass():
        if not rings:
            return
        given_now, joined = next_vectors() if len(vectors) <= len(hops) else ([], 0)
        if not given_now and len(attn.have) == count - 1:
            attn.have.append(attn.moving)
            return
        made = run(
            functools.partial(ring_pass, number=len(given_now), joined=joined),
            [(attn.moving.shape, bf16)] + ([((8, model), f32)] if given_now else []),
            attn.moving,
            *given_now,
        )
        attn.arrive(made[0])
        if given_now:
            add_vectors(made[1])

    def do_add_rows(m):
        (out_rows[m],) = run(add_rows, [block], resid[m], *shares_down[m], down_bias)

    def first_product(first, second):
        return run(product, [((first.shape[1], second.shape[1]), bf16)], first, second)[0]

    def ffn_grad(first, second, other, before=()):
        rows, cols = other.shape
        shapes = [((rows // chunks, cols), bf16)] * chunks
        if before:
            shapes.append(((2 * rows // chunks, cols), bf16))
        return run(
            functools.partial(weight_grad, before=len(before[:1])),
            shapes,
            first,
            second,
            other,
            *before[:1],
            smem=(where,),
            scratch=[pltpu.VMEM((rows, cols), bf16)],
            limit=16,
        )

    def attn_grad():
        made = run(
            functools.partial(projection_grad, micros=len(micros), pairs=len(pairs), parts=parts),
            [((4 * width // chunks, model), bf16)] * chunks,
            *normed_all,
            *[g for m in micros for g in pair_grads[m]],
            *[t for m in micros for t in top[m]],
            *mixed,
            smem=(where,),
            scratch=[pltpu.VMEM((4 * width, model), bf16)],
            limit=20,
        )
        attn.start(made[0], (made,))

    ffn_shapes = [(hidden, model), (model, hidden)]
    attn_shapes = [(3 * width, model), (width, model)]
    ffn = Ring(chain, where, ffn_shapes, True) if rings else Whole(ffn_shapes)
    attn = Ring(chain, where, attn_shapes, False) if rings else Whole(attn_shapes)

    do_norm_one(0)
    (weight,) = run(by_pairs, [((3 * width, model), bf16)], weight_t)
    chain.hold(normed[0][1])
    finish(normed[0])
    do_norm_one(1)
    do_scale(0)
    do_project(0)
    do_attend(0)
    chain.hold(normed[1][1], given[0][1])
    finish(normed[1], given[0], cover=True)
    do_scale(1)
    do_send(0)
    chain.hold(given[1][1])
    do_project(1)
    do_attend(1)
    chain.hold(given[1][2])
    do_norm_two(0)
    do_send(1)
    finish(given[1])
    chain.hold(normed_two_b[0][1])
    finish(normed_two_b[0], pieces=4)
    do_feed(0)
    do_norm_two(1)
    chain.hold(normed_two_b[1][1])
    do_up_back(0)
    down_first = first_product(activ[0], given_all[0])
    up_first = first_product(two_all[0], pre_grad[0])
    do_down(0)
    finish(normed_two_b[1], cover=True)
    do_send(0)
    do_feed(1)
    do_up_back(1)
    do_norm_two_back(0)
    chain.hold(top[0][1])
    down_chunks = ffn_grad(activ[1], given_all[1], down_first)
    *up_chunks, both = ffn_grad(two_all[1], pre_grad[1], up_first, down_chunks)
    ffn.start(both, (down_chunks, up_chunks))
    finish(top[0], cover=True)
    do_send(1)
    do_down(1)
    ffn.add()
    do_attend_back(0, 0)
    ffn.add()
    do_attend_back(0, 1)
    do_norm_two_back(1)
    ffn.add()
    do_attend_back(0, 2)
    do_project_back(0)
    ffn.add()
    chain.hold(top[1][1])
    finish(top[1], cover=True)
    do_attend_back(1, 0)
    do_send_down(0)
    ffn.add()
    do_send(0)
    do_attend_back(1, 1)
    ffn.add()
    do_attend_back(1, 2)
    attn_grad()
    ffn.add()
    attn.add()
    do_project_back(1)
    attn.add()
    ffn.forward()
    do_norm_one_back(0)
    attn.add()
    do_send(1)
    attn.add()
    do_send_down(1)
    ffn.forward()
    attn.add()
    attn.add()
    do_norm_one_back(1)
    do_vectors()
    ffn.forward()
    attn.add()
    do_pass()
    ffn.forward()
    do_pass()
    do_add_rows(0)
    attn.store()
    do_pass()
    ffn.forward()
    do_pass()
    do_add_rows(1)
    attn.store()
    do_pass()
    ffn.forward()
    do_pass()
    attn.store()
    ffn.forward()
    do_pass()
    attn.store()

    while len(vectors) <= len(hops):
        do_vectors()
    vector_sums = vectors[-1][0]
    up_bias_sum = vector_sums[6, :hidden]
    stack_sum = vector_sums[7, : 3 * width]

    def plain(j):
        return jnp.concatenate([stack_sum[3 * low + j * wide : 3 * low + (j + 1) * wide] for low, wide in pairs])

    return (
        jnp.stack(out_rows)[:, None],
        jnp.stack(grad_rows)[:, None],
        vector_sums[4],
        vector_sums[5],
        jnp.transpose(attn.outs[0].reshape(3, width, model), (2, 0, 1)),
        plain(0),
        plain(2),
        attn.outs[1],
        vector_sums[0],
        vector_sums[1],
        vector_sums[2],
        ffn.outs[1],
        up_bias_sum,
        ffn.outs[0],
        vector_sums[3],
    )


def solution(mesh):
    in_specs = (
        P(None, "wide", "narrow", None),
        P(None, "wide", "narrow", None),
        P(),
        P(),
        P(),
        P(),
        P(None, None, "narrow"),
        P("narrow"),
        P("narrow"),
        P("narrow", None),
        P(),
        P(),
        P(),
        P(None, "narrow"),
        P("narrow"),
        P("narrow", None),
        P(),
    )
    out_specs = (
        P(None, "wide", "narrow", None),
        P(None, "wide", "narrow", None),
        P(),
        P(),
        P(None, None, "narrow"),
        P("narrow"),
        P("narrow"),
        P("narrow", None),
        P(),
        P(),
        P(),
        P(None, "narrow"),
        P("narrow"),
        P("narrow", None),
        P(),
    )
    return jax.shard_map(local, mesh=mesh, in_specs=in_specs, out_specs=out_specs, check_vma=False)
```

```python
import functools

import jax
import jax.numpy as jnp
from jax import lax
from jax.experimental import pallas as pl
from jax.experimental.pallas import tpu as pltpu
from jax.sharding import PartitionSpec as P

HEAD = 64
LANES = 128
TILE = 256
norm_eps = 1e-05
score_scale = 0.125
bf16 = jnp.bfloat16
f32 = jnp.float32


class Chain:
    def __init__(self):
        self.last = []
        self.held = []

    def hold(self, *arrays):
        self.held += arrays

    def run(self, body, outs, *ins, smem=(), scratch=(), alias=None, anywhere=(), out_anywhere=(), limit=6, token=0, cover=False):
        unread = [*self.last, *self.held]
        count = len(smem) + len(ins)
        specs = [pl.BlockSpec(memory_space=pltpu.SMEM)] * len(smem)
        specs += [pl.BlockSpec(memory_space=pl.ANY if i in anywhere else pltpu.VMEM) for i in range(len(ins))]
        specs += [pl.BlockSpec(memory_space=pl.ANY)] * len(unread)

        def inner(*refs):
            body(*refs[:count], *refs[count + len(unread) :])

        made = pl.pallas_call(
            inner,
            out_shape=tuple(jax.ShapeDtypeStruct(*o) for o in outs),
            in_specs=specs,
            out_specs=tuple(
                pl.BlockSpec(memory_space=pl.ANY if i in out_anywhere else pltpu.VMEM) for i in range(len(outs))
            ),
            scratch_shapes=scratch,
            input_output_aliases={} if alias is None else {len(smem) + k: v for k, v in alias.items()},
            compiler_params=pltpu.CompilerParams(vmem_limit_bytes=limit << 20),
            cost_estimate=pl.CostEstimate(flops=10**12 if cover else 1, bytes_accessed=1, transcendentals=0),
            name=body.func.__name__ if isinstance(body, functools.partial) else body.__name__,
        )(*smem, *ins, *unread)
        self.last, self.held = [made[token]], []
        return made


def dot32(first, second, first_dim, second_dim):
    return lax.dot_general(
        first, second, (((first_dim,), (second_dim,)), ((), ())), preferred_element_type=f32
    )


def statistics(values):
    average = jnp.mean(values, axis=-1, keepdims=True)
    centred = values - average
    inverse = lax.rsqrt(jnp.mean(centred * centred, axis=-1, keepdims=True) + norm_eps)
    return centred * inverse, inverse


def norm_back(grad, normed, inverse, gain):
    scaled = grad * gain
    mean_one = jnp.mean(scaled, axis=-1, keepdims=True)
    mean_two = jnp.mean(scaled * normed, axis=-1, keepdims=True)
    return inverse * (scaled - mean_one - normed * mean_two)


def of_head(values, j, axis=1):
    if values.shape[axis] <= HEAD:
        return values
    place = lax.broadcasted_iota(jnp.int32, values.shape, axis)
    return jnp.where((place >= HEAD * j) & (place < HEAD * (j + 1)), values, jnp.zeros_like(values))


def head_pairs(width):
    return [(low, min(LANES, width - low)) for low in range(0, width, LANES)]


def relay(*refs, number):
    arrived, outs = refs[:number], refs[number:]
    each = len(outs) // number
    for i, rows in enumerate(arrived):
        size = rows.shape[0] // each
        for k in range(each):
            outs[i * each + k][...] = rows[k * size : (k + 1) * size, :]


def by_pairs(weight_t, out):
    width = out.shape[0] // 3
    for low, wide in head_pairs(width):
        for j in range(3):
            out[3 * low + j * wide : 3 * low + (j + 1) * wide, :] = weight_t[
                j * width + low : j * width + low + wide, :
            ]


def norm_one(tok, gain, bias, out, *, m):
    normed, _ = statistics(tok[m, 0].astype(f32))
    out[...] = (normed * gain[...].astype(f32) + bias[...].astype(f32)).astype(bf16)


def loss_grad(where, cells, queries, cot, m, count):
    number = queries[cells[where[0] + m * count]]
    scale = jnp.sqrt(jnp.full((1, cot.shape[3]), number, jnp.int32).astype(f32) / 500.0)
    return cot[m, 0].astype(f32) * scale


def scale_cot(where, cells, queries, cot, out, *, m, count):
    out[...] = loss_grad(where, cells, queries, cot, m, count).astype(bf16)


def project(*refs, parts):
    blocks = refs[:parts]
    weight, bias, scale = refs[parts : parts + 3]
    out, whole = refs[parts + 3 :]
    rows = blocks[0].shape[0]
    for b in range(parts):
        values = blocks[b][...]
        at = slice(b * rows, (b + 1) * rows)
        whole[at, :] = values
        out[at, :] = ((dot32(values, weight[...], 1, 1) + bias[...]) * scale[...]).astype(bf16)


def attend(qkv, out_weight, attended, logs, *outs, step):
    whole = qkv.shape[0]
    head = 0
    for low, wide in head_pairs(out_weight.shape[0]):
        heads = wide // HEAD
        key_pair = qkv[:, 3 * low + wide : 3 * low + 2 * wide]
        value_t = qkv[:, 3 * low + 2 * wide : 3 * low + 3 * wide].T
        keys = [of_head(key_pair, j) for j in range(heads)]
        values = [of_head(value_t, j, 0) for j in range(heads)]
        for start in range(0, whole, step):
            at = slice(start, start + step)
            query = qkv[at, 3 * low : 3 * low + wide]
            total = None
            for j in range(heads):
                scores = dot32(keys[j], query, 1, 1)
                top = jnp.max(scores, axis=0, keepdims=True)
                powers = jnp.exp(scores - top)
                length = jnp.sum(powers, axis=0, keepdims=True)
                mixed = dot32(values[j], powers.astype(bf16), 1, 0) * (1.0 / length)
                total = mixed if total is None else total + mixed
                logs[head + j : head + j + 1, at] = top + jnp.log(length)
            attended[at, low : low + wide] = total.T.astype(bf16)
        head += heads
    rows = whole // len(outs)
    for b, out in enumerate(outs):
        out[...] = dot32(attended[b * rows : (b + 1) * rows, :], out_weight[...], 1, 0).astype(bf16)


def pair_sum(first, second, out):
    out[...] = (first[...].astype(f32) + second[...].astype(f32)).astype(bf16)


def three(first, second, third):
    return first[...].astype(f32) + second[...].astype(f32) + third[...].astype(f32)


def norm_two(tok, first, second, third, out_bias, gain, bias, resid, normed, *, m):
    value = tok[m, 0].astype(f32) + three(first, second, third) + out_bias[...].astype(f32)
    resid[...] = value
    hat, _ = statistics(value)
    normed[...] = (hat * gain[...].astype(f32) + bias[...].astype(f32)).astype(bf16)


def feed(*refs, parts, blocks):
    normed, grads, refs = refs[:blocks], refs[blocks : blocks + parts], refs[blocks + parts :]
    up, up_bias, down, activ, pre_grad, bias_grad, normed_all, grads_all = refs
    for whole, pieces in ((normed_all, normed), (grads_all, grads)):
        low = 0
        for piece in pieces:
            whole[low : low + piece.shape[0], :] = piece[...]
            low += piece.shape[0]
    rows = grads[0].shape[0]
    for low in range(0, up.shape[1], TILE):
        cols = slice(low, low + TILE)
        total = None
        for b in range(parts):
            at = slice(b * rows, (b + 1) * rows)
            pre = dot32(normed_all[at, :], up[:, cols], 1, 0) + up_bias[:, cols].astype(f32)
            cumul = 0.5 + 0.5 * lax.erf(pre * 0.7071067811865476)
            density = jnp.exp(-0.5 * pre * pre) * 0.3989422804014327
            activ[at, cols] = (pre * cumul).astype(bf16)
            back = dot32(grads_all[at, :], down[cols, :], 1, 1)
            grad = (back * (cumul + pre * density)).astype(bf16)
            pre_grad[at, cols] = grad
            part = jnp.sum(grad.astype(f32), axis=0, keepdims=True)
            total = part if total is None else total + part
        bias_grad[:, cols] = total


def times(value, weight, *outs):
    put_tiles(outs, lambda at, cols: dot32(value[at, :], weight[:, cols], 1, 0), value.shape[0])


def times_back(value, weight, *outs):
    put_tiles(outs, lambda at, cols: dot32(value[at, :], weight[cols, :], 1, 1), value.shape[0])


def put_tiles(outs, share_of, whole):
    rows, model = outs[0].shape

    def tile(i, carry):
        cols = pl.ds(pl.multiple_of(i * TILE, TILE), TILE)
        for b, out in enumerate(outs):
            out[:, cols] = share_of(slice(b * rows, (b + 1) * rows), cols).astype(bf16)
        return carry

    lax.fori_loop(0, model // TILE, tile, 0)


def product(first, second, out):
    def tile(i, carry):
        rows = pl.ds(pl.multiple_of(i * TILE, TILE), TILE)
        out[rows, :] = dot32(first[:, rows], second[...], 0, 0).astype(bf16)
        return carry

    lax.fori_loop(0, out.shape[0] // TILE, tile, 0)


def weight_grad(where, first, second, other, *refs, before):
    chunks, whole = refs[before:-1], refs[-1]

    def tile(i, carry):
        rows = pl.ds(pl.multiple_of(i * TILE, TILE), TILE)
        total = dot32(first[:, rows], second[...], 0, 0) + other[rows, :].astype(f32)
        whole[rows, :] = total.astype(bf16)
        return carry

    lax.fori_loop(0, whole.shape[0] // TILE, tile, 0)
    if before:
        chunks, both = chunks[:-1], chunks[-1]
        size = chunks[0].shape[0]
        both[:size, :] = refs[0][...]
        put_chunks(where, chunks, whole)
        both[size:, :] = chunks[0][...]
    else:
        put_chunks(where, chunks, whole)


def ring_chunk(where, count, step):
    half = where[0] // 2
    place = jnp.where(where[0] % 2 == 0, half, count - 1 - half)
    return lax.rem(place + jnp.where(where[1] % 2 == 0, count - step, step), count)


def put_chunks(where, chunks, whole):
    for s, chunk in enumerate(chunks):
        size = chunk.shape[0]
        which = ring_chunk(where, len(chunks), (s + 1) % len(chunks)) if len(chunks) > 1 else 0
        chunk[...] = whole[pl.ds(pl.multiple_of(which * size, size), size), :]


def norm_two_back(where, cells, queries, cot, resid, first, second, third, gain, out, rounded, sums, *, m, count):
    top = loss_grad(where, cells, queries, cot, m, count)
    grad = three(first, second, third)
    hat, inverse = statistics(resid[...])
    back = top + norm_back(grad, hat, inverse, gain[...].astype(f32))
    out[...] = back
    rounded[...] = back.astype(bf16)
    sums[0:1, :] = jnp.sum(back, axis=0, keepdims=True)
    sums[1:2, :] = jnp.sum(grad * hat, axis=0, keepdims=True)
    sums[2:3, :] = jnp.sum(grad, axis=0, keepdims=True)
    sums[3:4, :] = jnp.sum(top, axis=0, keepdims=True)
    sums[4:8, :] = jnp.zeros_like(sums[4:8, :])


def attend_back(qkv, logs, mixed, out_weight, *refs, parts, step, low, wide):
    grads = refs[:parts]
    out, key_grad, value_grad, given, inner = refs[parts:]
    whole = qkv.shape[0]
    rows = whole // parts
    heads = wide // HEAD
    head = low // HEAD
    ones = jnp.concatenate([of_head(jnp.ones((8, wide), bf16), j) for j in range(heads)], axis=0)
    for b in range(parts):
        at = slice(b * rows, (b + 1) * rows)
        value = dot32(grads[b][...], out_weight[low : low + wide, :], 1, 1).astype(bf16)
        given[at, :] = value
        both = value.astype(f32) * mixed[at, low : low + wide].astype(f32)
        high = both.astype(bf16)
        rest = (both - high.astype(f32)).astype(bf16)
        inner[:, at] = dot32(ones, high, 1, 1) + dot32(ones, rest, 1, 1)
    key_pair = qkv[:, 3 * low + wide : 3 * low + 2 * wide]
    value_pair = qkv[:, 3 * low + 2 * wide : 3 * low + 3 * wide]
    key_t = key_pair.T
    keys = [of_head(key_pair, j) for j in range(heads)]
    values = [of_head(value_pair, j) for j in range(heads)]
    keys_t = [of_head(key_t, j, 0) for j in range(heads)]
    key_grad[...] = jnp.zeros_like(key_grad)
    value_grad[...] = jnp.zeros_like(value_grad)

    def block(i, carry):
        start = pl.multiple_of(i * step, step)
        query = qkv[pl.ds(start, step), 3 * low : 3 * low + wide]
        grad = given[pl.ds(start, step), :]
        total = None
        for j in range(heads):
            scores = dot32(keys[j], query, 1, 1)
            weights = jnp.exp(scores - logs[head + j : head + j + 1, pl.ds(start, step)])
            back = dot32(values[j], grad, 1, 1)
            score_grad = (weights * (back - inner[8 * j : 8 * j + 1, pl.ds(start, step)])).astype(bf16)
            value_grad[...] += dot32(weights.astype(bf16), of_head(grad, j), 1, 0)
            key_grad[...] += dot32(score_grad, of_head(query, j), 1, 0)
            part = dot32(keys_t[j], score_grad, 1, 0)
            total = part if total is None else total + part
        out[pl.ds(start, step), :wide] = (total.T * score_scale).astype(bf16)
        return carry

    lax.fori_loop(0, whole // step, block, 0)
    out[:, wide : 2 * wide] = key_grad[...].astype(bf16)
    out[:, 2 * wide :] = value_grad[...].astype(bf16)


def project_back(*refs, pairs):
    grads, weight, outs, sums = refs[:pairs], refs[pairs], refs[pairs + 1 : -1], refs[-1]

    def share_of(at, cols):
        total, low = None, 0
        for grad in grads:
            wide = grad.shape[1]
            part = dot32(grad[at, :], weight[low : low + wide, cols], 1, 0)
            total = part if total is None else total + part
            low += wide
        return total

    put_tiles(outs, share_of, grads[0].shape[0])
    low = 0
    for grad in grads:
        wide = grad.shape[1]
        sums[:, low : low + wide] = jnp.sum(grad[...].astype(f32), axis=0, keepdims=True)
        low += wide


def projection_grad(where, *refs, micros, pairs, parts):
    normed, refs = refs[:micros], refs[micros:]
    grads, refs = [refs[m * pairs : (m + 1) * pairs] for m in range(micros)], refs[micros * pairs :]
    tops, refs = [refs[m * parts : (m + 1) * parts] for m in range(micros)], refs[micros * parts :]
    mixed, refs = refs[:micros], refs[micros:]
    chunks, out = refs[:-1], refs[-1]
    width = mixed[0].shape[1]
    rows = tops[0][0].shape[0]
    for p, (low, wide) in enumerate(head_pairs(width)):
        total = None
        for m in range(micros):
            part = dot32(grads[m][p][...], normed[m][...], 0, 0)
            total = part if total is None else total + part
        for j in range(3):
            out[j * width + low : j * width + low + wide, :] = total[j * wide : (j + 1) * wide].astype(bf16)
        total = None
        for m in range(micros):
            for b in range(parts):
                part = dot32(mixed[m][b * rows : (b + 1) * rows, low : low + wide], tops[m][b][...], 0, 0)
                total = part if total is None else total + part
        out[3 * width + low : 3 * width + low + wide, :] = total.astype(bf16)
    put_chunks(where, chunks, out)


def ring_add(arrived, *refs):
    low = 0
    for part in refs[:-1]:
        at = slice(low, low + part.shape[0])
        refs[-1][at, :] = (arrived[at, :].astype(f32) + part[...].astype(f32)).astype(bf16)
        low += part.shape[0]


def ring_store(where, *refs, steps, count, stacked):
    moved, refs = refs[: len(steps)], refs[len(steps) :]
    ahead, first, second, buffer, sems = refs[-5:]
    ahead[...] = moved[-1][...]
    size = buffer.shape[1] // 2 if stacked else buffer.shape[1]
    copies = []
    for k, step in enumerate(steps):
        buffer[k] = moved[k][...].astype(f32)
        row = pl.multiple_of(ring_chunk(where, count, step) * size, size)
        if stacked:
            for i, target in enumerate((first, second)):
                source = buffer.at[k, pl.ds(i * size, size), :]
                copies.append(pltpu.make_async_copy(source, target.at[pl.ds(row, size), :], sems.at[2 * k + i]))
                copies[-1].start()
        else:
            last = first.shape[0] - size
            to_first = pl.multiple_of(jnp.minimum(row, last), 16)
            to_second = pl.multiple_of(jnp.maximum(row - first.shape[0], 0), 16)
            copy_first = pltpu.make_async_copy(buffer.at[k], first.at[pl.ds(to_first, size), :], sems.at[2 * k])
            copy_second = pltpu.make_async_copy(buffer.at[k], second.at[pl.ds(to_second, size), :], sems.at[2 * k])
            pl.when(row <= last)(copy_first.start)
            pl.when(row > last)(copy_second.start)
            copies.append(copy_first)
    for copy in copies:
        copy.wait()


def norm_one_back(tok, resid_grad, first, second, third, gain, out, sums, *, m):
    grad = three(first, second, third)
    hat, inverse = statistics(tok[m, 0].astype(f32))
    out[...] = resid_grad[...] + norm_back(grad, hat, inverse, gain[...].astype(f32))
    sums[0:4, :] = jnp.zeros_like(sums[0:4, :])
    sums[4:5, :] = jnp.sum(grad * hat, axis=0, keepdims=True)
    sums[5:6, :] = jnp.sum(grad, axis=0, keepdims=True)
    sums[6:8, :] = jnp.zeros_like(sums[6:8, :])


def vector_sum(*refs):
    total = refs[0][...]
    for ref in refs[1:-1]:
        total = total + ref[...]
    refs[-1][...] = total


def ring_pass(moving, *refs, number, joined):
    refs[number][...] = moving[...]
    if joined:
        vector_join(*refs[:number], refs[number + 1], number=joined)
    elif number:
        vector_sum(*refs[:number], refs[number + 1])


def vector_join(first, second, *refs, number):
    up_bias, stack, out = refs[:number], refs[number:-1], refs[-1]
    out[...] = first[...] + second[...]
    for row, parts in ((6, up_bias), (7, stack)):
        total = parts[0][...]
        for part in parts[1:]:
            total = total + part[...]
        out[row : row + 1, : total.shape[1]] = total


def add_rows(resid, first, second, third, bias, out):
    out[...] = (resid[...] + three(first, second, third) + bias[...].astype(f32)).astype(bf16)


def swap(values, axis, bit):
    return lax.ppermute(values, axis, [(i, i ^ bit) for i in range(lax.axis_size(axis))])


def ring_order(count):
    return list(range(0, count, 2)) + list(range(1, count, 2))[::-1]


class Ring:
    def __init__(self, chain, where, shapes, stacked):
        self.chain, self.where, self.shapes, self.stacked = chain, where, shapes, stacked
        self.count = lax.axis_size("wide")
        cores = lax.axis_size("narrow")
        order = ring_order(self.count)
        self.perm = [
            (order[i] * cores + n, order[(i + (1 if n % 2 == 0 else -1)) % self.count] * cores + n)
            for i in range(self.count)
            for n in range(cores)
        ]
        self.have, self.step, self.stored, self.outs = [], 1, 0, None

    def pass_on(self, chunk):
        self.moving = lax.ppermute(chunk, ("wide", "narrow"), self.perm)

    def start(self, chunk, parts):
        self.parts = parts
        self.pass_on(chunk)

    def hold(self):
        self.chain.hold(self.moving)

    def add(self, cover=False):
        (made,) = self.chain.run(
            ring_add,
            [(self.moving.shape, bf16)],
            self.moving,
            *[p[self.step] for p in self.parts],
            cover=cover,
        )
        self.step += 1
        if self.step == self.count:
            self.have.append(made)
        self.pass_on(made)

    def forward(self):
        self.have.append(self.moving)
        copy = self.store()
        if len(self.have) < self.count:
            self.pass_on(copy)

    def arrive(self, made):
        self.have.append(made)
        if len(self.have) < self.count:
            self.pass_on(made)

    def store(self):
        steps = range(self.stored, len(self.have))
        self.stored = len(self.have)
        moved = [self.have[s] for s in steps]
        kept = () if self.outs is None else self.outs
        number = len(moved)
        made = self.chain.run(
            functools.partial(ring_store, steps=tuple(steps), count=self.count, stacked=self.stacked),
            [(moved[-1].shape, bf16)] + [(s, f32) for s in self.shapes],
            *moved,
            *kept,
            smem=(self.where,),
            scratch=[pltpu.VMEM((number, *moved[0].shape), f32), pltpu.SemaphoreType.DMA((2 * number,))],
            alias={number: 1, number + 1: 2} if kept else None,
            anywhere=(number, number + 1) if kept else (),
            out_anywhere=(1, 2),
            limit=6 + (number * moved[0].size * 4 >> 20),
        )
        self.outs = made[1:]
        return made[0]


class Whole:
    def __init__(self, shapes):
        self.shapes = shapes

    def start(self, chunk, parts):
        total = lax.psum(chunk, "wide").astype(f32)
        self.outs = (total[: self.shapes[0][0]], total[self.shapes[0][0] :])

    def hold(self):
        pass

    def add(self, cover=False):
        pass

    def forward(self):
        pass

    def store(self):
        pass


def local(
    tokens,
    cotangent,
    cell_of,
    query_count,
    attn_norm_gain,
    attn_norm_bias,
    input_weight,
    query_bias,
    value_bias,
    out_weight,
    out_bias,
    ffn_norm_gain,
    ffn_norm_bias,
    up_weight,
    up_bias,
    down_weight,
    down_bias,
):
    micros = range(tokens.shape[0])
    rows, model = tokens.shape[2], tokens.shape[3]
    parts = lax.axis_size("narrow")
    whole = rows * parts
    width = input_weight.shape[2]
    hidden = up_weight.shape[1]
    count = lax.axis_size("wide")
    rings = count <= 8
    chunks = count if rings else 1
    pairs = head_pairs(width)
    step = min(512, whole)
    chain = Chain()
    run = chain.run
    where = jnp.stack([lax.axis_index("wide"), lax.axis_index("narrow")]).astype(jnp.int32)

    block = ((rows, model), bf16)
    outgoing = [block] * parts
    wide_rows = ((whole, model), bf16)
    row = lambda v: v.reshape(1, -1)
    gain_one, bias_one, gain_two, bias_two = map(row, (attn_norm_gain, attn_norm_bias, ffn_norm_gain, ffn_norm_bias))
    out_bias, down_bias, up_bias = row(out_bias), row(down_bias), row(up_bias)

    def columns(three_parts):
        return jnp.concatenate([v[:, low : low + wide] for low, wide in pairs for v in three_parts], axis=1)

    weight_t = jnp.transpose(input_weight, (1, 2, 0)).reshape(3 * width, model)
    zero = jnp.zeros((1, width), f32)
    project_bias = columns([row(query_bias).astype(f32), zero, row(value_bias).astype(f32)])
    project_scale = columns([zero + score_scale, zero + 1.0, zero + 1.0])

    def gather(own):
        return [own, swap(own, "narrow", 1), swap(own, "narrow", 2)]

    def finish(*arrived, pieces=1, cover=False):
        made = run(
            functools.partial(relay, number=len(arrived)),
            [((rows // pieces, model), bf16)] * (len(arrived) * pieces),
            *[a[2] for a in arrived],
            cover=cover,
        )
        for i, a in enumerate(arrived):
            own = made[i * pieces : (i + 1) * pieces]
            a[2:] = [*own, *[swap(piece, "narrow", 1) for piece in own]]

    def share(made):
        own, near, partner, far = made
        return [own, partner, swap(far, "narrow", 1), swap(near, "narrow", 1)]

    def send(shares):
        own, partner, far, near = shares
        (both,) = run(pair_sum, [block], partner, far)
        return [own, near, swap(both, "narrow", 2)]

    def fresh():
        return [None] * len(micros)

    normed, given, qkv, normed_all, mixed, logs, shares, shares_down, resid, normed_two_b = (fresh() for _ in range(10))
    activ, pre_grad, up_bias_grad, two_all, given_all, resid_grad, top = (fresh() for _ in range(7))
    sums_two, sums_one, stack_sums, out_rows, grad_rows = (fresh() for _ in range(5))
    pair_grads = [[] for _ in micros]

    def do_norm_one(m):
        (own,) = run(functools.partial(norm_one, m=m), [block], tokens, gain_one, bias_one)
        normed[m] = gather(own)

    def do_scale(m):
        (own,) = run(functools.partial(scale_cot, m=m, count=count), [block], cotangent, smem=(where, cell_of, query_count), cover=True)
        given[m] = gather(own)

    def do_project(m):
        qkv[m], normed_all[m] = run(
            functools.partial(project, parts=parts),
            [((whole, 3 * width), bf16), wide_rows],
            *normed[m],
            weight,
            project_bias,
            project_scale,
        )

    def do_attend(m):
        mixed[m], logs[m], *made = run(
            functools.partial(attend, step=whole),
            [((whole, width), bf16), ((8, whole), f32), *outgoing],
            qkv[m],
            out_weight,
            limit=24,
        )
        shares[m] = share(made)

    def do_send(m):
        shares[m] = send(shares[m])

    def do_norm_two(m):
        resid[m], own = run(
            functools.partial(norm_two, m=m),
            [((rows, model), f32), block],
            tokens,
            *shares[m],
            out_bias,
            gain_two,
            bias_two,
            cover=m == 0,
        )
        normed_two_b[m] = gather(own)

    def do_feed(m):
        activ[m], pre_grad[m], up_bias_grad[m], two_all[m], given_all[m] = run(
            functools.partial(feed, parts=parts, blocks=len(normed_two_b[m])),
            [((whole, hidden), bf16), ((whole, hidden), bf16), ((1, hidden), f32), wide_rows, wide_rows],
            *normed_two_b[m],
            *given[m],
            up_weight,
            up_bias,
            down_weight,
        )

    def do_up_back(m):
        shares[m] = share(run(times_back, outgoing, pre_grad[m], up_weight))

    def do_down(m):
        shares_down[m] = share(run(times, outgoing, activ[m], down_weight))

    def do_send_down(m):
        shares_down[m] = send(shares_down[m])

    def do_norm_two_back(m):
        resid_grad[m], own, sums_two[m] = run(
            functools.partial(norm_two_back, m=m, count=count),
            [((rows, model), f32), block, ((8, model), f32)],
            cotangent,
            resid[m],
            *shares[m],
            gain_two,
            smem=(where, cell_of, query_count),
            cover=True,
        )
        top[m] = gather(own)

    def do_attend_back(m, p):
        low, wide = pairs[p]
        (made,) = run(
            functools.partial(attend_back, parts=parts, step=step, low=low, wide=wide),
            [((whole, 3 * wide), bf16)],
            qkv[m],
            logs[m],
            mixed[m],
            out_weight,
            *top[m],
            scratch=[
                pltpu.VMEM((whole, wide), f32),
                pltpu.VMEM((whole, wide), f32),
                pltpu.VMEM((whole, wide), bf16),
                pltpu.VMEM((8 * (wide // HEAD), whole), f32),
            ],
            limit=20,
        )
        pair_grads[m].append(made)

    def do_project_back(m):
        *made, stack_sums[m] = run(
            functools.partial(project_back, pairs=len(pairs)),
            [*outgoing, ((1, 3 * width), f32)],
            *pair_grads[m],
            weight,
        )
        shares[m] = share(made)

    def do_norm_one_back(m):
        grad_rows[m], sums_one[m] = run(
            functools.partial(norm_one_back, m=m),
            [((rows, model), f32), ((8, model), f32)],
            tokens,
            resid_grad[m],
            *shares[m],
            gain_one,
        )

    hops = [("narrow", 1 << k) for k in range(parts.bit_length() - 1)]
    hops += [("wide", 1 << k) for k in range(count.bit_length() - 1)]
    vectors = []

    def next_vectors():
        done = len(vectors)
        if done == 0:
            return [*sums_one, *sums_two], 0
        if hops[done - 1][0] == "narrow" and hops[done][0] == "wide":
            return [*vectors[-1], *up_bias_grad, *stack_sums], len(micros)
        return vectors[-1], 0

    def add_vectors(own):
        done = len(vectors)
        vectors.append((own, swap(own, *hops[done])) if done < len(hops) else (own,))

    def do_vectors():
        given_now, joined = next_vectors()
        body = functools.partial(vector_join, number=joined) if joined else vector_sum
        add_vectors(run(body, [((8, model), f32)], *given_now)[0])

    def do_pass():
        if not rings:
            return
        given_now, joined = next_vectors() if len(vectors) <= len(hops) else ([], 0)
        if not given_now and len(attn.have) == count - 1:
            attn.have.append(attn.moving)
            return
        made = run(
            functools.partial(ring_pass, number=len(given_now), joined=joined),
            [(attn.moving.shape, bf16)] + ([((8, model), f32)] if given_now else []),
            attn.moving,
            *given_now,
        )
        attn.arrive(made[0])
        if given_now:
            add_vectors(made[1])

    def do_add_rows(m):
        (out_rows[m],) = run(add_rows, [block], resid[m], *shares_down[m], down_bias)

    def first_product(first, second):
        return run(product, [((first.shape[1], second.shape[1]), bf16)], first, second)[0]

    def ffn_grad(first, second, other, before=()):
        rows, cols = other.shape
        shapes = [((rows // chunks, cols), bf16)] * chunks
        if before:
            shapes.append(((2 * rows // chunks, cols), bf16))
        return run(
            functools.partial(weight_grad, before=len(before[:1])),
            shapes,
            first,
            second,
            other,
            *before[:1],
            smem=(where,),
            scratch=[pltpu.VMEM((rows, cols), bf16)],
            limit=16,
        )

    def attn_grad():
        made = run(
            functools.partial(projection_grad, micros=len(micros), pairs=len(pairs), parts=parts),
            [((4 * width // chunks, model), bf16)] * chunks,
            *normed_all,
            *[g for m in micros for g in pair_grads[m]],
            *[t for m in micros for t in top[m]],
            *mixed,
            smem=(where,),
            scratch=[pltpu.VMEM((4 * width, model), bf16)],
            limit=20,
        )
        attn.start(made[0], (made,))

    ffn_shapes = [(hidden, model), (model, hidden)]
    attn_shapes = [(3 * width, model), (width, model)]
    ffn = Ring(chain, where, ffn_shapes, True) if rings else Whole(ffn_shapes)
    attn = Ring(chain, where, attn_shapes, False) if rings else Whole(attn_shapes)

    do_norm_one(0)
    (weight,) = run(by_pairs, [((3 * width, model), bf16)], weight_t)
    chain.hold(normed[0][1])
    finish(normed[0])
    do_norm_one(1)
    do_scale(0)
    do_project(0)
    do_attend(0)
    chain.hold(normed[1][1], given[0][1])
    finish(normed[1], given[0], cover=True)
    do_scale(1)
    do_send(0)
    chain.hold(given[1][1])
    do_project(1)
    do_attend(1)
    chain.hold(given[1][2])
    do_norm_two(0)
    do_send(1)
    finish(given[1])
    chain.hold(normed_two_b[0][1])
    finish(normed_two_b[0], pieces=4)
    do_feed(0)
    do_norm_two(1)
    chain.hold(normed_two_b[1][1])
    do_up_back(0)
    down_first = first_product(activ[0], given_all[0])
    up_first = first_product(two_all[0], pre_grad[0])
    do_down(0)
    finish(normed_two_b[1], cover=True)
    do_send(0)
    do_feed(1)
    do_up_back(1)
    do_norm_two_back(0)
    chain.hold(top[0][1])
    down_chunks = ffn_grad(activ[1], given_all[1], down_first)
    *up_chunks, both = ffn_grad(two_all[1], pre_grad[1], up_first, down_chunks)
    ffn.start(both, (down_chunks, up_chunks))
    finish(top[0], cover=True)
    do_send(1)
    do_down(1)
    ffn.add()
    do_attend_back(0, 0)
    ffn.add()
    do_attend_back(0, 1)
    do_norm_two_back(1)
    ffn.add()
    do_attend_back(0, 2)
    do_project_back(0)
    ffn.add()
    do_send_down(0)
    chain.hold(top[1][1])
    finish(top[1], cover=True)
    do_attend_back(1, 0)
    ffn.add()
    do_send(0)
    do_attend_back(1, 1)
    ffn.add()
    do_attend_back(1, 2)
    attn_grad()
    chain.hold(shares_down[0][2])
    ffn.add()
    do_add_rows(0)
    attn.add()
    do_project_back(1)
    attn.add()
    ffn.forward()
    do_norm_one_back(0)
    attn.add()
    do_send(1)
    attn.add()
    do_send_down(1)
    ffn.forward()
    attn.add()
    attn.add()
    do_norm_one_back(1)
    do_vectors()
    ffn.forward()
    attn.add()
    do_pass()
    ffn.forward()
    do_pass()
    attn.store()
    do_pass()
    ffn.forward()
    do_pass()
    do_add_rows(1)
    attn.store()
    do_pass()
    ffn.forward()
    do_pass()
    attn.store()
    ffn.forward()
    do_pass()
    attn.store()

    while len(vectors) <= len(hops):
        do_vectors()
    vector_sums = vectors[-1][0]
    up_bias_sum = vector_sums[6, :hidden]
    stack_sum = vector_sums[7, : 3 * width]

    def plain(j):
        return jnp.concatenate([stack_sum[3 * low + j * wide : 3 * low + (j + 1) * wide] for low, wide in pairs])

    return (
        jnp.stack(out_rows)[:, None],
        jnp.stack(grad_rows)[:, None],
        vector_sums[4],
        vector_sums[5],
        jnp.transpose(attn.outs[0].reshape(3, width, model), (2, 0, 1)),
        plain(0),
        plain(2),
        attn.outs[1],
        vector_sums[0],
        vector_sums[1],
        vector_sums[2],
        ffn.outs[1],
        up_bias_sum,
        ffn.outs[0],
        vector_sums[3],
    )


def solution(mesh):
    in_specs = (
        P(None, "wide", "narrow", None),
        P(None, "wide", "narrow", None),
        P(),
        P(),
        P(),
        P(),
        P(None, None, "narrow"),
        P("narrow"),
        P("narrow"),
        P("narrow", None),
        P(),
        P(),
        P(),
        P(None, "narrow"),
        P("narrow"),
        P("narrow", None),
        P(),
    )
    out_specs = (
        P(None, "wide", "narrow", None),
        P(None, "wide", "narrow", None),
        P(),
        P(),
        P(None, None, "narrow"),
        P("narrow"),
        P("narrow"),
        P("narrow", None),
        P(),
        P(),
        P(),
        P(None, "narrow"),
        P("narrow"),
        P("narrow", None),
        P(),
    )
    return jax.shard_map(local, mesh=mesh, in_specs=in_specs, out_specs=out_specs, check_vma=False)
```

```python
import functools

import jax
import jax.numpy as jnp
from jax import lax
from jax.experimental import pallas as pl
from jax.experimental.pallas import tpu as pltpu
from jax.sharding import PartitionSpec as P

HEAD = 64
LANES = 128
TILE = 256
norm_eps = 1e-05
score_scale = 0.125
bf16 = jnp.bfloat16
f32 = jnp.float32


class Chain:
    def __init__(self):
        self.last = []
        self.held = []

    def hold(self, *arrays):
        self.held += arrays

    def run(self, body, outs, *ins, smem=(), scratch=(), alias=None, anywhere=(), out_anywhere=(), limit=6, token=0, cover=False):
        unread = [*self.last, *self.held]
        count = len(smem) + len(ins)
        specs = [pl.BlockSpec(memory_space=pltpu.SMEM)] * len(smem)
        specs += [pl.BlockSpec(memory_space=pl.ANY if i in anywhere else pltpu.VMEM) for i in range(len(ins))]
        specs += [pl.BlockSpec(memory_space=pl.ANY)] * len(unread)

        def inner(*refs):
            body(*refs[:count], *refs[count + len(unread) :])

        made = pl.pallas_call(
            inner,
            out_shape=tuple(jax.ShapeDtypeStruct(*o) for o in outs),
            in_specs=specs,
            out_specs=tuple(
                pl.BlockSpec(memory_space=pl.ANY if i in out_anywhere else pltpu.VMEM) for i in range(len(outs))
            ),
            scratch_shapes=scratch,
            input_output_aliases={} if alias is None else {len(smem) + k: v for k, v in alias.items()},
            compiler_params=pltpu.CompilerParams(vmem_limit_bytes=limit << 20),
            cost_estimate=pl.CostEstimate(flops=10**12 if cover else 1, bytes_accessed=1, transcendentals=0),
            name=body.func.__name__ if isinstance(body, functools.partial) else body.__name__,
        )(*smem, *ins, *unread)
        self.last, self.held = [made[token]], []
        return made


def dot32(first, second, first_dim, second_dim):
    return lax.dot_general(
        first, second, (((first_dim,), (second_dim,)), ((), ())), preferred_element_type=f32
    )


def statistics(values):
    average = jnp.mean(values, axis=-1, keepdims=True)
    centred = values - average
    inverse = lax.rsqrt(jnp.mean(centred * centred, axis=-1, keepdims=True) + norm_eps)
    return centred * inverse, inverse


def norm_back(grad, normed, inverse, gain):
    scaled = grad * gain
    mean_one = jnp.mean(scaled, axis=-1, keepdims=True)
    mean_two = jnp.mean(scaled * normed, axis=-1, keepdims=True)
    return inverse * (scaled - mean_one - normed * mean_two)


def of_head(values, j, axis=1):
    if values.shape[axis] <= HEAD:
        return values
    place = lax.broadcasted_iota(jnp.int32, values.shape, axis)
    return jnp.where((place >= HEAD * j) & (place < HEAD * (j + 1)), values, jnp.zeros_like(values))


def head_pairs(width):
    return [(low, min(LANES, width - low)) for low in range(0, width, LANES)]


def relay(*refs, number):
    arrived, outs = refs[:number], refs[number:]
    each = len(outs) // number
    for i, rows in enumerate(arrived):
        size = rows.shape[0] // each
        for k in range(each):
            outs[i * each + k][...] = rows[k * size : (k + 1) * size, :]


def by_pairs(weight_t, out):
    width = out.shape[0] // 3
    for low, wide in head_pairs(width):
        for j in range(3):
            out[3 * low + j * wide : 3 * low + (j + 1) * wide, :] = weight_t[
                j * width + low : j * width + low + wide, :
            ]


def norm_one(tok, gain, bias, out, *, m):
    normed, _ = statistics(tok[m, 0].astype(f32))
    out[...] = (normed * gain[...].astype(f32) + bias[...].astype(f32)).astype(bf16)


def loss_grad(where, cells, queries, cot, m, count):
    number = queries[cells[where[0] + m * count]]
    scale = jnp.sqrt(jnp.full((1, cot.shape[3]), number, jnp.int32).astype(f32) / 500.0)
    return cot[m, 0].astype(f32) * scale


def scale_cot(where, cells, queries, cot, out, *, m, count):
    out[...] = loss_grad(where, cells, queries, cot, m, count).astype(bf16)


def project(*refs, parts):
    blocks = refs[:parts]
    weight, bias, scale = refs[parts : parts + 3]
    out, whole = refs[parts + 3 :]
    rows = blocks[0].shape[0]
    for b in range(parts):
        values = blocks[b][...]
        at = slice(b * rows, (b + 1) * rows)
        whole[at, :] = values
        out[at, :] = ((dot32(values, weight[...], 1, 1) + bias[...]) * scale[...]).astype(bf16)


def attend(qkv, out_weight, attended, logs, *outs, step):
    whole = qkv.shape[0]
    head = 0
    for low, wide in head_pairs(out_weight.shape[0]):
        heads = wide // HEAD
        key_pair = qkv[:, 3 * low + wide : 3 * low + 2 * wide]
        value_t = qkv[:, 3 * low + 2 * wide : 3 * low + 3 * wide].T
        keys = [of_head(key_pair, j) for j in range(heads)]
        values = [of_head(value_t, j, 0) for j in range(heads)]
        for start in range(0, whole, step):
            at = slice(start, start + step)
            query = qkv[at, 3 * low : 3 * low + wide]
            total = None
            for j in range(heads):
                scores = dot32(keys[j], query, 1, 1)
                top = jnp.max(scores, axis=0, keepdims=True)
                powers = jnp.exp(scores - top)
                length = jnp.sum(powers, axis=0, keepdims=True)
                mixed = dot32(values[j], powers.astype(bf16), 1, 0) * (1.0 / length)
                total = mixed if total is None else total + mixed
                logs[head + j : head + j + 1, at] = top + jnp.log(length)
            attended[at, low : low + wide] = total.T.astype(bf16)
        head += heads
    rows = whole // len(outs)
    for b, out in enumerate(outs):
        out[...] = dot32(attended[b * rows : (b + 1) * rows, :], out_weight[...], 1, 0).astype(bf16)


def pair_sum(first, second, out):
    out[...] = (first[...].astype(f32) + second[...].astype(f32)).astype(bf16)


def three(first, second, third):
    return first[...].astype(f32) + second[...].astype(f32) + third[...].astype(f32)


def norm_two(tok, first, second, third, out_bias, gain, bias, resid, normed, *, m):
    value = tok[m, 0].astype(f32) + three(first, second, third) + out_bias[...].astype(f32)
    resid[...] = value
    hat, _ = statistics(value)
    normed[...] = (hat * gain[...].astype(f32) + bias[...].astype(f32)).astype(bf16)


def feed(*refs, parts, blocks):
    normed, grads, refs = refs[:blocks], refs[blocks : blocks + parts], refs[blocks + parts :]
    up, up_bias, down, activ, pre_grad, bias_grad, normed_all, grads_all = refs
    for whole, pieces in ((normed_all, normed), (grads_all, grads)):
        low = 0
        for piece in pieces:
            whole[low : low + piece.shape[0], :] = piece[...]
            low += piece.shape[0]
    rows = grads[0].shape[0]
    for low in range(0, up.shape[1], TILE):
        cols = slice(low, low + TILE)
        total = None
        for b in range(parts):
            at = slice(b * rows, (b + 1) * rows)
            pre = dot32(normed_all[at, :], up[:, cols], 1, 0) + up_bias[:, cols].astype(f32)
            cumul = 0.5 + 0.5 * lax.erf(pre * 0.7071067811865476)
            density = jnp.exp(-0.5 * pre * pre) * 0.3989422804014327
            activ[at, cols] = (pre * cumul).astype(bf16)
            back = dot32(grads_all[at, :], down[cols, :], 1, 1)
            grad = (back * (cumul + pre * density)).astype(bf16)
            pre_grad[at, cols] = grad
            part = jnp.sum(grad.astype(f32), axis=0, keepdims=True)
            total = part if total is None else total + part
        bias_grad[:, cols] = total


def times(value, weight, *outs):
    put_tiles(outs, lambda at, cols: dot32(value[at, :], weight[:, cols], 1, 0), value.shape[0])


def times_back(value, weight, *outs):
    put_tiles(outs, lambda at, cols: dot32(value[at, :], weight[cols, :], 1, 1), value.shape[0])


def put_tiles(outs, share_of, whole):
    rows, model = outs[0].shape

    def tile(i, carry):
        cols = pl.ds(pl.multiple_of(i * TILE, TILE), TILE)
        for b, out in enumerate(outs):
            out[:, cols] = share_of(slice(b * rows, (b + 1) * rows), cols).astype(bf16)
        return carry

    lax.fori_loop(0, model // TILE, tile, 0)


def product(first, second, out):
    def tile(i, carry):
        rows = pl.ds(pl.multiple_of(i * TILE, TILE), TILE)
        out[rows, :] = dot32(first[:, rows], second[...], 0, 0).astype(bf16)
        return carry

    lax.fori_loop(0, out.shape[0] // TILE, tile, 0)


def weight_grad(where, first, second, other, *refs, before):
    chunks, whole = refs[before:-1], refs[-1]

    def tile(i, carry):
        rows = pl.ds(pl.multiple_of(i * TILE, TILE), TILE)
        total = dot32(first[:, rows], second[...], 0, 0) + other[rows, :].astype(f32)
        whole[rows, :] = total.astype(bf16)
        return carry

    lax.fori_loop(0, whole.shape[0] // TILE, tile, 0)
    if before:
        chunks, both = chunks[:-1], chunks[-1]
        size = chunks[0].shape[0]
        both[:size, :] = refs[0][...]
        put_chunks(where, chunks, whole)
        both[size:, :] = chunks[0][...]
    else:
        put_chunks(where, chunks, whole)


def ring_chunk(where, count, step):
    half = where[0] // 2
    place = jnp.where(where[0] % 2 == 0, half, count - 1 - half)
    return lax.rem(place + jnp.where(where[1] % 2 == 0, count - step, step), count)


def put_chunks(where, chunks, whole):
    for s, chunk in enumerate(chunks):
        size = chunk.shape[0]
        which = ring_chunk(where, len(chunks), (s + 1) % len(chunks)) if len(chunks) > 1 else 0
        chunk[...] = whole[pl.ds(pl.multiple_of(which * size, size), size), :]


def norm_two_back(where, cells, queries, cot, resid, first, second, third, gain, out, rounded, sums, *, m, count):
    top = loss_grad(where, cells, queries, cot, m, count)
    grad = three(first, second, third)
    hat, inverse = statistics(resid[...])
    back = top + norm_back(grad, hat, inverse, gain[...].astype(f32))
    out[...] = back
    rounded[...] = back.astype(bf16)
    sums[0:1, :] = jnp.sum(back, axis=0, keepdims=True)
    sums[1:2, :] = jnp.sum(grad * hat, axis=0, keepdims=True)
    sums[2:3, :] = jnp.sum(grad, axis=0, keepdims=True)
    sums[3:4, :] = jnp.sum(top, axis=0, keepdims=True)
    sums[4:8, :] = jnp.zeros_like(sums[4:8, :])


def attend_back(qkv, logs, mixed, out_weight, *refs, parts, step, low, wide):
    grads = refs[:parts]
    out, key_grad, value_grad, given, inner = refs[parts:]
    whole = qkv.shape[0]
    rows = whole // parts
    heads = wide // HEAD
    head = low // HEAD
    ones = jnp.concatenate([of_head(jnp.ones((8, wide), bf16), j) for j in range(heads)], axis=0)
    for b in range(parts):
        at = slice(b * rows, (b + 1) * rows)
        value = dot32(grads[b][...], out_weight[low : low + wide, :], 1, 1).astype(bf16)
        given[at, :] = value
        both = value.astype(f32) * mixed[at, low : low + wide].astype(f32)
        high = both.astype(bf16)
        rest = (both - high.astype(f32)).astype(bf16)
        inner[:, at] = dot32(ones, high, 1, 1) + dot32(ones, rest, 1, 1)
    key_pair = qkv[:, 3 * low + wide : 3 * low + 2 * wide]
    value_pair = qkv[:, 3 * low + 2 * wide : 3 * low + 3 * wide]
    key_t = key_pair.T
    keys = [of_head(key_pair, j) for j in range(heads)]
    values = [of_head(value_pair, j) for j in range(heads)]
    keys_t = [of_head(key_t, j, 0) for j in range(heads)]
    key_grad[...] = jnp.zeros_like(key_grad)
    value_grad[...] = jnp.zeros_like(value_grad)

    def block(i, carry):
        start = pl.multiple_of(i * step, step)
        query = qkv[pl.ds(start, step), 3 * low : 3 * low + wide]
        grad = given[pl.ds(start, step), :]
        total = None
        for j in range(heads):
            scores = dot32(keys[j], query, 1, 1)
            weights = jnp.exp(scores - logs[head + j : head + j + 1, pl.ds(start, step)])
            back = dot32(values[j], grad, 1, 1)
            score_grad = (weights * (back - inner[8 * j : 8 * j + 1, pl.ds(start, step)])).astype(bf16)
            value_grad[...] += dot32(weights.astype(bf16), of_head(grad, j), 1, 0)
            key_grad[...] += dot32(score_grad, of_head(query, j), 1, 0)
            part = dot32(keys_t[j], score_grad, 1, 0)
            total = part if total is None else total + part
        out[pl.ds(start, step), :wide] = (total.T * score_scale).astype(bf16)
        return carry

    lax.fori_loop(0, whole // step, block, 0)
    out[:, wide : 2 * wide] = key_grad[...].astype(bf16)
    out[:, 2 * wide :] = value_grad[...].astype(bf16)


def project_back(*refs, pairs):
    grads, weight, outs, sums = refs[:pairs], refs[pairs], refs[pairs + 1 : -1], refs[-1]

    def share_of(at, cols):
        total, low = None, 0
        for grad in grads:
            wide = grad.shape[1]
            part = dot32(grad[at, :], weight[low : low + wide, cols], 1, 0)
            total = part if total is None else total + part
            low += wide
        return total

    put_tiles(outs, share_of, grads[0].shape[0])
    low = 0
    for grad in grads:
        wide = grad.shape[1]
        sums[:, low : low + wide] = jnp.sum(grad[...].astype(f32), axis=0, keepdims=True)
        low += wide


def projection_grad(where, *refs, micros, pairs, parts):
    normed, refs = refs[:micros], refs[micros:]
    grads, refs = [refs[m * pairs : (m + 1) * pairs] for m in range(micros)], refs[micros * pairs :]
    tops, refs = [refs[m * parts : (m + 1) * parts] for m in range(micros)], refs[micros * parts :]
    mixed, refs = refs[:micros], refs[micros:]
    chunks, out = refs[:-1], refs[-1]
    width = mixed[0].shape[1]
    rows = tops[0][0].shape[0]
    for p, (low, wide) in enumerate(head_pairs(width)):
        total = None
        for m in range(micros):
            part = dot32(grads[m][p][...], normed[m][...], 0, 0)
            total = part if total is None else total + part
        for j in range(3):
            out[j * width + low : j * width + low + wide, :] = total[j * wide : (j + 1) * wide].astype(bf16)
        total = None
        for m in range(micros):
            for b in range(parts):
                part = dot32(mixed[m][b * rows : (b + 1) * rows, low : low + wide], tops[m][b][...], 0, 0)
                total = part if total is None else total + part
        out[3 * width + low : 3 * width + low + wide, :] = total.astype(bf16)
    put_chunks(where, chunks, out)


def ring_add(arrived, *refs):
    low = 0
    for part in refs[:-1]:
        at = slice(low, low + part.shape[0])
        refs[-1][at, :] = (arrived[at, :].astype(f32) + part[...].astype(f32)).astype(bf16)
        low += part.shape[0]


def ring_store(where, *refs, steps, count, stacked):
    moved, refs = refs[: len(steps)], refs[len(steps) :]
    ahead, first, second, buffer, sems = refs[-5:]
    ahead[...] = moved[-1][...]
    size = buffer.shape[1] // 2 if stacked else buffer.shape[1]
    copies = []
    for k, step in enumerate(steps):
        buffer[k] = moved[k][...].astype(f32)
        row = pl.multiple_of(ring_chunk(where, count, step) * size, size)
        if stacked:
            for i, target in enumerate((first, second)):
                source = buffer.at[k, pl.ds(i * size, size), :]
                copies.append(pltpu.make_async_copy(source, target.at[pl.ds(row, size), :], sems.at[2 * k + i]))
                copies[-1].start()
        else:
            last = first.shape[0] - size
            to_first = pl.multiple_of(jnp.minimum(row, last), 16)
            to_second = pl.multiple_of(jnp.maximum(row - first.shape[0], 0), 16)
            copy_first = pltpu.make_async_copy(buffer.at[k], first.at[pl.ds(to_first, size), :], sems.at[2 * k])
            copy_second = pltpu.make_async_copy(buffer.at[k], second.at[pl.ds(to_second, size), :], sems.at[2 * k])
            pl.when(row <= last)(copy_first.start)
            pl.when(row > last)(copy_second.start)
            copies.append(copy_first)
    for copy in copies:
        copy.wait()


def norm_one_back(tok, resid_grad, first, second, third, gain, out, sums, *, m):
    grad = three(first, second, third)
    hat, inverse = statistics(tok[m, 0].astype(f32))
    out[...] = resid_grad[...] + norm_back(grad, hat, inverse, gain[...].astype(f32))
    sums[0:4, :] = jnp.zeros_like(sums[0:4, :])
    sums[4:5, :] = jnp.sum(grad * hat, axis=0, keepdims=True)
    sums[5:6, :] = jnp.sum(grad, axis=0, keepdims=True)
    sums[6:8, :] = jnp.zeros_like(sums[6:8, :])


def vector_sum(*refs):
    total = refs[0][...]
    for ref in refs[1:-1]:
        total = total + ref[...]
    refs[-1][...] = total


def ring_pass(moving, *refs, number, joined):
    refs[number][...] = moving[...]
    if joined:
        vector_join(*refs[:number], refs[number + 1], number=joined)
    elif number:
        vector_sum(*refs[:number], refs[number + 1])


def vector_join(first, second, *refs, number):
    up_bias, stack, out = refs[:number], refs[number:-1], refs[-1]
    out[...] = first[...] + second[...]
    for row, parts in ((6, up_bias), (7, stack)):
        total = parts[0][...]
        for part in parts[1:]:
            total = total + part[...]
        out[row : row + 1, : total.shape[1]] = total


def add_rows(resid, first, second, third, bias, out):
    out[...] = (resid[...] + three(first, second, third) + bias[...].astype(f32)).astype(bf16)


def swap(values, axis, bit):
    return lax.ppermute(values, axis, [(i, i ^ bit) for i in range(lax.axis_size(axis))])


def ring_order(count):
    return list(range(0, count, 2)) + list(range(1, count, 2))[::-1]


class Ring:
    def __init__(self, chain, where, shapes, stacked):
        self.chain, self.where, self.shapes, self.stacked = chain, where, shapes, stacked
        self.count = lax.axis_size("wide")
        cores = lax.axis_size("narrow")
        order = ring_order(self.count)
        self.perm = [
            (order[i] * cores + n, order[(i + (1 if n % 2 == 0 else -1)) % self.count] * cores + n)
            for i in range(self.count)
            for n in range(cores)
        ]
        self.have, self.step, self.stored, self.outs = [], 1, 0, None

    def pass_on(self, chunk):
        self.moving = lax.ppermute(chunk, ("wide", "narrow"), self.perm)

    def start(self, chunk, parts):
        self.parts = parts
        self.pass_on(chunk)

    def hold(self):
        self.chain.hold(self.moving)

    def add(self, cover=False):
        (made,) = self.chain.run(
            ring_add,
            [(self.moving.shape, bf16)],
            self.moving,
            *[p[self.step] for p in self.parts],
            cover=cover,
        )
        self.step += 1
        if self.step == self.count:
            self.have.append(made)
        self.pass_on(made)

    def forward(self):
        self.have.append(self.moving)
        copy = self.store()
        if len(self.have) < self.count:
            self.pass_on(copy)

    def arrive(self, made):
        self.have.append(made)
        if len(self.have) < self.count:
            self.pass_on(made)

    def store(self):
        steps = range(self.stored, len(self.have))
        self.stored = len(self.have)
        moved = [self.have[s] for s in steps]
        kept = () if self.outs is None else self.outs
        number = len(moved)
        made = self.chain.run(
            functools.partial(ring_store, steps=tuple(steps), count=self.count, stacked=self.stacked),
            [(moved[-1].shape, bf16)] + [(s, f32) for s in self.shapes],
            *moved,
            *kept,
            smem=(self.where,),
            scratch=[pltpu.VMEM((number, *moved[0].shape), f32), pltpu.SemaphoreType.DMA((2 * number,))],
            alias={number: 1, number + 1: 2} if kept else None,
            anywhere=(number, number + 1) if kept else (),
            out_anywhere=(1, 2),
            limit=6 + (number * moved[0].size * 4 >> 20),
        )
        self.outs = made[1:]
        return made[0]


class Whole:
    def __init__(self, shapes):
        self.shapes = shapes

    def start(self, chunk, parts):
        total = lax.psum(chunk, "wide").astype(f32)
        self.outs = (total[: self.shapes[0][0]], total[self.shapes[0][0] :])

    def hold(self):
        pass

    def add(self, cover=False):
        pass

    def forward(self):
        pass

    def store(self):
        pass


def local(
    tokens,
    cotangent,
    cell_of,
    query_count,
    attn_norm_gain,
    attn_norm_bias,
    input_weight,
    query_bias,
    value_bias,
    out_weight,
    out_bias,
    ffn_norm_gain,
    ffn_norm_bias,
    up_weight,
    up_bias,
    down_weight,
    down_bias,
):
    micros = range(tokens.shape[0])
    rows, model = tokens.shape[2], tokens.shape[3]
    parts = lax.axis_size("narrow")
    whole = rows * parts
    width = input_weight.shape[2]
    hidden = up_weight.shape[1]
    count = lax.axis_size("wide")
    rings = count <= 8
    chunks = count if rings else 1
    pairs = head_pairs(width)
    step = min(512, whole)
    chain = Chain()
    run = chain.run
    where = jnp.stack([lax.axis_index("wide"), lax.axis_index("narrow")]).astype(jnp.int32)

    block = ((rows, model), bf16)
    outgoing = [block] * parts
    wide_rows = ((whole, model), bf16)
    row = lambda v: v.reshape(1, -1)
    gain_one, bias_one, gain_two, bias_two = map(row, (attn_norm_gain, attn_norm_bias, ffn_norm_gain, ffn_norm_bias))
    out_bias, down_bias, up_bias = row(out_bias), row(down_bias), row(up_bias)

    def columns(three_parts):
        return jnp.concatenate([v[:, low : low + wide] for low, wide in pairs for v in three_parts], axis=1)

    weight_t = jnp.transpose(input_weight, (1, 2, 0)).reshape(3 * width, model)
    zero = jnp.zeros((1, width), f32)
    project_bias = columns([row(query_bias).astype(f32), zero, row(value_bias).astype(f32)])
    project_scale = columns([zero + score_scale, zero + 1.0, zero + 1.0])

    def gather(own):
        return [own, swap(own, "narrow", 1), swap(own, "narrow", 2)]

    def finish(*arrived, pieces=1, cover=False):
        made = run(
            functools.partial(relay, number=len(arrived)),
            [((rows // pieces, model), bf16)] * (len(arrived) * pieces),
            *[a[2] for a in arrived],
            cover=cover,
        )
        for i, a in enumerate(arrived):
            own = made[i * pieces : (i + 1) * pieces]
            a[2:] = [*own, *[swap(piece, "narrow", 1) for piece in own]]

    def share(made):
        own, near, partner, far = made
        return [own, partner, swap(far, "narrow", 1), swap(near, "narrow", 1)]

    def send(shares):
        own, partner, far, near = shares
        (both,) = run(pair_sum, [block], partner, far)
        return [own, near, swap(both, "narrow", 2)]

    def fresh():
        return [None] * len(micros)

    normed, given, qkv, normed_all, mixed, logs, shares, shares_down, resid, normed_two_b = (fresh() for _ in range(10))
    activ, pre_grad, up_bias_grad, two_all, given_all, resid_grad, top = (fresh() for _ in range(7))
    sums_two, sums_one, stack_sums, out_rows, grad_rows = (fresh() for _ in range(5))
    pair_grads = [[] for _ in micros]

    def do_norm_one(m):
        (own,) = run(functools.partial(norm_one, m=m), [block], tokens, gain_one, bias_one)
        normed[m] = gather(own)

    def do_scale(m):
        (own,) = run(functools.partial(scale_cot, m=m, count=count), [block], cotangent, smem=(where, cell_of, query_count), cover=True)
        given[m] = gather(own)

    def do_project(m):
        qkv[m], normed_all[m] = run(
            functools.partial(project, parts=parts),
            [((whole, 3 * width), bf16), wide_rows],
            *normed[m],
            weight,
            project_bias,
            project_scale,
        )

    def do_attend(m):
        mixed[m], logs[m], *made = run(
            functools.partial(attend, step=whole),
            [((whole, width), bf16), ((8, whole), f32), *outgoing],
            qkv[m],
            out_weight,
            limit=24,
        )
        shares[m] = share(made)

    def do_send(m):
        shares[m] = send(shares[m])

    def do_norm_two(m):
        resid[m], own = run(
            functools.partial(norm_two, m=m),
            [((rows, model), f32), block],
            tokens,
            *shares[m],
            out_bias,
            gain_two,
            bias_two,
            cover=m == 0,
        )
        normed_two_b[m] = gather(own)

    def do_feed(m):
        activ[m], pre_grad[m], up_bias_grad[m], two_all[m], given_all[m] = run(
            functools.partial(feed, parts=parts, blocks=len(normed_two_b[m])),
            [((whole, hidden), bf16), ((whole, hidden), bf16), ((1, hidden), f32), wide_rows, wide_rows],
            *normed_two_b[m],
            *given[m],
            up_weight,
            up_bias,
            down_weight,
        )

    def do_up_back(m):
        shares[m] = share(run(times_back, outgoing, pre_grad[m], up_weight))

    def do_down(m):
        shares_down[m] = share(run(times, outgoing, activ[m], down_weight))

    def do_send_down(m):
        shares_down[m] = send(shares_down[m])

    def do_norm_two_back(m):
        resid_grad[m], own, sums_two[m] = run(
            functools.partial(norm_two_back, m=m, count=count),
            [((rows, model), f32), block, ((8, model), f32)],
            cotangent,
            resid[m],
            *shares[m],
            gain_two,
            smem=(where, cell_of, query_count),
            cover=m > 0,
        )
        top[m] = gather(own)

    def do_attend_back(m, p):
        low, wide = pairs[p]
        (made,) = run(
            functools.partial(attend_back, parts=parts, step=step, low=low, wide=wide),
            [((whole, 3 * wide), bf16)],
            qkv[m],
            logs[m],
            mixed[m],
            out_weight,
            *top[m],
            scratch=[
                pltpu.VMEM((whole, wide), f32),
                pltpu.VMEM((whole, wide), f32),
                pltpu.VMEM((whole, wide), bf16),
                pltpu.VMEM((8 * (wide // HEAD), whole), f32),
            ],
            limit=20,
        )
        pair_grads[m].append(made)

    def do_project_back(m):
        *made, stack_sums[m] = run(
            functools.partial(project_back, pairs=len(pairs)),
            [*outgoing, ((1, 3 * width), f32)],
            *pair_grads[m],
            weight,
        )
        shares[m] = share(made)

    def do_norm_one_back(m):
        grad_rows[m], sums_one[m] = run(
            functools.partial(norm_one_back, m=m),
            [((rows, model), f32), ((8, model), f32)],
            tokens,
            resid_grad[m],
            *shares[m],
            gain_one,
        )

    hops = [("narrow", 1 << k) for k in range(parts.bit_length() - 1)]
    hops += [("wide", 1 << k) for k in range(count.bit_length() - 1)]
    vectors = []

    def next_vectors():
        done = len(vectors)
        if done == 0:
            return [*sums_one, *sums_two], 0
        if hops[done - 1][0] == "narrow" and hops[done][0] == "wide":
            return [*vectors[-1], *up_bias_grad, *stack_sums], len(micros)
        return vectors[-1], 0

    def add_vectors(own):
        done = len(vectors)
        vectors.append((own, swap(own, *hops[done])) if done < len(hops) else (own,))

    def do_vectors():
        given_now, joined = next_vectors()
        body = functools.partial(vector_join, number=joined) if joined else vector_sum
        add_vectors(run(body, [((8, model), f32)], *given_now)[0])

    def do_pass():
        if not rings:
            return
        given_now, joined = next_vectors() if len(vectors) <= len(hops) else ([], 0)
        if not given_now and len(attn.have) == count - 1:
            attn.have.append(attn.moving)
            return
        made = run(
            functools.partial(ring_pass, number=len(given_now), joined=joined),
            [(attn.moving.shape, bf16)] + ([((8, model), f32)] if given_now else []),
            attn.moving,
            *given_now,
        )
        attn.arrive(made[0])
        if given_now:
            add_vectors(made[1])

    def do_add_rows(m):
        (out_rows[m],) = run(add_rows, [block], resid[m], *shares_down[m], down_bias)

    def first_product(first, second):
        return run(product, [((first.shape[1], second.shape[1]), bf16)], first, second)[0]

    def ffn_grad(first, second, other, before=()):
        rows, cols = other.shape
        shapes = [((rows // chunks, cols), bf16)] * chunks
        if before:
            shapes.append(((2 * rows // chunks, cols), bf16))
        return run(
            functools.partial(weight_grad, before=len(before[:1])),
            shapes,
            first,
            second,
            other,
            *before[:1],
            smem=(where,),
            scratch=[pltpu.VMEM((rows, cols), bf16)],
            limit=16,
        )

    def attn_grad():
        made = run(
            functools.partial(projection_grad, micros=len(micros), pairs=len(pairs), parts=parts),
            [((4 * width // chunks, model), bf16)] * chunks,
            *normed_all,
            *[g for m in micros for g in pair_grads[m]],
            *[t for m in micros for t in top[m]],
            *mixed,
            smem=(where,),
            scratch=[pltpu.VMEM((4 * width, model), bf16)],
            limit=20,
        )
        attn.start(made[0], (made,))

    ffn_shapes = [(hidden, model), (model, hidden)]
    attn_shapes = [(3 * width, model), (width, model)]
    ffn = Ring(chain, where, ffn_shapes, True) if rings else Whole(ffn_shapes)
    attn = Ring(chain, where, attn_shapes, False) if rings else Whole(attn_shapes)

    do_norm_one(0)
    (weight,) = run(by_pairs, [((3 * width, model), bf16)], weight_t)
    chain.hold(normed[0][1])
    finish(normed[0])
    do_norm_one(1)
    do_scale(0)
    do_project(0)
    do_attend(0)
    chain.hold(normed[1][1], given[0][1])
    finish(normed[1], given[0], cover=True)
    do_scale(1)
    do_send(0)
    chain.hold(given[1][1])
    do_project(1)
    do_attend(1)
    chain.hold(given[1][2])
    do_norm_two(0)
    do_send(1)
    finish(given[1])
    chain.hold(normed_two_b[0][1])
    finish(normed_two_b[0], pieces=4)
    do_feed(0)
    do_norm_two(1)
    chain.hold(normed_two_b[1][1])
    do_up_back(0)
    down_first = first_product(activ[0], given_all[0])
    up_first = first_product(two_all[0], pre_grad[0])
    do_down(0)
    finish(normed_two_b[1], cover=True)
    do_send(0)
    do_feed(1)
    down_chunks = ffn_grad(activ[1], given_all[1], down_first)
    *up_chunks, both = ffn_grad(two_all[1], pre_grad[1], up_first, down_chunks)
    ffn.start(both, (down_chunks, up_chunks))
    do_up_back(1)
    do_norm_two_back(0)
    do_down(1)
    ffn.add()
    do_send(1)
    chain.hold(top[0][1])
    finish(top[0])
    do_attend_back(0, 0)
    ffn.add()
    do_attend_back(0, 1)
    do_norm_two_back(1)
    ffn.add()
    do_attend_back(0, 2)
    do_project_back(0)
    ffn.add()
    do_send_down(0)
    chain.hold(top[1][1])
    finish(top[1], cover=True)
    do_attend_back(1, 0)
    ffn.add()
    do_send(0)
    do_attend_back(1, 1)
    ffn.add()
    do_attend_back(1, 2)
    attn_grad()
    chain.hold(shares_down[0][2])
    ffn.add()
    do_add_rows(0)
    attn.add()
    do_project_back(1)
    attn.add()
    ffn.forward()
    do_norm_one_back(0)
    attn.add()
    do_send(1)
    attn.add()
    do_send_down(1)
    ffn.forward()
    attn.add()
    attn.add()
    do_norm_one_back(1)
    do_vectors()
    ffn.forward()
    attn.add()
    do_pass()
    ffn.forward()
    do_pass()
    attn.store()
    do_pass()
    ffn.forward()
    do_pass()
    do_add_rows(1)
    attn.store()
    do_pass()
    ffn.forward()
    do_pass()
    attn.store()
    ffn.forward()
    do_pass()
    attn.store()

    while len(vectors) <= len(hops):
        do_vectors()
    vector_sums = vectors[-1][0]
    up_bias_sum = vector_sums[6, :hidden]
    stack_sum = vector_sums[7, : 3 * width]

    def plain(j):
        return jnp.concatenate([stack_sum[3 * low + j * wide : 3 * low + (j + 1) * wide] for low, wide in pairs])

    return (
        jnp.stack(out_rows)[:, None],
        jnp.stack(grad_rows)[:, None],
        vector_sums[4],
        vector_sums[5],
        jnp.transpose(attn.outs[0].reshape(3, width, model), (2, 0, 1)),
        plain(0),
        plain(2),
        attn.outs[1],
        vector_sums[0],
        vector_sums[1],
        vector_sums[2],
        ffn.outs[1],
        up_bias_sum,
        ffn.outs[0],
        vector_sums[3],
    )


def solution(mesh):
    in_specs = (
        P(None, "wide", "narrow", None),
        P(None, "wide", "narrow", None),
        P(),
        P(),
        P(),
        P(),
        P(None, None, "narrow"),
        P("narrow"),
        P("narrow"),
        P("narrow", None),
        P(),
        P(),
        P(),
        P(None, "narrow"),
        P("narrow"),
        P("narrow", None),
        P(),
    )
    out_specs = (
        P(None, "wide", "narrow", None),
        P(None, "wide", "narrow", None),
        P(),
        P(),
        P(None, None, "narrow"),
        P("narrow"),
        P("narrow"),
        P("narrow", None),
        P(),
        P(),
        P(),
        P(None, "narrow"),
        P("narrow"),
        P("narrow", None),
        P(),
    )
    return jax.shard_map(local, mesh=mesh, in_specs=in_specs, out_specs=out_specs, check_vma=False)
```

```python
import functools

import jax
import jax.numpy as jnp
from jax import lax
from jax.experimental import pallas as pl
from jax.experimental.pallas import tpu as pltpu
from jax.sharding import PartitionSpec as P

HEAD = 64
LANES = 128
TILE = 256
norm_eps = 1e-05
score_scale = 0.125
bf16 = jnp.bfloat16
f32 = jnp.float32


class Chain:
    def __init__(self):
        self.last = []
        self.held = []

    def hold(self, *arrays):
        self.held += arrays

    def run(self, body, outs, *ins, smem=(), scratch=(), alias=None, anywhere=(), out_anywhere=(), limit=6, token=0, cover=False):
        unread = [*self.last, *self.held]
        count = len(smem) + len(ins)
        specs = [pl.BlockSpec(memory_space=pltpu.SMEM)] * len(smem)
        specs += [pl.BlockSpec(memory_space=pl.ANY if i in anywhere else pltpu.VMEM) for i in range(len(ins))]
        specs += [pl.BlockSpec(memory_space=pl.ANY)] * len(unread)

        def inner(*refs):
            body(*refs[:count], *refs[count + len(unread) :])

        made = pl.pallas_call(
            inner,
            out_shape=tuple(jax.ShapeDtypeStruct(*o) for o in outs),
            in_specs=specs,
            out_specs=tuple(
                pl.BlockSpec(memory_space=pl.ANY if i in out_anywhere else pltpu.VMEM) for i in range(len(outs))
            ),
            scratch_shapes=scratch,
            input_output_aliases={} if alias is None else {len(smem) + k: v for k, v in alias.items()},
            compiler_params=pltpu.CompilerParams(vmem_limit_bytes=limit << 20),
            cost_estimate=pl.CostEstimate(flops=10**12 if cover else 1, bytes_accessed=1, transcendentals=0),
            name=body.func.__name__ if isinstance(body, functools.partial) else body.__name__,
        )(*smem, *ins, *unread)
        self.last, self.held = [made[token]], []
        return made


def dot32(first, second, first_dim, second_dim):
    return lax.dot_general(
        first, second, (((first_dim,), (second_dim,)), ((), ())), preferred_element_type=f32
    )


def statistics(values):
    average = jnp.mean(values, axis=-1, keepdims=True)
    centred = values - average
    inverse = lax.rsqrt(jnp.mean(centred * centred, axis=-1, keepdims=True) + norm_eps)
    return centred * inverse, inverse


def norm_back(grad, normed, inverse, gain):
    scaled = grad * gain
    mean_one = jnp.mean(scaled, axis=-1, keepdims=True)
    mean_two = jnp.mean(scaled * normed, axis=-1, keepdims=True)
    return inverse * (scaled - mean_one - normed * mean_two)


def of_head(values, j, axis=1):
    if values.shape[axis] <= HEAD:
        return values
    place = lax.broadcasted_iota(jnp.int32, values.shape, axis)
    return jnp.where((place >= HEAD * j) & (place < HEAD * (j + 1)), values, jnp.zeros_like(values))


def head_pairs(width):
    return [(low, min(LANES, width - low)) for low in range(0, width, LANES)]


def relay(*refs, number):
    arrived, outs = refs[:number], refs[number:]
    each = len(outs) // number
    for i, rows in enumerate(arrived):
        size = rows.shape[0] // each
        for k in range(each):
            outs[i * each + k][...] = rows[k * size : (k + 1) * size, :]


def by_pairs(weight_t, out):
    width = out.shape[0] // 3
    for low, wide in head_pairs(width):
        for j in range(3):
            out[3 * low + j * wide : 3 * low + (j + 1) * wide, :] = weight_t[
                j * width + low : j * width + low + wide, :
            ]


def norm_one(tok, gain, bias, out, *, m):
    normed, _ = statistics(tok[m, 0].astype(f32))
    gain_row, bias_row = (v[...].astype(f32).reshape(1, -1) for v in (gain, bias))
    out[...] = (normed * gain_row + bias_row).astype(bf16)


def loss_grad(where, cells, queries, cot, m, count):
    number = queries[cells[where[0] + m * count]]
    scale = jnp.sqrt(jnp.full((1, cot.shape[3]), number, jnp.int32).astype(f32) / 500.0)
    return cot[m, 0].astype(f32) * scale


def scale_cot(where, cells, queries, cot, out, *, m, count):
    out[...] = loss_grad(where, cells, queries, cot, m, count).astype(bf16)


def project(*refs, parts):
    blocks = refs[:parts]
    weight, bias, scale = refs[parts : parts + 3]
    out, whole = refs[parts + 3 :]
    rows = blocks[0].shape[0]
    for b in range(parts):
        values = blocks[b][...]
        at = slice(b * rows, (b + 1) * rows)
        whole[at, :] = values
        out[at, :] = ((dot32(values, weight[...], 1, 1) + bias[...]) * scale[...]).astype(bf16)


def attend(qkv, out_weight, attended, logs, *outs, step):
    whole = qkv.shape[0]
    head = 0
    for low, wide in head_pairs(out_weight.shape[0]):
        heads = wide // HEAD
        key_pair = qkv[:, 3 * low + wide : 3 * low + 2 * wide]
        value_t = qkv[:, 3 * low + 2 * wide : 3 * low + 3 * wide].T
        keys = [of_head(key_pair, j) for j in range(heads)]
        values = [of_head(value_t, j, 0) for j in range(heads)]
        for start in range(0, whole, step):
            at = slice(start, start + step)
            query = qkv[at, 3 * low : 3 * low + wide]
            total = None
            for j in range(heads):
                scores = dot32(keys[j], query, 1, 1)
                top = jnp.max(scores, axis=0, keepdims=True)
                powers = jnp.exp(scores - top)
                length = jnp.sum(powers, axis=0, keepdims=True)
                mixed = dot32(values[j], powers.astype(bf16), 1, 0) * (1.0 / length)
                total = mixed if total is None else total + mixed
                logs[head + j : head + j + 1, at] = top + jnp.log(length)
            attended[at, low : low + wide] = total.T.astype(bf16)
        head += heads
    rows = whole // len(outs)
    for b, out in enumerate(outs):
        out[...] = dot32(attended[b * rows : (b + 1) * rows, :], out_weight[...], 1, 0).astype(bf16)


def pair_sum(first, second, out):
    out[...] = (first[...].astype(f32) + second[...].astype(f32)).astype(bf16)


def three(first, second, third):
    return first[...].astype(f32) + second[...].astype(f32) + third[...].astype(f32)


def norm_two(tok, first, second, third, out_bias, gain, bias, resid, normed, *, m):
    value = tok[m, 0].astype(f32) + three(first, second, third) + out_bias[...].astype(f32)
    resid[...] = value
    hat, _ = statistics(value)
    normed[...] = (hat * gain[...].astype(f32) + bias[...].astype(f32)).astype(bf16)


def feed(*refs, parts, blocks):
    normed, grads, refs = refs[:blocks], refs[blocks : blocks + parts], refs[blocks + parts :]
    up, up_bias, down, activ, pre_grad, bias_grad, normed_all, grads_all = refs
    for whole, pieces in ((normed_all, normed), (grads_all, grads)):
        low = 0
        for piece in pieces:
            whole[low : low + piece.shape[0], :] = piece[...]
            low += piece.shape[0]
    rows = grads[0].shape[0]
    for low in range(0, up.shape[1], TILE):
        cols = slice(low, low + TILE)
        total = None
        for b in range(parts):
            at = slice(b * rows, (b + 1) * rows)
            pre = dot32(normed_all[at, :], up[:, cols], 1, 0) + up_bias[:, cols].astype(f32)
            cumul = 0.5 + 0.5 * lax.erf(pre * 0.7071067811865476)
            density = jnp.exp(-0.5 * pre * pre) * 0.3989422804014327
            activ[at, cols] = (pre * cumul).astype(bf16)
            back = dot32(grads_all[at, :], down[cols, :], 1, 1)
            grad = (back * (cumul + pre * density)).astype(bf16)
            pre_grad[at, cols] = grad
            part = jnp.sum(grad.astype(f32), axis=0, keepdims=True)
            total = part if total is None else total + part
        bias_grad[:, cols] = total


def times(value, weight, *outs):
    put_tiles(outs, lambda at, cols: dot32(value[at, :], weight[:, cols], 1, 0), value.shape[0])


def times_back(value, weight, *outs):
    put_tiles(outs, lambda at, cols: dot32(value[at, :], weight[cols, :], 1, 1), value.shape[0])


def put_tiles(outs, share_of, whole):
    rows, model = outs[0].shape

    def tile(i, carry):
        cols = pl.ds(pl.multiple_of(i * TILE, TILE), TILE)
        for b, out in enumerate(outs):
            out[:, cols] = share_of(slice(b * rows, (b + 1) * rows), cols).astype(bf16)
        return carry

    lax.fori_loop(0, model // TILE, tile, 0)


def product(first, second, out):
    def tile(i, carry):
        rows = pl.ds(pl.multiple_of(i * TILE, TILE), TILE)
        out[rows, :] = dot32(first[:, rows], second[...], 0, 0).astype(bf16)
        return carry

    lax.fori_loop(0, out.shape[0] // TILE, tile, 0)


def weight_grad(where, first, second, other, *refs, before):
    chunks, whole = refs[before:-1], refs[-1]

    def tile(i, carry):
        rows = pl.ds(pl.multiple_of(i * TILE, TILE), TILE)
        total = dot32(first[:, rows], second[...], 0, 0) + other[rows, :].astype(f32)
        whole[rows, :] = total.astype(bf16)
        return carry

    lax.fori_loop(0, whole.shape[0] // TILE, tile, 0)
    if before:
        chunks, both = chunks[:-1], chunks[-1]
        size = chunks[0].shape[0]
        both[:size, :] = refs[0][...]
        put_chunks(where, chunks, whole)
        both[size:, :] = chunks[0][...]
    else:
        put_chunks(where, chunks, whole)


def ring_chunk(where, count, step):
    half = where[0] // 2
    place = jnp.where(where[0] % 2 == 0, half, count - 1 - half)
    return lax.rem(place + jnp.where(where[1] % 2 == 0, count - step, step), count)


def put_chunks(where, chunks, whole):
    for s, chunk in enumerate(chunks):
        size = chunk.shape[0]
        which = ring_chunk(where, len(chunks), (s + 1) % len(chunks)) if len(chunks) > 1 else 0
        chunk[...] = whole[pl.ds(pl.multiple_of(which * size, size), size), :]


def norm_two_back(where, cells, queries, cot, resid, first, second, third, gain, out, rounded, sums, *, m, count):
    top = loss_grad(where, cells, queries, cot, m, count)
    grad = three(first, second, third)
    hat, inverse = statistics(resid[...])
    back = top + norm_back(grad, hat, inverse, gain[...].astype(f32))
    out[...] = back
    rounded[...] = back.astype(bf16)
    sums[0:1, :] = jnp.sum(back, axis=0, keepdims=True)
    sums[1:2, :] = jnp.sum(grad * hat, axis=0, keepdims=True)
    sums[2:3, :] = jnp.sum(grad, axis=0, keepdims=True)
    sums[3:4, :] = jnp.sum(top, axis=0, keepdims=True)
    sums[4:8, :] = jnp.zeros_like(sums[4:8, :])


def attend_back(qkv, logs, mixed, out_weight, *refs, parts, step, low, wide):
    grads = refs[:parts]
    out, key_grad, value_grad, given, inner = refs[parts:]
    whole = qkv.shape[0]
    rows = whole // parts
    heads = wide // HEAD
    head = low // HEAD
    ones = jnp.concatenate([of_head(jnp.ones((8, wide), bf16), j) for j in range(heads)], axis=0)
    for b in range(parts):
        at = slice(b * rows, (b + 1) * rows)
        value = dot32(grads[b][...], out_weight[low : low + wide, :], 1, 1).astype(bf16)
        given[at, :] = value
        both = value.astype(f32) * mixed[at, low : low + wide].astype(f32)
        high = both.astype(bf16)
        rest = (both - high.astype(f32)).astype(bf16)
        inner[:, at] = dot32(ones, high, 1, 1) + dot32(ones, rest, 1, 1)
    key_pair = qkv[:, 3 * low + wide : 3 * low + 2 * wide]
    value_pair = qkv[:, 3 * low + 2 * wide : 3 * low + 3 * wide]
    key_t = key_pair.T
    keys = [of_head(key_pair, j) for j in range(heads)]
    values = [of_head(value_pair, j) for j in range(heads)]
    keys_t = [of_head(key_t, j, 0) for j in range(heads)]
    key_grad[...] = jnp.zeros_like(key_grad)
    value_grad[...] = jnp.zeros_like(value_grad)

    def block(i, carry):
        start = pl.multiple_of(i * step, step)
        query = qkv[pl.ds(start, step), 3 * low : 3 * low + wide]
        grad = given[pl.ds(start, step), :]
        total = None
        for j in range(heads):
            scores = dot32(keys[j], query, 1, 1)
            weights = jnp.exp(scores - logs[head + j : head + j + 1, pl.ds(start, step)])
            back = dot32(values[j], grad, 1, 1)
            score_grad = (weights * (back - inner[8 * j : 8 * j + 1, pl.ds(start, step)])).astype(bf16)
            value_grad[...] += dot32(weights.astype(bf16), of_head(grad, j), 1, 0)
            key_grad[...] += dot32(score_grad, of_head(query, j), 1, 0)
            part = dot32(keys_t[j], score_grad, 1, 0)
            total = part if total is None else total + part
        out[pl.ds(start, step), :wide] = (total.T * score_scale).astype(bf16)
        return carry

    lax.fori_loop(0, whole // step, block, 0)
    out[:, wide : 2 * wide] = key_grad[...].astype(bf16)
    out[:, 2 * wide :] = value_grad[...].astype(bf16)


def project_back(*refs, pairs):
    grads, weight, outs, sums = refs[:pairs], refs[pairs], refs[pairs + 1 : -1], refs[-1]

    def share_of(at, cols):
        total, low = None, 0
        for grad in grads:
            wide = grad.shape[1]
            part = dot32(grad[at, :], weight[low : low + wide, cols], 1, 0)
            total = part if total is None else total + part
            low += wide
        return total

    put_tiles(outs, share_of, grads[0].shape[0])
    low = 0
    for grad in grads:
        wide = grad.shape[1]
        sums[:, low : low + wide] = jnp.sum(grad[...].astype(f32), axis=0, keepdims=True)
        low += wide


def projection_grad(where, *refs, micros, pairs, parts):
    normed, refs = refs[:micros], refs[micros:]
    grads, refs = [refs[m * pairs : (m + 1) * pairs] for m in range(micros)], refs[micros * pairs :]
    tops, refs = [refs[m * parts : (m + 1) * parts] for m in range(micros)], refs[micros * parts :]
    mixed, refs = refs[:micros], refs[micros:]
    chunks, out = refs[:-1], refs[-1]
    width = mixed[0].shape[1]
    rows = tops[0][0].shape[0]
    for p, (low, wide) in enumerate(head_pairs(width)):
        total = None
        for m in range(micros):
            part = dot32(grads[m][p][...], normed[m][...], 0, 0)
            total = part if total is None else total + part
        for j in range(3):
            out[j * width + low : j * width + low + wide, :] = total[j * wide : (j + 1) * wide].astype(bf16)
        total = None
        for m in range(micros):
            for b in range(parts):
                part = dot32(mixed[m][b * rows : (b + 1) * rows, low : low + wide], tops[m][b][...], 0, 0)
                total = part if total is None else total + part
        out[3 * width + low : 3 * width + low + wide, :] = total.astype(bf16)
    put_chunks(where, chunks, out)


def ring_add(arrived, *refs):
    low = 0
    for part in refs[:-1]:
        at = slice(low, low + part.shape[0])
        refs[-1][at, :] = (arrived[at, :].astype(f32) + part[...].astype(f32)).astype(bf16)
        low += part.shape[0]


def ring_store(where, *refs, steps, count, stacked):
    moved, refs = refs[: len(steps)], refs[len(steps) :]
    ahead, first, second, buffer, sems = refs[-5:]
    ahead[...] = moved[-1][...]
    size = buffer.shape[1] // 2 if stacked else buffer.shape[1]
    copies = []
    for k, step in enumerate(steps):
        buffer[k] = moved[k][...].astype(f32)
        row = pl.multiple_of(ring_chunk(where, count, step) * size, size)
        if stacked:
            for i, target in enumerate((first, second)):
                source = buffer.at[k, pl.ds(i * size, size), :]
                copies.append(pltpu.make_async_copy(source, target.at[pl.ds(row, size), :], sems.at[2 * k + i]))
                copies[-1].start()
        else:
            last = first.shape[0] - size
            to_first = pl.multiple_of(jnp.minimum(row, last), 16)
            to_second = pl.multiple_of(jnp.maximum(row - first.shape[0], 0), 16)
            copy_first = pltpu.make_async_copy(buffer.at[k], first.at[pl.ds(to_first, size), :], sems.at[2 * k])
            copy_second = pltpu.make_async_copy(buffer.at[k], second.at[pl.ds(to_second, size), :], sems.at[2 * k])
            pl.when(row <= last)(copy_first.start)
            pl.when(row > last)(copy_second.start)
            copies.append(copy_first)
    for copy in copies:
        copy.wait()


def norm_one_back(tok, resid_grad, first, second, third, gain, out, sums, *, m):
    grad = three(first, second, third)
    hat, inverse = statistics(tok[m, 0].astype(f32))
    out[...] = resid_grad[...] + norm_back(grad, hat, inverse, gain[...].astype(f32))
    sums[0:4, :] = jnp.zeros_like(sums[0:4, :])
    sums[4:5, :] = jnp.sum(grad * hat, axis=0, keepdims=True)
    sums[5:6, :] = jnp.sum(grad, axis=0, keepdims=True)
    sums[6:8, :] = jnp.zeros_like(sums[6:8, :])


def vector_sum(*refs):
    total = refs[0][...]
    for ref in refs[1:-1]:
        total = total + ref[...]
    refs[-1][...] = total


def ring_pass(moving, *refs, number, joined):
    refs[number][...] = moving[...]
    if joined:
        vector_join(*refs[:number], refs[number + 1], number=joined)
    elif number:
        vector_sum(*refs[:number], refs[number + 1])


def vector_join(first, second, *refs, number):
    up_bias, stack, out = refs[:number], refs[number:-1], refs[-1]
    out[...] = first[...] + second[...]
    for row, parts in ((6, up_bias), (7, stack)):
        total = parts[0][...]
        for part in parts[1:]:
            total = total + part[...]
        out[row : row + 1, : total.shape[1]] = total


def add_rows(resid, first, second, third, bias, out):
    out[...] = (resid[...] + three(first, second, third) + bias[...].astype(f32)).astype(bf16)


def swap(values, axis, bit):
    return lax.ppermute(values, axis, [(i, i ^ bit) for i in range(lax.axis_size(axis))])


def ring_order(count):
    return list(range(0, count, 2)) + list(range(1, count, 2))[::-1]


class Ring:
    def __init__(self, chain, where, shapes, stacked):
        self.chain, self.where, self.shapes, self.stacked = chain, where, shapes, stacked
        self.count = lax.axis_size("wide")
        cores = lax.axis_size("narrow")
        order = ring_order(self.count)
        self.perm = [
            (order[i] * cores + n, order[(i + (1 if n % 2 == 0 else -1)) % self.count] * cores + n)
            for i in range(self.count)
            for n in range(cores)
        ]
        self.have, self.step, self.stored, self.outs = [], 1, 0, None

    def pass_on(self, chunk):
        self.moving = lax.ppermute(chunk, ("wide", "narrow"), self.perm)

    def start(self, chunk, parts):
        self.parts = parts
        self.pass_on(chunk)

    def hold(self):
        self.chain.hold(self.moving)

    def add(self, cover=False):
        (made,) = self.chain.run(
            ring_add,
            [(self.moving.shape, bf16)],
            self.moving,
            *[p[self.step] for p in self.parts],
            cover=cover,
        )
        self.step += 1
        if self.step == self.count:
            self.have.append(made)
        self.pass_on(made)

    def forward(self):
        self.have.append(self.moving)
        copy = self.store()
        if len(self.have) < self.count:
            self.pass_on(copy)

    def arrive(self, made):
        self.have.append(made)
        if len(self.have) < self.count:
            self.pass_on(made)

    def store(self):
        steps = range(self.stored, len(self.have))
        self.stored = len(self.have)
        moved = [self.have[s] for s in steps]
        kept = () if self.outs is None else self.outs
        number = len(moved)
        made = self.chain.run(
            functools.partial(ring_store, steps=tuple(steps), count=self.count, stacked=self.stacked),
            [(moved[-1].shape, bf16)] + [(s, f32) for s in self.shapes],
            *moved,
            *kept,
            smem=(self.where,),
            scratch=[pltpu.VMEM((number, *moved[0].shape), f32), pltpu.SemaphoreType.DMA((2 * number,))],
            alias={number: 1, number + 1: 2} if kept else None,
            anywhere=(number, number + 1) if kept else (),
            out_anywhere=(1, 2),
            limit=6 + (number * moved[0].size * 4 >> 20),
        )
        self.outs = made[1:]
        return made[0]


class Whole:
    def __init__(self, shapes):
        self.shapes = shapes

    def start(self, chunk, parts):
        total = lax.psum(chunk, "wide").astype(f32)
        self.outs = (total[: self.shapes[0][0]], total[self.shapes[0][0] :])

    def hold(self):
        pass

    def add(self, cover=False):
        pass

    def forward(self):
        pass

    def store(self):
        pass


def local(
    tokens,
    cotangent,
    cell_of,
    query_count,
    attn_norm_gain,
    attn_norm_bias,
    input_weight,
    query_bias,
    value_bias,
    out_weight,
    out_bias,
    ffn_norm_gain,
    ffn_norm_bias,
    up_weight,
    up_bias,
    down_weight,
    down_bias,
):
    micros = range(tokens.shape[0])
    rows, model = tokens.shape[2], tokens.shape[3]
    parts = lax.axis_size("narrow")
    whole = rows * parts
    width = input_weight.shape[2]
    hidden = up_weight.shape[1]
    count = lax.axis_size("wide")
    rings = count <= 8
    chunks = count if rings else 1
    pairs = head_pairs(width)
    step = min(512, whole)
    chain = Chain()
    run = chain.run
    where = jnp.stack([lax.axis_index("wide"), lax.axis_index("narrow")]).astype(jnp.int32)

    block = ((rows, model), bf16)
    outgoing = [block] * parts
    wide_rows = ((whole, model), bf16)
    row = lambda v: v.reshape(1, -1)
    gain_one, bias_one, gain_two, bias_two = map(row, (attn_norm_gain, attn_norm_bias, ffn_norm_gain, ffn_norm_bias))
    out_bias, down_bias, up_bias = row(out_bias), row(down_bias), row(up_bias)

    def columns(three_parts):
        return jnp.concatenate([v[:, low : low + wide] for low, wide in pairs for v in three_parts], axis=1)

    weight_t = jnp.transpose(input_weight, (1, 2, 0)).reshape(3 * width, model)
    zero = jnp.zeros((1, width), f32)
    project_bias = columns([row(query_bias).astype(f32), zero, row(value_bias).astype(f32)])
    project_scale = columns([zero + score_scale, zero + 1.0, zero + 1.0])

    def gather(own):
        return [own, swap(own, "narrow", 1), swap(own, "narrow", 2)]

    def finish(*arrived, pieces=1, cover=False):
        made = run(
            functools.partial(relay, number=len(arrived)),
            [((rows // pieces, model), bf16)] * (len(arrived) * pieces),
            *[a[2] for a in arrived],
            cover=cover,
        )
        for i, a in enumerate(arrived):
            own = made[i * pieces : (i + 1) * pieces]
            a[2:] = [*own, *[swap(piece, "narrow", 1) for piece in own]]

    def share(made):
        own, near, partner, far = made
        return [own, partner, swap(far, "narrow", 1), swap(near, "narrow", 1)]

    def send(shares):
        own, partner, far, near = shares
        (both,) = run(pair_sum, [block], partner, far)
        return [own, near, swap(both, "narrow", 2)]

    def fresh():
        return [None] * len(micros)

    normed, given, qkv, normed_all, mixed, logs, shares, shares_down, resid, normed_two_b = (fresh() for _ in range(10))
    activ, pre_grad, up_bias_grad, two_all, given_all, resid_grad, top = (fresh() for _ in range(7))
    sums_two, sums_one, stack_sums, out_rows, grad_rows = (fresh() for _ in range(5))
    pair_grads = [[] for _ in micros]

    def do_norm_one(m):
        (own,) = run(functools.partial(norm_one, m=m), [block], tokens, attn_norm_gain, attn_norm_bias)
        normed[m] = gather(own)

    def do_scale(m):
        (own,) = run(functools.partial(scale_cot, m=m, count=count), [block], cotangent, smem=(where, cell_of, query_count), cover=True)
        given[m] = gather(own)

    def do_project(m):
        qkv[m], normed_all[m] = run(
            functools.partial(project, parts=parts),
            [((whole, 3 * width), bf16), wide_rows],
            *normed[m],
            weight,
            project_bias,
            project_scale,
        )

    def do_attend(m):
        mixed[m], logs[m], *made = run(
            functools.partial(attend, step=whole),
            [((whole, width), bf16), ((8, whole), f32), *outgoing],
            qkv[m],
            out_weight,
            limit=24,
        )
        shares[m] = share(made)

    def do_send(m):
        shares[m] = send(shares[m])

    def do_norm_two(m):
        resid[m], own = run(
            functools.partial(norm_two, m=m),
            [((rows, model), f32), block],
            tokens,
            *shares[m],
            out_bias,
            gain_two,
            bias_two,
            cover=m == 0,
        )
        normed_two_b[m] = gather(own)

    def do_feed(m):
        activ[m], pre_grad[m], up_bias_grad[m], two_all[m], given_all[m] = run(
            functools.partial(feed, parts=parts, blocks=len(normed_two_b[m])),
            [((whole, hidden), bf16), ((whole, hidden), bf16), ((1, hidden), f32), wide_rows, wide_rows],
            *normed_two_b[m],
            *given[m],
            up_weight,
            up_bias,
            down_weight,
        )

    def do_up_back(m):
        shares[m] = share(run(times_back, outgoing, pre_grad[m], up_weight))

    def do_down(m):
        shares_down[m] = share(run(times, outgoing, activ[m], down_weight))

    def do_send_down(m):
        shares_down[m] = send(shares_down[m])

    def do_norm_two_back(m):
        resid_grad[m], own, sums_two[m] = run(
            functools.partial(norm_two_back, m=m, count=count),
            [((rows, model), f32), block, ((8, model), f32)],
            cotangent,
            resid[m],
            *shares[m],
            gain_two,
            smem=(where, cell_of, query_count),
            cover=m > 0,
        )
        top[m] = gather(own)

    def do_attend_back(m, p):
        low, wide = pairs[p]
        (made,) = run(
            functools.partial(attend_back, parts=parts, step=step, low=low, wide=wide),
            [((whole, 3 * wide), bf16)],
            qkv[m],
            logs[m],
            mixed[m],
            out_weight,
            *top[m],
            scratch=[
                pltpu.VMEM((whole, wide), f32),
                pltpu.VMEM((whole, wide), f32),
                pltpu.VMEM((whole, wide), bf16),
                pltpu.VMEM((8 * (wide // HEAD), whole), f32),
            ],
            limit=20,
        )
        pair_grads[m].append(made)

    def do_project_back(m):
        *made, stack_sums[m] = run(
            functools.partial(project_back, pairs=len(pairs)),
            [*outgoing, ((1, 3 * width), f32)],
            *pair_grads[m],
            weight,
        )
        shares[m] = share(made)

    def do_norm_one_back(m):
        grad_rows[m], sums_one[m] = run(
            functools.partial(norm_one_back, m=m),
            [((rows, model), f32), ((8, model), f32)],
            tokens,
            resid_grad[m],
            *shares[m],
            gain_one,
        )

    hops = [("narrow", 1 << k) for k in range(parts.bit_length() - 1)]
    hops += [("wide", 1 << k) for k in range(count.bit_length() - 1)]
    vectors = []

    def next_vectors():
        done = len(vectors)
        if done == 0:
            return [*sums_one, *sums_two], 0
        if hops[done - 1][0] == "narrow" and hops[done][0] == "wide":
            return [*vectors[-1], *up_bias_grad, *stack_sums], len(micros)
        return vectors[-1], 0

    def add_vectors(own):
        done = len(vectors)
        vectors.append((own, swap(own, *hops[done])) if done < len(hops) else (own,))

    def do_vectors():
        given_now, joined = next_vectors()
        body = functools.partial(vector_join, number=joined) if joined else vector_sum
        add_vectors(run(body, [((8, model), f32)], *given_now)[0])

    def do_pass():
        if not rings:
            return
        given_now, joined = next_vectors() if len(vectors) <= len(hops) else ([], 0)
        if not given_now and len(attn.have) == count - 1:
            attn.have.append(attn.moving)
            return
        made = run(
            functools.partial(ring_pass, number=len(given_now), joined=joined),
            [(attn.moving.shape, bf16)] + ([((8, model), f32)] if given_now else []),
            attn.moving,
            *given_now,
        )
        attn.arrive(made[0])
        if given_now:
            add_vectors(made[1])

    def do_add_rows(m):
        (out_rows[m],) = run(add_rows, [block], resid[m], *shares_down[m], down_bias)

    def first_product(first, second):
        return run(product, [((first.shape[1], second.shape[1]), bf16)], first, second)[0]

    def ffn_grad(first, second, other, before=()):
        rows, cols = other.shape
        shapes = [((rows // chunks, cols), bf16)] * chunks
        if before:
            shapes.append(((2 * rows // chunks, cols), bf16))
        return run(
            functools.partial(weight_grad, before=len(before[:1])),
            shapes,
            first,
            second,
            other,
            *before[:1],
            smem=(where,),
            scratch=[pltpu.VMEM((rows, cols), bf16)],
            limit=16,
        )

    def attn_grad():
        made = run(
            functools.partial(projection_grad, micros=len(micros), pairs=len(pairs), parts=parts),
            [((4 * width // chunks, model), bf16)] * chunks,
            *normed_all,
            *[g for m in micros for g in pair_grads[m]],
            *[t for m in micros for t in top[m]],
            *mixed,
            smem=(where,),
            scratch=[pltpu.VMEM((4 * width, model), bf16)],
            limit=20,
        )
        attn.start(made[0], (made,))

    ffn_shapes = [(hidden, model), (model, hidden)]
    attn_shapes = [(3 * width, model), (width, model)]
    ffn = Ring(chain, where, ffn_shapes, True) if rings else Whole(ffn_shapes)
    attn = Ring(chain, where, attn_shapes, False) if rings else Whole(attn_shapes)

    do_norm_one(0)
    (weight,) = run(by_pairs, [((3 * width, model), bf16)], weight_t)
    chain.hold(normed[0][1])
    finish(normed[0])
    do_norm_one(1)
    do_scale(0)
    do_project(0)
    do_attend(0)
    chain.hold(normed[1][1], given[0][1])
    finish(normed[1], given[0], cover=True)
    do_scale(1)
    do_send(0)
    chain.hold(given[1][1])
    do_project(1)
    do_attend(1)
    chain.hold(given[1][2])
    do_norm_two(0)
    do_send(1)
    finish(given[1])
    chain.hold(normed_two_b[0][1])
    finish(normed_two_b[0], pieces=4)
    do_feed(0)
    do_norm_two(1)
    chain.hold(normed_two_b[1][1])
    do_up_back(0)
    down_first = first_product(activ[0], given_all[0])
    up_first = first_product(two_all[0], pre_grad[0])
    do_down(0)
    finish(normed_two_b[1], cover=True)
    do_send(0)
    do_feed(1)
    down_chunks = ffn_grad(activ[1], given_all[1], down_first)
    *up_chunks, both = ffn_grad(two_all[1], pre_grad[1], up_first, down_chunks)
    ffn.start(both, (down_chunks, up_chunks))
    do_up_back(1)
    do_norm_two_back(0)
    do_down(1)
    ffn.add()
    do_send(1)
    chain.hold(top[0][1])
    finish(top[0])
    chain.hold(top[0][3])
    ffn.add()
    do_attend_back(0, 0)
    ffn.add()
    do_attend_back(0, 1)
    do_norm_two_back(1)
    ffn.add()
    do_attend_back(0, 2)
    do_project_back(0)
    ffn.add()
    do_send_down(0)
    chain.hold(top[1][1])
    finish(top[1], cover=True)
    do_attend_back(1, 0)
    ffn.add()
    do_send(0)
    do_attend_back(1, 1)
    ffn.add()
    do_attend_back(1, 2)
    attn_grad()
    chain.hold(shares_down[0][2])
    ffn.forward()
    do_add_rows(0)
    attn.add()
    do_project_back(1)
    attn.add()
    ffn.forward()
    do_norm_one_back(0)
    attn.add()
    do_send(1)
    attn.add()
    do_send_down(1)
    ffn.forward()
    attn.add()
    attn.add()
    do_norm_one_back(1)
    do_vectors()
    ffn.forward()
    attn.add()
    do_pass()
    ffn.forward()
    do_pass()
    attn.store()
    do_pass()
    ffn.forward()
    do_pass()
    do_add_rows(1)
    attn.store()
    do_pass()
    ffn.forward()
    do_pass()
    attn.store()
    do_pass()
    attn.store()

    while len(vectors) <= len(hops):
        do_vectors()
    vector_sums = vectors[-1][0]
    up_bias_sum = vector_sums[6, :hidden]
    stack_sum = vector_sums[7, : 3 * width]

    def plain(j):
        return jnp.concatenate([stack_sum[3 * low + j * wide : 3 * low + (j + 1) * wide] for low, wide in pairs])

    return (
        jnp.stack(out_rows)[:, None],
        jnp.stack(grad_rows)[:, None],
        vector_sums[4],
        vector_sums[5],
        jnp.transpose(attn.outs[0].reshape(3, width, model), (2, 0, 1)),
        plain(0),
        plain(2),
        attn.outs[1],
        vector_sums[0],
        vector_sums[1],
        vector_sums[2],
        ffn.outs[1],
        up_bias_sum,
        ffn.outs[0],
        vector_sums[3],
    )


def solution(mesh):
    in_specs = (
        P(None, "wide", "narrow", None),
        P(None, "wide", "narrow", None),
        P(),
        P(),
        P(),
        P(),
        P(None, None, "narrow"),
        P("narrow"),
        P("narrow"),
        P("narrow", None),
        P(),
        P(),
        P(),
        P(None, "narrow"),
        P("narrow"),
        P("narrow", None),
        P(),
    )
    out_specs = (
        P(None, "wide", "narrow", None),
        P(None, "wide", "narrow", None),
        P(),
        P(),
        P(None, None, "narrow"),
        P("narrow"),
        P("narrow"),
        P("narrow", None),
        P(),
        P(),
        P(),
        P(None, "narrow"),
        P("narrow"),
        P("narrow", None),
        P(),
    )
    return jax.shard_map(local, mesh=mesh, in_specs=in_specs, out_specs=out_specs, check_vma=False)
```

```python
import functools

import jax
import jax.numpy as jnp
from jax import lax
from jax.experimental import pallas as pl
from jax.experimental.pallas import tpu as pltpu
from jax.sharding import PartitionSpec as P

HEAD = 64
LANES = 128
TILE = 256
norm_eps = 1e-05
score_scale = 0.125
bf16 = jnp.bfloat16
f32 = jnp.float32


class Chain:
    def __init__(self):
        self.last = []
        self.held = []

    def hold(self, *arrays):
        self.held += arrays

    def run(self, body, outs, *ins, smem=(), scratch=(), alias=None, anywhere=(), out_anywhere=(), limit=6, token=0, cover=False):
        unread = [*self.last, *self.held]
        count = len(smem) + len(ins)
        specs = [pl.BlockSpec(memory_space=pltpu.SMEM)] * len(smem)
        specs += [pl.BlockSpec(memory_space=pl.ANY if i in anywhere else pltpu.VMEM) for i in range(len(ins))]
        specs += [pl.BlockSpec(memory_space=pl.ANY)] * len(unread)

        def inner(*refs):
            body(*refs[:count], *refs[count + len(unread) :])

        made = pl.pallas_call(
            inner,
            out_shape=tuple(jax.ShapeDtypeStruct(*o) for o in outs),
            in_specs=specs,
            out_specs=tuple(
                pl.BlockSpec(memory_space=pl.ANY if i in out_anywhere else pltpu.VMEM) for i in range(len(outs))
            ),
            scratch_shapes=scratch,
            input_output_aliases={} if alias is None else {len(smem) + k: v for k, v in alias.items()},
            compiler_params=pltpu.CompilerParams(vmem_limit_bytes=limit << 20),
            cost_estimate=pl.CostEstimate(flops=10**12 if cover else 1, bytes_accessed=1, transcendentals=0),
            name=body.func.__name__ if isinstance(body, functools.partial) else body.__name__,
        )(*smem, *ins, *unread)
        self.last, self.held = [made[token]], []
        return made


def dot32(first, second, first_dim, second_dim):
    return lax.dot_general(
        first, second, (((first_dim,), (second_dim,)), ((), ())), preferred_element_type=f32
    )


def statistics(values):
    average = jnp.mean(values, axis=-1, keepdims=True)
    centred = values - average
    inverse = lax.rsqrt(jnp.mean(centred * centred, axis=-1, keepdims=True) + norm_eps)
    return centred * inverse, inverse


def norm_back(grad, normed, inverse, gain):
    scaled = grad * gain
    mean_one = jnp.mean(scaled, axis=-1, keepdims=True)
    mean_two = jnp.mean(scaled * normed, axis=-1, keepdims=True)
    return inverse * (scaled - mean_one - normed * mean_two)


def of_head(values, j, axis=1):
    if values.shape[axis] <= HEAD:
        return values
    place = lax.broadcasted_iota(jnp.int32, values.shape, axis)
    return jnp.where((place >= HEAD * j) & (place < HEAD * (j + 1)), values, jnp.zeros_like(values))


def head_pairs(width):
    return [(low, min(LANES, width - low)) for low in range(0, width, LANES)]


def relay(*refs, number):
    arrived, outs = refs[:number], refs[number:]
    each = len(outs) // number
    for i, rows in enumerate(arrived):
        size = rows.shape[0] // each
        for k in range(each):
            outs[i * each + k][...] = rows[k * size : (k + 1) * size, :]


def by_pairs(weight_t, out):
    width = out.shape[0] // 3
    for low, wide in head_pairs(width):
        for j in range(3):
            out[3 * low + j * wide : 3 * low + (j + 1) * wide, :] = weight_t[
                j * width + low : j * width + low + wide, :
            ]


def norm_one(tok, gain, bias, out, *, m):
    normed, _ = statistics(tok[m, 0].astype(f32))
    gain_row, bias_row = (v[...].astype(f32).reshape(1, -1) for v in (gain, bias))
    out[...] = (normed * gain_row + bias_row).astype(bf16)


def loss_grad(where, cells, queries, cot, m, count):
    number = queries[cells[where[0] + m * count]]
    scale = jnp.sqrt(jnp.full((1, cot.shape[3]), number, jnp.int32).astype(f32) / 500.0)
    return cot[m, 0].astype(f32) * scale


def scale_cot(where, cells, queries, cot, out, *, m, count):
    out[...] = loss_grad(where, cells, queries, cot, m, count).astype(bf16)


def project(*refs, parts):
    blocks = refs[:parts]
    weight, bias, scale = refs[parts : parts + 3]
    out, whole = refs[parts + 3 :]
    rows = blocks[0].shape[0]
    for b in range(parts):
        values = blocks[b][...]
        at = slice(b * rows, (b + 1) * rows)
        whole[at, :] = values
        out[at, :] = ((dot32(values, weight[...], 1, 1) + bias[...]) * scale[...]).astype(bf16)


def attend(qkv, out_weight, attended, logs, *outs, step):
    whole = qkv.shape[0]
    head = 0
    for low, wide in head_pairs(out_weight.shape[0]):
        heads = wide // HEAD
        key_pair = qkv[:, 3 * low + wide : 3 * low + 2 * wide]
        value_t = qkv[:, 3 * low + 2 * wide : 3 * low + 3 * wide].T
        keys = [of_head(key_pair, j) for j in range(heads)]
        values = [of_head(value_t, j, 0) for j in range(heads)]
        for start in range(0, whole, step):
            at = slice(start, start + step)
            query = qkv[at, 3 * low : 3 * low + wide]
            total = None
            for j in range(heads):
                scores = dot32(keys[j], query, 1, 1)
                top = jnp.max(scores, axis=0, keepdims=True)
                powers = jnp.exp(scores - top)
                length = jnp.sum(powers, axis=0, keepdims=True)
                mixed = dot32(values[j], powers.astype(bf16), 1, 0) * (1.0 / length)
                total = mixed if total is None else total + mixed
                logs[head + j : head + j + 1, at] = top + jnp.log(length)
            attended[at, low : low + wide] = total.T.astype(bf16)
        head += heads
    rows = whole // len(outs)
    for b, out in enumerate(outs):
        out[...] = dot32(attended[b * rows : (b + 1) * rows, :], out_weight[...], 1, 0).astype(bf16)


def pair_sum(first, second, out):
    out[...] = (first[...].astype(f32) + second[...].astype(f32)).astype(bf16)


def three(first, second, third):
    return first[...].astype(f32) + second[...].astype(f32) + third[...].astype(f32)


def norm_two(tok, first, second, third, out_bias, gain, bias, resid, normed, *, m):
    value = tok[m, 0].astype(f32) + three(first, second, third) + out_bias[...].astype(f32)
    resid[...] = value
    hat, _ = statistics(value)
    normed[...] = (hat * gain[...].astype(f32) + bias[...].astype(f32)).astype(bf16)


def feed(*refs, parts, blocks):
    normed, grads, refs = refs[:blocks], refs[blocks : blocks + parts], refs[blocks + parts :]
    up, up_bias, down, activ, pre_grad, bias_grad, normed_all, grads_all = refs
    for whole, pieces in ((normed_all, normed), (grads_all, grads)):
        low = 0
        for piece in pieces:
            whole[low : low + piece.shape[0], :] = piece[...]
            low += piece.shape[0]
    rows = grads[0].shape[0]
    for low in range(0, up.shape[1], TILE):
        cols = slice(low, low + TILE)
        total = None
        for b in range(parts):
            at = slice(b * rows, (b + 1) * rows)
            pre = dot32(normed_all[at, :], up[:, cols], 1, 0) + up_bias[:, cols].astype(f32)
            cumul = 0.5 + 0.5 * lax.erf(pre * 0.7071067811865476)
            density = jnp.exp(-0.5 * pre * pre) * 0.3989422804014327
            activ[at, cols] = (pre * cumul).astype(bf16)
            back = dot32(grads_all[at, :], down[cols, :], 1, 1)
            grad = (back * (cumul + pre * density)).astype(bf16)
            pre_grad[at, cols] = grad
            part = jnp.sum(grad.astype(f32), axis=0, keepdims=True)
            total = part if total is None else total + part
        bias_grad[:, cols] = total


def times(value, weight, *outs):
    put_tiles(outs, lambda at, cols: dot32(value[at, :], weight[:, cols], 1, 0), value.shape[0])


def times_back(value, weight, *outs):
    put_tiles(outs, lambda at, cols: dot32(value[at, :], weight[cols, :], 1, 1), value.shape[0])


def put_tiles(outs, share_of, whole):
    rows, model = outs[0].shape

    def tile(i, carry):
        cols = pl.ds(pl.multiple_of(i * TILE, TILE), TILE)
        for b, out in enumerate(outs):
            out[:, cols] = share_of(slice(b * rows, (b + 1) * rows), cols).astype(bf16)
        return carry

    lax.fori_loop(0, model // TILE, tile, 0)


def product(first, second, out):
    def tile(i, carry):
        rows = pl.ds(pl.multiple_of(i * TILE, TILE), TILE)
        out[rows, :] = dot32(first[:, rows], second[...], 0, 0).astype(bf16)
        return carry

    lax.fori_loop(0, out.shape[0] // TILE, tile, 0)


def weight_grad(where, first, second, other, *refs, before):
    chunks, whole = refs[before:-1], refs[-1]

    def tile(i, carry):
        rows = pl.ds(pl.multiple_of(i * TILE, TILE), TILE)
        total = dot32(first[:, rows], second[...], 0, 0) + other[rows, :].astype(f32)
        whole[rows, :] = total.astype(bf16)
        return carry

    lax.fori_loop(0, whole.shape[0] // TILE, tile, 0)
    if before:
        chunks, both = chunks[:-1], chunks[-1]
        size = chunks[0].shape[0]
        both[:size, :] = refs[0][...]
        put_chunks(where, chunks, whole)
        both[size:, :] = chunks[0][...]
    else:
        put_chunks(where, chunks, whole)


def ring_chunk(where, count, step):
    half = where[0] // 2
    place = jnp.where(where[0] % 2 == 0, half, count - 1 - half)
    return lax.rem(place + jnp.where(where[1] % 2 == 0, count - step, step), count)


def put_chunks(where, chunks, whole):
    for s, chunk in enumerate(chunks):
        size = chunk.shape[0]
        which = ring_chunk(where, len(chunks), (s + 1) % len(chunks)) if len(chunks) > 1 else 0
        chunk[...] = whole[pl.ds(pl.multiple_of(which * size, size), size), :]


def norm_two_back(where, cells, queries, cot, resid, first, second, third, gain, out, rounded, sums, *, m, count):
    top = loss_grad(where, cells, queries, cot, m, count)
    grad = three(first, second, third)
    hat, inverse = statistics(resid[...])
    back = top + norm_back(grad, hat, inverse, gain[...].astype(f32))
    out[...] = back
    rounded[...] = back.astype(bf16)
    sums[0:1, :] = jnp.sum(back, axis=0, keepdims=True)
    sums[1:2, :] = jnp.sum(grad * hat, axis=0, keepdims=True)
    sums[2:3, :] = jnp.sum(grad, axis=0, keepdims=True)
    sums[3:4, :] = jnp.sum(top, axis=0, keepdims=True)
    sums[4:8, :] = jnp.zeros_like(sums[4:8, :])


def attend_back(qkv, logs, mixed, out_weight, *refs, parts, step, low, wide):
    grads = refs[:parts]
    out, key_grad, value_grad, given, inner = refs[parts:]
    whole = qkv.shape[0]
    rows = whole // parts
    heads = wide // HEAD
    head = low // HEAD
    ones = jnp.concatenate([of_head(jnp.ones((8, wide), bf16), j) for j in range(heads)], axis=0)
    for b in range(parts):
        at = slice(b * rows, (b + 1) * rows)
        value = dot32(grads[b][...], out_weight[low : low + wide, :], 1, 1).astype(bf16)
        given[at, :] = value
        both = value.astype(f32) * mixed[at, low : low + wide].astype(f32)
        high = both.astype(bf16)
        rest = (both - high.astype(f32)).astype(bf16)
        inner[:, at] = dot32(ones, high, 1, 1) + dot32(ones, rest, 1, 1)
    key_pair = qkv[:, 3 * low + wide : 3 * low + 2 * wide]
    value_pair = qkv[:, 3 * low + 2 * wide : 3 * low + 3 * wide]
    key_t = key_pair.T
    keys = [of_head(key_pair, j) for j in range(heads)]
    values = [of_head(value_pair, j) for j in range(heads)]
    keys_t = [of_head(key_t, j, 0) for j in range(heads)]
    key_grad[...] = jnp.zeros_like(key_grad)
    value_grad[...] = jnp.zeros_like(value_grad)

    def block(i, carry):
        start = pl.multiple_of(i * step, step)
        query = qkv[pl.ds(start, step), 3 * low : 3 * low + wide]
        grad = given[pl.ds(start, step), :]
        total = None
        for j in range(heads):
            scores = dot32(keys[j], query, 1, 1)
            weights = jnp.exp(scores - logs[head + j : head + j + 1, pl.ds(start, step)])
            back = dot32(values[j], grad, 1, 1)
            score_grad = (weights * (back - inner[8 * j : 8 * j + 1, pl.ds(start, step)])).astype(bf16)
            value_grad[...] += dot32(weights.astype(bf16), of_head(grad, j), 1, 0)
            key_grad[...] += dot32(score_grad, of_head(query, j), 1, 0)
            part = dot32(keys_t[j], score_grad, 1, 0)
            total = part if total is None else total + part
        out[pl.ds(start, step), :wide] = (total.T * score_scale).astype(bf16)
        return carry

    lax.fori_loop(0, whole // step, block, 0)
    out[:, wide : 2 * wide] = key_grad[...].astype(bf16)
    out[:, 2 * wide :] = value_grad[...].astype(bf16)


def project_back(*refs, pairs):
    grads, weight, outs, sums = refs[:pairs], refs[pairs], refs[pairs + 1 : -1], refs[-1]

    def share_of(at, cols):
        total, low = None, 0
        for grad in grads:
            wide = grad.shape[1]
            part = dot32(grad[at, :], weight[low : low + wide, cols], 1, 0)
            total = part if total is None else total + part
            low += wide
        return total

    put_tiles(outs, share_of, grads[0].shape[0])
    low = 0
    for grad in grads:
        wide = grad.shape[1]
        sums[:, low : low + wide] = jnp.sum(grad[...].astype(f32), axis=0, keepdims=True)
        low += wide


def projection_grad(where, *refs, micros, pairs, parts):
    normed, refs = refs[:micros], refs[micros:]
    grads, refs = [refs[m * pairs : (m + 1) * pairs] for m in range(micros)], refs[micros * pairs :]
    tops, refs = [refs[m * parts : (m + 1) * parts] for m in range(micros)], refs[micros * parts :]
    mixed, refs = refs[:micros], refs[micros:]
    chunks, out = refs[:-1], refs[-1]
    width = mixed[0].shape[1]
    rows = tops[0][0].shape[0]
    for p, (low, wide) in enumerate(head_pairs(width)):
        total = None
        for m in range(micros):
            part = dot32(grads[m][p][...], normed[m][...], 0, 0)
            total = part if total is None else total + part
        for j in range(3):
            out[j * width + low : j * width + low + wide, :] = total[j * wide : (j + 1) * wide].astype(bf16)
        total = None
        for m in range(micros):
            for b in range(parts):
                part = dot32(mixed[m][b * rows : (b + 1) * rows, low : low + wide], tops[m][b][...], 0, 0)
                total = part if total is None else total + part
        out[3 * width + low : 3 * width + low + wide, :] = total.astype(bf16)
    put_chunks(where, chunks, out)


def ring_add(arrived, *refs):
    low = 0
    for part in refs[:-1]:
        at = slice(low, low + part.shape[0])
        refs[-1][at, :] = (arrived[at, :].astype(f32) + part[...].astype(f32)).astype(bf16)
        low += part.shape[0]


def ring_store(where, *refs, steps, count, stacked):
    moved, refs = refs[: len(steps)], refs[len(steps) :]
    ahead, first, second, buffer, sems = refs[-5:]
    ahead[...] = moved[-1][...]
    size = buffer.shape[1] // 2 if stacked else buffer.shape[1]
    copies = []
    for k, step in enumerate(steps):
        buffer[k] = moved[k][...].astype(f32)
        row = pl.multiple_of(ring_chunk(where, count, step) * size, size)
        if stacked:
            for i, target in enumerate((first, second)):
                source = buffer.at[k, pl.ds(i * size, size), :]
                copies.append(pltpu.make_async_copy(source, target.at[pl.ds(row, size), :], sems.at[2 * k + i]))
                copies[-1].start()
        else:
            last = first.shape[0] - size
            to_first = pl.multiple_of(jnp.minimum(row, last), 16)
            to_second = pl.multiple_of(jnp.maximum(row - first.shape[0], 0), 16)
            copy_first = pltpu.make_async_copy(buffer.at[k], first.at[pl.ds(to_first, size), :], sems.at[2 * k])
            copy_second = pltpu.make_async_copy(buffer.at[k], second.at[pl.ds(to_second, size), :], sems.at[2 * k])
            pl.when(row <= last)(copy_first.start)
            pl.when(row > last)(copy_second.start)
            copies.append(copy_first)
    for copy in copies:
        copy.wait()


def norm_one_back(tok, resid_grad, first, second, third, gain, out, sums, *, m):
    grad = three(first, second, third)
    hat, inverse = statistics(tok[m, 0].astype(f32))
    out[...] = resid_grad[...] + norm_back(grad, hat, inverse, gain[...].astype(f32))
    sums[0:4, :] = jnp.zeros_like(sums[0:4, :])
    sums[4:5, :] = jnp.sum(grad * hat, axis=0, keepdims=True)
    sums[5:6, :] = jnp.sum(grad, axis=0, keepdims=True)
    sums[6:8, :] = jnp.zeros_like(sums[6:8, :])


def vector_sum(*refs):
    total = refs[0][...]
    for ref in refs[1:-1]:
        total = total + ref[...]
    refs[-1][...] = total


def ring_pass(moving, *refs, number, joined):
    refs[number][...] = moving[...]
    if joined:
        vector_join(*refs[:number], refs[number + 1], number=joined)
    elif number:
        vector_sum(*refs[:number], refs[number + 1])


def vector_join(first, second, *refs, number):
    up_bias, stack, out = refs[:number], refs[number:-1], refs[-1]
    out[...] = first[...] + second[...]
    for row, parts in ((6, up_bias), (7, stack)):
        total = parts[0][...]
        for part in parts[1:]:
            total = total + part[...]
        out[row : row + 1, : total.shape[1]] = total


def add_rows(resid, first, second, third, bias, out):
    out[...] = (resid[...] + three(first, second, third) + bias[...].astype(f32)).astype(bf16)


def swap(values, axis, bit):
    return lax.ppermute(values, axis, [(i, i ^ bit) for i in range(lax.axis_size(axis))])


def ring_order(count):
    return list(range(0, count, 2)) + list(range(1, count, 2))[::-1]


class Ring:
    def __init__(self, chain, where, shapes, stacked):
        self.chain, self.where, self.shapes, self.stacked = chain, where, shapes, stacked
        self.count = lax.axis_size("wide")
        cores = lax.axis_size("narrow")
        order = ring_order(self.count)
        self.perm = [
            (order[i] * cores + n, order[(i + (1 if n % 2 == 0 else -1)) % self.count] * cores + n)
            for i in range(self.count)
            for n in range(cores)
        ]
        self.have, self.step, self.stored, self.outs = [], 1, 0, None

    def pass_on(self, chunk):
        self.moving = lax.ppermute(chunk, ("wide", "narrow"), self.perm)

    def start(self, chunk, parts):
        self.parts = parts
        self.pass_on(chunk)

    def hold(self):
        self.chain.hold(self.moving)

    def add(self, cover=False):
        (made,) = self.chain.run(
            ring_add,
            [(self.moving.shape, bf16)],
            self.moving,
            *[p[self.step] for p in self.parts],
            cover=cover,
        )
        self.step += 1
        if self.step == self.count:
            self.have.append(made)
        self.pass_on(made)

    def forward(self):
        self.have.append(self.moving)
        copy = self.store()
        if len(self.have) < self.count:
            self.pass_on(copy)

    def arrive(self, made):
        self.have.append(made)
        if len(self.have) < self.count:
            self.pass_on(made)

    def store(self):
        steps = range(self.stored, len(self.have))
        self.stored = len(self.have)
        moved = [self.have[s] for s in steps]
        kept = () if self.outs is None else self.outs
        number = len(moved)
        made = self.chain.run(
            functools.partial(ring_store, steps=tuple(steps), count=self.count, stacked=self.stacked),
            [(moved[-1].shape, bf16)] + [(s, f32) for s in self.shapes],
            *moved,
            *kept,
            smem=(self.where,),
            scratch=[pltpu.VMEM((number, *moved[0].shape), f32), pltpu.SemaphoreType.DMA((2 * number,))],
            alias={number: 1, number + 1: 2} if kept else None,
            anywhere=(number, number + 1) if kept else (),
            out_anywhere=(1, 2),
            limit=6 + (number * moved[0].size * 4 >> 20),
        )
        self.outs = made[1:]
        return made[0]


class Whole:
    def __init__(self, shapes):
        self.shapes = shapes

    def start(self, chunk, parts):
        total = lax.psum(chunk, "wide").astype(f32)
        self.outs = (total[: self.shapes[0][0]], total[self.shapes[0][0] :])

    def hold(self):
        pass

    def add(self, cover=False):
        pass

    def forward(self):
        pass

    def store(self):
        pass


def local(
    tokens,
    cotangent,
    cell_of,
    query_count,
    attn_norm_gain,
    attn_norm_bias,
    input_weight,
    query_bias,
    value_bias,
    out_weight,
    out_bias,
    ffn_norm_gain,
    ffn_norm_bias,
    up_weight,
    up_bias,
    down_weight,
    down_bias,
):
    micros = range(tokens.shape[0])
    rows, model = tokens.shape[2], tokens.shape[3]
    parts = lax.axis_size("narrow")
    whole = rows * parts
    width = input_weight.shape[2]
    hidden = up_weight.shape[1]
    count = lax.axis_size("wide")
    rings = count <= 8
    chunks = count if rings else 1
    pairs = head_pairs(width)
    step = min(512, whole)
    chain = Chain()
    run = chain.run
    where = jnp.stack([lax.axis_index("wide"), lax.axis_index("narrow")]).astype(jnp.int32)

    block = ((rows, model), bf16)
    outgoing = [block] * parts
    wide_rows = ((whole, model), bf16)
    row = lambda v: v.reshape(1, -1)
    gain_one, bias_one, gain_two, bias_two = map(row, (attn_norm_gain, attn_norm_bias, ffn_norm_gain, ffn_norm_bias))
    out_bias, down_bias, up_bias = row(out_bias), row(down_bias), row(up_bias)

    def columns(three_parts):
        return jnp.concatenate([v[:, low : low + wide] for low, wide in pairs for v in three_parts], axis=1)

    weight_t = jnp.transpose(input_weight, (1, 2, 0)).reshape(3 * width, model)
    zero = jnp.zeros((1, width), f32)
    project_bias = columns([row(query_bias).astype(f32), zero, row(value_bias).astype(f32)])
    project_scale = columns([zero + score_scale, zero + 1.0, zero + 1.0])

    def gather(own):
        return [own, swap(own, "narrow", 1), swap(own, "narrow", 2)]

    def finish(*arrived, pieces=1, cover=False):
        made = run(
            functools.partial(relay, number=len(arrived)),
            [((rows // pieces, model), bf16)] * (len(arrived) * pieces),
            *[a[2] for a in arrived],
            cover=cover,
        )
        for i, a in enumerate(arrived):
            own = made[i * pieces : (i + 1) * pieces]
            a[2:] = [*own, *[swap(piece, "narrow", 1) for piece in own]]

    def share(made):
        own, near, partner, far = made
        return [own, partner, swap(far, "narrow", 1), swap(near, "narrow", 1)]

    def send(shares):
        own, partner, far, near = shares
        (both,) = run(pair_sum, [block], partner, far)
        return [own, near, swap(both, "narrow", 2)]

    def fresh():
        return [None] * len(micros)

    normed, given, qkv, normed_all, mixed, logs, shares, shares_down, resid, normed_two_b = (fresh() for _ in range(10))
    activ, pre_grad, up_bias_grad, two_all, given_all, resid_grad, top = (fresh() for _ in range(7))
    sums_two, sums_one, stack_sums, out_rows, grad_rows = (fresh() for _ in range(5))
    pair_grads = [[] for _ in micros]

    def do_norm_one(m):
        (own,) = run(functools.partial(norm_one, m=m), [block], tokens, attn_norm_gain, attn_norm_bias)
        normed[m] = gather(own)

    def do_scale(m):
        (own,) = run(functools.partial(scale_cot, m=m, count=count), [block], cotangent, smem=(where, cell_of, query_count), cover=True)
        given[m] = gather(own)

    def do_project(m):
        qkv[m], normed_all[m] = run(
            functools.partial(project, parts=parts),
            [((whole, 3 * width), bf16), wide_rows],
            *normed[m],
            weight,
            project_bias,
            project_scale,
        )

    def do_attend(m):
        mixed[m], logs[m], *made = run(
            functools.partial(attend, step=whole),
            [((whole, width), bf16), ((8, whole), f32), *outgoing],
            qkv[m],
            out_weight,
            limit=24,
        )
        shares[m] = share(made)

    def do_send(m):
        shares[m] = send(shares[m])

    def do_norm_two(m):
        resid[m], own = run(
            functools.partial(norm_two, m=m),
            [((rows, model), f32), block],
            tokens,
            *shares[m],
            out_bias,
            gain_two,
            bias_two,
            cover=m == 0,
        )
        normed_two_b[m] = gather(own)

    def do_feed(m):
        activ[m], pre_grad[m], up_bias_grad[m], two_all[m], given_all[m] = run(
            functools.partial(feed, parts=parts, blocks=len(normed_two_b[m])),
            [((whole, hidden), bf16), ((whole, hidden), bf16), ((1, hidden), f32), wide_rows, wide_rows],
            *normed_two_b[m],
            *given[m],
            up_weight,
            up_bias,
            down_weight,
        )

    def do_up_back(m):
        shares[m] = share(run(times_back, outgoing, pre_grad[m], up_weight))

    def do_down(m):
        shares_down[m] = share(run(times, outgoing, activ[m], down_weight))

    def do_send_down(m):
        shares_down[m] = send(shares_down[m])

    def do_norm_two_back(m):
        resid_grad[m], own, sums_two[m] = run(
            functools.partial(norm_two_back, m=m, count=count),
            [((rows, model), f32), block, ((8, model), f32)],
            cotangent,
            resid[m],
            *shares[m],
            gain_two,
            smem=(where, cell_of, query_count),
            cover=m > 0,
        )
        top[m] = gather(own)

    def do_attend_back(m, p):
        low, wide = pairs[p]
        (made,) = run(
            functools.partial(attend_back, parts=parts, step=step, low=low, wide=wide),
            [((whole, 3 * wide), bf16)],
            qkv[m],
            logs[m],
            mixed[m],
            out_weight,
            *top[m],
            scratch=[
                pltpu.VMEM((whole, wide), f32),
                pltpu.VMEM((whole, wide), f32),
                pltpu.VMEM((whole, wide), bf16),
                pltpu.VMEM((8 * (wide // HEAD), whole), f32),
            ],
            limit=20,
        )
        pair_grads[m].append(made)

    def do_project_back(m):
        *made, stack_sums[m] = run(
            functools.partial(project_back, pairs=len(pairs)),
            [*outgoing, ((1, 3 * width), f32)],
            *pair_grads[m],
            weight,
        )
        shares[m] = share(made)

    def do_norm_one_back(m):
        grad_rows[m], sums_one[m] = run(
            functools.partial(norm_one_back, m=m),
            [((rows, model), f32), ((8, model), f32)],
            tokens,
            resid_grad[m],
            *shares[m],
            gain_one,
        )

    hops = [("narrow", 1 << k) for k in range(parts.bit_length() - 1)]
    hops += [("wide", 1 << k) for k in range(count.bit_length() - 1)]
    vectors = []

    def next_vectors():
        done = len(vectors)
        if done == 0:
            return [*sums_one, *sums_two], 0
        if hops[done - 1][0] == "narrow" and hops[done][0] == "wide":
            return [*vectors[-1], *up_bias_grad, *stack_sums], len(micros)
        return vectors[-1], 0

    def add_vectors(own):
        done = len(vectors)
        vectors.append((own, swap(own, *hops[done])) if done < len(hops) else (own,))

    def do_vectors():
        given_now, joined = next_vectors()
        body = functools.partial(vector_join, number=joined) if joined else vector_sum
        add_vectors(run(body, [((8, model), f32)], *given_now)[0])

    def do_pass():
        if not rings:
            return
        given_now, joined = next_vectors() if len(vectors) <= len(hops) else ([], 0)
        if not given_now and len(attn.have) == count - 1:
            attn.have.append(attn.moving)
            return
        made = run(
            functools.partial(ring_pass, number=len(given_now), joined=joined),
            [(attn.moving.shape, bf16)] + ([((8, model), f32)] if given_now else []),
            attn.moving,
            *given_now,
        )
        attn.arrive(made[0])
        if given_now:
            add_vectors(made[1])

    def do_add_rows(m):
        (out_rows[m],) = run(add_rows, [block], resid[m], *shares_down[m], down_bias)

    def first_product(first, second):
        return run(product, [((first.shape[1], second.shape[1]), bf16)], first, second)[0]

    def ffn_grad(first, second, other, before=()):
        rows, cols = other.shape
        shapes = [((rows // chunks, cols), bf16)] * chunks
        if before:
            shapes.append(((2 * rows // chunks, cols), bf16))
        return run(
            functools.partial(weight_grad, before=len(before[:1])),
            shapes,
            first,
            second,
            other,
            *before[:1],
            smem=(where,),
            scratch=[pltpu.VMEM((rows, cols), bf16)],
            limit=16,
        )

    def attn_grad():
        made = run(
            functools.partial(projection_grad, micros=len(micros), pairs=len(pairs), parts=parts),
            [((4 * width // chunks, model), bf16)] * chunks,
            *normed_all,
            *[g for m in micros for g in pair_grads[m]],
            *[t for m in micros for t in top[m]],
            *mixed,
            smem=(where,),
            scratch=[pltpu.VMEM((4 * width, model), bf16)],
            limit=20,
        )
        attn.start(made[0], (made,))

    ffn_shapes = [(hidden, model), (model, hidden)]
    attn_shapes = [(3 * width, model), (width, model)]
    ffn = Ring(chain, where, ffn_shapes, True) if rings else Whole(ffn_shapes)
    attn = Ring(chain, where, attn_shapes, False) if rings else Whole(attn_shapes)

    do_norm_one(0)
    (weight,) = run(by_pairs, [((3 * width, model), bf16)], weight_t)
    chain.hold(normed[0][1])
    finish(normed[0])
    do_norm_one(1)
    do_scale(0)
    do_project(0)
    do_attend(0)
    chain.hold(normed[1][1], given[0][1])
    finish(normed[1], given[0], cover=True)
    do_scale(1)
    do_send(0)
    chain.hold(given[1][1])
    do_project(1)
    do_attend(1)
    chain.hold(given[1][2])
    do_norm_two(0)
    do_send(1)
    finish(given[1])
    chain.hold(normed_two_b[0][1])
    finish(normed_two_b[0], pieces=4)
    do_feed(0)
    do_norm_two(1)
    chain.hold(normed_two_b[1][1])
    do_up_back(0)
    down_first = first_product(activ[0], given_all[0])
    up_first = first_product(two_all[0], pre_grad[0])
    do_down(0)
    finish(normed_two_b[1], cover=True)
    do_send(0)
    do_feed(1)
    down_chunks = ffn_grad(activ[1], given_all[1], down_first)
    *up_chunks, both = ffn_grad(two_all[1], pre_grad[1], up_first, down_chunks)
    ffn.start(both, (down_chunks, up_chunks))
    do_up_back(1)
    do_norm_two_back(0)
    do_down(1)
    ffn.add()
    do_send(1)
    chain.hold(top[0][1])
    finish(top[0])
    do_attend_back(0, 0)
    ffn.add()
    do_attend_back(0, 1)
    do_norm_two_back(1)
    ffn.add()
    do_attend_back(0, 2)
    do_project_back(0)
    ffn.add()
    do_send_down(0)
    chain.hold(top[1][1])
    finish(top[1], cover=True)
    do_attend_back(1, 0)
    ffn.add()
    do_send(0)
    do_attend_back(1, 1)
    ffn.add()
    do_attend_back(1, 2)
    attn_grad()
    chain.hold(shares_down[0][2])
    ffn.add()
    do_add_rows(0)
    attn.add()
    do_project_back(1)
    attn.add()
    ffn.forward()
    do_norm_one_back(0)
    attn.add()
    do_send(1)
    attn.add()
    do_send_down(1)
    ffn.forward()
    attn.add()
    attn.add()
    do_norm_one_back(1)
    do_vectors()
    ffn.forward()
    attn.add()
    chain.hold(shares_down[1][2])
    do_pass()
    do_add_rows(1)
    ffn.forward()
    do_pass()
    attn.store()
    do_pass()
    ffn.forward()
    do_pass()
    attn.store()
    do_pass()
    ffn.forward()
    do_pass()
    attn.store()
    ffn.forward()
    do_pass()
    attn.store()

    while len(vectors) <= len(hops):
        do_vectors()
    vector_sums = vectors[-1][0]
    up_bias_sum = vector_sums[6, :hidden]
    stack_sum = vector_sums[7, : 3 * width]

    def plain(j):
        return jnp.concatenate([stack_sum[3 * low + j * wide : 3 * low + (j + 1) * wide] for low, wide in pairs])

    return (
        jnp.stack(out_rows)[:, None],
        jnp.stack(grad_rows)[:, None],
        vector_sums[4],
        vector_sums[5],
        jnp.transpose(attn.outs[0].reshape(3, width, model), (2, 0, 1)),
        plain(0),
        plain(2),
        attn.outs[1],
        vector_sums[0],
        vector_sums[1],
        vector_sums[2],
        ffn.outs[1],
        up_bias_sum,
        ffn.outs[0],
        vector_sums[3],
    )


def solution(mesh):
    in_specs = (
        P(None, "wide", "narrow", None),
        P(None, "wide", "narrow", None),
        P(),
        P(),
        P(),
        P(),
        P(None, None, "narrow"),
        P("narrow"),
        P("narrow"),
        P("narrow", None),
        P(),
        P(),
        P(),
        P(None, "narrow"),
        P("narrow"),
        P("narrow", None),
        P(),
    )
    out_specs = (
        P(None, "wide", "narrow", None),
        P(None, "wide", "narrow", None),
        P(),
        P(),
        P(None, None, "narrow"),
        P("narrow"),
        P("narrow"),
        P("narrow", None),
        P(),
        P(),
        P(),
        P(None, "narrow"),
        P("narrow"),
        P("narrow", None),
        P(),
    )
    return jax.shard_map(local, mesh=mesh, in_specs=in_specs, out_specs=out_specs, check_vma=False)
```

```python
import functools

import jax
import jax.numpy as jnp
from jax import lax
from jax.experimental import pallas as pl
from jax.experimental.pallas import tpu as pltpu
from jax.sharding import PartitionSpec as P

HEAD = 64
LANES = 128
TILE = 256
norm_eps = 1e-05
score_scale = 0.125
bf16 = jnp.bfloat16
f32 = jnp.float32


class Chain:
    def __init__(self):
        self.last = []
        self.held = []

    def hold(self, *arrays):
        self.held += arrays

    def run(self, body, outs, *ins, smem=(), scratch=(), alias=None, anywhere=(), out_anywhere=(), limit=6, token=0, cover=False):
        unread = [*self.last, *self.held]
        count = len(smem) + len(ins)
        specs = [pl.BlockSpec(memory_space=pltpu.SMEM)] * len(smem)
        specs += [pl.BlockSpec(memory_space=pl.ANY if i in anywhere else pltpu.VMEM) for i in range(len(ins))]
        specs += [pl.BlockSpec(memory_space=pl.ANY)] * len(unread)

        def inner(*refs):
            body(*refs[:count], *refs[count + len(unread) :])

        made = pl.pallas_call(
            inner,
            out_shape=tuple(jax.ShapeDtypeStruct(*o) for o in outs),
            in_specs=specs,
            out_specs=tuple(
                pl.BlockSpec(memory_space=pl.ANY if i in out_anywhere else pltpu.VMEM) for i in range(len(outs))
            ),
            scratch_shapes=scratch,
            input_output_aliases={} if alias is None else {len(smem) + k: v for k, v in alias.items()},
            compiler_params=pltpu.CompilerParams(vmem_limit_bytes=limit << 20),
            cost_estimate=pl.CostEstimate(flops=10**12 if cover else 1, bytes_accessed=1, transcendentals=0),
            name=body.func.__name__ if isinstance(body, functools.partial) else body.__name__,
        )(*smem, *ins, *unread)
        self.last, self.held = [made[token]], []
        return made


def dot32(first, second, first_dim, second_dim):
    return lax.dot_general(
        first, second, (((first_dim,), (second_dim,)), ((), ())), preferred_element_type=f32
    )


def statistics(values):
    average = jnp.mean(values, axis=-1, keepdims=True)
    centred = values - average
    inverse = lax.rsqrt(jnp.mean(centred * centred, axis=-1, keepdims=True) + norm_eps)
    return centred * inverse, inverse


def norm_back(grad, normed, inverse, gain):
    scaled = grad * gain
    mean_one = jnp.mean(scaled, axis=-1, keepdims=True)
    mean_two = jnp.mean(scaled * normed, axis=-1, keepdims=True)
    return inverse * (scaled - mean_one - normed * mean_two)


def of_head(values, j, axis=1):
    if values.shape[axis] <= HEAD:
        return values
    place = lax.broadcasted_iota(jnp.int32, values.shape, axis)
    return jnp.where((place >= HEAD * j) & (place < HEAD * (j + 1)), values, jnp.zeros_like(values))


def head_pairs(width):
    return [(low, min(LANES, width - low)) for low in range(0, width, LANES)]


def relay(*refs, number):
    arrived, outs = refs[:number], refs[number:]
    each = len(outs) // number
    for i, rows in enumerate(arrived):
        size = rows.shape[0] // each
        for k in range(each):
            outs[i * each + k][...] = rows[k * size : (k + 1) * size, :]


def by_pairs(weight_t, out):
    width = out.shape[0] // 3
    for low, wide in head_pairs(width):
        for j in range(3):
            out[3 * low + j * wide : 3 * low + (j + 1) * wide, :] = weight_t[
                j * width + low : j * width + low + wide, :
            ]


def norm_one(tok, gain, bias, out, *, m):
    normed, _ = statistics(tok[m, 0].astype(f32))
    gain_row, bias_row = (v[...].astype(f32).reshape(1, -1) for v in (gain, bias))
    out[...] = (normed * gain_row + bias_row).astype(bf16)


def loss_grad(where, cells, queries, cot, m, count):
    number = queries[cells[where[0] + m * count]]
    scale = jnp.sqrt(jnp.full((1, cot.shape[3]), number, jnp.int32).astype(f32) / 500.0)
    return cot[m, 0].astype(f32) * scale


def scale_cot(where, cells, queries, cot, out, *, m, count):
    out[...] = loss_grad(where, cells, queries, cot, m, count).astype(bf16)


def project(*refs, parts):
    blocks = refs[:parts]
    weight, bias, scale = refs[parts : parts + 3]
    out, whole = refs[parts + 3 :]
    rows = blocks[0].shape[0]
    for b in range(parts):
        values = blocks[b][...]
        at = slice(b * rows, (b + 1) * rows)
        whole[at, :] = values
        out[at, :] = ((dot32(values, weight[...], 1, 1) + bias[...]) * scale[...]).astype(bf16)


def attend(qkv, out_weight, attended, logs, *outs, step):
    whole = qkv.shape[0]
    head = 0
    for low, wide in head_pairs(out_weight.shape[0]):
        heads = wide // HEAD
        key_pair = qkv[:, 3 * low + wide : 3 * low + 2 * wide]
        value_t = qkv[:, 3 * low + 2 * wide : 3 * low + 3 * wide].T
        keys = [of_head(key_pair, j) for j in range(heads)]
        values = [of_head(value_t, j, 0) for j in range(heads)]
        for start in range(0, whole, step):
            at = slice(start, start + step)
            query = qkv[at, 3 * low : 3 * low + wide]
            total = None
            for j in range(heads):
                scores = dot32(keys[j], query, 1, 1)
                top = jnp.max(scores, axis=0, keepdims=True)
                powers = jnp.exp(scores - top)
                length = jnp.sum(powers, axis=0, keepdims=True)
                mixed = dot32(values[j], powers.astype(bf16), 1, 0) * (1.0 / length)
                total = mixed if total is None else total + mixed
                logs[head + j : head + j + 1, at] = top + jnp.log(length)
            attended[at, low : low + wide] = total.T.astype(bf16)
        head += heads
    rows = whole // len(outs)
    for b, out in enumerate(outs):
        out[...] = dot32(attended[b * rows : (b + 1) * rows, :], out_weight[...], 1, 0).astype(bf16)


def pair_sum(first, second, out):
    out[...] = (first[...].astype(f32) + second[...].astype(f32)).astype(bf16)


def three(first, second, third):
    return first[...].astype(f32) + second[...].astype(f32) + third[...].astype(f32)


def norm_two(tok, first, second, third, out_bias, gain, bias, resid, normed, *, m):
    value = tok[m, 0].astype(f32) + three(first, second, third) + out_bias[...].astype(f32)
    resid[...] = value
    hat, _ = statistics(value)
    normed[...] = (hat * gain[...].astype(f32) + bias[...].astype(f32)).astype(bf16)


def feed(*refs, parts, blocks):
    normed, grads, refs = refs[:blocks], refs[blocks : blocks + parts], refs[blocks + parts :]
    up, up_bias, down, activ, pre_grad, bias_grad, normed_all, grads_all = refs
    for whole, pieces in ((normed_all, normed), (grads_all, grads)):
        low = 0
        for piece in pieces:
            whole[low : low + piece.shape[0], :] = piece[...]
            low += piece.shape[0]
    rows = grads[0].shape[0]
    for low in range(0, up.shape[1], TILE):
        cols = slice(low, low + TILE)
        total = None
        for b in range(parts):
            at = slice(b * rows, (b + 1) * rows)
            pre = dot32(normed_all[at, :], up[:, cols], 1, 0) + up_bias[:, cols].astype(f32)
            cumul = 0.5 + 0.5 * lax.erf(pre * 0.7071067811865476)
            density = jnp.exp(-0.5 * pre * pre) * 0.3989422804014327
            activ[at, cols] = (pre * cumul).astype(bf16)
            back = dot32(grads_all[at, :], down[cols, :], 1, 1)
            grad = (back * (cumul + pre * density)).astype(bf16)
            pre_grad[at, cols] = grad
            part = jnp.sum(grad.astype(f32), axis=0, keepdims=True)
            total = part if total is None else total + part
        bias_grad[:, cols] = total


def times(value, weight, *outs):
    put_tiles(outs, lambda at, cols: dot32(value[at, :], weight[:, cols], 1, 0), value.shape[0])


def times_back(value, weight, *outs):
    put_tiles(outs, lambda at, cols: dot32(value[at, :], weight[cols, :], 1, 1), value.shape[0])


def put_tiles(outs, share_of, whole):
    rows, model = outs[0].shape

    def tile(i, carry):
        cols = pl.ds(pl.multiple_of(i * TILE, TILE), TILE)
        for b, out in enumerate(outs):
            out[:, cols] = share_of(slice(b * rows, (b + 1) * rows), cols).astype(bf16)
        return carry

    lax.fori_loop(0, model // TILE, tile, 0)


def product(first, second, out):
    def tile(i, carry):
        rows = pl.ds(pl.multiple_of(i * TILE, TILE), TILE)
        out[rows, :] = dot32(first[:, rows], second[...], 0, 0).astype(bf16)
        return carry

    lax.fori_loop(0, out.shape[0] // TILE, tile, 0)


def weight_grad(where, first, second, other, *refs, before):
    chunks, whole = refs[before:-1], refs[-1]

    def tile(i, carry):
        rows = pl.ds(pl.multiple_of(i * TILE, TILE), TILE)
        total = dot32(first[:, rows], second[...], 0, 0) + other[rows, :].astype(f32)
        whole[rows, :] = total.astype(bf16)
        return carry

    lax.fori_loop(0, whole.shape[0] // TILE, tile, 0)
    if before:
        chunks, both = chunks[:-1], chunks[-1]
        size = chunks[0].shape[0]
        both[:size, :] = refs[0][...]
        put_chunks(where, chunks, whole)
        both[size:, :] = chunks[0][...]
    else:
        put_chunks(where, chunks, whole)


def ring_chunk(where, count, step):
    half = where[0] // 2
    place = jnp.where(where[0] % 2 == 0, half, count - 1 - half)
    return lax.rem(place + jnp.where(where[1] % 2 == 0, count - step, step), count)


def put_chunks(where, chunks, whole):
    for s, chunk in enumerate(chunks):
        size = chunk.shape[0]
        which = ring_chunk(where, len(chunks), (s + 1) % len(chunks)) if len(chunks) > 1 else 0
        chunk[...] = whole[pl.ds(pl.multiple_of(which * size, size), size), :]


def norm_two_back(where, cells, queries, cot, resid, first, second, third, gain, out, rounded, sums, *, m, count):
    top = loss_grad(where, cells, queries, cot, m, count)
    grad = three(first, second, third)
    hat, inverse = statistics(resid[...])
    back = top + norm_back(grad, hat, inverse, gain[...].astype(f32))
    out[...] = back
    rounded[...] = back.astype(bf16)
    sums[0:1, :] = jnp.sum(back, axis=0, keepdims=True)
    sums[1:2, :] = jnp.sum(grad * hat, axis=0, keepdims=True)
    sums[2:3, :] = jnp.sum(grad, axis=0, keepdims=True)
    sums[3:4, :] = jnp.sum(top, axis=0, keepdims=True)
    sums[4:8, :] = jnp.zeros_like(sums[4:8, :])


def attend_back(qkv, logs, mixed, out_weight, *refs, parts, step, low, wide):
    grads = refs[:parts]
    out, key_grad, value_grad, given, inner = refs[parts:]
    whole = qkv.shape[0]
    rows = whole // parts
    heads = wide // HEAD
    head = low // HEAD
    ones = jnp.concatenate([of_head(jnp.ones((8, wide), bf16), j) for j in range(heads)], axis=0)
    for b in range(parts):
        at = slice(b * rows, (b + 1) * rows)
        value = dot32(grads[b][...], out_weight[low : low + wide, :], 1, 1).astype(bf16)
        given[at, :] = value
        both = value.astype(f32) * mixed[at, low : low + wide].astype(f32)
        high = both.astype(bf16)
        rest = (both - high.astype(f32)).astype(bf16)
        inner[:, at] = dot32(ones, high, 1, 1) + dot32(ones, rest, 1, 1)
    key_pair = qkv[:, 3 * low + wide : 3 * low + 2 * wide]
    value_pair = qkv[:, 3 * low + 2 * wide : 3 * low + 3 * wide]
    key_t = key_pair.T
    keys = [of_head(key_pair, j) for j in range(heads)]
    values = [of_head(value_pair, j) for j in range(heads)]
    keys_t = [of_head(key_t, j, 0) for j in range(heads)]
    key_grad[...] = jnp.zeros_like(key_grad)
    value_grad[...] = jnp.zeros_like(value_grad)

    def block(i, carry):
        start = pl.multiple_of(i * step, step)
        query = qkv[pl.ds(start, step), 3 * low : 3 * low + wide]
        grad = given[pl.ds(start, step), :]
        total = None
        for j in range(heads):
            top = logs[head + j : head + j + 1, pl.ds(start, step)]
            row_sum = inner[8 * j : 8 * j + 1, pl.ds(start, step)]
            for row in range(0, whole, rows):
                at = slice(row, row + rows)
                weights = jnp.exp(dot32(keys[j][at], query, 1, 1) - top)
                score_grad = (weights * (dot32(values[j][at], grad, 1, 1) - row_sum)).astype(bf16)
                value_grad[at, :] += dot32(weights.astype(bf16), of_head(grad, j), 1, 0)
                key_grad[at, :] += dot32(score_grad, of_head(query, j), 1, 0)
                part = dot32(keys_t[j][:, at], score_grad, 1, 0)
                total = part if total is None else total + part
        out[pl.ds(start, step), :wide] = (total.T * score_scale).astype(bf16)
        return carry

    lax.fori_loop(0, whole // step, block, 0)
    out[:, wide : 2 * wide] = key_grad[...].astype(bf16)
    out[:, 2 * wide :] = value_grad[...].astype(bf16)


def project_back(*refs, pairs):
    grads, weight, outs, sums = refs[:pairs], refs[pairs], refs[pairs + 1 : -1], refs[-1]

    def share_of(at, cols):
        total, low = None, 0
        for grad in grads:
            wide = grad.shape[1]
            part = dot32(grad[at, :], weight[low : low + wide, cols], 1, 0)
            total = part if total is None else total + part
            low += wide
        return total

    put_tiles(outs, share_of, grads[0].shape[0])
    low = 0
    for grad in grads:
        wide = grad.shape[1]
        sums[:, low : low + wide] = jnp.sum(grad[...].astype(f32), axis=0, keepdims=True)
        low += wide


def projection_grad(where, *refs, micros, pairs, parts):
    normed, refs = refs[:micros], refs[micros:]
    grads, refs = [refs[m * pairs : (m + 1) * pairs] for m in range(micros)], refs[micros * pairs :]
    tops, refs = [refs[m * parts : (m + 1) * parts] for m in range(micros)], refs[micros * parts :]
    mixed, refs = refs[:micros], refs[micros:]
    chunks, out = refs[:-1], refs[-1]
    width = mixed[0].shape[1]
    rows = tops[0][0].shape[0]
    for p, (low, wide) in enumerate(head_pairs(width)):
        total = None
        for m in range(micros):
            part = dot32(grads[m][p][...], normed[m][...], 0, 0)
            total = part if total is None else total + part
        for j in range(3):
            out[j * width + low : j * width + low + wide, :] = total[j * wide : (j + 1) * wide].astype(bf16)
        total = None
        for m in range(micros):
            for b in range(parts):
                part = dot32(mixed[m][b * rows : (b + 1) * rows, low : low + wide], tops[m][b][...], 0, 0)
                total = part if total is None else total + part
        out[3 * width + low : 3 * width + low + wide, :] = total.astype(bf16)
    put_chunks(where, chunks, out)


def ring_add(arrived, *refs):
    low = 0
    for part in refs[:-1]:
        at = slice(low, low + part.shape[0])
        refs[-1][at, :] = (arrived[at, :].astype(f32) + part[...].astype(f32)).astype(bf16)
        low += part.shape[0]


def ring_store(where, *refs, steps, count, stacked):
    moved, refs = refs[: len(steps)], refs[len(steps) :]
    ahead, first, second, buffer, sems = refs[-5:]
    ahead[...] = moved[-1][...]
    size = buffer.shape[1] // 2 if stacked else buffer.shape[1]
    copies = []
    for k, step in enumerate(steps):
        buffer[k] = moved[k][...].astype(f32)
        row = pl.multiple_of(ring_chunk(where, count, step) * size, size)
        if stacked:
            for i, target in enumerate((first, second)):
                source = buffer.at[k, pl.ds(i * size, size), :]
                copies.append(pltpu.make_async_copy(source, target.at[pl.ds(row, size), :], sems.at[2 * k + i]))
                copies[-1].start()
        else:
            last = first.shape[0] - size
            to_first = pl.multiple_of(jnp.minimum(row, last), 16)
            to_second = pl.multiple_of(jnp.maximum(row - first.shape[0], 0), 16)
            copy_first = pltpu.make_async_copy(buffer.at[k], first.at[pl.ds(to_first, size), :], sems.at[2 * k])
            copy_second = pltpu.make_async_copy(buffer.at[k], second.at[pl.ds(to_second, size), :], sems.at[2 * k])
            pl.when(row <= last)(copy_first.start)
            pl.when(row > last)(copy_second.start)
            copies.append(copy_first)
    for copy in copies:
        copy.wait()


def norm_one_back(tok, resid_grad, first, second, third, gain, out, sums, *, m):
    grad = three(first, second, third)
    hat, inverse = statistics(tok[m, 0].astype(f32))
    out[...] = resid_grad[...] + norm_back(grad, hat, inverse, gain[...].astype(f32))
    sums[0:4, :] = jnp.zeros_like(sums[0:4, :])
    sums[4:5, :] = jnp.sum(grad * hat, axis=0, keepdims=True)
    sums[5:6, :] = jnp.sum(grad, axis=0, keepdims=True)
    sums[6:8, :] = jnp.zeros_like(sums[6:8, :])


def vector_sum(*refs):
    total = refs[0][...]
    for ref in refs[1:-1]:
        total = total + ref[...]
    refs[-1][...] = total


def ring_pass(moving, *refs, number, joined):
    refs[number][...] = moving[...]
    if joined:
        vector_join(*refs[:number], refs[number + 1], number=joined)
    elif number:
        vector_sum(*refs[:number], refs[number + 1])


def vector_join(first, second, *refs, number):
    up_bias, stack, out = refs[:number], refs[number:-1], refs[-1]
    out[...] = first[...] + second[...]
    for row, parts in ((6, up_bias), (7, stack)):
        total = parts[0][...]
        for part in parts[1:]:
            total = total + part[...]
        out[row : row + 1, : total.shape[1]] = total


def add_rows(resid, first, second, third, bias, out):
    out[...] = (resid[...] + three(first, second, third) + bias[...].astype(f32)).astype(bf16)


def swap(values, axis, bit):
    return lax.ppermute(values, axis, [(i, i ^ bit) for i in range(lax.axis_size(axis))])


def ring_order(count):
    return list(range(0, count, 2)) + list(range(1, count, 2))[::-1]


class Ring:
    def __init__(self, chain, where, shapes, stacked):
        self.chain, self.where, self.shapes, self.stacked = chain, where, shapes, stacked
        self.count = lax.axis_size("wide")
        cores = lax.axis_size("narrow")
        order = ring_order(self.count)
        self.perm = [
            (order[i] * cores + n, order[(i + (1 if n % 2 == 0 else -1)) % self.count] * cores + n)
            for i in range(self.count)
            for n in range(cores)
        ]
        self.have, self.step, self.stored, self.outs = [], 1, 0, None

    def pass_on(self, chunk):
        self.moving = lax.ppermute(chunk, ("wide", "narrow"), self.perm)

    def start(self, chunk, parts):
        self.parts = parts
        self.pass_on(chunk)

    def hold(self):
        self.chain.hold(self.moving)

    def add(self, cover=False):
        (made,) = self.chain.run(
            ring_add,
            [(self.moving.shape, bf16)],
            self.moving,
            *[p[self.step] for p in self.parts],
            cover=cover,
        )
        self.step += 1
        if self.step == self.count:
            self.have.append(made)
        self.pass_on(made)

    def forward(self):
        self.have.append(self.moving)
        copy = self.store()
        if len(self.have) < self.count:
            self.pass_on(copy)

    def arrive(self, made):
        self.have.append(made)
        if len(self.have) < self.count:
            self.pass_on(made)

    def store(self):
        steps = range(self.stored, len(self.have))
        self.stored = len(self.have)
        moved = [self.have[s] for s in steps]
        kept = () if self.outs is None else self.outs
        number = len(moved)
        made = self.chain.run(
            functools.partial(ring_store, steps=tuple(steps), count=self.count, stacked=self.stacked),
            [(moved[-1].shape, bf16)] + [(s, f32) for s in self.shapes],
            *moved,
            *kept,
            smem=(self.where,),
            scratch=[pltpu.VMEM((number, *moved[0].shape), f32), pltpu.SemaphoreType.DMA((2 * number,))],
            alias={number: 1, number + 1: 2} if kept else None,
            anywhere=(number, number + 1) if kept else (),
            out_anywhere=(1, 2),
            limit=6 + (number * moved[0].size * 4 >> 20),
        )
        self.outs = made[1:]
        return made[0]


class Whole:
    def __init__(self, shapes):
        self.shapes = shapes

    def start(self, chunk, parts):
        total = lax.psum(chunk, "wide").astype(f32)
        self.outs = (total[: self.shapes[0][0]], total[self.shapes[0][0] :])

    def hold(self):
        pass

    def add(self, cover=False):
        pass

    def forward(self):
        pass

    def store(self):
        pass


def local(
    tokens,
    cotangent,
    cell_of,
    query_count,
    attn_norm_gain,
    attn_norm_bias,
    input_weight,
    query_bias,
    value_bias,
    out_weight,
    out_bias,
    ffn_norm_gain,
    ffn_norm_bias,
    up_weight,
    up_bias,
    down_weight,
    down_bias,
):
    micros = range(tokens.shape[0])
    rows, model = tokens.shape[2], tokens.shape[3]
    parts = lax.axis_size("narrow")
    whole = rows * parts
    width = input_weight.shape[2]
    hidden = up_weight.shape[1]
    count = lax.axis_size("wide")
    rings = count <= 8
    chunks = count if rings else 1
    pairs = head_pairs(width)
    chain = Chain()
    run = chain.run
    where = jnp.stack([lax.axis_index("wide"), lax.axis_index("narrow")]).astype(jnp.int32)

    block = ((rows, model), bf16)
    outgoing = [block] * parts
    wide_rows = ((whole, model), bf16)
    row = lambda v: v.reshape(1, -1)
    gain_one, bias_one, gain_two, bias_two = map(row, (attn_norm_gain, attn_norm_bias, ffn_norm_gain, ffn_norm_bias))
    out_bias, down_bias, up_bias = row(out_bias), row(down_bias), row(up_bias)

    def columns(three_parts):
        return jnp.concatenate([v[:, low : low + wide] for low, wide in pairs for v in three_parts], axis=1)

    weight_t = jnp.transpose(input_weight, (1, 2, 0)).reshape(3 * width, model)
    zero = jnp.zeros((1, width), f32)
    project_bias = columns([row(query_bias).astype(f32), zero, row(value_bias).astype(f32)])
    project_scale = columns([zero + score_scale, zero + 1.0, zero + 1.0])

    def gather(own):
        return [own, swap(own, "narrow", 1), swap(own, "narrow", 2)]

    def finish(*arrived, pieces=1, cover=False):
        made = run(
            functools.partial(relay, number=len(arrived)),
            [((rows // pieces, model), bf16)] * (len(arrived) * pieces),
            *[a[2] for a in arrived],
            cover=cover,
        )
        for i, a in enumerate(arrived):
            own = made[i * pieces : (i + 1) * pieces]
            a[2:] = [*own, *[swap(piece, "narrow", 1) for piece in own]]

    def share(made):
        own, near, partner, far = made
        return [own, partner, swap(far, "narrow", 1), swap(near, "narrow", 1)]

    def send(shares):
        own, partner, far, near = shares
        (both,) = run(pair_sum, [block], partner, far)
        return [own, near, swap(both, "narrow", 2)]

    def fresh():
        return [None] * len(micros)

    normed, given, qkv, normed_all, mixed, logs, shares, shares_down, resid, normed_two_b = (fresh() for _ in range(10))
    activ, pre_grad, up_bias_grad, two_all, given_all, resid_grad, top = (fresh() for _ in range(7))
    sums_two, sums_one, stack_sums, out_rows, grad_rows = (fresh() for _ in range(5))
    pair_grads = [[] for _ in micros]

    def do_norm_one(m):
        (own,) = run(functools.partial(norm_one, m=m), [block], tokens, attn_norm_gain, attn_norm_bias)
        normed[m] = gather(own)

    def do_scale(m):
        (own,) = run(functools.partial(scale_cot, m=m, count=count), [block], cotangent, smem=(where, cell_of, query_count), cover=True)
        given[m] = gather(own)

    def do_project(m):
        qkv[m], normed_all[m] = run(
            functools.partial(project, parts=parts),
            [((whole, 3 * width), bf16), wide_rows],
            *normed[m],
            weight,
            project_bias,
            project_scale,
        )

    def do_attend(m):
        mixed[m], logs[m], *made = run(
            functools.partial(attend, step=whole),
            [((whole, width), bf16), ((8, whole), f32), *outgoing],
            qkv[m],
            out_weight,
            limit=24,
        )
        shares[m] = share(made)

    def do_send(m):
        shares[m] = send(shares[m])

    def do_norm_two(m):
        resid[m], own = run(
            functools.partial(norm_two, m=m),
            [((rows, model), f32), block],
            tokens,
            *shares[m],
            out_bias,
            gain_two,
            bias_two,
            cover=m == 0,
        )
        normed_two_b[m] = gather(own)

    def do_feed(m):
        activ[m], pre_grad[m], up_bias_grad[m], two_all[m], given_all[m] = run(
            functools.partial(feed, parts=parts, blocks=len(normed_two_b[m])),
            [((whole, hidden), bf16), ((whole, hidden), bf16), ((1, hidden), f32), wide_rows, wide_rows],
            *normed_two_b[m],
            *given[m],
            up_weight,
            up_bias,
            down_weight,
        )

    def do_up_back(m):
        shares[m] = share(run(times_back, outgoing, pre_grad[m], up_weight))

    def do_down(m):
        shares_down[m] = share(run(times, outgoing, activ[m], down_weight))

    def do_send_down(m):
        shares_down[m] = send(shares_down[m])

    def do_norm_two_back(m):
        resid_grad[m], own, sums_two[m] = run(
            functools.partial(norm_two_back, m=m, count=count),
            [((rows, model), f32), block, ((8, model), f32)],
            cotangent,
            resid[m],
            *shares[m],
            gain_two,
            smem=(where, cell_of, query_count),
            cover=m > 0,
        )
        top[m] = gather(own)

    def do_attend_back(m, p):
        low, wide = pairs[p]
        (made,) = run(
            functools.partial(attend_back, parts=parts, step=whole, low=low, wide=wide),
            [((whole, 3 * wide), bf16)],
            qkv[m],
            logs[m],
            mixed[m],
            out_weight,
            *top[m],
            scratch=[
                pltpu.VMEM((whole, wide), f32),
                pltpu.VMEM((whole, wide), f32),
                pltpu.VMEM((whole, wide), bf16),
                pltpu.VMEM((8 * (wide // HEAD), whole), f32),
            ],
            limit=20,
        )
        pair_grads[m].append(made)

    def do_project_back(m):
        *made, stack_sums[m] = run(
            functools.partial(project_back, pairs=len(pairs)),
            [*outgoing, ((1, 3 * width), f32)],
            *pair_grads[m],
            weight,
        )
        shares[m] = share(made)

    def do_norm_one_back(m):
        grad_rows[m], sums_one[m] = run(
            functools.partial(norm_one_back, m=m),
            [((rows, model), f32), ((8, model), f32)],
            tokens,
            resid_grad[m],
            *shares[m],
            gain_one,
        )

    hops = [("narrow", 1 << k) for k in range(parts.bit_length() - 1)]
    hops += [("wide", 1 << k) for k in range(count.bit_length() - 1)]
    vectors = []

    def next_vectors():
        done = len(vectors)
        if done == 0:
            return [*sums_one, *sums_two], 0
        if hops[done - 1][0] == "narrow" and hops[done][0] == "wide":
            return [*vectors[-1], *up_bias_grad, *stack_sums], len(micros)
        return vectors[-1], 0

    def add_vectors(own):
        done = len(vectors)
        vectors.append((own, swap(own, *hops[done])) if done < len(hops) else (own,))

    def do_vectors():
        given_now, joined = next_vectors()
        body = functools.partial(vector_join, number=joined) if joined else vector_sum
        add_vectors(run(body, [((8, model), f32)], *given_now)[0])

    def do_pass():
        if not rings:
            return
        given_now, joined = next_vectors() if len(vectors) <= len(hops) else ([], 0)
        if not given_now and len(attn.have) == count - 1:
            attn.have.append(attn.moving)
            return
        made = run(
            functools.partial(ring_pass, number=len(given_now), joined=joined),
            [(attn.moving.shape, bf16)] + ([((8, model), f32)] if given_now else []),
            attn.moving,
            *given_now,
        )
        attn.arrive(made[0])
        if given_now:
            add_vectors(made[1])

    def do_add_rows(m):
        (out_rows[m],) = run(add_rows, [block], resid[m], *shares_down[m], down_bias)

    def first_product(first, second):
        return run(product, [((first.shape[1], second.shape[1]), bf16)], first, second)[0]

    def ffn_grad(first, second, other, before=()):
        rows, cols = other.shape
        shapes = [((rows // chunks, cols), bf16)] * chunks
        if before:
            shapes.append(((2 * rows // chunks, cols), bf16))
        return run(
            functools.partial(weight_grad, before=len(before[:1])),
            shapes,
            first,
            second,
            other,
            *before[:1],
            smem=(where,),
            scratch=[pltpu.VMEM((rows, cols), bf16)],
            limit=16,
        )

    def attn_grad():
        made = run(
            functools.partial(projection_grad, micros=len(micros), pairs=len(pairs), parts=parts),
            [((4 * width // chunks, model), bf16)] * chunks,
            *normed_all,
            *[g for m in micros for g in pair_grads[m]],
            *[t for m in micros for t in top[m]],
            *mixed,
            smem=(where,),
            scratch=[pltpu.VMEM((4 * width, model), bf16)],
            limit=20,
        )
        attn.start(made[0], (made,))

    ffn_shapes = [(hidden, model), (model, hidden)]
    attn_shapes = [(3 * width, model), (width, model)]
    ffn = Ring(chain, where, ffn_shapes, True) if rings else Whole(ffn_shapes)
    attn = Ring(chain, where, attn_shapes, False) if rings else Whole(attn_shapes)

    do_norm_one(0)
    (weight,) = run(by_pairs, [((3 * width, model), bf16)], weight_t)
    chain.hold(normed[0][1])
    finish(normed[0])
    do_norm_one(1)
    do_scale(0)
    do_project(0)
    do_attend(0)
    chain.hold(normed[1][1], given[0][1])
    finish(normed[1], given[0], cover=True)
    do_scale(1)
    do_send(0)
    chain.hold(given[1][1])
    do_project(1)
    do_attend(1)
    chain.hold(given[1][2])
    do_norm_two(0)
    do_send(1)
    finish(given[1])
    chain.hold(normed_two_b[0][1])
    finish(normed_two_b[0], pieces=4)
    do_feed(0)
    do_norm_two(1)
    chain.hold(normed_two_b[1][1])
    do_up_back(0)
    down_first = first_product(activ[0], given_all[0])
    up_first = first_product(two_all[0], pre_grad[0])
    do_down(0)
    finish(normed_two_b[1], cover=True)
    do_send(0)
    do_feed(1)
    down_chunks = ffn_grad(activ[1], given_all[1], down_first)
    *up_chunks, both = ffn_grad(two_all[1], pre_grad[1], up_first, down_chunks)
    ffn.start(both, (down_chunks, up_chunks))
    do_up_back(1)
    do_norm_two_back(0)
    do_down(1)
    ffn.add()
    do_send(1)
    chain.hold(top[0][1])
    finish(top[0])
    do_attend_back(0, 0)
    ffn.add()
    do_attend_back(0, 1)
    do_norm_two_back(1)
    ffn.add()
    do_attend_back(0, 2)
    do_project_back(0)
    ffn.add()
    do_send_down(0)
    chain.hold(top[1][1])
    finish(top[1], cover=True)
    do_attend_back(1, 0)
    ffn.add()
    do_send(0)
    do_attend_back(1, 1)
    ffn.add()
    do_attend_back(1, 2)
    attn_grad()
    chain.hold(shares_down[0][2])
    ffn.add()
    do_add_rows(0)
    attn.add()
    do_project_back(1)
    attn.add()
    ffn.forward()
    do_norm_one_back(0)
    attn.add()
    do_send(1)
    attn.add()
    do_send_down(1)
    ffn.forward()
    attn.add()
    attn.add()
    do_norm_one_back(1)
    do_vectors()
    ffn.forward()
    attn.add()
    chain.hold(shares_down[1][2])
    do_pass()
    do_add_rows(1)
    ffn.forward()
    do_pass()
    attn.store()
    do_pass()
    ffn.forward()
    do_pass()
    attn.store()
    do_pass()
    ffn.forward()
    do_pass()
    attn.store()
    ffn.forward()
    do_pass()
    attn.store()

    while len(vectors) <= len(hops):
        do_vectors()
    vector_sums = vectors[-1][0]
    up_bias_sum = vector_sums[6, :hidden]
    stack_sum = vector_sums[7, : 3 * width]

    def plain(j):
        return jnp.concatenate([stack_sum[3 * low + j * wide : 3 * low + (j + 1) * wide] for low, wide in pairs])

    return (
        jnp.stack(out_rows)[:, None],
        jnp.stack(grad_rows)[:, None],
        vector_sums[4],
        vector_sums[5],
        jnp.transpose(attn.outs[0].reshape(3, width, model), (2, 0, 1)),
        plain(0),
        plain(2),
        attn.outs[1],
        vector_sums[0],
        vector_sums[1],
        vector_sums[2],
        ffn.outs[1],
        up_bias_sum,
        ffn.outs[0],
        vector_sums[3],
    )


def solution(mesh):
    in_specs = (
        P(None, "wide", "narrow", None),
        P(None, "wide", "narrow", None),
        P(),
        P(),
        P(),
        P(),
        P(None, None, "narrow"),
        P("narrow"),
        P("narrow"),
        P("narrow", None),
        P(),
        P(),
        P(),
        P(None, "narrow"),
        P("narrow"),
        P("narrow", None),
        P(),
    )
    out_specs = (
        P(None, "wide", "narrow", None),
        P(None, "wide", "narrow", None),
        P(),
        P(),
        P(None, None, "narrow"),
        P("narrow"),
        P("narrow"),
        P("narrow", None),
        P(),
        P(),
        P(),
        P(None, "narrow"),
        P("narrow"),
        P("narrow", None),
        P(),
    )
    return jax.shard_map(local, mesh=mesh, in_specs=in_specs, out_specs=out_specs, check_vma=False)
```
